32 devices in a mesh: section: 2 (over x), dp: 4 (over y, core), shard: 4 (over z).
Axes of the slice: x: 2, y: 2, z: 4, core: 2. Of those that a mesh axis runs over, the one named last changes fastest.
Arguments:
- token_ids: int32 [2, 16, 256], P(None, ('dp', 'shard')), may hold values from 0 to 30527
- targets: int32 [2, 16, 256], P(None, ('dp', 'shard')), may hold values from 0 to 30527
- segment_ids: int32 [2, 16, 256], P(None, ('dp', 'shard')), may hold values from 0 to 7, never falling along the last dimension, each value on 1 to 128 neighbouring positions
- word_table: bfloat16 [30528, 768], P('shard'), may hold values from -0.59765625 to 0.59765625
- pos_table: bfloat16 [512, 768], P('shard'), may hold values from -0.59765625 to 0.59765625
- embed_gain: bfloat16 [768], P('shard'), may hold values from 0.5 to 1.5
- embed_shift: bfloat16 [768], P('shard'), may hold values from -1.1953125 to 1.1953125
- qkv_weight: bfloat16 [2, 3, 4, 192, 192], P('section', None, None, 'shard'), may hold values from -0.4375 to 0.4375
- out_weight: bfloat16 [2, 768, 768], P('section', 'shard'), may hold values from -0.875 to 0.875
- ffn_in: bfloat16 [2, 4, 192, 768], P('section', None, 'shard'), may hold values from -0.4375 to 0.4375
- ffn_out: bfloat16 [2, 4, 768, 192], P('section', None, 'shard'), may hold values from -0.21875 to 0.21875
- layer_gains: bfloat16 [2, 2, 768], P('section', None, 'shard'), may hold values from 0.5 to 1.5
- layer_biases: bfloat16 [2, 9, 768], P('section', None, 'shard'), may hold values from -1.1953125 to 1.1953125
Outputs:
- layer_outputs: bfloat16 [2, 2, 16, 256, 768], P('section', None, ('dp', 'shard'))
- input_grads: float32 [2, 2, 16, 256, 768], P('section', None, ('dp', 'shard'))
- word_grad: float32 [30528, 768], P('shard', ('section', 'dp'))
- pos_grad: float32 [512, 768], P('shard')
- embed_gain_grad: float32 [768], P('shard')
- embed_shift_grad: float32 [768], P('shard')
- qkv_grad: float32 [2, 3, 4, 192, 192], P('section', None, None, 'shard')
- out_grad: float32 [2, 768, 768], P('section', 'shard')
- ffn_in_grad: float32 [2, 4, 192, 768], P('section', None, 'shard')
- ffn_out_grad: float32 [2, 4, 768, 192], P('section', None, 'shard')
- gains_grad: float32 [2, 2, 768], P('section', None, 'shard')
- biases_grad: float32 [2, 9, 768], P('section', None, 'shard')
The draws below stay inside these ranges and needn't reach their ends.
Inputs may be any that keep to these rules, and one draw needn't show every extreme that they name: `targets`: token ids. `segment_ids`: within each row of 256 positions the document number never falls; each document has 1 to 128 positions, and one has exactly 128.
All inputs are finite; a program needn't handle non-finite values.
Results may differ from the reference program's by a relative error of at most 0.018.
Values may be sent and summed in bfloat16 or wider, within the bound.
No kernel may reach another device: no remote copies, remote signals or barrier semaphores. Data moves between devices by JAX's collectives and lax.ppermute only.
A program may use at most 320 MiB of HBM per device.

```python
import math
import jax
import jax.numpy as jnp
import numpy as np
from jax import lax

D = 768
HEADS = 12
GROUPS = 4
VOCAB = 30528
POS = 512
SEQ = 256
MICRO = 2
SEGS = 8
GW = 192
GF = 768
ROWS = 16


def touch_ends(values, own_key, low, largest):
    longest = values.shape.index(max(values.shape))
    spots = []
    for shift in (0, 1):
        where = [jax.random.randint(jax.random.fold_in(own_key, axis), (), 0, length) for axis, length in enumerate(values.shape)]
        where[longest] = (where[longest] + shift) % values.shape[longest]
        spots.append(tuple(where))
    return values.at[spots[0]].set(low).at[spots[1]].set(largest)


def level_of(rng, dims, pieces, smallest, high):
    loudness = 1.0
    for position, shards_of in pieces:
        draws = jax.random.uniform(jax.random.fold_in(jax.random.fold_in(rng, 6), position), (shards_of,), jnp.float32, smallest / len(pieces), high / len(pieces))
        loudness = loudness * jnp.repeat(jnp.exp(draws), dims[position] // shards_of).reshape((-1,) + (1,) * (len(dims) - 1 - position))
    return loudness


def rank_table(number_of, lean):
    weights = [(1 << 20) // math.isqrt(standing ** lean) + 1 for standing in range(1, number_of + 1)]
    deviation = 1 + sum(weights) // (1 << 30)
    return np.cumsum(np.array([max(1, weight // deviation) for weight in weights]))


def ranked(own_key, shape, amount, lean):
    grid = rank_table(amount, lean)
    ticket = jax.random.randint(jax.random.fold_in(own_key, 1), shape, 0, int(grid[amount - 1]))
    grade = jnp.searchsorted(jnp.asarray(grid, jnp.int32), ticket, side="right")
    return jax.random.permutation(jax.random.fold_in(own_key, 2), amount)[grade].astype(jnp.int32)


def length_profile(amount, total, limit, skew):
    loads = [(1 << 20) // math.isqrt(standing ** skew) + 1 for standing in range(2, amount + 1)]
    spare, holding = total - limit - (amount - 1), [1] * (amount - 1)
    while spare > 0:
        free = [i for i in range(amount - 1) if holding[i] < limit]
        mass, budget = sum([loads[i] for i in free]), spare
        for i in free:
            more = min(limit - holding[i], max(1, budget * loads[i] // mass), spare)
            holding[i] = holding[i] + more
            spare = spare - more
    return np.array([limit] + holding)


def ragged_sizes(stream_key, number_of, total, most, lean):
    if number_of == 2:
        one = jax.random.randint(stream_key, (), max(1, total - most), min(most, total - 1) + 1)
        return jnp.stack([one, total - one])
    tallies = jnp.asarray(length_profile(number_of, total, most, lean), jnp.int32)
    pairs = (number_of - 1) // 2
    source_of, sink = tallies[1:1 + 2 * pairs:2], tallies[2:2 + 2 * pairs:2]
    room = jnp.minimum(source_of - 1, most - sink)
    moved = jax.random.randint(jax.random.fold_in(stream_key, 1), (pairs,), 0, 1 << 20) % (room + 1)
    tallies = tallies.at[1:1 + 2 * pairs:2].set(source_of - moved).at[2:2 + 2 * pairs:2].set(sink + moved)
    return tallies[jax.random.permutation(jax.random.fold_in(stream_key, 2), number_of)]


def centred(own_key, dims, width, limit, pieces=(), kind=jnp.bfloat16):
    result = width * jax.random.normal(own_key, dims, jnp.float32)
    if pieces:
        result = result * level_of(own_key, dims, pieces, -0.22, 0.18)
    return jnp.clip(result, -limit, limit).astype(kind)


def setup_inputs(seed: int = 0) -> dict:
    key_of = jax.random.split(jax.random.key(seed), 14)
    return {
        "token_ids": touch_ends(ranked(key_of[0], (MICRO, ROWS, SEQ), VOCAB, 2), jax.random.fold_in(key_of[0], 3), 0, VOCAB - 1).astype(jnp.int32),
        "targets": touch_ends(ranked(key_of[1], (MICRO, ROWS, SEQ), VOCAB, 2), jax.random.fold_in(key_of[1], 3), 0, VOCAB - 1).astype(jnp.int32),
        "segment_ids": jax.vmap(lambda own: jnp.searchsorted(jnp.cumsum(ragged_sizes(own, SEGS, SEQ, SEQ // 2, 1)), jnp.arange(SEQ), side="right"))(jax.random.split(key_of[2], MICRO * ROWS)).reshape((MICRO, ROWS, SEQ)).astype(jnp.int32),
        "word_table": centred(key_of[3], (VOCAB, D), 0.1, 0.59765625, ((0, 4),)),
        "pos_table": centred(key_of[4], (POS, D), 0.1, 0.59765625, ((0, 4),)),
        "embed_gain": jnp.clip(1.0 + 0.1 * jax.random.normal(key_of[5], (D,), jnp.float32), 0.5, 1.5).astype(jnp.bfloat16),
        "embed_shift": centred(key_of[6], (D,), 0.3, 1.1953125, ((0, 4),)),
        "qkv_weight": centred(key_of[7], (2, 3, GROUPS, GW, GW), GW ** -0.5, 0.4375, ((0, 2), (3, 4))),
        "out_weight": centred(key_of[8], (2, D, D), (D // 16) ** -0.5, 0.875, ((0, 2), (1, 4))),
        "ffn_in": centred(key_of[9], (2, GROUPS, GW, GF), GW ** -0.5, 0.4375, ((0, 2), (2, 4))),
        "ffn_out": centred(key_of[10], (2, GROUPS, GF, GW), GF ** -0.5, 0.21875, ((0, 2), (2, 4))),
        "layer_gains": jnp.clip(1.0 + 0.1 * jax.random.normal(key_of[11], (2, 2, D), jnp.float32), 0.5, 1.5).astype(jnp.bfloat16),
        "layer_biases": centred(key_of[12], (2, 9, D), 0.3, 1.1953125, ((0, 2), (2, 4))),
    }


@jax.custom_vjp
def low(v):
    return lax.optimization_barrier(v.astype(jnp.bfloat16)).astype(jnp.float32)

@jax.custom_vjp
def low_back(v):
    return v

def low_keep(v):
    return (low(v), None)

def low_pass(kept, grad):
    return (grad,)

def back_keep(v):
    return (v, None)

def back_low(kept, grad):
    return (low(grad),)
low.defvjp(low_keep, low_pass)
low_back.defvjp(back_keep, back_low)
EPSILON = 1e-06
MASKED = -1000000000.0
HIGHEST = lax.Precision.HIGHEST

def layer_norm(inputs, gain_row, shift_row):
    centered = inputs - lax.optimization_barrier(jnp.mean(inputs, axis=-1, keepdims=True))
    variance = lax.optimization_barrier(jnp.mean(centered * centered, axis=-1, keepdims=True))
    return centered * lax.rsqrt(variance + EPSILON) * gain_row + shift_row

def grouped(inputs, weight):
    seq_len = inputs.shape[0]
    group_count = weight.shape[0]
    split = inputs.reshape(seq_len, group_count, -1)
    return jnp.einsum('sgi,gio->sgo', split, weight, precision=HIGHEST).reshape(seq_len, -1)

def places(segments):
    seq_len = segments.shape[0]
    same_doc = segments[:, None] == segments[None, :]
    order = jnp.arange(seq_len, dtype=jnp.int32)
    before = order[None, :] < order[:, None]
    return (lax.optimization_barrier(jnp.sum((same_doc & before).astype(jnp.int32), axis=1)).astype(jnp.int32), same_doc)

def layer_apply(layer_in, same_doc, w_qkv, w_out, w_in, w_back, norm_gains, biases):
    seq_len, model_width = layer_in.shape
    head_size = model_width // HEADS
    input_low = low(layer_in)
    queries = low_back(low(grouped(input_low, w_qkv[0])))
    key_low = low_back(low(grouped(input_low, w_qkv[1])))
    value_low = low_back(low(grouped(input_low, w_qkv[2]) + biases[0]))
    q_heads = queries.reshape(seq_len, HEADS, head_size)
    k_heads = key_low.reshape(seq_len, HEADS, head_size)
    v_heads = value_low.reshape(seq_len, HEADS, head_size)
    scores = low_back(jnp.einsum('qhd,khd->hqk', q_heads, k_heads, precision=HIGHEST) * (1.0 / math.sqrt(head_size)))
    scores = jnp.where(same_doc[None], scores, MASKED)
    attn_probs = jax.nn.softmax(scores, axis=-1)
    attended = low_back(low(jnp.einsum('hqk,khd->qhd', low(attn_probs), v_heads, precision=HIGHEST).reshape(seq_len, model_width)))
    branch = low_back(jnp.dot(attended, w_out, precision=HIGHEST) + biases[1])
    middle = layer_norm(layer_in + branch, norm_gains[0], biases[2])
    pre_gelu = low_back(grouped(low(middle), w_in) + biases[3:7].reshape(-1))
    activated = low(jax.nn.gelu(pre_gelu, approximate=False))
    ffn_branch = low_back(grouped(activated, w_back) + biases[7])
    return layer_norm(middle + ffn_branch, norm_gains[1], biases[8])

def reference(token_ids, targets, segment_ids, word_table, pos_table, embed_gain, embed_shift, qkv_weight, out_weight, ffn_in, ffn_out, layer_gains, layer_biases):
    micro_count, row_count, seq_len = token_ids.shape
    model_width = word_table.shape[1]
    flat_rows = micro_count * row_count
    id_flat = token_ids.reshape(flat_rows, seq_len)
    target_flat = targets.reshape(flat_rows, seq_len)
    doc_flat = segment_ids.reshape(flat_rows, seq_len)
    params = tuple((item.astype(jnp.float32) for item in (word_table, pos_table, embed_gain, embed_shift, qkv_weight, out_weight, ffn_in, ffn_out, layer_gains, layer_biases)))
    zero_rows = jnp.zeros((flat_rows, seq_len, model_width), jnp.float32)

    def total_loss(weights, first_add, second_add):
        table, ptable, egain, eshift, w_qkv, w_out, w_in, w_back, norm_gains, biases = weights

        def per_row(running, inputs):
            ids_row, target_row, doc_row, add_one, add_two = inputs
            where_at, same_doc = places(doc_row)
            embedded = layer_norm(jnp.take(table, ids_row, axis=0) + jnp.take(ptable, where_at, axis=0), egain, eshift)
            first_out = layer_apply(embedded + add_one, same_doc, w_qkv[0], w_out[0], w_in[0], w_back[0], norm_gains[0], biases[0])
            first_low = low(first_out)
            second_out = layer_apply(low_back(first_low) + add_two, same_doc, w_qkv[1], w_out[1], w_in[1], w_back[1], norm_gains[1], biases[1])
            second_low = low(second_out)
            logits = low_back(jnp.dot(second_low, table.T, precision=HIGHEST))
            picked = jnp.take_along_axis(logits, target_row[:, None], axis=-1)[:, 0]
            row_loss = jnp.sum(jax.nn.logsumexp(logits, axis=-1) - picked)
            return (running + row_loss, (first_low, second_low))
        summed, outputs = lax.scan(jax.checkpoint(per_row), jnp.zeros((), jnp.float32), (id_flat, target_flat, doc_flat, first_add, second_add))
        return (summed, outputs)
    summed, pullback, outputs = jax.vjp(total_loss, params, zero_rows, zero_rows, has_aux=True)
    weight_grads, first_grad, second_grad = pullback(jnp.ones((), jnp.float32))
    shape_out = (2, micro_count, row_count, seq_len, model_width)
    layer_outputs = jnp.stack([outputs[0], outputs[1]]).reshape(shape_out).astype(jnp.bfloat16)
    input_grads = jnp.stack([first_grad, second_grad]).reshape(shape_out)
    return (layer_outputs, input_grads, weight_grads[0], weight_grads[1], weight_grads[2], weight_grads[3], weight_grads[4], weight_grads[5], weight_grads[6], weight_grads[7], weight_grads[8], weight_grads[9])
```

```python
import math

import jax
import jax.numpy as jnp
from jax import lax
from jax.experimental import pallas as pl
from jax.experimental.pallas import tpu as pltpu
from jax.sharding import PartitionSpec as P

HEADS = 12
EPSILON = 1e-06
MASKED = -1000000000.0
F32 = jnp.float32
BF16 = jnp.bfloat16
MIB = 1 << 20


def nn(a, b):
    return jnp.dot(a, b, preferred_element_type=F32)


def nt(a, b):
    return lax.dot_general(a, b, (((1,), (1,)), ((), ())), preferred_element_type=F32)


def tn(a, b):
    return lax.dot_general(a, b, (((0,), (0,)), ((), ())), preferred_element_type=F32)


def iota(shape, axis):
    return lax.broadcasted_iota(jnp.int32, shape, axis)


def group_of(index, width, count):
    total = jnp.zeros(index.shape, jnp.int32)
    for step in range(1, count):
        total = total + (index >= step * width).astype(jnp.int32)
    return total


def normed(value):
    centered = value - jnp.mean(value, axis=-1, keepdims=True)
    scale = lax.rsqrt(jnp.mean(centered * centered, axis=-1, keepdims=True) + EPSILON)
    return centered * scale, scale


def norm_back(grad, unit, scale, gain):
    inner = grad * gain
    first = jnp.mean(inner, axis=-1, keepdims=True)
    second = jnp.mean(inner * unit, axis=-1, keepdims=True)
    return scale * (inner - first - unit * second)


def col_sum(value):
    return jnp.sum(value, axis=0, keepdims=True)


def call(kernel, outs, ins, specs=None, scratch=(), limit=56, flops=0, moved=0, grid=None, out_specs=None, name=None):
    vmem = pl.BlockSpec(memory_space=pltpu.VMEM)
    extra = {} if grid is None else {"grid": grid}
    return pl.pallas_call(
        kernel,
        out_shape=outs,
        in_specs=[vmem if s is None else s for s in (specs or [None] * len(ins))],
        out_specs=out_specs if out_specs is not None else [vmem] * len(outs),
        scratch_shapes=list(scratch),
        compiler_params=pltpu.CompilerParams(vmem_limit_bytes=limit * MIB),
        cost_estimate=pl.CostEstimate(flops=flops, bytes_accessed=moved, transcendentals=0),
        name=name,
        **extra,
    )(*ins)


def like(shape, dtype):
    return jax.ShapeDtypeStruct(shape, dtype)


def turned(block, axis, by):
    size = lax.axis_size(axis)
    return lax.ppermute(block, axis, [(i, (i + by) % size) for i in range(size)])


def crossed(block, axis, bit):
    return lax.ppermute(block, axis, [(i, i ^ bit) for i in range(lax.axis_size(axis))])


def ring_gather(block, axis):
    half = block.shape[0] // 2
    before = turned(block, axis, 1)
    after = turned(block, axis, -1)
    return before, after, turned(before[:half], axis, 1), turned(after[half:], axis, -1)


class Sizes:
    def __init__(self, qkv, out, shards, pos_rows):
        _, _, groups, part, width = qkv
        self.shards, self.groups, self.gw, self.gi = shards, groups, width, part
        self.d = out[2]
        self.ds = out[1]
        self.gf = self.d // shards
        self.at_qkv = self.ds
        self.at_small = self.ds + 3 * part
        self.at_out = groups * part
        self.rows = self.at_out + self.gf
        self.extra = pos_rows // 2 + 16


def pack_weights(z, qkv, out, fin, fout, gains, biases, egain, eshift):
    def kernel(qkv_ref, out_ref, fin_ref, fout_ref, gain_ref, bias_ref, eg_ref, es_ref, o_ref):
        core = lax.axis_index("dp") % 2
        shard = lax.axis_index("shard")

        def spread(pieces):
            return jnp.concatenate([piece.astype(F32) for piece in pieces], axis=1)

        @pl.when(core == 0)
        def _():
            o_ref[0 : z.ds] = out_ref[...]
            for c in range(3):
                row = z.at_qkv + c * z.gi
                o_ref[row : row + z.gi] = spread([qkv_ref[c, g] for g in range(z.groups)]).astype(BF16)
            tall = jnp.concatenate(
                [gain_ref[...].astype(F32), bias_ref[...].astype(F32), eg_ref[...].astype(F32), es_ref[...].astype(F32), jnp.zeros((3, z.ds), F32)],
                axis=0,
            )
            wide = jnp.concatenate([tall] * z.shards, axis=1)
            lane = group_of(iota(wide.shape, 1), z.ds, z.shards)
            o_ref[z.at_small : z.at_small + 16] = jnp.where(lane == shard, wide, 0.0).astype(BF16)
            o_ref[z.at_small + 16 : z.rows] = jnp.zeros((z.rows - z.at_small - 16, z.d), BF16)

        @pl.when(core == 1)
        def _():
            o_ref[0 : z.at_out] = fin_ref[...].reshape(z.at_out, z.d)
            o_ref[z.at_out : z.rows] = spread([fout_ref[g] for g in range(z.groups)]).astype(BF16)

    return call(kernel, [like((z.rows, z.d), BF16)], (qkv, out, fin, fout, gains, biases, egain, eshift), name="pack")[0]


def piece_specs():
    return [pl.BlockSpec(memory_space=pl.ANY)] * 10


def piece_copies(z, refs, w_ref, sems):
    core = lax.axis_index("dp") % 2
    shard = lax.axis_index("shard")
    half = z.rows // 2
    copies = []
    for side in range(2):
        own, before, after, far_a, far_b = refs[5 * side : 5 * side + 5]
        place = core if side == 0 else 1 - core
        for ref, by, row, many in ((own, 0, 0, z.rows), (before, 3, 0, z.rows), (after, 1, 0, z.rows), (far_a, 2, 0, half), (far_b, 2, half, half)):
            index = (shard + by) % z.shards
            copies.append(
                pltpu.make_async_copy(ref, w_ref.at[place, index, pl.ds(row, many)], sems.at[len(copies)])
            )
    return copies


class Weights:
    def __init__(self, z, w_ref):
        self.z, self.w = z, w_ref

    def out(self):
        z = self.z
        return self.w[0, :, 0 : z.ds, :].reshape(z.d, z.d)

    def small(self):
        z = self.z
        return sum(self.w[0, h, z.at_small : z.at_small + 16, :].astype(F32) for h in range(z.shards))

    def proj(self, c):
        z = self.z
        row = z.at_qkv + c * z.gi
        dense = self.w[0, :, row : row + z.gi, :].reshape(z.gw, z.d)
        tall = jnp.concatenate([dense] * z.groups, axis=0)
        keep = group_of(iota(tall.shape, 0), z.gw, z.groups) == group_of(iota(tall.shape, 1), z.gw, z.groups)
        return jnp.where(keep, tall, jnp.zeros_like(tall))

    def fin(self, g):
        z = self.z
        dense = self.w[1, :, g * z.gi : (g + 1) * z.gi, :].reshape(z.gw, z.d)
        blank = jnp.zeros_like(dense)
        return jnp.concatenate([dense, blank] if g % 2 == 0 else [blank, dense], axis=0)

    def fout(self, g):
        z = self.z
        at = (g // 2) * 2 * z.gw
        pair = self.w[1, :, z.at_out : z.rows, at : at + 2 * z.gw].reshape(z.d, 2 * z.gw)
        keep = (iota(pair.shape, 1) >= z.gw) == (g % 2 == 1)
        return jnp.where(keep, pair, jnp.zeros_like(pair))


def embed_parts(picked, inside, seg_col, seg_row, pos_table):
    count, seq = seg_row.shape
    width = picked.shape[1]
    half = seq // 2
    rows = pos_table.shape[0]

    def kernel(p_ref, i_ref, c_ref, r_ref, t_ref, c0, c1, c2a, c2b, c3):
        start = lax.axis_index("shard") * rows
        for k in range(count):
            span = slice(k * seq, (k + 1) * seq)
            same = c_ref[span] == r_ref[k : k + 1]
            earlier = iota((seq, seq), 1) < iota((seq, seq), 0)
            place = jnp.sum(jnp.where(same & earlier, 1.0, 0.0), axis=1, keepdims=True).astype(jnp.int32) - start
            spot = (iota((seq, rows), 1) == place).astype(BF16)
            word = jnp.where(i_ref[span] > 0, p_ref[span].astype(F32), 0.0)
            total = (word + nn(spot, t_ref[...])).astype(BF16)
            if k == 2:
                c2a[...] = total[:half]
                c2b[...] = total[half:]
            else:
                (c0, c1, None, c3)[k][...] = total

    full, part = like((seq, width), BF16), like((half, width), BF16)
    return call(kernel, [full, full, part, part, full], (picked, inside, seg_col, seg_row, pos_table), name="embed_parts")


def layer_forward(z, pieces, seg_col, seg_row, first, words=None, layer_in=None):
    seq = seg_col.shape[0]
    d, wide = z.d, z.groups * z.d
    names = ["out", "q", "k", "v", "p", "att", "n1", "mid", "act", "slope", "n2", "stats"]
    shapes = [
        like((seq, d), BF16),
        like((seq, d), BF16),
        like((seq, d), BF16),
        like((seq, d), BF16),
        like((HEADS, seq, seq), BF16),
        like((seq, d), BF16),
        like((seq, d), F32),
        like((seq, d), BF16),
        like((seq, wide), BF16),
        like((seq, wide), BF16),
        like((seq, d), F32),
        like((seq, 128), F32),
    ]
    if first:
        names += ["x", "n0"]
        shapes += [like((seq, d), BF16), like((seq, d), F32)]
    head = d // HEADS
    inputs = list(words) if first else [layer_in]

    def kernel(*refs):
        piece_refs, refs = refs[:10], refs[10:]
        col_ref, row_ref, refs = refs[0], refs[1], refs[2:]
        in_refs, refs = refs[: len(inputs)], refs[len(inputs) :]
        o = dict(zip(names, refs))
        w_ref, sems = refs[len(names)], refs[len(names) + 1]
        copies = piece_copies(z, piece_refs, w_ref, sems)
        for copy in copies:
            copy.start()
        for copy in copies:
            copy.wait()
        w = Weights(z, w_ref)
        small = w.small()
        if first:
            embed_sum = sum(ref[...].astype(F32) for ref in in_refs)
            unit, r0 = normed(embed_sum)
            o["n0"][...] = unit
            x = unit * small[11:12] + small[12:13]
            x_low = x.astype(BF16)
            o["x"][...] = x_low
        else:
            r0 = jnp.zeros((seq, 1), F32)
            x_low = in_refs[0][...]
            x = x_low.astype(F32)
        q = (nn(x_low, w.proj(0)).astype(BF16).astype(F32) * (1.0 / math.sqrt(head))).astype(BF16)
        k = nn(x_low, w.proj(1)).astype(BF16)
        v = (nn(x_low, w.proj(2)) + small[2:3]).astype(BF16)
        o["q"][...], o["k"][...], o["v"][...] = q, k, v
        same = col_ref[...] == row_ref[...]
        second = iota((seq, 128), 1) >= head
        tiles = []
        for t in range(d // 128):
            lanes = slice(t * 128, (t + 1) * 128)
            q_t, k_t, v_t = q[:, lanes], k[:, lanes], v[:, lanes]
            results = []
            for j in range(2):
                picked = jnp.where(second == (j == 1), q_t, jnp.zeros_like(q_t))
                scores = jnp.where(same, nt(picked, k_t), MASKED)
                scores = jnp.exp(scores - jnp.max(scores, axis=-1, keepdims=True))
                probs = (scores * (1.0 / jnp.sum(scores, axis=-1, keepdims=True))).astype(BF16)
                o["p"][2 * t + j] = probs
                results.append(nn(probs, v_t))
            tiles.append(jnp.where(second, results[1], results[0]).astype(BF16))
        attended = jnp.concatenate(tiles, axis=1)
        o["att"][...] = attended
        unit, r1 = normed(x + (nn(attended, w.out()) + small[3:4]))
        o["n1"][...] = unit
        middle = unit * small[0:1] + small[4:5]
        middle_low = middle.astype(BF16)
        o["mid"][...] = middle_low
        back = [None] * (z.groups // 2)
        for g in range(z.groups):
            pair = slice((g // 2) * 2 * z.gw, (g // 2 + 1) * 2 * z.gw)
            span = slice(g * d, (g + 1) * d)
            pre = nn(middle_low[:, pair], w.fin(g)) + small[5 + g : 6 + g]
            half = 0.5 + 0.5 * lax.erf(pre * math.sqrt(0.5))
            slope = half + pre * (jnp.exp(-0.5 * pre * pre) * (1.0 / math.sqrt(2.0 * math.pi)))
            active = (pre * half).astype(BF16)
            o["act"][:, span] = active
            o["slope"][:, span] = slope.astype(BF16)
            added = nn(active, w.fout(g))
            back[g // 2] = added if back[g // 2] is None else back[g // 2] + added
        unit, r2 = normed(middle + (jnp.concatenate(back, axis=1) + small[9:10]))
        o["n2"][...] = unit
        o["out"][...] = (unit * small[1:2] + small[10:11]).astype(BF16)
        lane = iota((seq, 128), 1)
        o["stats"][...] = jnp.where(lane == 0, r0, jnp.where(lane == 1, r1, r2))

    outs = call(
        kernel,
        shapes,
        (*pieces, seg_col, seg_row, *inputs),
        specs=piece_specs() + [None] * (2 + len(inputs)),
        scratch=[pltpu.VMEM((2, z.shards, z.rows, d), BF16), pltpu.SemaphoreType.DMA((10,))],
        flops=3 * 10**9,
        moved=16 * MIB,
        name="layer_first" if first else "layer_second",
    )
    return dict(zip(names, outs))


def layer_backward(z, pieces, state, out_grad, first, seg_col=None, seg_row=None, pos_rows=0):
    seq, d = state["q"].shape
    wide = z.groups * d
    head = d // HEADS
    keys = ["x", "q", "k", "v", "p", "att", "n1", "mid", "act", "slope", "n2", "stats"] + (["n0"] if first else [])
    inputs = [state[key] for key in keys] + [out_grad] + ([seg_col, seg_row] if first else [])
    rows = z.rows + (z.extra if first else 0)
    outs = [like((seq, d), F32), like((2, z.shards, rows, d), BF16)]
    if first:
        outs.append(like((d, seq), BF16))

    def kernel(*refs):
        piece_refs, refs = refs[:10], refs[10:]
        s = dict(zip(keys, refs))
        refs = refs[len(keys) :]
        dy_ref, refs = refs[0], refs[1:]
        if first:
            col_ref, row_ref, refs = refs[0], refs[1], refs[2:]
        dx_ref, g_ref = refs[0], refs[1]
        de_ref = refs[2] if first else None
        w_ref, sems = refs[len(outs)], refs[len(outs) + 1]
        core = lax.axis_index("dp") % 2
        keep0 = core
        keep1 = 1 - core
        copies = piece_copies(z, piece_refs, w_ref, sems)
        for copy in copies:
            copy.start()
        for copy in copies:
            copy.wait()
        w = Weights(z, w_ref)
        small = w.small()
        stats = s["stats"][...]
        r0, r1, r2 = stats[:, 0:1], stats[:, 1:2], stats[:, 2:3]
        dy = dy_ref[...].astype(F32)
        n2 = s["n2"][...]
        gain_two, shift_two = col_sum(dy * n2), col_sum(dy)
        d_final = norm_back(dy, n2, r2, small[1:2])
        d_ffn = d_final.astype(BF16)
        ffn_shift = col_sum(d_ffn.astype(F32))
        middle_t = s["mid"][...].T
        pre_shift = []
        pair_back = [None] * (z.groups // 2)
        for p in range(z.groups // 2):
            lanes = slice(p * 2 * z.gw, (p + 1) * 2 * z.gw)
            out_pair = d_ffn[:, lanes]
            back_pair = []
            for g in (2 * p, 2 * p + 1):
                span = slice(g * d, (g + 1) * d)
                d_pre = (nt(out_pair, w.fout(g)) * s["slope"][:, span].astype(F32)).astype(BF16)
                pre_shift.append(col_sum(d_pre.astype(F32)))
                back_pair.append(tn(s["act"][:, span], out_pair))
                grad_in = nn(middle_t[g * z.gw : (g + 1) * z.gw], d_pre)
                g_ref[keep1, :, g * z.gi : (g + 1) * z.gi, :] = grad_in.astype(BF16).reshape(z.shards, z.gi, d)
                added = nt(d_pre, w.fin(g))
                pair_back[p] = added if pair_back[p] is None else pair_back[p] + added
            odd = iota(back_pair[0].shape, 1) >= z.gw
            both = jnp.where(odd, back_pair[1], back_pair[0]).astype(BF16)
            g_ref[keep1, :, z.at_out : z.rows, lanes] = both.reshape(z.shards, z.gf, 2 * z.gw)
        d_middle = d_final + jnp.concatenate(pair_back, axis=1)
        n1 = s["n1"][...]
        gain_one, shift_one = col_sum(d_middle * n1), col_sum(d_middle)
        d_mid = norm_back(d_middle, n1, r1, small[0:1])
        d_branch = d_mid.astype(BF16)
        branch_shift = col_sum(d_branch.astype(F32))
        attended = s["att"][...]
        g_ref[keep0, :, 0 : z.ds, :] = tn(attended, d_branch).astype(BF16).reshape(z.shards, z.ds, d)
        d_att = nt(d_branch, w.out()).astype(BF16)
        second = iota((seq, 128), 1) >= head
        scale = 1.0 / math.sqrt(head)
        dq, dk, dv = [], [], []
        for t in range(d // 128):
            lanes = slice(t * 128, (t + 1) * 128)
            q_t, k_t, v_t, a_t = s["q"][:, lanes], s["k"][:, lanes], s["v"][:, lanes], d_att[:, lanes]
            parts = []
            for j in range(2):
                a_j = jnp.where(second == (j == 1), a_t, jnp.zeros_like(a_t))
                probs_low = s["p"][2 * t + j]
                probs = probs_low.astype(F32)
                d_probs = nt(a_j, v_t)
                inner = jnp.sum(probs * d_probs, axis=-1, keepdims=True)
                d_scores = (probs * (d_probs - inner)).astype(BF16)
                parts.append((nn(d_scores, k_t), tn(d_scores, q_t), tn(probs_low, a_t)))
            dq.append((jnp.where(second, parts[1][0], parts[0][0]) * scale).astype(BF16))
            dk.append(jnp.where(second, parts[1][1], parts[0][1]).astype(BF16))
            dv.append(jnp.where(second, parts[1][2], parts[0][2]).astype(BF16))
        value_shift = col_sum(jnp.concatenate(dv, axis=1).astype(F32))
        x_t = s["x"][...].T
        d_in = d_mid
        for c, parts in enumerate((dq, dk, dv)):
            d_c = jnp.concatenate(parts, axis=1)
            full = nn(x_t, d_c)
            lane = group_of(iota((z.gw, d), 1), z.gw, z.groups)
            grad = full[0 : z.gw]
            for g in range(1, z.groups):
                grad = jnp.where(lane == g, full[g * z.gw : (g + 1) * z.gw], grad)
            row = z.at_qkv + c * z.gi
            g_ref[keep0, :, row : row + z.gi, :] = grad.astype(BF16).reshape(z.shards, z.gi, d)
            d_in = d_in + nt(d_c, w.proj(c))
        dx_ref[...] = d_in
        small_grads = jnp.concatenate(
            [gain_one, gain_two, value_shift, branch_shift, shift_one, *pre_shift, ffn_shift, shift_two, jnp.zeros((5, d), F32)], axis=0
        ).astype(BF16)
        blank = jnp.zeros((z.rows - z.at_small - 16, d), BF16)
        for h in range(z.shards):
            g_ref[keep0, h, z.at_small : z.at_small + 16, :] = small_grads
            g_ref[keep0, h, z.at_small + 16 : z.rows, :] = blank
        if first:
            n0 = s["n0"][...]
            embed_grads = jnp.concatenate([col_sum(d_in * n0), col_sum(d_in), jnp.zeros((14, d), F32)], axis=0).astype(BF16)
            d_embed = norm_back(d_in, n0, r0, small[11:12])
            d_embed_low = d_embed.astype(BF16)
            de_ref[...] = d_embed.T.astype(BF16)
            same = col_ref[...] == row_ref[...]
            later = iota((seq, seq), 0) < iota((seq, seq), 1)
            place = jnp.sum(jnp.where(same & later, 1.0, 0.0), axis=0, keepdims=True).astype(jnp.int32)
            spot = (iota((pos_rows, seq), 0) == place).astype(BF16)
            pos_grad = nn(spot, d_embed_low).astype(BF16)
            half = pos_rows // 2
            for side, place in enumerate((keep0, keep1)):
                for h in range(z.shards):
                    part = pos_grad[side * half : (side + 1) * half]
                    g_ref[place, h, z.rows : z.rows + half, :] = part if h == 0 else jnp.zeros_like(part)
                    g_ref[place, h, z.rows + half : z.rows + half + 16, :] = embed_grads

    return call(
        kernel,
        outs,
        (*pieces, *inputs),
        specs=piece_specs() + [None] * len(inputs),
        scratch=[pltpu.VMEM((2, z.shards, z.rows, d), BF16), pltpu.SemaphoreType.DMA((10,))],
        flops=8 * 10**9,
        moved=20 * MIB,
        limit=60,
        name="layer_first_back" if first else "layer_second_back",
    )


def head_forward(rows, table):
    count, d = rows.shape
    vocab = table.shape[0]
    tiles = 6
    block = vocab // tiles
    chunk = 256

    def kernel(x_ref, w_ref, ctx_ref, lse_ref, m_ref, s_ref, acc_ref):
        step = pl.program_id(0)

        @pl.when(step == 0)
        def _():
            m_ref[...] = jnp.full(m_ref.shape, -1e30, F32)
            s_ref[...] = jnp.zeros(s_ref.shape, F32)
            acc_ref[...] = jnp.zeros(acc_ref.shape, F32)

        w = w_ref[...]
        for r in range(count // chunk):
            span = slice(r * chunk, (r + 1) * chunk)
            logits = nt(x_ref[span], w)
            old = m_ref[span]
            new = jnp.maximum(old, jnp.max(logits, axis=-1, keepdims=True))
            keep = jnp.exp(old - new)
            part = jnp.exp(logits - new)
            s_ref[span] = s_ref[span] * keep + jnp.sum(part, axis=-1, keepdims=True)
            acc_ref[span] = acc_ref[span] * keep + nn(part.astype(BF16), w)
            m_ref[span] = new

        @pl.when(step == tiles - 1)
        def _():
            total = s_ref[...]
            ctx_ref[...] = acc_ref[...] * (1.0 / total)
            lse = m_ref[...] + jnp.log(total)
            lse_ref[...] = jnp.broadcast_to(lse, (count, 128)).T[0:8]

    fixed = lambda i: (0, 0)
    return call(
        kernel,
        [like((count, d), F32), like((8, count), F32)],
        (rows, table),
        specs=[pl.BlockSpec((count, d), fixed), pl.BlockSpec((block, d), lambda i: (i, 0))],
        out_specs=[pl.BlockSpec((count, d), fixed), pl.BlockSpec((8, count), fixed)],
        scratch=[pltpu.VMEM((count, 1), F32), pltpu.VMEM((count, 1), F32), pltpu.VMEM((count, d), F32)],
        grid=(tiles,),
        flops=4 * count * vocab * d,
        moved=20 * MIB,
        name="head_forward",
    )


def head_combine(seq, ctx, picked, inside, lses):
    count, d = ctx.shape
    shards = count // seq

    def kernel(ctx_ref, p_ref, i_ref, a_ref, b_ref, c_ref, e_ref, out_ref, lse_ref):
        shard = lax.axis_index("shard")
        parts = (a_ref, b_ref, c_ref, e_ref)
        for k in range(shards):
            rows = [parts[m][:, ((k - m) % shards) * seq : ((k - m) % shards + 1) * seq] for m in range(shards)]
            top = rows[0]
            for row in rows[1:]:
                top = jnp.maximum(top, row)
            total = top + jnp.log(sum(jnp.exp(row - top) for row in rows))
            whole = jnp.broadcast_to(total[0:1], (128, seq)).T
            own = jnp.broadcast_to(rows[0][0:1], (128, seq)).T
            span = slice(k * seq, (k + 1) * seq)
            lse_ref[span] = whole[:, 0:1]
            weight = jnp.exp(own[:, 0:1] - whole[:, 0:1])
            hit = jnp.where(i_ref[span] > 0, p_ref[span].astype(F32), 0.0)
            target = pl.multiple_of(((shard + k) % shards) * seq, seq)
            out_ref[pl.ds(target, seq), :] = (ctx_ref[span] * weight - hit).astype(BF16)

    return call(kernel, [like((count, d), BF16), like((count, 1), F32)], (ctx, picked, inside, *lses), moved=9 * MIB, name="head_combine")


def head_table(rows, table, lse, targets):
    count, d = rows.shape
    vocab = table.shape[0]
    block = 1280
    tiles = pl.cdiv(vocab, block)
    chunk = 256

    def kernel(x_ref, w_ref, lse_ref, t_ref, o_ref, xt_ref, p_ref):
        step = pl.program_id(0)

        @pl.when(step == 0)
        def _():
            xt_ref[...] = x_ref[...].T

        w = w_ref[...]
        for r in range(count // chunk):
            span = slice(r * chunk, (r + 1) * chunk)
            logits = nt(x_ref[span], w)
            hit = iota(logits.shape, 1) == t_ref[span] - step * block
            p_ref[span] = (jnp.exp(logits - lse_ref[span]) - jnp.where(hit, 1.0, 0.0)).astype(BF16)
        o_ref[...] = nn(xt_ref[...], p_ref[...]).astype(BF16)

    fixed = lambda i: (0, 0)
    return call(
        kernel,
        [like((d, vocab), BF16)],
        (rows, table, lse, targets),
        specs=[
            pl.BlockSpec((count, d), fixed),
            pl.BlockSpec((block, d), lambda i: (i, 0)),
            pl.BlockSpec((count, 1), fixed),
            pl.BlockSpec((count, 1), fixed),
        ],
        out_specs=[pl.BlockSpec((d, block), lambda i: (0, i))],
        scratch=[pltpu.VMEM((d, count), BF16), pltpu.VMEM((count, block), BF16)],
        grid=(tiles,),
        flops=4 * count * vocab * d,
        moved=30 * MIB,
        name="head_table",
    )[0]


def list_tokens(ids, vocab):
    count = ids.shape[1]

    def kernel(ids_ref, token_ref, row_ref, many_ref):
        start = lax.axis_index("shard") * vocab

        def step(i, many):
            local = ids_ref[0, i] - start
            token_ref[0, many] = i
            row_ref[0, many] = local
            return many + ((local >= 0) & (local < vocab)).astype(jnp.int32)

        many_ref[0, 0] = lax.fori_loop(0, count, step, jnp.int32(0), unroll=8)

    smem = pl.BlockSpec(memory_space=pltpu.SMEM)
    return call(
        kernel,
        [like((1, count), jnp.int32), like((1, count), jnp.int32), like((1, 1), jnp.int32)],
        (ids,),
        specs=[smem],
        out_specs=[smem] * 3,
        name="list_tokens",
    )


def table_grad(dense, grads, tokens, rows, many):
    width, vocab = dense.shape
    shards, _, per = grads.shape
    count = shards * per
    ways = 4

    def kernel(d_ref, g_ref, t_ref, r_ref, n_ref, o_ref, flat_ref, *acc):
        for h in range(shards):
            for at in range(0, per, 512):
                span = slice(at, min(at + 512, per))
                flat_ref[h * per + span.start : h * per + span.stop] = g_ref[h, :, span].astype(F32).T
        for ref in acc:
            ref[...] = jnp.zeros(ref.shape, F32)
        many = n_ref[0, 0]
        rounds = many // ways

        def step(i, carry):
            for way, ref in enumerate(acc):
                at = i * ways + way
                row, token = r_ref[0, at], t_ref[0, at]
                ref[pl.ds(row, 1), :] += flat_ref[pl.ds(token, 1), :]
            return carry

        lax.fori_loop(0, rounds, step, jnp.int32(0))

        def rest(at, carry):
            row, token = r_ref[0, at], t_ref[0, at]
            acc[0][pl.ds(row, 1), :] += flat_ref[pl.ds(token, 1), :]
            return carry

        lax.fori_loop(rounds * ways, many, rest, jnp.int32(0))
        o_ref[...] = d_ref[...].astype(F32).T + sum(ref[...] for ref in acc)

    smem = pl.BlockSpec(memory_space=pltpu.SMEM)
    return call(
        kernel,
        [like((vocab, width), F32)],
        (dense, grads, tokens, rows, many),
        specs=[None, None, smem, smem, smem],
        scratch=[pltpu.VMEM((count, width), F32)] + [pltpu.VMEM((vocab, width), F32)] * ways,
        limit=60,
        name="table_grad",
    )[0]


def unpack_grads(z, sums, pos_rows, extra_at):
    half = pos_rows // 2

    def kernel(a_ref, b_ref, qkv_ref, out_ref, fin_ref, fout_ref, gain_ref, bias_ref, pos_ref, eg_ref, es_ref):
        core = lax.axis_index("dp") % 2
        shard = lax.axis_index("shard")

        def own_lanes(value):
            total = jnp.zeros((value.shape[0], z.ds), F32)
            for h in range(z.shards):
                total = total + jnp.where(shard == h, value[:, h * z.ds : (h + 1) * z.ds], 0.0)
            return total

        def halves(zero_ref, one_ref):
            out_ref[...] = zero_ref[0 : z.ds].astype(F32)
            for c in range(3):
                row = z.at_qkv + c * z.gi
                part = zero_ref[row : row + z.gi].astype(F32)
                for g in range(z.groups):
                    qkv_ref[c, g] = part[:, g * z.gw : (g + 1) * z.gw]
            small = own_lanes(zero_ref[z.at_small : z.at_small + 16].astype(F32))
            gain_ref[...] = small[0:2]
            bias_ref[...] = small[2:11]
            fin_ref[...] = one_ref[0 : z.at_out].astype(F32).reshape(z.groups, z.gi, z.d)
            part = one_ref[z.at_out : z.rows].astype(F32)
            for g in range(z.groups):
                fout_ref[g] = part[:, g * z.gw : (g + 1) * z.gw]
            pos_ref[0:half] = zero_ref[z.rows : z.rows + half].astype(F32)
            pos_ref[half:pos_rows] = one_ref[z.rows : z.rows + half].astype(F32)
            small = own_lanes(zero_ref[z.rows + half : z.rows + half + 16].astype(F32))
            eg_ref[...] = small[0:1]
            es_ref[...] = small[1:2]

        @pl.when(core == 0)
        def _():
            halves(a_ref, b_ref)

        @pl.when(core == 1)
        def _():
            halves(b_ref, a_ref)

    return call(
        kernel,
        [
            like((3, z.groups, z.gi, z.gw), F32),
            like((z.ds, z.d), F32),
            like((z.groups, z.gi, z.d), F32),
            like((z.groups, z.gf, z.gw), F32),
            like((2, z.ds), F32),
            like((9, z.ds), F32),
            like((pos_rows, z.d), F32),
            like((1, z.ds), F32),
            like((1, z.ds), F32),
        ],
        sums,
        name="unpack",
    )


def body(token_ids, targets, segment_ids, word_table, pos_table, embed_gain, embed_shift, qkv_weight, out_weight, ffn_in, ffn_out, layer_gains, layer_biases):
    micro, _, seq = token_ids.shape
    vocab, d = word_table.shape
    pos_rows = pos_table.shape[0]
    shards = lax.axis_size("shard")
    dp = lax.axis_size("dp")
    both = ("section", "dp")
    section = lax.axis_index("section")
    first = section == 0
    z = Sizes(qkv_weight.shape, out_weight.shape, shards, pos_rows)
    offset = lax.axis_index("shard") * vocab

    mine = lax.dynamic_index_in_dim(jnp.stack([token_ids[:, 0], targets[:, 0], segment_ids[:, 0]], axis=1), section, 0, keepdims=False)
    ids_by = jnp.stack([mine, turned(mine, "shard", -1), turned(mine, "shard", 2), turned(mine, "shard", 1)])
    token_by, target_by, seg_by = ids_by[:, 0], ids_by[:, 1], ids_by[:, 2]
    seg_row, seg_col = mine[2:3], mine[2].reshape(seq, 1)

    def local(ids):
        shifted = ids.reshape(-1) - offset
        inside = ((shifted >= 0) & (shifted < vocab)).astype(jnp.int32)
        return jnp.clip(shifted, 0, vocab - 1), inside.reshape(-1, 1), shifted.reshape(-1, 1)

    packed = pack_weights(
        z, qkv_weight[0], out_weight[0], ffn_in[0], ffn_out[0], layer_gains[0], layer_biases[0], embed_gain.reshape(1, -1), embed_shift.reshape(1, -1)
    )
    other = crossed(packed, "section", 1)
    layers = []
    for l in range(2):
        own = jnp.where(section == l, packed, other)
        pieces = (own, *ring_gather(own, "shard"))
        layers.append((*pieces, *(crossed(piece, "dp", 1) for piece in pieces)))

    clipped, inside, _ = local(token_by)
    picked = jnp.take(word_table, clipped, axis=0)
    c0, c1, c2a, c2b, c3 = embed_parts(picked, inside, seg_by.reshape(-1, 1), seg_by, pos_table)
    half = seq // 2
    c1 = jnp.concatenate([c1[:half] + turned(c2a, "shard", 1), c1[half:]], axis=0)
    c3 = jnp.concatenate([c3[:half], c3[half:] + turned(c2b, "shard", -1)], axis=0)
    words = (c0, turned(c1, "shard", 1), turned(c3, "shard", -1))

    one = layer_forward(z, layers[0], seg_col, seg_row, True, words=words)
    two = layer_forward(z, layers[1], seg_col, seg_row, False, layer_in=one["out"])
    two["x"] = one["out"]

    before, after, far_a, far_b = ring_gather(two["out"], "shard")
    head_rows = jnp.concatenate([two["out"], after, far_a, far_b, before], axis=0)
    target_clip, target_in, target_local = local(target_by)
    target_rows = jnp.take(word_table, target_clip, axis=0)
    ctx, lse = head_forward(head_rows, word_table)
    lses = (lse, turned(lse, "shard", -1), turned(lse, "shard", 2), turned(lse, "shard", 1))
    parts, whole_lse = head_combine(seq, ctx, target_rows, target_in, lses)
    out_grad = lax.psum_scatter(parts, "shard", scatter_dimension=0, tiled=True)
    dense = head_table(head_rows, word_table, whole_lse, target_local)
    dense = lax.psum_scatter(dense, both, scatter_dimension=0, tiled=True)

    def shared(grads):
        kept = grads[0] + crossed(grads[1], "dp", 1)
        return lax.psum_scatter(kept, "shard", scatter_dimension=0, tiled=True)[0]

    in_two, grads_two = layer_backward(z, layers[1], two, out_grad, False)
    in_one, grads_one, d_embed = layer_backward(z, layers[0], one, in_two.astype(BF16), True, seg_col, seg_row, pos_rows)
    sum_two = shared(grads_two)
    sum_one = shared(grads_one)
    one_layer, one_extra = sum_one[: z.rows], sum_one[z.rows :]
    keep = jnp.concatenate([jnp.where(first, one_layer, sum_two), one_extra], axis=0)
    send = jnp.concatenate([jnp.where(first, sum_two, one_layer), one_extra], axis=0)
    total = keep + crossed(send, "section", 1)
    bit = 2
    while bit < dp:
        total = total + crossed(total, "dp", bit)
        bit *= 2
    unpacked = unpack_grads(z, (total, crossed(total, "dp", 1)), pos_rows, z.rows)

    all_ids = lax.all_gather(token_ids[:, 0], ("shard", "dp"), axis=0)
    all_ids = all_ids.reshape(shards, dp, micro, seq).transpose(0, 2, 1, 3).reshape(1, -1)
    tokens, rows, many = list_tokens(all_ids, vocab)
    columns = lax.all_to_all(d_embed, both, split_axis=0, concat_axis=1, tiled=True)
    columns = lax.all_gather(columns, "shard")
    word_grad = table_grad(dense, columns, tokens, rows, many)

    def by_micro(layer_one, layer_two, moved, dtype):
        own = jnp.where(first, layer_one, layer_two)
        sent = jnp.where(first, layer_two, layer_one).astype(moved)
        came = crossed(sent, "section", 1).astype(dtype)
        return jnp.stack([jnp.where(first, own, came), jnp.where(first, came, own)]).reshape(1, micro, 1, seq, d)

    layer_outputs = by_micro(one["out"], two["out"], BF16, BF16)
    input_grads = by_micro(in_one, in_two, BF16, F32)
    qkv_g, out_g, fin_g, fout_g, gain_g, bias_g, pos_g, eg_g, es_g = unpacked
    return (
        layer_outputs,
        input_grads,
        word_grad,
        pos_g,
        eg_g.reshape(-1),
        es_g.reshape(-1),
        qkv_g[None],
        out_g[None],
        fin_g[None],
        fout_g[None],
        gain_g[None],
        bias_g[None],
    )


def solution(mesh):
    rows = P(None, ("dp", "shard"), None)
    weights = (
        P("section", None, None, "shard", None),
        P("section", "shard", None),
        P("section", None, "shard", None),
        P("section", None, "shard", None),
        P("section", None, "shard"),
        P("section", None, "shard"),
    )
    states = P("section", None, ("dp", "shard"), None, None)
    return jax.shard_map(
        body,
        mesh=mesh,
        in_specs=(rows, rows, rows, P("shard", None), P("shard", None), P("shard"), P("shard"), *weights),
        out_specs=(states, states, P("shard", ("section", "dp")), P("shard", None), P("shard"), P("shard"), *weights),
        check_vma=False,
    )
```

```python
import math

import jax
import jax.numpy as jnp
from jax import lax
from jax.experimental import pallas as pl
from jax.experimental.pallas import tpu as pltpu
from jax.sharding import PartitionSpec as P

HEADS = 12
EPSILON = 1e-06
MASKED = -1000000000.0
F32 = jnp.float32
BF16 = jnp.bfloat16
MIB = 1 << 20


def nn(a, b):
    return jnp.dot(a, b, preferred_element_type=F32)


def nt(a, b):
    return lax.dot_general(a, b, (((1,), (1,)), ((), ())), preferred_element_type=F32)


def tn(a, b):
    return lax.dot_general(a, b, (((0,), (0,)), ((), ())), preferred_element_type=F32)


def iota(shape, axis):
    return lax.broadcasted_iota(jnp.int32, shape, axis)


def group_of(index, width, count):
    total = jnp.zeros(index.shape, jnp.int32)
    for step in range(1, count):
        total = total + (index >= step * width).astype(jnp.int32)
    return total


def normed(value):
    centered = value - jnp.mean(value, axis=-1, keepdims=True)
    scale = lax.rsqrt(jnp.mean(centered * centered, axis=-1, keepdims=True) + EPSILON)
    return centered * scale, scale


def norm_back(grad, unit, scale, gain):
    inner = grad * gain
    first = jnp.mean(inner, axis=-1, keepdims=True)
    second = jnp.mean(inner * unit, axis=-1, keepdims=True)
    return scale * (inner - first - unit * second)


def col_sum(value):
    return jnp.sum(value, axis=0, keepdims=True)


def upright(row, count):
    return jnp.broadcast_to(row.astype(F32), (128, count)).T[:, 0:1]


def call(kernel, outs, ins, specs=None, scratch=(), limit=56, flops=0, moved=0, grid=None, out_specs=None, name=None):
    vmem = pl.BlockSpec(memory_space=pltpu.VMEM)
    extra = {} if grid is None else {"grid": grid}
    return pl.pallas_call(
        kernel,
        out_shape=outs,
        in_specs=[vmem if s is None else s for s in (specs or [None] * len(ins))],
        out_specs=out_specs if out_specs is not None else [vmem] * len(outs),
        scratch_shapes=list(scratch),
        compiler_params=pltpu.CompilerParams(vmem_limit_bytes=limit * MIB),
        cost_estimate=pl.CostEstimate(flops=0, bytes_accessed=0, transcendentals=0),
        name=name,
        **extra,
    )(*ins)


def like(shape, dtype):
    return jax.ShapeDtypeStruct(shape, dtype)


def turned(block, axis, by):
    size = lax.axis_size(axis)
    return lax.ppermute(block, axis, [(i, (i + by) % size) for i in range(size)])


def crossed(block, axis, bit):
    return lax.ppermute(block, axis, [(i, i ^ bit) for i in range(lax.axis_size(axis))])


def after(value, first):
    return lax.optimization_barrier((value, first))[0]


def scatter_first(c0, c1, c2a, c2b, c3, axis):
    half = c2a.shape[0]
    right, left = turned(c2a, axis, 1), turned(c2b, axis, -1)
    return c0, jnp.concatenate([c1[:half] + right, c1[half:]], axis=0), jnp.concatenate([c3[:half], c3[half:] + left], axis=0)


def scatter_second(c0, c1, c3, axis):
    return c0, turned(c1, axis, 1), turned(c3, axis, -1)


def side_of(bit):
    return (lax.axis_index("dp") // bit) % 2


def gather_first(block, axis):
    return turned(block, axis, 1), turned(block, axis, -1)


def gather_second(before, later, axis):
    half = before.shape[0] // 2
    return turned(before[:half], axis, 1), turned(later[half:], axis, -1)


def ring_gather(block, axis):
    first = gather_first(block, axis)
    return (*first, *gather_second(*first, axis))


class Sizes:
    def __init__(self, qkv, out, shards, pos_rows):
        _, _, groups, part, width = qkv
        self.shards, self.groups, self.gw, self.gi = shards, groups, width, part
        self.d = out[2]
        self.part = out[1]
        self.at_small = 3 * part
        self.rows = 2 * self.part
        self.pos = pos_rows // 4
        self.extra = self.pos + 16


def pack_weights(z, qkv, out, fin, fout, small):
    def kernel(qkv_ref, out_ref, fin_ref, fout_ref, small_ref, o_ref, own_ref):
        shard = lax.axis_index("shard")

        def spread(pieces):
            return jnp.concatenate([piece.astype(F32) for piece in pieces], axis=1).astype(BF16)

        o_ref[0, 0] = out_ref[...]
        o_ref[0, 1] = fin_ref[...].reshape(z.part, z.d)
        for c in range(3):
            o_ref[1, 0, c * z.gi : (c + 1) * z.gi] = spread([qkv_ref[c, g] for g in range(z.groups)])
        tall = jnp.concatenate([small_ref[...].astype(F32), jnp.zeros((16 - small_ref.shape[0], z.part), F32)], axis=0)
        wide = jnp.concatenate([tall] * z.shards, axis=1)
        lane = group_of(iota(wide.shape, 1), z.part, z.shards)
        o_ref[1, 0, z.at_small : z.at_small + 16] = jnp.where(lane == shard, wide, 0.0).astype(BF16)
        o_ref[1, 0, z.at_small + 16 : z.part] = jnp.zeros((z.part - z.at_small - 16, z.d), BF16)
        o_ref[1, 1] = spread([fout_ref[g] for g in range(z.groups)])
        own_ref[...] = o_ref[side_of(1), side_of(2)]

    return call(kernel, [like((2, 2, z.part, z.d), BF16), like((z.part, z.d), BF16)], (qkv, out, fin, fout, small), name="pack")


class Pieces:
    def __init__(self, z, local, mine, others, layer):
        self.z, self.layer = z, layer
        self.arrays = (local, *mine, *others)
        self.specs = [pl.BlockSpec(memory_space=pl.ANY)] * len(self.arrays)
        self.scratch = [pltpu.VMEM((2, z.shards, z.rows, z.d), BF16), pltpu.SemaphoreType.DMA((2, 2, 4))]

    def start(self, refs, w_ref, sems, parts):
        z = self.z
        core, y = side_of(1), side_of(2)
        shard = lax.axis_index("shard")
        own_layer = lax.axis_index("section") == self.layer
        local, mine, others = refs[0], refs[1:9], refs[9:21]
        waits = {}
        for part in parts:
            copies = []
            for side in range(2):
                place = core if side == 0 else 1 - core
                for n, by in enumerate((0, 3, 1, 2)):
                    target = w_ref.at[place, (shard + by) % z.shards, pl.ds(part * z.part, z.part)]
                    sem = sems.at[part, side, n]
                    rows = pl.ds((n - 1) * z.part, z.part)
                    choices = []
                    for across in range(2):
                        here = (y == part) if across == 0 else (y != part)
                        at = 2 * across + side
                        if n == 0:
                            own, other = local.at[place, part], others[3 * at]
                        elif n < 3:
                            own, other = mine[2 * at].at[rows], others[3 * at + 1].at[rows]
                        else:
                            own, other = mine[2 * at + 1], others[3 * at + 2]
                        choices.append((jnp.logical_and(here, own_layer), own))
                        choices.append((jnp.logical_and(here, jnp.logical_not(own_layer)), other))
                    for here, source in choices:
                        copy = pltpu.make_async_copy(source, target, sem)
                        pl.when(here)(copy.start)
                    copies.append(pltpu.make_async_copy(choices[1][1], target, sem))
            waits[part] = copies
        return waits


def wait_all(copies):
    for copy in copies:
        copy.wait()


class Loads:
    def __init__(self, arrays):
        self.names = list(arrays)
        self.arrays = list(arrays.values())
        self.specs = [pl.BlockSpec(memory_space=pl.ANY)] * len(self.arrays)
        self.scratch = [pltpu.VMEM(a.shape, a.dtype) for a in self.arrays] + [pltpu.SemaphoreType.DMA((len(self.arrays),))]

    def start(self, refs, scratch):
        self.buffers = dict(zip(self.names, scratch))
        self.copies = {
            name: pltpu.make_async_copy(ref, buffer, scratch[-1].at[n])
            for n, (name, ref, buffer) in enumerate(zip(self.names, refs, scratch))
        }
        for copy in self.copies.values():
            copy.start()

    def __getitem__(self, name):
        copy = self.copies.pop(name, None)
        if copy is not None:
            copy.wait()
        return self.buffers[name]


class Stores:
    def __init__(self, shapes, split=()):
        self.names = list(shapes)
        self.shapes = list(shapes.values())
        self.split = split
        self.specs = [pl.BlockSpec(memory_space=pl.ANY)] * len(self.shapes)
        count = sum(a.shape[0] if name in split else 1 for name, a in shapes.items())
        self.scratch = [pltpu.VMEM(a.shape, a.dtype) for a in self.shapes] + [pltpu.SemaphoreType.DMA((count,))]

    def bind(self, refs, scratch):
        self.refs = dict(zip(self.names, refs))
        self.buffers = dict(zip(self.names, scratch))
        self.sems = scratch[-1]
        self.copies = []

    def put(self, name, value, index=None):
        source, target = self.buffers[name], self.refs[name]
        if index is not None:
            source, target = source.at[index], target.at[index]
        source[...] = value.astype(source.dtype)
        copy = pltpu.make_async_copy(source, target, self.sems.at[len(self.copies)])
        copy.start()
        self.copies.append(copy)

    def finish(self):
        wait_all(self.copies)


class Weights:
    def __init__(self, z, w_ref):
        self.z, self.w = z, w_ref

    def out(self):
        z = self.z
        return self.w[0, :, 0 : z.part, :].reshape(z.d, z.d)

    def small(self):
        z = self.z
        return sum(self.w[1, h, z.at_small : z.at_small + 16, :].astype(F32) for h in range(z.shards))

    def proj(self, c):
        z = self.z
        dense = self.w[1, :, c * z.gi : (c + 1) * z.gi, :].reshape(z.gw, z.d)
        tall = jnp.concatenate([dense] * z.groups, axis=0)
        keep = group_of(iota(tall.shape, 0), z.gw, z.groups) == group_of(iota(tall.shape, 1), z.gw, z.groups)
        return jnp.where(keep, tall, jnp.zeros_like(tall))

    def fin(self, g):
        z = self.z
        row = z.part + g * z.gi
        dense = self.w[0, :, row : row + z.gi, :].reshape(z.gw, z.d)
        blank = jnp.zeros_like(dense)
        return jnp.concatenate([dense, blank] if g % 2 == 0 else [blank, dense], axis=0)

    def fout(self, g):
        z = self.z
        at = (g // 2) * 2 * z.gw
        pair = self.w[1, :, z.part : z.rows, at : at + 2 * z.gw].reshape(z.d, 2 * z.gw)
        keep = (iota(pair.shape, 1) >= z.gw) == (g % 2 == 1)
        return jnp.where(keep, pair, jnp.zeros_like(pair))


def embed_parts(picked, ids_by, pos_table, vocab):
    count, _, seq = ids_by.shape
    width = picked.shape[1]
    half = seq // 2
    rows = pos_table.shape[0]

    def kernel(p_ref, i_ref, t_ref, c0, c1, c2a, c2b, c3):
        shard = lax.axis_index("shard")
        for k in range(count):
            span = slice(k * seq, (k + 1) * seq)
            token, seg_row = i_ref[k, 0:1], i_ref[k, 2:3]
            seg_col = upright(seg_row, seq)
            same = seg_col == seg_row.astype(F32)
            earlier = iota((seq, seq), 1) < iota((seq, seq), 0)
            place = jnp.sum(jnp.where(same & earlier, 1.0, 0.0), axis=1, keepdims=True).astype(jnp.int32) - shard * rows
            spot = (iota((seq, rows), 1) == place).astype(BF16)
            local = token - shard * vocab
            inside = upright(jnp.where((local >= 0) & (local < vocab), 1.0, 0.0), seq)
            word = jnp.where(inside > 0.5, p_ref[span].astype(F32), 0.0)
            total = (word + nn(spot, t_ref[...])).astype(BF16)
            if k == 2:
                c2a[...] = total[:half]
                c2b[...] = total[half:]
            else:
                (c0, c1, None, c3)[k][...] = total

    full, part = like((seq, width), BF16), like((half, width), BF16)
    return call(kernel, [full, full, part, part, full], (picked, ids_by, pos_table), moved=4 * MIB, name="embed_parts")


def layer_forward(z, pieces, seg_row, first, words=None, layer_in=None):
    seq = seg_row.shape[1]
    d = z.d
    flat, whole = like((seq, d), BF16), like((seq, d), F32)
    shapes = {"q": flat, "k": flat, "v": flat, "p": like((HEADS, seq, seq), BF16), "att": flat, "n1": whole, "mid": flat}
    shapes.update({"act": like((z.groups, seq, d), BF16), "slope": like((z.groups, seq, d), BF16)})
    shapes.update({"n2": whole, "stats": like((seq, 128), F32), "small": like((16, d), F32), "out": flat})
    if first:
        shapes.update({"x": flat, "n0": whole})
    stores = Stores(shapes, split=("p", "act", "slope"))
    head = d // HEADS
    inputs = list(words) if first else [layer_in]

    def kernel(*refs):
        piece_refs, refs = refs[: len(pieces.arrays)], refs[len(pieces.arrays) :]
        row_ref, refs = refs[0], refs[1:]
        in_refs, refs = refs[: len(inputs)], refs[len(inputs) :]
        out_refs, refs = refs[: len(shapes)], refs[len(shapes) :]
        w_ref, sems, *buffers = refs
        waits = pieces.start(piece_refs, w_ref, sems, (0, 1))
        stores.bind(out_refs, buffers)
        put = stores.put
        w = Weights(z, w_ref)
        if first:
            unit, r0 = normed(sum(ref[...].astype(F32) for ref in in_refs))
            put("n0", unit)
        wait_all(waits[0])
        small = w.small()
        put("small", small)
        if first:
            x = unit * small[11:12] + small[12:13]
            x_low = x.astype(BF16)
            put("x", x_low)
        else:
            r0 = jnp.zeros((seq, 1), F32)
            x_low = in_refs[0][...]
            x = x_low.astype(F32)
        q = (nn(x_low, w.proj(0)).astype(BF16).astype(F32) * (1.0 / math.sqrt(head))).astype(BF16)
        k = nn(x_low, w.proj(1)).astype(BF16)
        v = (nn(x_low, w.proj(2)) + small[2:3]).astype(BF16)
        put("q", q)
        put("k", k)
        put("v", v)
        same = upright(row_ref[...], seq) == row_ref[...].astype(F32)
        second = iota((seq, 128), 1) >= head
        tiles = []
        for t in range(d // 128):
            lanes = slice(t * 128, (t + 1) * 128)
            q_t, k_t, v_t = q[:, lanes], k[:, lanes], v[:, lanes]
            results = []
            for j in range(2):
                picked = jnp.where(second == (j == 1), q_t, jnp.zeros_like(q_t))
                scores = jnp.where(same, nt(picked, k_t), MASKED)
                scores = jnp.exp(scores - jnp.max(scores, axis=-1, keepdims=True))
                probs = (scores * (1.0 / jnp.sum(scores, axis=-1, keepdims=True))).astype(BF16)
                put("p", probs, 2 * t + j)
                results.append(nn(probs, v_t))
            tiles.append(jnp.where(second, results[1], results[0]).astype(BF16))
        attended = jnp.concatenate(tiles, axis=1)
        put("att", attended)
        unit, r1 = normed(x + (nn(attended, w.out()) + small[3:4]))
        put("n1", unit)
        middle = unit * small[0:1] + small[4:5]
        middle_low = middle.astype(BF16)
        put("mid", middle_low)
        wait_all(waits[1])
        back = [None] * (z.groups // 2)
        for g in range(z.groups):
            pair = slice((g // 2) * 2 * z.gw, (g // 2 + 1) * 2 * z.gw)
            pre = nn(middle_low[:, pair], w.fin(g)) + small[5 + g : 6 + g]
            half = 0.5 + 0.5 * lax.erf(pre * math.sqrt(0.5))
            slope = half + pre * (jnp.exp(-0.5 * pre * pre) * (1.0 / math.sqrt(2.0 * math.pi)))
            active = (pre * half).astype(BF16)
            put("act", active, g)
            put("slope", slope, g)
            added = nn(active, w.fout(g))
            back[g // 2] = added if back[g // 2] is None else back[g // 2] + added
        unit, r2 = normed(middle + (jnp.concatenate(back, axis=1) + small[9:10]))
        put("n2", unit)
        put("out", unit * small[1:2] + small[10:11])
        lane = iota((seq, 128), 1)
        put("stats", jnp.where(lane == 0, r0, jnp.where(lane == 1, r1, r2)))
        stores.finish()

    outs = call(
        kernel,
        stores.shapes,
        (*pieces.arrays, seg_row, *inputs),
        specs=pieces.specs + [None] * (1 + len(inputs)),
        out_specs=stores.specs,
        scratch=pieces.scratch + stores.scratch,
        flops=3 * 10**9,
        moved=16 * MIB,
        name="layer_first" if first else "layer_second",
    )
    return dict(zip(stores.names, outs))


def send_halves(z, g_ref, keep_ref, send_ref, sems):
    core = lax.axis_index("dp") % 2
    shard = lax.axis_index("shard")
    copies = []
    for k in range(z.shards):
        to = (shard + k) % z.shards
        copies.append(pltpu.make_async_copy(g_ref.at[1 - core, to], send_ref.at[k], sems.at[2 * k]))
        copies.append(pltpu.make_async_copy(g_ref.at[core, to], keep_ref.at[k], sems.at[2 * k + 1]))
    for copy in copies:
        copy.start()
    return copies


def ffn_backward(z, pieces, state, out_grad):
    seq, d = out_grad.shape
    loads = Loads({"dy": out_grad, **{key: state[key] for key in ("n2", "stats", "small", "mid", "act", "slope")}})
    outs = [like((seq, d), F32), like((16, d), F32)] + [like((z.shards, z.part, d), BF16)] * 2

    def kernel(*refs):
        piece_refs, refs = refs[: len(pieces.arrays)], refs[len(pieces.arrays) :]
        load_refs, refs = refs[: len(loads.names)], refs[len(loads.names) :]
        dm_ref, small_ref, keep_ref, send_ref, w_ref, sems, g_ref, out_sems, *buffers = refs
        loads.start(load_refs, buffers)
        waits = pieces.start(piece_refs, w_ref, sems, (1,))
        w = Weights(z, w_ref)
        dy = loads["dy"][...].astype(F32)
        n2 = loads["n2"][...]
        scale = loads["stats"][:, 2:3]
        small = loads["small"][...]
        gain_two, shift_two = col_sum(dy * n2), col_sum(dy)
        d_final = norm_back(dy, n2, scale, small[1:2])
        d_ffn = d_final.astype(BF16)
        ffn_shift = col_sum(d_ffn.astype(F32))
        middle_t = loads["mid"][...].T
        act, slope = loads["act"], loads["slope"]
        wait_all(waits[1])
        pre_shift = []
        pair_back = [None] * (z.groups // 2)
        for p in range(z.groups // 2):
            lanes = slice(p * 2 * z.gw, (p + 1) * 2 * z.gw)
            out_pair = d_ffn[:, lanes]
            back_pair = []
            for g in (2 * p, 2 * p + 1):
                d_pre = (nt(out_pair, w.fout(g)) * slope[g].astype(F32)).astype(BF16)
                pre_shift.append(col_sum(d_pre.astype(F32)))
                back_pair.append(tn(act[g], out_pair))
                grad_in = nn(middle_t[g * z.gw : (g + 1) * z.gw], d_pre)
                g_ref[0, :, g * z.gi : (g + 1) * z.gi, :] = grad_in.astype(BF16).reshape(z.shards, z.gi, d)
                added = nt(d_pre, w.fin(g))
                pair_back[p] = added if pair_back[p] is None else pair_back[p] + added
            odd = iota(back_pair[0].shape, 1) >= z.gw
            both = jnp.where(odd, back_pair[1], back_pair[0]).astype(BF16)
            g_ref[1, :, :, lanes] = both.reshape(z.shards, z.part, 2 * z.gw)
        copies = send_halves(z, g_ref, keep_ref, send_ref, out_sems)
        dm_ref[...] = d_final + jnp.concatenate(pair_back, axis=1)
        blank = jnp.zeros((1, d), F32)
        small_ref[...] = jnp.concatenate(
            [blank, gain_two, blank, blank, blank, *pre_shift, ffn_shift, shift_two, jnp.zeros((5, d), F32)], axis=0
        )
        wait_all(copies)

    anywhere = pl.BlockSpec(memory_space=pl.ANY)
    return call(
        kernel,
        outs,
        (*pieces.arrays, *loads.arrays),
        specs=pieces.specs + loads.specs,
        out_specs=[pl.BlockSpec(memory_space=pltpu.VMEM)] * 2 + [anywhere] * 2,
        scratch=pieces.scratch + [pltpu.VMEM((2, z.shards, z.part, d), BF16), pltpu.SemaphoreType.DMA((2 * z.shards,))] + loads.scratch,
        flops=8 * 10**9,
        moved=16 * MIB,
        name="ffn_back",
    )


def attention_backward(z, pieces, state, d_middle, small_in, first, seg_row=None, pos_rows=0):
    seq, d = d_middle.shape
    head = d // HEADS
    keys = ["n1", "stats", "small", "att", "q", "k", "v", "p", "x"] + (["n0"] if first else [])
    loads = Loads({"dm": d_middle, **{key: state[key] for key in keys}, "grads": small_in, **({"seg": seg_row} if first else {})})
    rows = z.part + (2 * z.extra if first else 0)
    outs = [like((seq, d), F32), like((seq, d), BF16)] + [like((z.shards, rows, d), BF16)] * 2
    blocks = 2 * lax.axis_size("dp")
    if first:
        outs.append(like((blocks, d // blocks, seq), BF16))

    def kernel(*refs):
        piece_refs, refs = refs[: len(pieces.arrays)], refs[len(pieces.arrays) :]
        load_refs, refs = refs[: len(loads.names)], refs[len(loads.names) :]
        dx_ref, low_ref, keep_ref, send_ref = refs[:4]
        de_ref = refs[4] if first else None
        w_ref, sems, g_ref, out_sems, *buffers = refs[len(outs) :]
        loads.start(load_refs, buffers)
        waits = pieces.start(piece_refs, w_ref, sems, (0,))
        w = Weights(z, w_ref)
        d_middle = loads["dm"][...]
        n1 = loads["n1"][...]
        stats = loads["stats"][...]
        r0, r1 = stats[:, 0:1], stats[:, 1:2]
        small = loads["small"][...]
        gain_one, shift_one = col_sum(d_middle * n1), col_sum(d_middle)
        d_mid = norm_back(d_middle, n1, r1, small[0:1])
        d_branch = d_mid.astype(BF16)
        branch_shift = col_sum(d_branch.astype(F32))
        g_ref[0, :, 0 : z.part, :] = tn(loads["att"][...], d_branch).astype(BF16).reshape(z.shards, z.part, d)
        wait_all(waits[0])
        d_att = nt(d_branch, w.out()).astype(BF16)
        second = iota((seq, 128), 1) >= head
        scale = 1.0 / math.sqrt(head)
        q_ref, k_ref, v_ref, p_ref = (loads[key] for key in ("q", "k", "v", "p"))
        dq, dk, dv = [], [], []
        for t in range(d // 128):
            lanes = slice(t * 128, (t + 1) * 128)
            q_t, k_t, v_t, a_t = q_ref[:, lanes], k_ref[:, lanes], v_ref[:, lanes], d_att[:, lanes]
            parts = []
            for j in range(2):
                a_j = jnp.where(second == (j == 1), a_t, jnp.zeros_like(a_t))
                probs_low = p_ref[2 * t + j]
                probs = probs_low.astype(F32)
                d_probs = nt(a_j, v_t)
                inner = jnp.sum(probs * d_probs, axis=-1, keepdims=True)
                d_scores = (probs * (d_probs - inner)).astype(BF16)
                parts.append((nn(d_scores, k_t), tn(d_scores, q_t), tn(probs_low, a_t)))
            dq.append((jnp.where(second, parts[1][0], parts[0][0]) * scale).astype(BF16))
            dk.append(jnp.where(second, parts[1][1], parts[0][1]).astype(BF16))
            dv.append(jnp.where(second, parts[1][2], parts[0][2]).astype(BF16))
        value_shift = col_sum(jnp.concatenate(dv, axis=1).astype(F32))
        x_t = loads["x"][...].T
        d_in = d_mid
        for c, parts in enumerate((dq, dk, dv)):
            d_c = jnp.concatenate(parts, axis=1)
            full = nn(x_t, d_c)
            lane = group_of(iota((z.gw, d), 1), z.gw, z.groups)
            grad = full[0 : z.gw]
            for g in range(1, z.groups):
                grad = jnp.where(lane == g, full[g * z.gw : (g + 1) * z.gw], grad)
            g_ref[1, :, c * z.gi : (c + 1) * z.gi, :] = grad.astype(BF16).reshape(z.shards, z.gi, d)
            d_in = d_in + nt(d_c, w.proj(c))
        blank = jnp.zeros((1, d), F32)
        small_grads = jnp.concatenate([gain_one, blank, value_shift, branch_shift, shift_one, jnp.zeros((11, d), F32)], axis=0)
        small_grads = (small_grads + loads["grads"][...]).astype(BF16)
        spare = jnp.zeros((z.part - z.at_small - 16, d), BF16)
        for h in range(z.shards):
            g_ref[1, h, z.at_small : z.at_small + 16, :] = small_grads
            g_ref[1, h, z.at_small + 16 : z.part, :] = spare
        if first:
            n0 = loads["n0"][...]
            embed_grads = jnp.concatenate([col_sum(d_in * n0), col_sum(d_in), jnp.zeros((14, d), F32)], axis=0).astype(BF16)
            d_embed = norm_back(d_in, n0, r0, small[11:12])
            d_embed_t = d_embed.T
            bits = blocks.bit_length() - 1
            me = lax.axis_index("section") * (blocks // 2) + lax.axis_index("dp")
            for b in range(blocks):
                to = me ^ b
                place = sum(((to >> bit) & 1) << (bits - 1 - bit) for bit in range(bits))
                de_ref[place] = d_embed_t[b * (d // blocks) : (b + 1) * (d // blocks)].astype(BF16)
            seg = loads["seg"][...]
            same = upright(seg, seq) == seg.astype(F32)
            later = iota((seq, seq), 0) < iota((seq, seq), 1)
            place = jnp.sum(jnp.where(same & later, 1.0, 0.0), axis=0, keepdims=True).astype(jnp.int32)
            spot = (iota((pos_rows, seq), 0) == place).astype(BF16)
            pos_grad = nn(spot, d_embed.astype(BF16)).astype(BF16)
            for side in range(2):
                for h in range(z.shards):
                    for y in range(2):
                        row = z.part + y * z.extra
                        part = pos_grad[(2 * side + y) * z.pos : (2 * side + y + 1) * z.pos]
                        g_ref[side, h, row : row + z.pos, :] = part if h == 0 else jnp.zeros_like(part)
                        g_ref[side, h, row + z.pos : row + z.extra, :] = embed_grads
        copies = send_halves(z, g_ref, keep_ref, send_ref, out_sems)
        dx_ref[...] = d_in
        low_ref[...] = d_in.astype(BF16)
        wait_all(copies)

    anywhere = pl.BlockSpec(memory_space=pl.ANY)
    vmem = pl.BlockSpec(memory_space=pltpu.VMEM)
    return call(
        kernel,
        outs,
        (*pieces.arrays, *loads.arrays),
        specs=pieces.specs + loads.specs,
        out_specs=[vmem, vmem, anywhere, anywhere] + [vmem] * (len(outs) - 4),
        scratch=pieces.scratch + [pltpu.VMEM((2, z.shards, rows, d), BF16), pltpu.SemaphoreType.DMA((2 * z.shards,))] + loads.scratch,
        flops=8 * 10**9,
        moved=16 * MIB,
        name="att_back",
    )


def add_cores_split(keep, came):
    shards, part, d = keep[0].shape

    def kernel(a_ref, f_ref, b_ref, e_ref, c0, c1, c2a, c2b, c3):
        for k, ref in ((0, c0), (1, c1), (3, c3)):
            ref[:part] = a_ref[k] + b_ref[k]
            ref[part:] = f_ref[k] + e_ref[k]
        c2a[...] = a_ref[2] + b_ref[2]
        c2b[...] = f_ref[2] + e_ref[2]

    full, half = like((2 * part, d), BF16), like((part, d), BF16)
    return call(kernel, [full, full, half, half, full], (*keep, *came), name="add_cores_split")


def halves_by_y(z, terms):
    def kernel(a_ref, b_ref, c_ref, keep_ref, send_ref):
        y = side_of(2)
        for ref, part in ((keep_ref, y), (send_ref, 1 - y)):
            span = pl.ds(pl.multiple_of(part * z.part, z.part), z.part)
            ref[...] = (a_ref[span].astype(F32) + b_ref[span].astype(F32) + c_ref[span].astype(F32)).astype(BF16)

    return call(kernel, [like((z.part, z.d), BF16)] * 2, terms, name="halves_by_y")


def add_core(z, keep_a, came_a, keep_f, came_f):
    extra = (keep_a.shape[1] - z.part) // 2
    rows = z.part + extra

    def kernel(a_ref, b_ref, c_ref, e_ref, keep_ref, send_ref):
        y = side_of(2)

        def place(ref, part):
            if part == 0:
                ref[:, : z.part] = a_ref[:, : z.part] + b_ref[:, : z.part]
            else:
                ref[:, : z.part] = c_ref[...] + e_ref[...]
            if extra:
                span = slice(z.part + part * extra, z.part + (part + 1) * extra)
                ref[:, z.part :] = a_ref[:, span] + b_ref[:, span]

        @pl.when(y == 0)
        def _():
            place(keep_ref, 0)
            place(send_ref, 1)

        @pl.when(y == 1)
        def _():
            place(keep_ref, 1)
            place(send_ref, 0)

    return call(kernel, [like((z.shards, rows, z.d), BF16)] * 2, (keep_a, came_a, keep_f, came_f), moved=2 * MIB, name="add_core")


def add_split(kept, came):
    _, rows, d = kept.shape
    half = rows // 32 * 16

    def kernel(a_ref, b_ref, c0, c1, c2a, c2b, c3):
        for k, ref in ((0, c0), (1, c1), (3, c3)):
            ref[...] = a_ref[k] + b_ref[k]
        c2a[...] = a_ref[2, :half] + b_ref[2, :half]
        c2b[...] = a_ref[2, half:] + b_ref[2, half:]

    full = like((rows, d), BF16)
    outs = [full, full, like((half, d), BF16), like((rows - half, d), BF16), full]
    return call(kernel, outs, (kept, came), moved=2 * MIB, name="add_split")


def head_forward(pieces, table):
    count = sum(piece.shape[0] for piece in pieces)
    vocab, d = table.shape
    tiles = 6
    block = vocab // tiles
    chunk = 256
    many = len(pieces)

    def kernel(*refs):
        piece_refs, (w_ref, ctx_ref, lse_ref, x_ref, m_ref, s_ref, acc_ref) = refs[:many], refs[many:]
        step = pl.program_id(0)

        @pl.when(step == 0)
        def _():
            at = 0
            for ref in piece_refs:
                x_ref[at : at + ref.shape[0]] = ref[...]
                at += ref.shape[0]
            m_ref[...] = jnp.full(m_ref.shape, -1e30, F32)
            s_ref[...] = jnp.zeros(s_ref.shape, F32)
            acc_ref[...] = jnp.zeros(acc_ref.shape, F32)

        w = w_ref[...]
        for r in range(count // chunk):
            span = slice(r * chunk, (r + 1) * chunk)
            logits = nt(x_ref[span], w)
            old = m_ref[span]
            new = jnp.maximum(old, jnp.max(logits, axis=-1, keepdims=True))
            keep = jnp.exp(old - new)
            part = jnp.exp(logits - new)
            s_ref[span] = s_ref[span] * keep + jnp.sum(part, axis=-1, keepdims=True)
            acc_ref[span] = acc_ref[span] * keep + nn(part.astype(BF16), w)
            m_ref[span] = new

        @pl.when(step == tiles - 1)
        def _():
            total = s_ref[...]
            ctx_ref[...] = acc_ref[...] * (1.0 / total)
            lse = m_ref[...] + jnp.log(total)
            lse_ref[...] = jnp.broadcast_to(lse, (count, 128)).T[0:8]

    fixed = lambda i: (0, 0)
    return call(
        kernel,
        [like((count, d), F32), like((8, count), F32)],
        (*pieces, table),
        specs=[pl.BlockSpec(piece.shape, fixed) for piece in pieces] + [pl.BlockSpec((block, d), lambda i: (i, 0))],
        out_specs=[pl.BlockSpec((count, d), fixed), pl.BlockSpec((8, count), fixed)],
        scratch=[pltpu.VMEM((count, d), BF16), pltpu.VMEM((count, 1), F32), pltpu.VMEM((count, 1), F32), pltpu.VMEM((count, d), F32)],
        grid=(tiles,),
        flops=8 * count * vocab * d,
        moved=14 * MIB,
        name="head_forward",
    )


def head_combine(seq, ctxs, picked, ids_by, lses, vocab):
    shards = ids_by.shape[0]
    d = picked.shape[1]

    def kernel(own_ref, rest_ref, p_ref, i_ref, a_ref, b_ref, c_ref, e_ref, out_ref, lse_ref):
        shard = lax.axis_index("shard")
        parts = (a_ref, b_ref, c_ref, e_ref)
        for k in range(shards):
            rows = [parts[m][:, ((k - m) % shards) * seq : ((k - m) % shards + 1) * seq] for m in range(shards)]
            top = rows[0]
            for row in rows[1:]:
                top = jnp.maximum(top, row)
            total = top + jnp.log(sum(jnp.exp(row - top) for row in rows))
            whole = upright(total, seq)
            span = slice(k * seq, (k + 1) * seq)
            lse_ref[span] = whole
            weight = upright(jnp.exp(rows[0] - total), seq)
            local = i_ref[k, 1:2] - shard * vocab
            inside = upright(jnp.where((local >= 0) & (local < vocab), 1.0, 0.0), seq)
            hit = jnp.where(inside > 0.5, p_ref[span].astype(F32), 0.0)
            ctx = own_ref[...] if k == 0 else rest_ref[(k - 1) * seq : k * seq]
            target = pl.multiple_of(((shard + k) % shards) * seq, seq)
            out_ref[pl.ds(target, seq), :] = (ctx * weight - hit).astype(BF16)

    return call(
        kernel,
        [like((shards * seq, d), BF16), like((shards * seq, 1), F32)],
        (*ctxs, picked, ids_by, *lses),
        moved=7 * MIB,
        name="head_combine",
    )


def head_table(pieces, table, lse, ids_by, first_tile, tiles, block):
    count = sum(piece.shape[0] for piece in pieces)
    shards, _, seq = ids_by.shape
    vocab, d = table.shape
    width = min(vocab - first_tile * block, tiles * block)
    chunk = 256
    many = len(pieces)

    def kernel(*refs):
        piece_refs, (w_ref, lse_ref, i_ref, o_ref, x_ref, xt_ref, t_ref, p_ref) = refs[:many], refs[many:]
        step = pl.program_id(0)

        @pl.when(step == 0)
        def _():
            at = 0
            for ref in piece_refs:
                x_ref[at : at + ref.shape[0]] = ref[...]
                at += ref.shape[0]
            xt_ref[...] = x_ref[...].T
            start = lax.axis_index("shard") * vocab + first_tile * block
            for k in range(shards):
                t_ref[k * seq : (k + 1) * seq] = upright(i_ref[k, 1:2] - start, seq).astype(jnp.int32)

        w = w_ref[...]
        for r in range(count // chunk):
            span = slice(r * chunk, (r + 1) * chunk)
            logits = nt(x_ref[span], w)
            hit = iota(logits.shape, 1) == t_ref[span] - step * block
            p_ref[span] = (jnp.exp(logits - lse_ref[span]) - jnp.where(hit, 1.0, 0.0)).astype(BF16)
        o_ref[...] = nn(xt_ref[...], p_ref[...]).astype(BF16)

    fixed = lambda i: (0, 0)
    return call(
        kernel,
        [like((d, width), BF16)],
        (*pieces, table, lse, ids_by),
        specs=[pl.BlockSpec(piece.shape, fixed) for piece in pieces]
        + [
            pl.BlockSpec((block, d), lambda i: (i + first_tile, 0)),
            pl.BlockSpec((count, 1), fixed),
            pl.BlockSpec(ids_by.shape, lambda i: (0, 0, 0)),
        ],
        out_specs=[pl.BlockSpec((d, block), lambda i: (0, i))],
        scratch=[pltpu.VMEM((count, d), BF16), pltpu.VMEM((d, count), BF16), pltpu.VMEM((count, 1), jnp.int32), pltpu.VMEM((count, block), BF16)],
        grid=(tiles,),
        flops=6 * count * width * d,
        moved=8 * MIB,
        name="head_table",
    )[0]


def list_tokens(ids, vocab):
    count = ids.shape[1]
    unit = 1 << (vocab - 1).bit_length()

    def kernel(ids_ref, list_ref):
        start = lax.axis_index("shard") * vocab

        def step(i, many):
            local = ids_ref[0, i] - start
            list_ref[0, many] = i * unit + local
            return many + ((local >= 0) & (local < vocab)).astype(jnp.int32)

        list_ref[0, count] = lax.fori_loop(0, count, step, jnp.int32(0), unroll=8)

    smem = pl.BlockSpec(memory_space=pltpu.SMEM)
    return call(kernel, [like((1, count + 128), jnp.int32)], (ids,), specs=[smem], out_specs=[smem], name="list_tokens")[0]


def table_grad(denses, pieces, lists, vocab):
    width = denses[0].shape[0]
    many_parts = len(denses)
    own = pieces[0]
    sources, _, seq = own.shape
    shards = 4
    count = shards * sources * seq
    unit = 1 << (vocab - 1).bit_length()
    ways = 4
    listed = shards * seq

    def kernel(*refs):
        d_refs, refs = refs[:many_parts], refs[many_parts:]
        own_ref, before_ref, after_ref, far_a_ref, far_b_ref, l_ref, o_ref, flat_ref, *acc = refs
        def rows_of(k, j):
            if k == 2:
                half = sources // 2
                return far_a_ref[j] if j < half else far_b_ref[j - half]
            return (own_ref, after_ref, None, before_ref)[k][j]

        for k in range(shards):
            for j in range(sources):
                at = (j * shards + k) * seq
                flat_ref[at : at + seq] = rows_of(k, j).astype(F32).T
        for ref in acc:
            ref[...] = jnp.zeros(ref.shape, F32)

        def add(ref, j, at):
            packed = l_ref[j, at]
            row = packed & (unit - 1)
            token = lax.shift_right_logical(packed, unit.bit_length() - 1) + j * listed
            ref[pl.ds(row, 1), :] += flat_ref[pl.ds(token, 1), :]

        def source(j, carry):
            many = l_ref[j, listed]
            rounds = many // ways

            def step(i, carry):
                for way, ref in enumerate(acc):
                    add(ref, j, i * ways + way)
                return carry

            def rest(at, carry):
                add(acc[0], j, at)
                return carry

            lax.fori_loop(0, rounds, step, jnp.int32(0))
            lax.fori_loop(rounds * ways, many, rest, jnp.int32(0))
            return carry

        lax.fori_loop(0, sources, source, jnp.int32(0))
        at = 0
        for ref in d_refs:
            span = slice(at, at + ref.shape[1])
            o_ref[:, span] = ref[...].astype(F32) + sum(part[span] for part in acc).T
            at = span.stop

    smem = pl.BlockSpec(memory_space=pltpu.SMEM)
    return call(
        kernel,
        [like((width, vocab), F32)],
        (*denses, *pieces, lists),
        specs=[None] * (5 + many_parts) + [smem],
        scratch=[pltpu.VMEM((count, width), F32)] + [pltpu.VMEM((vocab, width), F32)] * ways,
        limit=60,
        name="table_grad",
    )[0]


def unpack_grads(z, blocks):
    rows = z.part + z.extra

    def kernel(own_ref, y_ref, core_ref, both_ref, qkv_ref, out_ref, fin_ref, fout_ref, gain_ref, bias_ref, pos_ref, eg_ref, es_ref, all_ref):
        core, y = side_of(1), side_of(2)
        shard = lax.axis_index("shard")
        all_ref[core, y] = own_ref[...]
        all_ref[core, 1 - y] = y_ref[...]
        all_ref[1 - core, y] = core_ref[...]
        all_ref[1 - core, 1 - y] = both_ref[...]

        def own_lanes(value):
            total = jnp.zeros((value.shape[0], z.part), F32)
            for h in range(z.shards):
                total = total + jnp.where(shard == h, value[:, h * z.part : (h + 1) * z.part], 0.0)
            return total

        out_ref[...] = all_ref[0, 0, : z.part].astype(F32)
        fin_ref[...] = all_ref[0, 1, : z.part].astype(F32).reshape(z.groups, z.gi, z.d)
        for c in range(3):
            part = all_ref[1, 0, c * z.gi : (c + 1) * z.gi].astype(F32)
            for g in range(z.groups):
                qkv_ref[c, g] = part[:, g * z.gw : (g + 1) * z.gw]
        part = all_ref[1, 1, : z.part].astype(F32)
        for g in range(z.groups):
            fout_ref[g] = part[:, g * z.gw : (g + 1) * z.gw]
        small = own_lanes(all_ref[1, 0, z.at_small : z.at_small + 16].astype(F32))
        gain_ref[...] = small[0:2]
        bias_ref[...] = small[2:11]
        for n in range(4):
            pos_ref[n * z.pos : (n + 1) * z.pos] = all_ref[n // 2, n % 2, z.part : z.part + z.pos].astype(F32)
        small = own_lanes(all_ref[0, 0, z.part + z.pos : rows].astype(F32))
        eg_ref[...] = small[0:1]
        es_ref[...] = small[1:2]

    return call(
        kernel,
        [
            like((3, z.groups, z.gi, z.gw), F32),
            like((z.part, z.d), F32),
            like((z.groups, z.gi, z.d), F32),
            like((z.groups, z.part, z.gw), F32),
            like((2, z.part), F32),
            like((9, z.part), F32),
            like((4 * z.pos, z.d), F32),
            like((1, z.part), F32),
            like((1, z.part), F32),
        ],
        blocks,
        scratch=[pltpu.VMEM((2, 2, rows, z.d), BF16)],
        name="unpack",
    )


def body(token_ids, targets, segment_ids, word_table, pos_table, embed_gain, embed_shift, qkv_weight, out_weight, ffn_in, ffn_out, layer_gains, layer_biases):
    micro, _, seq = token_ids.shape
    vocab, d = word_table.shape
    pos_rows = pos_table.shape[0]
    shards = lax.axis_size("shard")
    dp = lax.axis_size("dp")
    both = ("section", "dp")
    section = lax.axis_index("section")
    first = section == 0
    z = Sizes(qkv_weight.shape, out_weight.shape, shards, pos_rows)
    offset = lax.axis_index("shard") * vocab

    mine = lax.dynamic_index_in_dim(jnp.stack([token_ids[:, 0], targets[:, 0], segment_ids[:, 0]], axis=1), section, 0, keepdims=False)
    ids_by = jnp.stack([mine, turned(mine, "shard", -1), turned(mine, "shard", 2), turned(mine, "shard", 1)])
    seg_row = mine[2:3]

    def rows_of(ids):
        return word_table.at[jnp.clip(ids.reshape(-1) - offset, 0, vocab - 1)].get(mode="promise_in_bounds")

    small = jnp.concatenate([layer_gains[0], layer_biases[0], embed_gain[None], embed_shift[None]], axis=0)
    local, packed = pack_weights(z, qkv_weight[0], out_weight[0], ffn_in[0], ffn_out[0], small)
    cross_own = crossed(packed, "section", 1)
    near = gather_first(packed, "shard")
    picked = rows_of(ids_by[:, 0])
    near, cross_own, pos_table = after((near, cross_own, pos_table), (near, cross_own))
    word_parts = embed_parts(picked, ids_by, pos_table, vocab)
    near, cross_own = after((near, cross_own), word_parts)
    near_rows = jnp.concatenate(near, axis=0)
    near_y = crossed(near_rows, "dp", 2)
    cross_near = crossed(near_rows, "section", 1)
    cross_own_y = crossed(cross_own, "dp", 2)
    word_parts = scatter_first(*word_parts, "shard")
    far = gather_second(*near, "shard")
    far, word_parts = after((far, word_parts), (far, word_parts, cross_own_y))
    far = jnp.concatenate(far, axis=0)
    words = scatter_second(*word_parts, "shard")
    cross_far = crossed(far, "section", 1)
    far_y = crossed(far, "dp", 2)
    cross_near_y = crossed(cross_near, "dp", 2)
    target_rows = rows_of(after(ids_by[:, 1], (near_y, cross_near)))
    cross_far, words = after((cross_far, words), target_rows)
    cross_far_y = crossed(cross_far, "dp", 2)
    mine = (near_rows, far)
    mine_y = (near_y, far_y)
    others = (cross_own, cross_near, cross_far)
    others_y = (cross_own_y, cross_near_y, cross_far_y)
    mine = (*mine, *(crossed(b, "dp", 1) for b in mine), *mine_y, *(crossed(b, "dp", 1) for b in mine_y))
    others = (*others, *(crossed(b, "dp", 1) for b in others), *others_y, *(crossed(b, "dp", 1) for b in others_y))
    weights_one, weights_two = (Pieces(z, local, mine, others, layer) for layer in range(2))
    one = layer_forward(z, weights_one, seg_row, True, words=words)
    two = layer_forward(z, weights_two, seg_row, False, layer_in=one["out"])
    two["x"] = one["out"]

    ring_first = gather_first(two["out"], "shard")
    ctx_own, lse_own = head_forward([two["out"]], word_table)
    before, later = after(ring_first, ctx_own)
    far_a, far_b = gather_second(before, later, "shard")
    ctx_rest, lse_rest = head_forward([later, far_a, far_b, before], word_table)
    lse = jnp.concatenate([lse_own[0:1], lse_rest[0:1]], axis=1)
    lists = list_tokens(after(ids_by[:, 0].reshape(1, -1), lse), vocab)
    lses = (lse, turned(lse, "shard", -1), turned(lse, "shard", 2), turned(lse, "shard", 1))
    lses = after(lses, lists)
    parts, whole_lse = head_combine(seq, (ctx_own, ctx_rest), target_rows, ids_by, lses, vocab)
    out_grad = lax.psum_scatter(parts, "shard", scatter_dimension=0, tiled=True)
    dense = head_table([two["out"], later, far_a, far_b, before], word_table, whole_lse, ids_by, 0, 6, 1280)

    bit = 1
    while bit < dp:
        lists = jnp.concatenate([lists, crossed(lists, "dp", bit)], axis=0)
        bit *= 2
    lists = jnp.concatenate([lists, crossed(lists, "section", 1)], axis=0)
    out_grad = after(out_grad, (dense, lists))
    dense = lax.psum_scatter(dense, both, scatter_dimension=0, tiled=True)

    d_middle, small_grads, keep_f, send_f = ffn_backward(z, weights_two, two, out_grad)
    in_two, in_low, keep_a, send_a = attention_backward(z, weights_two, two, d_middle, small_grads, False)
    came_f, came_a = crossed(send_f, "dp", 1), crossed(send_a, "dp", 1)
    d_middle, small_grads, keep_one_f, send_one_f = ffn_backward(z, weights_one, one, in_low)
    keep_f, came_f, keep_a, came_a = after((keep_f, came_f, keep_a, came_a), d_middle)
    split_two = add_cores_split((keep_a, keep_f), (came_a, came_f))
    d_middle = after(d_middle, split_two)
    terms_two = scatter_first(*split_two, "shard")
    came_one_f = crossed(send_one_f, "dp", 1)
    in_one, in_one_low, keep_one_a, send_one_a, d_embed = attention_backward(z, weights_one, one, d_middle, small_grads, True, seg_row, pos_rows)
    keep_one_f, came_one_f = after((keep_one_f, came_one_f), d_embed)
    send_one_a, d_embed = after((send_one_a, d_embed), terms_two)
    came_one_a = crossed(send_one_a, "dp", 1)
    columns = d_embed[None]
    steps = [("dp", 1 << n) for n in range(dp.bit_length() - 1)] + [("section", 1)]
    for n, (axis, bit) in enumerate(steps):
        middle = columns.shape[1] // 2
        columns = jnp.concatenate([columns[:, :middle], crossed(columns[:, middle:], axis, bit)], axis=0)
        if n == 0:
            came_one_a = after(came_one_a, columns)
    columns = columns[:, 0]
    stay_one, leave_one = add_core(z, keep_one_a, came_one_a, keep_one_f, came_one_f)
    came_one = crossed(leave_one, "dp", 2)
    terms_two = scatter_second(*terms_two, "shard")
    terms_two, columns = after((terms_two, columns), (stay_one, columns))
    stay_two, leave_two = halves_by_y(z, terms_two)
    ring_columns = gather_first(after(columns, stay_two), "shard")
    stay_one = after(stay_one, stay_two)
    split_one = add_split(stay_one, came_one)
    terms_one = scatter_first(*split_one, "shard")
    sum_two = stay_two + crossed(leave_two, "dp", 2)
    ring_columns = after(ring_columns, terms_one)
    sum_one = sum(scatter_second(*terms_one, "shard"))
    layer_one, extra = sum_one[: z.part], sum_one[z.part :]
    keep = jnp.concatenate([jnp.where(first, layer_one, sum_two), extra], axis=0)
    send = jnp.concatenate([jnp.where(first, sum_two, layer_one), extra], axis=0)
    total = keep + crossed(send, "section", 1)
    far_columns = gather_second(*after(ring_columns, sum_one), "shard")
    bit = 4
    while bit < dp:
        total = total + crossed(total, "dp", bit)
        bit *= 2
    total_y = crossed(total, "dp", 2)
    unpacked = unpack_grads(z, (total, total_y, crossed(total, "dp", 1), crossed(total_y, "dp", 1)))

    word_grad = table_grad([dense], (columns, *ring_columns, *far_columns), lists, vocab).T

    def by_micro(layer_one, layer_two, moved, dtype):
        own = jnp.where(first, layer_one, layer_two)
        sent = jnp.where(first, layer_two, layer_one).astype(moved)
        came = crossed(sent, "section", 1).astype(dtype)
        return jnp.stack([jnp.where(first, own, came), jnp.where(first, came, own)]).reshape(1, micro, 1, seq, d)

    layer_outputs = by_micro(one["out"], two["out"], BF16, BF16)
    input_grads = by_micro(in_one, in_two, BF16, F32)
    qkv_g, out_g, fin_g, fout_g, gain_g, bias_g, pos_g, eg_g, es_g = unpacked
    return (
        layer_outputs,
        input_grads,
        word_grad,
        pos_g,
        eg_g.reshape(-1),
        es_g.reshape(-1),
        qkv_g[None],
        out_g[None],
        fin_g[None],
        fout_g[None],
        gain_g[None],
        bias_g[None],
    )


def solution(mesh):
    rows = P(None, ("dp", "shard"), None)
    weights = (
        P("section", None, None, "shard", None),
        P("section", "shard", None),
        P("section", None, "shard", None),
        P("section", None, "shard", None),
        P("section", None, "shard"),
        P("section", None, "shard"),
    )
    states = P("section", None, ("dp", "shard"), None, None)
    return jax.shard_map(
        body,
        mesh=mesh,
        in_specs=(rows, rows, rows, P("shard", None), P("shard", None), P("shard"), P("shard"), *weights),
        out_specs=(states, states, P("shard", ("section", "dp")), P("shard", None), P("shard"), P("shard"), *weights),
        check_vma=False,
    )
```

```python
import math

import jax
import jax.numpy as jnp
from jax import lax
from jax.experimental import pallas as pl
from jax.experimental.pallas import tpu as pltpu
from jax.sharding import PartitionSpec as P

HEADS = 12
EPSILON = 1e-06
MASKED = -1000000000.0
F32 = jnp.float32
BF16 = jnp.bfloat16
MIB = 1 << 20


def nn(a, b):
    return jnp.dot(a, b, preferred_element_type=F32)


def nt(a, b):
    return lax.dot_general(a, b, (((1,), (1,)), ((), ())), preferred_element_type=F32)


def tn(a, b):
    return lax.dot_general(a, b, (((0,), (0,)), ((), ())), preferred_element_type=F32)


def iota(shape, axis):
    return lax.broadcasted_iota(jnp.int32, shape, axis)


def group_of(index, width, count):
    total = jnp.zeros(index.shape, jnp.int32)
    for step in range(1, count):
        total = total + (index >= step * width).astype(jnp.int32)
    return total


def normed(value):
    centered = value - jnp.mean(value, axis=-1, keepdims=True)
    scale = lax.rsqrt(jnp.mean(centered * centered, axis=-1, keepdims=True) + EPSILON)
    return centered * scale, scale


def norm_back(grad, unit, scale, gain):
    inner = grad * gain
    first = jnp.mean(inner, axis=-1, keepdims=True)
    second = jnp.mean(inner * unit, axis=-1, keepdims=True)
    return scale * (inner - first - unit * second)


def col_sum(value):
    return jnp.sum(value, axis=0, keepdims=True)


def upright(row, count):
    return jnp.broadcast_to(row.astype(F32), (128, count)).T[:, 0:1]


def call(kernel, outs, ins, specs=None, scratch=(), limit=56, flops=0, moved=0, grid=None, out_specs=None, name=None):
    vmem = pl.BlockSpec(memory_space=pltpu.VMEM)
    extra = {} if grid is None else {"grid": grid}
    return pl.pallas_call(
        kernel,
        out_shape=outs,
        in_specs=[vmem if s is None else s for s in (specs or [None] * len(ins))],
        out_specs=out_specs if out_specs is not None else [vmem] * len(outs),
        scratch_shapes=list(scratch),
        compiler_params=pltpu.CompilerParams(vmem_limit_bytes=limit * MIB),
        cost_estimate=pl.CostEstimate(flops=0, bytes_accessed=0, transcendentals=0),
        name=name,
        **extra,
    )(*ins)


def like(shape, dtype):
    return jax.ShapeDtypeStruct(shape, dtype)


def turned(block, axis, by):
    size = lax.axis_size(axis)
    return lax.ppermute(block, axis, [(i, (i + by) % size) for i in range(size)])


def crossed(block, axis, bit):
    return lax.ppermute(block, axis, [(i, i ^ bit) for i in range(lax.axis_size(axis))])


def after(value, first):
    return lax.optimization_barrier((value, first))[0]


def scatter_first(c0, c1, c2a, c2b, c3, axis, wait=()):
    half = c2a.shape[0]
    right, left = after((turned(c2a, axis, 1), turned(c2b, axis, -1)), wait)
    return c0, jnp.concatenate([c1[:half] + right, c1[half:]], axis=0), jnp.concatenate([c3[:half], c3[half:] + left], axis=0)


def scatter_second(c0, c1, c3, axis):
    return c0, turned(c1, axis, 1), turned(c3, axis, -1)


def side_of(bit):
    return (lax.axis_index("dp") // bit) % 2


def gather_first(block, axis):
    return turned(block, axis, 1), turned(block, axis, -1)


def gather_second(before, later, axis):
    half = before.shape[0] // 2
    return turned(before[:half], axis, 1), turned(later[half:], axis, -1)


def ring_gather(block, axis):
    first = gather_first(block, axis)
    return (*first, *gather_second(*first, axis))


class Sizes:
    def __init__(self, qkv, out, shards, pos_rows):
        _, _, groups, part, width = qkv
        self.shards, self.groups, self.gw, self.gi = shards, groups, width, part
        self.d = out[2]
        self.part = out[1]
        self.at_small = 3 * part
        self.rows = 2 * self.part
        self.pos = pos_rows // 4
        self.extra = self.pos + 16


def pack_weights(z, qkv, out, fin, fout, small):
    def kernel(qkv_ref, out_ref, fin_ref, fout_ref, small_ref, o_ref, pair_ref, own_ref):
        shard = lax.axis_index("shard")

        def spread(pieces):
            return jnp.concatenate([piece.astype(F32) for piece in pieces], axis=1).astype(BF16)

        o_ref[0, 0] = out_ref[...]
        o_ref[0, 1] = fin_ref[...].reshape(z.part, z.d)
        for c in range(3):
            o_ref[1, 0, c * z.gi : (c + 1) * z.gi] = spread([qkv_ref[c, g] for g in range(z.groups)])
        tall = jnp.concatenate([small_ref[...].astype(F32), jnp.zeros((16 - small_ref.shape[0], z.part), F32)], axis=0)
        wide = jnp.concatenate([tall] * z.shards, axis=1)
        lane = group_of(iota(wide.shape, 1), z.part, z.shards)
        o_ref[1, 0, z.at_small : z.at_small + 16] = jnp.where(lane == shard, wide, 0.0).astype(BF16)
        o_ref[1, 0, z.at_small + 16 : z.part] = jnp.zeros((z.part - z.at_small - 16, z.d), BF16)
        o_ref[1, 1] = spread([fout_ref[g] for g in range(z.groups)])
        pair_ref[...] = o_ref[side_of(1)]
        own_ref[...] = o_ref[side_of(1), side_of(2)]

    outs = [like((2, 2, z.part, z.d), BF16), like((2, z.part, z.d), BF16), like((z.part, z.d), BF16)]
    return call(kernel, outs, (qkv, out, fin, fout, small), name="pack")


class Pieces:
    def __init__(self, z, local, mine, pairs, others, layer):
        self.z, self.layer = z, layer
        self.arrays = (local, *mine, *pairs, *others)
        self.specs = [pl.BlockSpec(memory_space=pl.ANY)] * len(self.arrays)
        self.scratch = [pltpu.VMEM((2, z.shards, z.rows, z.d), BF16), pltpu.SemaphoreType.DMA((2, 2, 4))]

    def start(self, refs, w_ref, sems, parts):
        z = self.z
        core, y = side_of(1), side_of(2)
        shard = lax.axis_index("shard")
        own_layer = lax.axis_index("section") == self.layer
        local, mine, pairs, others = refs[0], refs[1:9], refs[9:11], refs[11:19]
        waits = {}
        for part in parts:
            copies = []
            for side in range(2):
                place = core if side == 0 else 1 - core
                for n, by in enumerate((0, 3, 1, 2)):
                    target = w_ref.at[place, (shard + by) % z.shards, pl.ds(part * z.part, z.part)]
                    sem = sems.at[part, side, n]
                    rows = pl.ds((n - 1) * z.part, z.part)
                    choices = []
                    for across in range(2):
                        here = (y == part) if across == 0 else (y != part)
                        at = 2 * across + side
                        if n == 0:
                            own, other = local.at[place, part], pairs[side].at[part]
                        elif n < 3:
                            own, other = mine[2 * at].at[rows], others[2 * at].at[rows]
                        else:
                            own, other = mine[2 * at + 1], others[2 * at + 1]
                        choices.append((jnp.logical_and(here, own_layer), own))
                        choices.append((jnp.logical_and(here, jnp.logical_not(own_layer)), other))
                    for here, source in choices:
                        copy = pltpu.make_async_copy(source, target, sem)
                        pl.when(here)(copy.start)
                    copies.append(pltpu.make_async_copy(choices[1][1], target, sem))
            waits[part] = copies
        return waits


def wait_all(copies):
    for copy in copies:
        copy.wait()


class Loads:
    def __init__(self, arrays):
        self.names = list(arrays)
        self.arrays = list(arrays.values())
        self.specs = [pl.BlockSpec(memory_space=pl.ANY)] * len(self.arrays)
        self.scratch = [pltpu.VMEM(a.shape, a.dtype) for a in self.arrays] + [pltpu.SemaphoreType.DMA((len(self.arrays),))]

    def start(self, refs, scratch):
        self.buffers = dict(zip(self.names, scratch))
        self.copies = {
            name: pltpu.make_async_copy(ref, buffer, scratch[-1].at[n])
            for n, (name, ref, buffer) in enumerate(zip(self.names, refs, scratch))
        }
        for copy in self.copies.values():
            copy.start()

    def __getitem__(self, name):
        copy = self.copies.pop(name, None)
        if copy is not None:
            copy.wait()
        return self.buffers[name]


class Stores:
    def __init__(self, shapes, split=()):
        self.names = list(shapes)
        self.shapes = list(shapes.values())
        self.split = split
        self.specs = [pl.BlockSpec(memory_space=pl.ANY)] * len(self.shapes)
        count = sum(a.shape[0] if name in split else 1 for name, a in shapes.items())
        self.scratch = [pltpu.VMEM(a.shape, a.dtype) for a in self.shapes] + [pltpu.SemaphoreType.DMA((count,))]

    def bind(self, refs, scratch):
        self.refs = dict(zip(self.names, refs))
        self.buffers = dict(zip(self.names, scratch))
        self.sems = scratch[-1]
        self.copies = []

    def put(self, name, value, index=None):
        source, target = self.buffers[name], self.refs[name]
        if index is not None:
            source, target = source.at[index], target.at[index]
        source[...] = value.astype(source.dtype)
        copy = pltpu.make_async_copy(source, target, self.sems.at[len(self.copies)])
        copy.start()
        self.copies.append(copy)

    def finish(self):
        wait_all(self.copies)


class Weights:
    def __init__(self, z, w_ref):
        self.z, self.w = z, w_ref

    def out(self):
        z = self.z
        return self.w[0, :, 0 : z.part, :].reshape(z.d, z.d)

    def small(self):
        z = self.z
        return sum(self.w[1, h, z.at_small : z.at_small + 16, :].astype(F32) for h in range(z.shards))

    def proj(self, c):
        z = self.z
        dense = self.w[1, :, c * z.gi : (c + 1) * z.gi, :].reshape(z.gw, z.d)
        tall = jnp.concatenate([dense] * z.groups, axis=0)
        keep = group_of(iota(tall.shape, 0), z.gw, z.groups) == group_of(iota(tall.shape, 1), z.gw, z.groups)
        return jnp.where(keep, tall, jnp.zeros_like(tall))

    def fin(self, g):
        z = self.z
        row = z.part + g * z.gi
        dense = self.w[0, :, row : row + z.gi, :].reshape(z.gw, z.d)
        blank = jnp.zeros_like(dense)
        return jnp.concatenate([dense, blank] if g % 2 == 0 else [blank, dense], axis=0)

    def fout(self, g):
        z = self.z
        at = (g // 2) * 2 * z.gw
        pair = self.w[1, :, z.part : z.rows, at : at + 2 * z.gw].reshape(z.d, 2 * z.gw)
        keep = (iota(pair.shape, 1) >= z.gw) == (g % 2 == 1)
        return jnp.where(keep, pair, jnp.zeros_like(pair))


def embed_parts(picked, ids_by, pos_table, vocab):
    count, _, seq = ids_by.shape
    width = picked.shape[1]
    half = seq // 2
    rows = pos_table.shape[0]

    def kernel(p_ref, i_ref, t_ref, c0, c1, c2a, c2b, c3):
        shard = lax.axis_index("shard")
        for k in range(count):
            span = slice(k * seq, (k + 1) * seq)
            token, seg_row = i_ref[k, 0:1], i_ref[k, 2:3]
            seg_col = upright(seg_row, seq)
            same = seg_col == seg_row.astype(F32)
            earlier = iota((seq, seq), 1) < iota((seq, seq), 0)
            place = jnp.sum(jnp.where(same & earlier, 1.0, 0.0), axis=1, keepdims=True).astype(jnp.int32) - shard * rows
            spot = (iota((seq, rows), 1) == place).astype(BF16)
            local = token - shard * vocab
            inside = upright(jnp.where((local >= 0) & (local < vocab), 1.0, 0.0), seq)
            word = jnp.where(inside > 0.5, p_ref[span].astype(F32), 0.0)
            total = (word + nn(spot, t_ref[...])).astype(BF16)
            if k == 2:
                c2a[...] = total[:half]
                c2b[...] = total[half:]
            else:
                (c0, c1, None, c3)[k][...] = total

    full, part = like((seq, width), BF16), like((half, width), BF16)
    return call(kernel, [full, full, part, part, full], (picked, ids_by, pos_table), moved=4 * MIB, name="embed_parts")


def layer_forward(z, pieces, seg_row, first, words=None, layer_in=None):
    seq = seg_row.shape[1]
    d = z.d
    flat, whole = like((seq, d), BF16), like((seq, d), F32)
    shapes = {"q": flat, "k": flat, "v": flat, "p": like((HEADS, seq, seq), BF16), "att": flat, "n1": whole, "mid": flat}
    shapes.update({"act": like((z.groups, seq, d), BF16), "slope": like((z.groups, seq, d), BF16)})
    shapes.update({"n2": whole, "stats": like((seq, 128), F32), "small": like((16, d), F32), "out": flat})
    if first:
        shapes.update({"x": flat, "n0": whole})
    stores = Stores(shapes, split=("p", "act", "slope"))
    head = d // HEADS
    inputs = list(words) if first else [layer_in]

    def kernel(*refs):
        piece_refs, refs = refs[: len(pieces.arrays)], refs[len(pieces.arrays) :]
        row_ref, refs = refs[0], refs[1:]
        in_refs, refs = refs[: len(inputs)], refs[len(inputs) :]
        out_refs, refs = refs[: len(shapes)], refs[len(shapes) :]
        w_ref, sems, *buffers = refs
        waits = pieces.start(piece_refs, w_ref, sems, (0, 1))
        stores.bind(out_refs, buffers)
        put = stores.put
        w = Weights(z, w_ref)
        if first:
            unit, r0 = normed(sum(ref[...].astype(F32) for ref in in_refs))
            put("n0", unit)
        wait_all(waits[0])
        small = w.small()
        put("small", small)
        if first:
            x = unit * small[11:12] + small[12:13]
            x_low = x.astype(BF16)
            put("x", x_low)
        else:
            r0 = jnp.zeros((seq, 1), F32)
            x_low = in_refs[0][...]
            x = x_low.astype(F32)
        q = (nn(x_low, w.proj(0)).astype(BF16).astype(F32) * (1.0 / math.sqrt(head))).astype(BF16)
        k = nn(x_low, w.proj(1)).astype(BF16)
        v = (nn(x_low, w.proj(2)) + small[2:3]).astype(BF16)
        put("q", q)
        put("k", k)
        put("v", v)
        same = upright(row_ref[...], seq) == row_ref[...].astype(F32)
        second = iota((seq, 128), 1) >= head
        tiles = []
        for t in range(d // 128):
            lanes = slice(t * 128, (t + 1) * 128)
            q_t, k_t, v_t = q[:, lanes], k[:, lanes], v[:, lanes]
            results = []
            for j in range(2):
                picked = jnp.where(second == (j == 1), q_t, jnp.zeros_like(q_t))
                scores = jnp.where(same, nt(picked, k_t), MASKED)
                scores = jnp.exp(scores - jnp.max(scores, axis=-1, keepdims=True))
                probs = (scores * (1.0 / jnp.sum(scores, axis=-1, keepdims=True))).astype(BF16)
                put("p", probs, 2 * t + j)
                results.append(nn(probs, v_t))
            tiles.append(jnp.where(second, results[1], results[0]).astype(BF16))
        attended = jnp.concatenate(tiles, axis=1)
        put("att", attended)
        unit, r1 = normed(x + (nn(attended, w.out()) + small[3:4]))
        put("n1", unit)
        middle = unit * small[0:1] + small[4:5]
        middle_low = middle.astype(BF16)
        put("mid", middle_low)
        wait_all(waits[1])
        back = [None] * (z.groups // 2)
        for g in range(z.groups):
            pair = slice((g // 2) * 2 * z.gw, (g // 2 + 1) * 2 * z.gw)
            pre = nn(middle_low[:, pair], w.fin(g)) + small[5 + g : 6 + g]
            half = 0.5 + 0.5 * lax.erf(pre * math.sqrt(0.5))
            slope = half + pre * (jnp.exp(-0.5 * pre * pre) * (1.0 / math.sqrt(2.0 * math.pi)))
            active = (pre * half).astype(BF16)
            put("act", active, g)
            put("slope", slope, g)
            added = nn(active, w.fout(g))
            back[g // 2] = added if back[g // 2] is None else back[g // 2] + added
        unit, r2 = normed(middle + (jnp.concatenate(back, axis=1) + small[9:10]))
        put("n2", unit)
        put("out", unit * small[1:2] + small[10:11])
        lane = iota((seq, 128), 1)
        put("stats", jnp.where(lane == 0, r0, jnp.where(lane == 1, r1, r2)))
        stores.finish()

    outs = call(
        kernel,
        stores.shapes,
        (*pieces.arrays, seg_row, *inputs),
        specs=pieces.specs + [None] * (1 + len(inputs)),
        out_specs=stores.specs,
        scratch=pieces.scratch + stores.scratch,
        flops=3 * 10**9,
        moved=16 * MIB,
        name="layer_first" if first else "layer_second",
    )
    return dict(zip(stores.names, outs))


def send_halves(z, g_ref, keep_ref, send_ref, sems):
    core = lax.axis_index("dp") % 2
    shard = lax.axis_index("shard")
    copies = []
    for k in range(z.shards):
        to = (shard + k) % z.shards
        copies.append(pltpu.make_async_copy(g_ref.at[1 - core, to], send_ref.at[k], sems.at[2 * k]))
        copies.append(pltpu.make_async_copy(g_ref.at[core, to], keep_ref.at[k], sems.at[2 * k + 1]))
    for copy in copies:
        copy.start()
    return copies


def ffn_backward(z, pieces, state, out_grad):
    seq, d = out_grad.shape
    loads = Loads({"dy": out_grad, **{key: state[key] for key in ("n2", "stats", "small", "mid", "act", "slope")}})
    outs = [like((seq, d), F32), like((16, d), F32)] + [like((z.shards, z.part, d), BF16)] * 2

    def kernel(*refs):
        piece_refs, refs = refs[: len(pieces.arrays)], refs[len(pieces.arrays) :]
        load_refs, refs = refs[: len(loads.names)], refs[len(loads.names) :]
        dm_ref, small_ref, keep_ref, send_ref, w_ref, sems, g_ref, out_sems, *buffers = refs
        loads.start(load_refs, buffers)
        waits = pieces.start(piece_refs, w_ref, sems, (1,))
        w = Weights(z, w_ref)
        dy = loads["dy"][...].astype(F32)
        n2 = loads["n2"][...]
        scale = loads["stats"][:, 2:3]
        small = loads["small"][...]
        gain_two, shift_two = col_sum(dy * n2), col_sum(dy)
        d_final = norm_back(dy, n2, scale, small[1:2])
        d_ffn = d_final.astype(BF16)
        ffn_shift = col_sum(d_ffn.astype(F32))
        middle_t = loads["mid"][...].T
        act, slope = loads["act"], loads["slope"]
        wait_all(waits[1])
        pre_shift = []
        pair_back = [None] * (z.groups // 2)
        for p in range(z.groups // 2):
            lanes = slice(p * 2 * z.gw, (p + 1) * 2 * z.gw)
            out_pair = d_ffn[:, lanes]
            back_pair = []
            for g in (2 * p, 2 * p + 1):
                d_pre = (nt(out_pair, w.fout(g)) * slope[g].astype(F32)).astype(BF16)
                pre_shift.append(col_sum(d_pre.astype(F32)))
                back_pair.append(tn(act[g], out_pair))
                grad_in = nn(middle_t[g * z.gw : (g + 1) * z.gw], d_pre)
                g_ref[0, :, g * z.gi : (g + 1) * z.gi, :] = grad_in.astype(BF16).reshape(z.shards, z.gi, d)
                added = nt(d_pre, w.fin(g))
                pair_back[p] = added if pair_back[p] is None else pair_back[p] + added
            odd = iota(back_pair[0].shape, 1) >= z.gw
            both = jnp.where(odd, back_pair[1], back_pair[0]).astype(BF16)
            g_ref[1, :, :, lanes] = both.reshape(z.shards, z.part, 2 * z.gw)
        copies = send_halves(z, g_ref, keep_ref, send_ref, out_sems)
        dm_ref[...] = d_final + jnp.concatenate(pair_back, axis=1)
        blank = jnp.zeros((1, d), F32)
        small_ref[...] = jnp.concatenate(
            [blank, gain_two, blank, blank, blank, *pre_shift, ffn_shift, shift_two, jnp.zeros((5, d), F32)], axis=0
        )
        wait_all(copies)

    anywhere = pl.BlockSpec(memory_space=pl.ANY)
    return call(
        kernel,
        outs,
        (*pieces.arrays, *loads.arrays),
        specs=pieces.specs + loads.specs,
        out_specs=[pl.BlockSpec(memory_space=pltpu.VMEM)] * 2 + [anywhere] * 2,
        scratch=pieces.scratch + [pltpu.VMEM((2, z.shards, z.part, d), BF16), pltpu.SemaphoreType.DMA((2 * z.shards,))] + loads.scratch,
        flops=8 * 10**9,
        moved=16 * MIB,
        name="ffn_back",
    )


def attention_backward(z, pieces, state, d_middle, small_in, first, seg_row=None, pos_rows=0):
    seq, d = d_middle.shape
    head = d // HEADS
    keys = ["n1", "stats", "small", "att", "q", "k", "v", "p", "x"] + (["n0"] if first else [])
    loads = Loads({"dm": d_middle, **{key: state[key] for key in keys}, "grads": small_in, **({"seg": seg_row} if first else {})})
    rows = z.part + (2 * z.extra if first else 0)
    outs = [like((seq, d), F32), like((seq, d), BF16)] + [like((z.shards, rows, d), BF16)] * 2
    blocks = 2 * lax.axis_size("dp")
    if first:
        outs.append(like((blocks, d // blocks, seq), BF16))

    def kernel(*refs):
        piece_refs, refs = refs[: len(pieces.arrays)], refs[len(pieces.arrays) :]
        load_refs, refs = refs[: len(loads.names)], refs[len(loads.names) :]
        dx_ref, low_ref, keep_ref, send_ref = refs[:4]
        de_ref = refs[4] if first else None
        w_ref, sems, g_ref, out_sems, *buffers = refs[len(outs) :]
        loads.start(load_refs, buffers)
        waits = pieces.start(piece_refs, w_ref, sems, (0,))
        w = Weights(z, w_ref)
        d_middle = loads["dm"][...]
        n1 = loads["n1"][...]
        stats = loads["stats"][...]
        r0, r1 = stats[:, 0:1], stats[:, 1:2]
        small = loads["small"][...]
        gain_one, shift_one = col_sum(d_middle * n1), col_sum(d_middle)
        d_mid = norm_back(d_middle, n1, r1, small[0:1])
        d_branch = d_mid.astype(BF16)
        branch_shift = col_sum(d_branch.astype(F32))
        g_ref[0, :, 0 : z.part, :] = tn(loads["att"][...], d_branch).astype(BF16).reshape(z.shards, z.part, d)
        wait_all(waits[0])
        d_att = nt(d_branch, w.out()).astype(BF16)
        second = iota((seq, 128), 1) >= head
        scale = 1.0 / math.sqrt(head)
        q_ref, k_ref, v_ref, p_ref = (loads[key] for key in ("q", "k", "v", "p"))
        dq, dk, dv = [], [], []
        for t in range(d // 128):
            lanes = slice(t * 128, (t + 1) * 128)
            q_t, k_t, v_t, a_t = q_ref[:, lanes], k_ref[:, lanes], v_ref[:, lanes], d_att[:, lanes]
            parts = []
            for j in range(2):
                a_j = jnp.where(second == (j == 1), a_t, jnp.zeros_like(a_t))
                probs_low = p_ref[2 * t + j]
                probs = probs_low.astype(F32)
                d_probs = nt(a_j, v_t)
                inner = jnp.sum(probs * d_probs, axis=-1, keepdims=True)
                d_scores = (probs * (d_probs - inner)).astype(BF16)
                parts.append((nn(d_scores, k_t), tn(d_scores, q_t), tn(probs_low, a_t)))
            dq.append((jnp.where(second, parts[1][0], parts[0][0]) * scale).astype(BF16))
            dk.append(jnp.where(second, parts[1][1], parts[0][1]).astype(BF16))
            dv.append(jnp.where(second, parts[1][2], parts[0][2]).astype(BF16))
        value_shift = col_sum(jnp.concatenate(dv, axis=1).astype(F32))
        x_t = loads["x"][...].T
        d_in = d_mid
        for c, parts in enumerate((dq, dk, dv)):
            d_c = jnp.concatenate(parts, axis=1)
            full = nn(x_t, d_c)
            lane = group_of(iota((z.gw, d), 1), z.gw, z.groups)
            grad = full[0 : z.gw]
            for g in range(1, z.groups):
                grad = jnp.where(lane == g, full[g * z.gw : (g + 1) * z.gw], grad)
            g_ref[1, :, c * z.gi : (c + 1) * z.gi, :] = grad.astype(BF16).reshape(z.shards, z.gi, d)
            d_in = d_in + nt(d_c, w.proj(c))
        blank = jnp.zeros((1, d), F32)
        small_grads = jnp.concatenate([gain_one, blank, value_shift, branch_shift, shift_one, jnp.zeros((11, d), F32)], axis=0)
        small_grads = (small_grads + loads["grads"][...]).astype(BF16)
        spare = jnp.zeros((z.part - z.at_small - 16, d), BF16)
        for h in range(z.shards):
            g_ref[1, h, z.at_small : z.at_small + 16, :] = small_grads
            g_ref[1, h, z.at_small + 16 : z.part, :] = spare
        if first:
            n0 = loads["n0"][...]
            embed_grads = jnp.concatenate([col_sum(d_in * n0), col_sum(d_in), jnp.zeros((14, d), F32)], axis=0).astype(BF16)
            d_embed = norm_back(d_in, n0, r0, small[11:12])
            d_embed_t = d_embed.T
            bits = blocks.bit_length() - 1
            me = lax.axis_index("section") * (blocks // 2) + lax.axis_index("dp")
            for b in range(blocks):
                to = me ^ b
                place = sum(((to >> bit) & 1) << (bits - 1 - bit) for bit in range(bits))
                de_ref[place] = d_embed_t[b * (d // blocks) : (b + 1) * (d // blocks)].astype(BF16)
            seg = loads["seg"][...]
            same = upright(seg, seq) == seg.astype(F32)
            later = iota((seq, seq), 0) < iota((seq, seq), 1)
            place = jnp.sum(jnp.where(same & later, 1.0, 0.0), axis=0, keepdims=True).astype(jnp.int32)
            spot = (iota((pos_rows, seq), 0) == place).astype(BF16)
            pos_grad = nn(spot, d_embed.astype(BF16)).astype(BF16)
            for side in range(2):
                for h in range(z.shards):
                    for y in range(2):
                        row = z.part + y * z.extra
                        part = pos_grad[(2 * side + y) * z.pos : (2 * side + y + 1) * z.pos]
                        g_ref[side, h, row : row + z.pos, :] = part if h == 0 else jnp.zeros_like(part)
                        g_ref[side, h, row + z.pos : row + z.extra, :] = embed_grads
        copies = send_halves(z, g_ref, keep_ref, send_ref, out_sems)
        dx_ref[...] = d_in
        low_ref[...] = d_in.astype(BF16)
        wait_all(copies)

    anywhere = pl.BlockSpec(memory_space=pl.ANY)
    vmem = pl.BlockSpec(memory_space=pltpu.VMEM)
    return call(
        kernel,
        outs,
        (*pieces.arrays, *loads.arrays),
        specs=pieces.specs + loads.specs,
        out_specs=[vmem, vmem, anywhere, anywhere] + [vmem] * (len(outs) - 4),
        scratch=pieces.scratch + [pltpu.VMEM((2, z.shards, rows, d), BF16), pltpu.SemaphoreType.DMA((2 * z.shards,))] + loads.scratch,
        flops=8 * 10**9,
        moved=16 * MIB,
        name="att_back",
    )


def add_cores_split(z, keep, came):
    shards, high, d = keep[0].shape
    rows = high + z.part
    half = rows // 32 * 16

    def kernel(a_ref, f_ref, b_ref, e_ref, c0, c1, c2a, c2b, c3):
        for k, ref in ((0, c0), (1, c1), (3, c3)):
            ref[:high] = a_ref[k] + b_ref[k]
            ref[high:] = f_ref[k] + e_ref[k]
        c2a[...] = a_ref[2, :half] + b_ref[2, :half]
        if half < high:
            c2b[: high - half] = a_ref[2, half:] + b_ref[2, half:]
        c2b[high - half :] = f_ref[2] + e_ref[2]

    full = like((rows, d), BF16)
    outs = [full, full, like((half, d), BF16), like((rows - half, d), BF16), full]
    return call(kernel, outs, (*keep, *came), name="add_cores_split")


def head_forward(pieces, table):
    count = sum(piece.shape[0] for piece in pieces)
    vocab, d = table.shape
    tiles = 3
    block = vocab // tiles
    part = block // 2
    chunk = 256
    many = len(pieces)

    def kernel(*refs):
        piece_refs, (w_ref, ctx_ref, lse_ref, x_ref, m_ref, s_ref, acc_ref) = refs[:many], refs[many:]
        step = pl.program_id(0)

        @pl.when(step == 0)
        def _():
            at = 0
            for ref in piece_refs:
                x_ref[at : at + ref.shape[0]] = ref[...]
                at += ref.shape[0]
            m_ref[...] = jnp.full(m_ref.shape, -1e30, F32)
            s_ref[...] = jnp.zeros(s_ref.shape, F32)
            acc_ref[...] = jnp.zeros(acc_ref.shape, F32)

        units = [(c, r) for c in range(2) for r in range(count // chunk)]

        def logits_of(unit):
            c, r = unit
            return nt(x_ref[r * chunk : (r + 1) * chunk], w_ref[c * part : (c + 1) * part])

        logits = logits_of(units[0])
        for n, (c, r) in enumerate(units):
            following = logits_of(units[n + 1]) if n + 1 < len(units) else None
            span = slice(r * chunk, (r + 1) * chunk)
            old = m_ref[span]
            new = jnp.maximum(old, jnp.max(logits, axis=-1, keepdims=True))
            keep = jnp.exp(old - new)
            weight = jnp.exp(logits - new)
            s_ref[span] = s_ref[span] * keep + jnp.sum(weight, axis=-1, keepdims=True)
            acc_ref[span] = acc_ref[span] * keep + nn(weight.astype(BF16), w_ref[c * part : (c + 1) * part])
            m_ref[span] = new
            logits = following

        @pl.when(step == tiles - 1)
        def _():
            total = s_ref[...]
            ctx_ref[...] = acc_ref[...] * (1.0 / total)
            lse = m_ref[...] + jnp.log(total)
            lse_ref[...] = jnp.broadcast_to(lse, (count, 128)).T[0:8]

    fixed = lambda i: (0, 0)
    return call(
        kernel,
        [like((count, d), F32), like((8, count), F32)],
        (*pieces, table),
        specs=[pl.BlockSpec(piece.shape, fixed) for piece in pieces] + [pl.BlockSpec((block, d), lambda i: (i, 0))],
        out_specs=[pl.BlockSpec((count, d), fixed), pl.BlockSpec((8, count), fixed)],
        scratch=[pltpu.VMEM((count, d), BF16), pltpu.VMEM((count, 1), F32), pltpu.VMEM((count, 1), F32), pltpu.VMEM((count, d), F32)],
        grid=(tiles,),
        flops=8 * count * vocab * d,
        moved=14 * MIB,
        name="head_forward",
    )


def head_combine(seq, ctxs, picked, ids_by, lses, vocab):
    shards = ids_by.shape[0]
    d = picked.shape[1]

    def kernel(x0_ref, x1_ref, x2_ref, x3_ref, p_ref, i_ref, a_ref, b_ref, c_ref, e_ref, out_ref, lse_ref):
        shard = lax.axis_index("shard")
        parts = (a_ref, b_ref, c_ref, e_ref)
        for k in range(shards):
            rows = [parts[m][:, ((k - m) % shards) * seq : ((k - m) % shards + 1) * seq] for m in range(shards)]
            top = rows[0]
            for row in rows[1:]:
                top = jnp.maximum(top, row)
            total = top + jnp.log(sum(jnp.exp(row - top) for row in rows))
            whole = upright(total, seq)
            span = slice(k * seq, (k + 1) * seq)
            lse_ref[span] = whole
            weight = upright(jnp.exp(rows[0] - total), seq)
            local = i_ref[k, 1:2] - shard * vocab
            inside = upright(jnp.where((local >= 0) & (local < vocab), 1.0, 0.0), seq)
            hit = jnp.where(inside > 0.5, p_ref[span].astype(F32), 0.0)
            ctx = (x0_ref, x1_ref, x2_ref, x3_ref)[k][...]
            target = pl.multiple_of(((shard + k) % shards) * seq, seq)
            out_ref[pl.ds(target, seq), :] = (ctx * weight - hit).astype(BF16)

    return call(
        kernel,
        [like((shards * seq, d), BF16), like((shards * seq, 1), F32)],
        (*ctxs, picked, ids_by, *lses),
        moved=7 * MIB,
        name="head_combine",
    )


def head_table(pieces, table, lse, ids_by, first_tile, tiles, block):
    count = sum(piece.shape[0] for piece in pieces)
    shards, _, seq = ids_by.shape
    vocab, d = table.shape
    width = min(vocab - first_tile * block, tiles * block)
    chunk = 256
    many = len(pieces)

    def kernel(*refs):
        piece_refs, (w_ref, lse_ref, i_ref, o_ref, x_ref, xt_ref, t_ref, p_ref) = refs[:many], refs[many:]
        step = pl.program_id(0)

        @pl.when(step == 0)
        def _():
            at = 0
            for ref in piece_refs:
                x_ref[at : at + ref.shape[0]] = ref[...]
                at += ref.shape[0]
            xt_ref[...] = x_ref[...].T
            start = lax.axis_index("shard") * vocab + first_tile * block
            for k in range(shards):
                t_ref[k * seq : (k + 1) * seq] = upright(i_ref[k, 1:2] - start, seq).astype(jnp.int32)

        w = w_ref[...]
        for r in range(count // chunk):
            span = slice(r * chunk, (r + 1) * chunk)
            logits = nt(x_ref[span], w)
            hit = iota(logits.shape, 1) == t_ref[span] - step * block
            p_ref[span] = (jnp.exp(logits - lse_ref[span]) - jnp.where(hit, 1.0, 0.0)).astype(BF16)
        o_ref[...] = nn(xt_ref[...], p_ref[...]).astype(BF16)

    fixed = lambda i: (0, 0)
    return call(
        kernel,
        [like((d, width), BF16)],
        (*pieces, table, lse, ids_by),
        specs=[pl.BlockSpec(piece.shape, fixed) for piece in pieces]
        + [
            pl.BlockSpec((block, d), lambda i: (i + first_tile, 0)),
            pl.BlockSpec((count, 1), fixed),
            pl.BlockSpec(ids_by.shape, lambda i: (0, 0, 0)),
        ],
        out_specs=[pl.BlockSpec((d, block), lambda i: (0, i))],
        scratch=[pltpu.VMEM((count, d), BF16), pltpu.VMEM((d, count), BF16), pltpu.VMEM((count, 1), jnp.int32), pltpu.VMEM((count, block), BF16)],
        grid=(tiles,),
        flops=6 * count * width * d,
        moved=8 * MIB,
        name="head_table",
    )[0]


def list_tokens(ids, vocab):
    count = ids.shape[1]
    unit = 1 << (vocab - 1).bit_length()

    def kernel(ids_ref, list_ref):
        start = lax.axis_index("shard") * vocab

        def step(i, many):
            local = ids_ref[0, i] - start
            list_ref[0, many] = i * unit + local
            return many + ((local >= 0) & (local < vocab)).astype(jnp.int32)

        list_ref[0, count] = lax.fori_loop(0, count, step, jnp.int32(0), unroll=8)

    smem = pl.BlockSpec(memory_space=pltpu.SMEM)
    return call(kernel, [like((1, count + 128), jnp.int32)], (ids,), specs=[smem], out_specs=[smem], name="list_tokens")[0]


def table_grad(dense, pieces, lists, vocab):
    width = dense.shape[0]
    sources, _, seq = pieces[0].shape
    shards = 4
    listed = shards * seq
    unit = 1 << (vocab - 1).bit_length()
    ways = 4

    def kernel(d_ref, own_ref, later_ref, before_ref, far_a_ref, far_b_ref, l_ref, o_ref, flat_ref, *acc):
        half = sources // 2
        for j in range(sources):
            far = far_a_ref[j] if j < half else far_b_ref[j - half]
            for k, block in enumerate((own_ref[j], later_ref[j], before_ref[j], far)):
                at = j * listed + k * seq
                flat_ref[at : at + seq] = block.astype(F32).T
        for ref in acc:
            ref[...] = jnp.zeros(ref.shape, F32)

        def add(ref, j, at):
            packed = l_ref[j, at]
            row = packed & (unit - 1)
            token = lax.shift_right_logical(packed, unit.bit_length() - 1) + j * listed
            ref[pl.ds(row, 1), :] += flat_ref[pl.ds(token, 1), :]

        def source(j, carry):
            many = l_ref[j, listed]
            rounds = many // ways

            def step(i, carry):
                for way, ref in enumerate(acc):
                    add(ref, j, i * ways + way)
                return carry

            def rest(at, carry):
                add(acc[0], j, at)
                return carry

            lax.fori_loop(0, rounds, step, jnp.int32(0))
            lax.fori_loop(rounds * ways, many, rest, jnp.int32(0))
            return carry

        lax.fori_loop(0, sources, source, jnp.int32(0))
        o_ref[...] = d_ref[...].astype(F32) + sum(ref[...] for ref in acc).T

    smem = pl.BlockSpec(memory_space=pltpu.SMEM)
    return call(
        kernel,
        [like((width, vocab), F32)],
        (dense, *pieces, lists),
        specs=[None] * 6 + [smem],
        scratch=[pltpu.VMEM((sources * listed, width), F32)] + [pltpu.VMEM((vocab, width), F32)] * ways,
        limit=60,
        name="table_grad",
    )[0]


def unpack_grads(z, own, other):
    rows = z.rows + 2 * z.extra

    def kernel(own_ref, other_ref, qkv_ref, out_ref, fin_ref, fout_ref, gain_ref, bias_ref, pos_ref, eg_ref, es_ref, all_ref):
        core = side_of(1)
        shard = lax.axis_index("shard")
        all_ref[core] = own_ref[...]
        all_ref[1 - core] = other_ref[...]

        def own_lanes(value):
            total = jnp.zeros((value.shape[0], z.part), F32)
            for h in range(z.shards):
                total = total + jnp.where(shard == h, value[:, h * z.part : (h + 1) * z.part], 0.0)
            return total

        out_ref[...] = all_ref[0, : z.part].astype(F32)
        fin_ref[...] = all_ref[0, z.part : z.rows].astype(F32).reshape(z.groups, z.gi, z.d)
        for c in range(3):
            part = all_ref[1, c * z.gi : (c + 1) * z.gi].astype(F32)
            for g in range(z.groups):
                qkv_ref[c, g] = part[:, g * z.gw : (g + 1) * z.gw]
        part = all_ref[1, z.part : z.rows].astype(F32)
        for g in range(z.groups):
            fout_ref[g] = part[:, g * z.gw : (g + 1) * z.gw]
        small = own_lanes(all_ref[1, z.at_small : z.at_small + 16].astype(F32))
        gain_ref[...] = small[0:2]
        bias_ref[...] = small[2:11]
        for n in range(4):
            row = z.rows + (n % 2) * z.extra
            pos_ref[n * z.pos : (n + 1) * z.pos] = all_ref[n // 2, row : row + z.pos].astype(F32)
        small = own_lanes(all_ref[0, z.rows + z.pos : z.rows + z.extra].astype(F32))
        eg_ref[...] = small[0:1]
        es_ref[...] = small[1:2]

    return call(
        kernel,
        [
            like((3, z.groups, z.gi, z.gw), F32),
            like((z.part, z.d), F32),
            like((z.groups, z.gi, z.d), F32),
            like((z.groups, z.part, z.gw), F32),
            like((2, z.part), F32),
            like((9, z.part), F32),
            like((4 * z.pos, z.d), F32),
            like((1, z.part), F32),
            like((1, z.part), F32),
        ],
        (own, other),
        scratch=[pltpu.VMEM((2, rows, z.d), BF16)],
        name="unpack",
    )


def body(token_ids, targets, segment_ids, word_table, pos_table, embed_gain, embed_shift, qkv_weight, out_weight, ffn_in, ffn_out, layer_gains, layer_biases):
    micro, _, seq = token_ids.shape
    vocab, d = word_table.shape
    pos_rows = pos_table.shape[0]
    shards = lax.axis_size("shard")
    dp = lax.axis_size("dp")
    both = ("section", "dp")
    section = lax.axis_index("section")
    first = section == 0
    z = Sizes(qkv_weight.shape, out_weight.shape, shards, pos_rows)
    offset = lax.axis_index("shard") * vocab

    mine = lax.dynamic_index_in_dim(jnp.stack([token_ids[:, 0], targets[:, 0], segment_ids[:, 0]], axis=1), section, 0, keepdims=False)
    ids_by = jnp.stack([mine, turned(mine, "shard", -1), turned(mine, "shard", 2), turned(mine, "shard", 1)])
    seg_row = mine[2:3]

    def rows_of(ids):
        return word_table.at[jnp.clip(ids.reshape(-1) - offset, 0, vocab - 1)].get(mode="promise_in_bounds")

    small = jnp.concatenate([layer_gains[0], layer_biases[0], embed_gain[None], embed_shift[None]], axis=0)
    local, pair, packed = pack_weights(z, qkv_weight[0], out_weight[0], ffn_in[0], ffn_out[0], small)
    cross_pair = crossed(pair, "section", 1)
    near = gather_first(packed, "shard")
    picked = rows_of(ids_by[:, 0])
    near, pos_table = after((near, pos_table), near)
    word_parts = embed_parts(picked, ids_by, pos_table, vocab)
    near = after(near, word_parts)
    near_rows = jnp.concatenate(near, axis=0)
    near_y = crossed(near_rows, "dp", 2)
    cross_near = crossed(near_rows, "section", 1)
    target_rows = rows_of(after(ids_by[:, 1], near_rows))
    c0, c1, c2a, c2b, c3 = word_parts
    half, quarter = seq // 2, z.part // 2
    right = turned(jnp.concatenate([c2a, near[0][:quarter]], axis=0), "shard", 1)
    left = turned(jnp.concatenate([c2b, near[1][quarter:]], axis=0), "shard", -1)
    right, left = after((right, left), target_rows)
    c1 = jnp.concatenate([c1[:half] + right[:half], c1[half:]], axis=0)
    c3 = jnp.concatenate([c3[:half], c3[half:] + left[:half]], axis=0)
    words = scatter_second(c0, c1, c3, "shard")
    far = jnp.concatenate([right[half:], left[half:]], axis=0)
    cross_far = crossed(far, "section", 1)
    both_y = crossed(jnp.concatenate([far, cross_near], axis=0), "dp", 2)
    far_y, cross_near_y = both_y[: z.part], both_y[z.part :]
    cross_far_y = crossed(cross_far, "dp", 2)
    mine = (near_rows, far)
    mine = (*mine, *(crossed(b, "dp", 1) for b in mine), near_y, far_y, crossed(near_y, "dp", 1), crossed(far_y, "dp", 1))
    others = (cross_near, cross_far)
    others = (*others, *(crossed(b, "dp", 1) for b in others))
    others = (*others, cross_near_y, cross_far_y, crossed(cross_near_y, "dp", 1), crossed(cross_far_y, "dp", 1))
    pairs = (cross_pair, crossed(cross_pair, "dp", 1))
    weights_one, weights_two = (Pieces(z, local, mine, pairs, others, layer) for layer in range(2))
    one = layer_forward(z, weights_one, seg_row, True, words=words)
    two = layer_forward(z, weights_two, seg_row, False, layer_in=one["out"])
    two["x"] = one["out"]

    own_out = jnp.where(first, one["out"], two["out"])
    came_out = crossed(jnp.where(first, two["out"], one["out"]), "section", 1)

    before, later = gather_first(two["out"], "shard")
    ctx_own, lse_own = head_forward([two["out"]], word_table)
    before = after(before, ctx_own)
    far_a = turned(before[: seq // 2], "shard", 1)
    ctx_before, lse_before = head_forward([before], word_table)
    later = after(later, ctx_before)
    far_b = turned(later[seq // 2 :], "shard", -1)
    ctx_later, lse_later = head_forward([later], word_table)
    far_a, far_b = after((far_a, far_b), ctx_later)
    ctx_far, lse_far = head_forward([far_a, far_b], word_table)
    lse = jnp.concatenate([lse_own[0:1], lse_later[0:1], lse_far[0:1], lse_before[0:1]], axis=1)
    listed = jnp.stack([ids_by[0, 0], ids_by[1, 0], ids_by[3, 0], ids_by[2, 0]]).reshape(1, -1)
    lists = list_tokens(after(listed, lse), vocab)
    lses = (lse, turned(lse, "shard", -1), turned(lse, "shard", 2), turned(lse, "shard", 1))
    lses = after(lses, (lists, came_out))
    parts, whole_lse = head_combine(seq, (ctx_own, ctx_later, ctx_far, ctx_before), target_rows, ids_by, lses, vocab)
    out_grad = lax.psum_scatter(parts, "shard", scatter_dimension=0, tiled=True)
    dense = head_table([two["out"], later, far_a, far_b, before], word_table, whole_lse, ids_by, 0, 6, 1280)

    out_grad = after(out_grad, dense)
    dense = lax.psum_scatter(dense, both, scatter_dimension=0, tiled=True)

    d_middle, small_grads, keep_f, send_f = ffn_backward(z, weights_two, two, out_grad)
    in_two, in_low, keep_a, send_a = attention_backward(z, weights_two, two, d_middle, small_grads, False)
    came_f, came_a = crossed(send_f, "dp", 1), crossed(send_a, "dp", 1)
    d_middle, small_grads, keep_one_f, send_one_f = ffn_backward(z, weights_one, one, in_low)
    keep_f, came_f, keep_a, came_a = after((keep_f, came_f, keep_a, came_a), d_middle)
    split_two = add_cores_split(z, (keep_a, keep_f), (came_a, came_f))
    d_middle = after(d_middle, split_two)
    terms_two = scatter_first(*split_two, "shard")
    came_one_f = crossed(send_one_f, "dp", 1)
    in_one, in_one_low, keep_one_a, send_one_a, d_embed = attention_backward(z, weights_one, one, d_middle, small_grads, True, seg_row, pos_rows)
    keep_one_f, came_one_f = after((keep_one_f, came_one_f), d_embed)
    send_one_a, d_embed = after((send_one_a, d_embed), terms_two)
    came_one_a = crossed(send_one_a, "dp", 1)
    columns = d_embed[None]
    steps = [("dp", 1 << n) for n in range(dp.bit_length() - 1)]
    for n, (axis, bit) in enumerate(steps):
        middle = columns.shape[1] // 2
        columns = jnp.concatenate([columns[:, :middle], crossed(columns[:, middle:], axis, bit)], axis=0)
        if n == 0:
            came_one_a = after(came_one_a, columns)
    split_one = add_cores_split(z, (keep_one_a, keep_one_f), (came_one_a, came_one_f))
    columns = after(columns, split_one)
    columns = jnp.concatenate([columns[:, 0], crossed(columns[:, 1], "section", 1)], axis=0)
    second_two = scatter_second(*terms_two, "shard")
    terms_one = scatter_first(*split_one, "shard")
    own_in = jnp.where(first, in_one, in_two)
    came_in = crossed(jnp.where(first, in_two, in_one).astype(BF16), "section", 1)
    lists = after(lists, columns)
    bit = 1
    while bit < dp:
        lists = jnp.concatenate([lists, crossed(lists, "dp", bit)], axis=0)
        bit *= 2
    lists = jnp.concatenate([lists, crossed(lists, "section", 1)], axis=0)
    sum_two = sum(after(second_two, (columns, split_one)))
    second_one = scatter_second(*after(terms_one, sum_two), "shard")
    sum_one = sum(after(second_one, (sum_two, lists, came_in)))
    columns = after(columns, sum_one)
    ring_columns = gather_first(columns, "shard")
    high = z.part + 2 * z.extra
    extra = sum_one[z.part : high]
    layer_one = jnp.concatenate([sum_one[: z.part], sum_one[high:]], axis=0)
    total = jnp.concatenate([jnp.where(first, layer_one, sum_two), extra], axis=0)
    total = total + crossed(jnp.concatenate([jnp.where(first, sum_two, layer_one), extra], axis=0), "section", 1)
    total, ring_columns = after((total, ring_columns), ())
    far_columns = gather_second(*ring_columns, "shard")
    bit = 2
    while bit < dp:
        total = total + after(crossed(total, "dp", bit), far_columns)
        bit *= 2
    unpacked = unpack_grads(z, total, crossed(total, "dp", 1))

    word_grad = table_grad(dense, (columns, ring_columns[1], ring_columns[0], *far_columns), lists, vocab).T

    def by_micro(own, came):
        return jnp.stack([jnp.where(first, own, came), jnp.where(first, came, own)]).reshape(1, micro, 1, seq, d)

    layer_outputs = by_micro(own_out, came_out)
    input_grads = by_micro(own_in, came_in.astype(F32))
    qkv_g, out_g, fin_g, fout_g, gain_g, bias_g, pos_g, eg_g, es_g = unpacked
    return (
        layer_outputs,
        input_grads,
        word_grad,
        pos_g,
        eg_g.reshape(-1),
        es_g.reshape(-1),
        qkv_g[None],
        out_g[None],
        fin_g[None],
        fout_g[None],
        gain_g[None],
        bias_g[None],
    )


def solution(mesh):
    rows = P(None, ("dp", "shard"), None)
    weights = (
        P("section", None, None, "shard", None),
        P("section", "shard", None),
        P("section", None, "shard", None),
        P("section", None, "shard", None),
        P("section", None, "shard"),
        P("section", None, "shard"),
    )
    states = P("section", None, ("dp", "shard"), None, None)
    return jax.shard_map(
        body,
        mesh=mesh,
        in_specs=(rows, rows, rows, P("shard", None), P("shard", None), P("shard"), P("shard"), *weights),
        out_specs=(states, states, P("shard", ("section", "dp")), P("shard", None), P("shard"), P("shard"), *weights),
        check_vma=False,
    )
```

```python
import math

import jax
import jax.numpy as jnp
from jax import lax
from jax.experimental import pallas as pl
from jax.experimental.pallas import tpu as pltpu
from jax.sharding import PartitionSpec as P

HEADS = 12
EPSILON = 1e-06
MASKED = -1000000000.0
F32 = jnp.float32
BF16 = jnp.bfloat16
MIB = 1 << 20


def nn(a, b):
    return jnp.dot(a, b, preferred_element_type=F32)


def nt(a, b):
    return lax.dot_general(a, b, (((1,), (1,)), ((), ())), preferred_element_type=F32)


def tn(a, b):
    return lax.dot_general(a, b, (((0,), (0,)), ((), ())), preferred_element_type=F32)


def iota(shape, axis):
    return lax.broadcasted_iota(jnp.int32, shape, axis)


def group_of(index, width, count):
    total = jnp.zeros(index.shape, jnp.int32)
    for step in range(1, count):
        total = total + (index >= step * width).astype(jnp.int32)
    return total


def normed(value):
    centered = value - jnp.mean(value, axis=-1, keepdims=True)
    scale = lax.rsqrt(jnp.mean(centered * centered, axis=-1, keepdims=True) + EPSILON)
    return centered * scale, scale


def norm_back(grad, unit, scale, gain):
    inner = grad * gain
    first = jnp.mean(inner, axis=-1, keepdims=True)
    second = jnp.mean(inner * unit, axis=-1, keepdims=True)
    return scale * (inner - first - unit * second)


def col_sum(value):
    return jnp.sum(value, axis=0, keepdims=True)


def upright(row, count):
    return jnp.broadcast_to(row.astype(F32), (128, count)).T[:, 0:1]


def call(kernel, outs, ins, specs=None, scratch=(), limit=56, flops=0, moved=0, grid=None, out_specs=None, name=None):
    vmem = pl.BlockSpec(memory_space=pltpu.VMEM)
    extra = {} if grid is None else {"grid": grid}
    return pl.pallas_call(
        kernel,
        out_shape=outs,
        in_specs=[vmem if s is None else s for s in (specs or [None] * len(ins))],
        out_specs=out_specs if out_specs is not None else [vmem] * len(outs),
        scratch_shapes=list(scratch),
        compiler_params=pltpu.CompilerParams(vmem_limit_bytes=limit * MIB),
        cost_estimate=pl.CostEstimate(flops=0, bytes_accessed=0, transcendentals=0),
        name=name,
        **extra,
    )(*ins)


def like(shape, dtype):
    return jax.ShapeDtypeStruct(shape, dtype)


def turned(block, axis, by):
    size = lax.axis_size(axis)
    return lax.ppermute(block, axis, [(i, (i + by) % size) for i in range(size)])


def crossed(block, axis, bit):
    return lax.ppermute(block, axis, [(i, i ^ bit) for i in range(lax.axis_size(axis))])


def after(value, first):
    return lax.optimization_barrier((value, first))[0]


def scatter_first(c0, c1, c2a, c2b, c3, axis, wait=()):
    half = c2a.shape[0]
    right, left = after((turned(c2a, axis, 1), turned(c2b, axis, -1)), wait)
    return c0, jnp.concatenate([c1[:half] + right, c1[half:]], axis=0), jnp.concatenate([c3[:half], c3[half:] + left], axis=0)


def scatter_second(c0, c1, c3, axis):
    return c0, turned(c1, axis, 1), turned(c3, axis, -1)


def side_of(bit):
    return (lax.axis_index("dp") // bit) % 2


def gather_first(block, axis):
    return turned(block, axis, 1), turned(block, axis, -1)


def gather_second(before, later, axis):
    half = before.shape[0] // 2
    return turned(before[:half], axis, 1), turned(later[half:], axis, -1)


def ring_gather(block, axis):
    first = gather_first(block, axis)
    return (*first, *gather_second(*first, axis))


class Sizes:
    def __init__(self, qkv, out, shards, pos_rows):
        _, _, groups, part, width = qkv
        self.shards, self.groups, self.gw, self.gi = shards, groups, width, part
        self.d = out[2]
        self.part = out[1]
        self.at_small = 3 * part
        self.rows = 2 * self.part
        self.pos = self.part - self.at_small - 16
        self.extra = (pos_rows - self.pos) // 2


def pack_weights(z, qkv, out, fin, fout, small):
    def kernel(qkv_ref, out_ref, fin_ref, fout_ref, small_ref, o_ref, pair_ref, own_ref):
        shard = lax.axis_index("shard")

        def spread(pieces):
            return jnp.concatenate([piece.astype(F32) for piece in pieces], axis=1).astype(BF16)

        o_ref[0, 0] = out_ref[...]
        o_ref[0, 1] = fin_ref[...].reshape(z.part, z.d)
        for c in range(3):
            o_ref[1, 0, c * z.gi : (c + 1) * z.gi] = spread([qkv_ref[c, g] for g in range(z.groups)])
        tall = jnp.concatenate([small_ref[...].astype(F32), jnp.zeros((16 - small_ref.shape[0], z.part), F32)], axis=0)
        wide = jnp.concatenate([tall] * z.shards, axis=1)
        lane = group_of(iota(wide.shape, 1), z.part, z.shards)
        o_ref[1, 0, z.at_small : z.at_small + 16] = jnp.where(lane == shard, wide, 0.0).astype(BF16)
        o_ref[1, 0, z.at_small + 16 : z.part] = jnp.zeros((z.part - z.at_small - 16, z.d), BF16)
        o_ref[1, 1] = spread([fout_ref[g] for g in range(z.groups)])
        pair_ref[...] = o_ref[side_of(1)]
        own_ref[...] = o_ref[side_of(1), side_of(2)]

    outs = [like((2, 2, z.part, z.d), BF16), like((2, z.part, z.d), BF16), like((z.part, z.d), BF16)]
    return call(kernel, outs, (qkv, out, fin, fout, small), name="pack")


class Pieces:
    def __init__(self, z, local, mine, pairs, others, layer):
        self.z, self.layer = z, layer
        self.arrays = (local, *mine, *pairs, *others)
        self.specs = [pl.BlockSpec(memory_space=pl.ANY)] * len(self.arrays)
        self.scratch = [pltpu.VMEM((2, z.shards, z.rows, z.d), BF16), pltpu.SemaphoreType.DMA((2, 2, 4))]

    def start(self, refs, w_ref, sems, parts):
        z = self.z
        core, y = side_of(1), side_of(2)
        shard = lax.axis_index("shard")
        own_layer = lax.axis_index("section") == self.layer
        local, mine, pairs, others = refs[0], refs[1:9], refs[9:11], refs[11:19]
        waits = {}
        for part in parts:
            copies = []
            for side in range(2):
                place = core if side == 0 else 1 - core
                for n, by in enumerate((0, 3, 1, 2)):
                    target = w_ref.at[place, (shard + by) % z.shards, pl.ds(part * z.part, z.part)]
                    sem = sems.at[part, side, n]
                    rows = pl.ds((n - 1) * z.part, z.part)
                    choices = []
                    for across in range(2):
                        here = (y == part) if across == 0 else (y != part)
                        at = 2 * across + side
                        if n == 0:
                            own, other = local.at[place, part], pairs[side].at[part]
                        elif n < 3:
                            own, other = mine[2 * at].at[rows], others[2 * at].at[rows]
                        else:
                            own, other = mine[2 * at + 1], others[2 * at + 1]
                        choices.append((jnp.logical_and(here, own_layer), own))
                        choices.append((jnp.logical_and(here, jnp.logical_not(own_layer)), other))
                    for here, source in choices:
                        copy = pltpu.make_async_copy(source, target, sem)
                        pl.when(here)(copy.start)
                    copies.append(pltpu.make_async_copy(choices[1][1], target, sem))
            waits[part] = copies
        return waits


def wait_all(copies):
    for copy in copies:
        copy.wait()


class Loads:
    def __init__(self, arrays):
        self.names = list(arrays)
        self.arrays = list(arrays.values())
        self.specs = [pl.BlockSpec(memory_space=pl.ANY)] * len(self.arrays)
        self.scratch = [pltpu.VMEM(a.shape, a.dtype) for a in self.arrays] + [pltpu.SemaphoreType.DMA((len(self.arrays),))]

    def start(self, refs, scratch):
        self.buffers = dict(zip(self.names, scratch))
        self.copies = {
            name: pltpu.make_async_copy(ref, buffer, scratch[-1].at[n])
            for n, (name, ref, buffer) in enumerate(zip(self.names, refs, scratch))
        }
        for copy in self.copies.values():
            copy.start()

    def __getitem__(self, name):
        copy = self.copies.pop(name, None)
        if copy is not None:
            copy.wait()
        return self.buffers[name]


class Stores:
    def __init__(self, shapes, split=()):
        self.names = list(shapes)
        self.shapes = list(shapes.values())
        self.split = split
        self.specs = [pl.BlockSpec(memory_space=pl.ANY)] * len(self.shapes)
        count = sum(a.shape[0] if name in split else 1 for name, a in shapes.items())
        self.scratch = [pltpu.VMEM(a.shape, a.dtype) for a in self.shapes] + [pltpu.SemaphoreType.DMA((count,))]

    def bind(self, refs, scratch):
        self.refs = dict(zip(self.names, refs))
        self.buffers = dict(zip(self.names, scratch))
        self.sems = scratch[-1]
        self.copies = []

    def put(self, name, value, index=None):
        source = self.buffers[name] if index is None else self.buffers[name].at[index]
        source[...] = value.astype(source.dtype)
        self.send(name, index)

    def send(self, name, index=None):
        source, target = self.buffers[name], self.refs[name]
        if index is not None:
            source, target = source.at[index], target.at[index]
        copy = pltpu.make_async_copy(source, target, self.sems.at[len(self.copies)])
        copy.start()
        self.copies.append(copy)

    def finish(self):
        wait_all(self.copies)


class Weights:
    def __init__(self, z, w_ref):
        self.z, self.w = z, w_ref

    def out(self):
        z = self.z
        return self.w[0, :, 0 : z.part, :].reshape(z.d, z.d)

    def small(self):
        z = self.z
        return sum(self.w[1, h, z.at_small : z.at_small + 16, :].astype(F32) for h in range(z.shards))

    def proj(self, c, p):
        z = self.z
        lanes = slice(2 * p * z.gw, 2 * (p + 1) * z.gw)
        dense = self.w[1, :, c * z.gi : (c + 1) * z.gi, lanes].reshape(z.gw, 2 * z.gw)
        high = iota(dense.shape, 1) >= z.gw
        blank = jnp.zeros_like(dense)
        return jnp.concatenate([jnp.where(high, blank, dense), jnp.where(high, dense, blank)], axis=0)

    def project(self, value, c):
        z = self.z
        wide = 2 * z.gw
        return jnp.concatenate([nn(value[:, p * wide : (p + 1) * wide], self.proj(c, p)) for p in range(z.groups // 2)], axis=1)

    def fin(self, g):
        z = self.z
        row = z.part + g * z.gi
        dense = self.w[0, :, row : row + z.gi, :].reshape(z.gw, z.d)
        blank = jnp.zeros_like(dense)
        return jnp.concatenate([dense, blank] if g % 2 == 0 else [blank, dense], axis=0)

    def fout(self, g):
        z = self.z
        at = (g // 2) * 2 * z.gw
        pair = self.w[1, :, z.part : z.rows, at : at + 2 * z.gw].reshape(z.d, 2 * z.gw)
        keep = (iota(pair.shape, 1) >= z.gw) == (g % 2 == 1)
        return jnp.where(keep, pair, jnp.zeros_like(pair))


def embed_parts(picked, ids_by, pos_table, vocab):
    count, _, seq = ids_by.shape
    width = picked.shape[1]
    half = seq // 2
    rows = pos_table.shape[0]

    def kernel(p_ref, i_ref, t_ref, c0, c1, c2a, c2b, c3):
        shard = lax.axis_index("shard")
        for k in range(count):
            span = slice(k * seq, (k + 1) * seq)
            token, seg_row = i_ref[k, 0:1], i_ref[k, 2:3]
            seg_col = upright(seg_row, seq)
            same = seg_col == seg_row.astype(F32)
            earlier = iota((seq, seq), 1) < iota((seq, seq), 0)
            place = jnp.sum(jnp.where(same & earlier, 1.0, 0.0), axis=1, keepdims=True).astype(jnp.int32) - shard * rows
            spot = (iota((seq, rows), 1) == place).astype(BF16)
            local = token - shard * vocab
            inside = upright(jnp.where((local >= 0) & (local < vocab), 1.0, 0.0), seq)
            word = jnp.where(inside > 0.5, p_ref[span].astype(F32), 0.0)
            total = (word + nn(spot, t_ref[...])).astype(BF16)
            if k == 2:
                c2a[...] = total[:half]
                c2b[...] = total[half:]
            else:
                (c0, c1, None, c3)[k][...] = total

    full, part = like((seq, width), BF16), like((half, width), BF16)
    return call(kernel, [full, full, part, part, full], (picked, ids_by, pos_table), moved=4 * MIB, name="embed_parts")


def layer_forward(z, pieces, seg_row, first, words=None, layer_in=None):
    seq = seg_row.shape[1]
    d = z.d
    flat = like((seq, d), BF16)
    shapes = {"q": flat, "k": flat, "v": flat, "p": like((HEADS, seq, seq), BF16), "att": flat, "n1": flat, "mid": flat}
    shapes.update({"act": like((z.groups, seq, d), BF16), "slope": like((z.groups, seq, d), BF16)})
    shapes.update({"n2": flat, "stats": like((seq, 128), F32), "small": like((16, d), F32), "out": flat})
    if first:
        shapes.update({"x": flat, "n0": flat})
    stores = Stores(shapes, split=("p", "act", "slope"))
    head = d // HEADS
    inputs = list(words) if first else [layer_in]

    def kernel(*refs):
        piece_refs, refs = refs[: len(pieces.arrays)], refs[len(pieces.arrays) :]
        row_ref, refs = refs[0], refs[1:]
        in_refs, refs = refs[: len(inputs)], refs[len(inputs) :]
        out_refs, refs = refs[: len(shapes)], refs[len(shapes) :]
        w_ref, sems, *buffers = refs
        waits = pieces.start(piece_refs, w_ref, sems, (0, 1))
        stores.bind(out_refs, buffers)
        put, send = stores.put, stores.send
        w = Weights(z, w_ref)
        if first:
            unit, r0 = normed(sum(ref[...].astype(F32) for ref in in_refs))
            put("n0", unit)
        wait_all(waits[0])
        small = w.small()
        put("small", small)
        if first:
            x = unit * small[11:12] + small[12:13]
            x_low = x.astype(BF16)
            put("x", x_low)
        else:
            r0 = jnp.zeros((seq, 1), F32)
            x_low = in_refs[0][...]
            x = x_low.astype(F32)
        q = (w.project(x_low, 0).astype(BF16).astype(F32) * (1.0 / math.sqrt(head))).astype(BF16)
        k = w.project(x_low, 1).astype(BF16)
        v = (w.project(x_low, 2) + small[2:3]).astype(BF16)
        put("q", q)
        put("k", k)
        put("v", v)
        same = upright(row_ref[...], seq) == row_ref[...].astype(F32)
        second = iota((seq, 128), 1) >= head
        q_ref, k_ref, v_ref, att_ref = (stores.buffers[name] for name in ("q", "k", "v", "att"))

        def heads(t, carry):
            lanes = pl.ds(pl.multiple_of(t * 128, 128), 128)
            q_t, k_t, v_t = q_ref[:, lanes], k_ref[:, lanes], v_ref[:, lanes]
            raw = [nt(jnp.where(second == (j == 1), q_t, jnp.zeros_like(q_t)), k_t) for j in range(2)]
            results = []
            for j in range(2):
                scores = jnp.where(same, raw[j], MASKED)
                scores = jnp.exp(scores - jnp.max(scores, axis=-1, keepdims=True))
                probs = (scores * (1.0 / jnp.sum(scores, axis=-1, keepdims=True))).astype(BF16)
                stores.buffers["p"][2 * t + j] = probs
                results.append(nn(probs, v_t))
            att_ref[:, lanes] = jnp.where(second, results[1], results[0]).astype(BF16)
            return carry

        lax.fori_loop(0, d // 128, heads, jnp.int32(0))
        attended = att_ref[...]
        send("p")
        send("att")
        unit, r1 = normed(x + (nn(attended, w.out()) + small[3:4]))
        put("n1", unit)
        middle = unit * small[0:1] + small[4:5]
        middle_low = middle.astype(BF16)
        put("mid", middle_low)
        wait_all(waits[1])
        back = [None] * (z.groups // 2)

        def pre_of(g):
            pair = slice((g // 2) * 2 * z.gw, (g // 2 + 1) * 2 * z.gw)
            return nn(middle_low[:, pair], w.fin(g))

        raw = pre_of(0)
        for g in range(z.groups):
            following = pre_of(g + 1) if g + 1 < z.groups else None
            pre = raw + small[5 + g : 6 + g]
            half = 0.5 + 0.5 * lax.erf(pre * math.sqrt(0.5))
            slope = half + pre * (jnp.exp(-0.5 * pre * pre) * (1.0 / math.sqrt(2.0 * math.pi)))
            active = (pre * half).astype(BF16)
            put("act", active, g)
            put("slope", slope, g)
            added = nn(active, w.fout(g))
            back[g // 2] = added if back[g // 2] is None else back[g // 2] + added
            raw = following
        unit, r2 = normed(middle + (jnp.concatenate(back, axis=1) + small[9:10]))
        put("n2", unit)
        put("out", unit * small[1:2] + small[10:11])
        lane = iota((seq, 128), 1)
        put("stats", jnp.where(lane == 0, r0, jnp.where(lane == 1, r1, r2)))
        stores.finish()

    outs = call(
        kernel,
        stores.shapes,
        (*pieces.arrays, seg_row, *inputs),
        specs=pieces.specs + [None] * (1 + len(inputs)),
        out_specs=stores.specs,
        scratch=pieces.scratch + stores.scratch,
        flops=3 * 10**9,
        moved=16 * MIB,
        name="layer_first" if first else "layer_second",
    )
    return dict(zip(stores.names, outs))


def send_halves(z, g_ref, keep_ref, send_ref, sems):
    core = lax.axis_index("dp") % 2
    shard = lax.axis_index("shard")
    copies = []
    for k in range(z.shards):
        to = (shard + k) % z.shards
        copies.append(pltpu.make_async_copy(g_ref.at[1 - core, to], send_ref.at[k], sems.at[2 * k]))
        copies.append(pltpu.make_async_copy(g_ref.at[core, to], keep_ref.at[k], sems.at[2 * k + 1]))
    for copy in copies:
        copy.start()
    return copies


def ffn_backward(z, pieces, state, out_grad):
    seq, d = out_grad.shape
    loads = Loads({"dy": out_grad, **{key: state[key] for key in ("n2", "stats", "small", "mid", "act", "slope")}})
    outs = [like((seq, d), F32), like((16, d), F32)] + [like((z.shards, z.part, d), BF16)] * 2

    def kernel(*refs):
        piece_refs, refs = refs[: len(pieces.arrays)], refs[len(pieces.arrays) :]
        load_refs, refs = refs[: len(loads.names)], refs[len(loads.names) :]
        dm_ref, small_ref, keep_ref, send_ref, w_ref, sems, g_ref, out_sems, *buffers = refs
        loads.start(load_refs, buffers)
        waits = pieces.start(piece_refs, w_ref, sems, (1,))
        w = Weights(z, w_ref)
        dy = loads["dy"][...].astype(F32)
        n2 = loads["n2"][...].astype(F32)
        scale = loads["stats"][:, 2:3]
        small = loads["small"][...]
        gain_two, shift_two = col_sum(dy * n2), col_sum(dy)
        d_final = norm_back(dy, n2, scale, small[1:2])
        d_ffn = d_final.astype(BF16)
        ffn_shift = col_sum(d_ffn.astype(F32))
        middle_t = loads["mid"][...].T
        act, slope = loads["act"], loads["slope"]
        wait_all(waits[1])
        pre_shift = []
        pair_back = [None] * (z.groups // 2)
        wide = 2 * z.gw

        def act_grad(g):
            p = g // 2
            return nt(d_ffn[:, p * wide : (p + 1) * wide], w.fout(g))

        raw = act_grad(0)
        for p in range(z.groups // 2):
            lanes = slice(p * wide, (p + 1) * wide)
            out_pair = d_ffn[:, lanes]
            back_pair = []
            for g in (2 * p, 2 * p + 1):
                following = act_grad(g + 1) if g + 1 < z.groups else None
                d_pre = (raw * slope[g].astype(F32)).astype(BF16)
                pre_shift.append(col_sum(d_pre.astype(F32)))
                back_pair.append(tn(act[g], out_pair))
                grad_in = nn(middle_t[g * z.gw : (g + 1) * z.gw], d_pre)
                g_ref[0, :, g * z.gi : (g + 1) * z.gi, :] = grad_in.astype(BF16).reshape(z.shards, z.gi, d)
                added = nt(d_pre, w.fin(g))
                pair_back[p] = added if pair_back[p] is None else pair_back[p] + added
                raw = following
            odd = iota(back_pair[0].shape, 1) >= z.gw
            both = jnp.where(odd, back_pair[1], back_pair[0]).astype(BF16)
            g_ref[1, :, :, lanes] = both.reshape(z.shards, z.part, wide)
        copies = send_halves(z, g_ref, keep_ref, send_ref, out_sems)
        dm_ref[...] = d_final + jnp.concatenate(pair_back, axis=1)
        blank = jnp.zeros((1, d), F32)
        small_ref[...] = jnp.concatenate(
            [blank, gain_two, blank, blank, blank, *pre_shift, ffn_shift, shift_two, jnp.zeros((5, d), F32)], axis=0
        )
        wait_all(copies)

    anywhere = pl.BlockSpec(memory_space=pl.ANY)
    return call(
        kernel,
        outs,
        (*pieces.arrays, *loads.arrays),
        specs=pieces.specs + loads.specs,
        out_specs=[pl.BlockSpec(memory_space=pltpu.VMEM)] * 2 + [anywhere] * 2,
        scratch=pieces.scratch + [pltpu.VMEM((2, z.shards, z.part, d), BF16), pltpu.SemaphoreType.DMA((2 * z.shards,))] + loads.scratch,
        flops=8 * 10**9,
        moved=16 * MIB,
        name="ffn_back",
    )


def attention_backward(z, pieces, state, d_middle, small_in, first, seg_row=None, pos_rows=0):
    seq, d = d_middle.shape
    head = d // HEADS
    keys = ["n1", "stats", "small", "att", "q", "k", "v", "p", "x"] + (["n0"] if first else [])
    loads = Loads({"dm": d_middle, **{key: state[key] for key in keys}, "grads": small_in, **({"seg": seg_row} if first else {})})
    rows = z.part + (z.extra if first else 0)
    outs = [like((seq, d), F32), like((seq, d), BF16)] + [like((z.shards, rows, d), BF16)] * 2
    blocks = 2 * lax.axis_size("dp")
    if first:
        outs.append(like((blocks, d // blocks, seq), BF16))

    def kernel(*refs):
        piece_refs, refs = refs[: len(pieces.arrays)], refs[len(pieces.arrays) :]
        load_refs, refs = refs[: len(loads.names)], refs[len(loads.names) :]
        dx_ref, low_ref, keep_ref, send_ref = refs[:4]
        de_ref = refs[4] if first else None
        w_ref, sems, g_ref, out_sems, *buffers = refs[len(outs) :]
        loads.start(load_refs, buffers)
        waits = pieces.start(piece_refs, w_ref, sems, (0,))
        w = Weights(z, w_ref)
        d_middle = loads["dm"][...]
        n1 = loads["n1"][...].astype(F32)
        stats = loads["stats"][...]
        r0, r1 = stats[:, 0:1], stats[:, 1:2]
        small = loads["small"][...]
        gain_one, shift_one = col_sum(d_middle * n1), col_sum(d_middle)
        d_mid = norm_back(d_middle, n1, r1, small[0:1])
        d_branch = d_mid.astype(BF16)
        branch_shift = col_sum(d_branch.astype(F32))
        g_ref[0, :, 0 : z.part, :] = tn(loads["att"][...], d_branch).astype(BF16).reshape(z.shards, z.part, d)
        wait_all(waits[0])
        d_att = nt(d_branch, w.out()).astype(BF16)
        second = iota((seq, 128), 1) >= head
        scale = 1.0 / math.sqrt(head)
        q_ref, k_ref, v_ref, p_ref = (loads[key] for key in ("q", "k", "v", "p"))
        units = [(t, j) for t in range(d // 128) for j in range(2)]

        def probs_grad(unit):
            t, j = unit
            lanes = slice(t * 128, (t + 1) * 128)
            a_j = jnp.where(second == (j == 1), d_att[:, lanes], jnp.zeros((seq, 128), BF16))
            return nt(a_j, v_ref[:, lanes])

        dq, dk, dv = [], [], []
        raw = probs_grad(units[0])
        for n, (t, j) in enumerate(units):
            following = probs_grad(units[n + 1]) if n + 1 < len(units) else None
            lanes = slice(t * 128, (t + 1) * 128)
            probs_low = p_ref[n]
            probs = probs_low.astype(F32)
            inner = jnp.sum(probs * raw, axis=-1, keepdims=True)
            d_scores = (probs * (raw - inner)).astype(BF16)
            result = (nn(d_scores, k_ref[:, lanes]), tn(d_scores, q_ref[:, lanes]), tn(probs_low, d_att[:, lanes]))
            if j == 0:
                kept = result
            else:
                dq.append((jnp.where(second, result[0], kept[0]) * scale).astype(BF16))
                dk.append(jnp.where(second, result[1], kept[1]).astype(BF16))
                dv.append(jnp.where(second, result[2], kept[2]).astype(BF16))
            raw = following
        value_shift = col_sum(jnp.concatenate(dv, axis=1).astype(F32))
        x_t = loads["x"][...].T
        d_in = [d_mid[:, : 2 * z.gw], d_mid[:, 2 * z.gw :]]
        high = iota((z.gw, 2 * z.gw), 1) >= z.gw
        for c, parts in enumerate((dq, dk, dv)):
            d_c = jnp.concatenate(parts, axis=1)
            for p in range(z.groups // 2):
                lanes = slice(2 * p * z.gw, 2 * (p + 1) * z.gw)
                full = nn(x_t[lanes], d_c[:, lanes])
                grad = jnp.where(high, full[z.gw :], full[: z.gw]).astype(BF16)
                g_ref[1, :, c * z.gi : (c + 1) * z.gi, lanes] = grad.reshape(z.shards, z.gi, 2 * z.gw)
                d_in[p] = d_in[p] + nt(d_c[:, lanes], w.proj(c, p))
        d_in = jnp.concatenate(d_in, axis=1)
        blank = jnp.zeros((1, d), F32)
        embed_grads = [blank, blank]
        if first:
            n0 = loads["n0"][...].astype(F32)
            embed_grads = [col_sum(d_in * n0), col_sum(d_in)]
            d_embed = norm_back(d_in, n0, r0, small[11:12])
            d_embed_t = d_embed.T
            bits = blocks.bit_length() - 1
            me = lax.axis_index("section") * (blocks // 2) + lax.axis_index("dp")
            for b in range(blocks):
                to = me ^ b
                place = sum(((to >> bit) & 1) << (bits - 1 - bit) for bit in range(bits))
                de_ref[place] = d_embed_t[b * (d // blocks) : (b + 1) * (d // blocks)].astype(BF16)
            seg = loads["seg"][...]
            same = upright(seg, seq) == seg.astype(F32)
            later = iota((seq, seq), 0) < iota((seq, seq), 1)
            place = jnp.sum(jnp.where(same & later, 1.0, 0.0), axis=0, keepdims=True).astype(jnp.int32)
            spot = (iota((pos_rows, seq), 0) == place).astype(BF16)
            pos_grad = nn(spot, d_embed.astype(BF16)).astype(BF16)
        small_grads = jnp.concatenate([gain_one, blank, value_shift, branch_shift, shift_one, jnp.zeros((6, d), F32), *embed_grads, jnp.zeros((3, d), F32)], axis=0)
        small_grads = (small_grads + loads["grads"][...]).astype(BF16)
        for h in range(z.shards):
            g_ref[1, h, z.at_small : z.at_small + 16, :] = small_grads
            if first and h == 0:
                g_ref[1, h, z.at_small + 16 : z.part, :] = pos_grad[: z.pos]
                for side in range(2):
                    g_ref[side, h, z.part : rows, :] = pos_grad[z.pos + side * z.extra : z.pos + (side + 1) * z.extra]
            else:
                g_ref[1, h, z.at_small + 16 : z.part, :] = jnp.zeros((z.pos, d), BF16)
                if first:
                    for side in range(2):
                        g_ref[side, h, z.part : rows, :] = jnp.zeros((z.extra, d), BF16)
        copies = send_halves(z, g_ref, keep_ref, send_ref, out_sems)
        dx_ref[...] = d_in
        low_ref[...] = d_in.astype(BF16)
        wait_all(copies)

    anywhere = pl.BlockSpec(memory_space=pl.ANY)
    vmem = pl.BlockSpec(memory_space=pltpu.VMEM)
    return call(
        kernel,
        outs,
        (*pieces.arrays, *loads.arrays),
        specs=pieces.specs + loads.specs,
        out_specs=[vmem, vmem, anywhere, anywhere] + [vmem] * (len(outs) - 4),
        scratch=pieces.scratch + [pltpu.VMEM((2, z.shards, rows, d), BF16), pltpu.SemaphoreType.DMA((2 * z.shards,))] + loads.scratch,
        flops=8 * 10**9,
        moved=16 * MIB,
        name="att_back",
    )


def add_cores_split(z, keep, came):
    shards, high, d = keep[0].shape
    rows = high + z.part
    half = rows // 32 * 16

    def kernel(a_ref, f_ref, b_ref, e_ref, c0, c1, c2a, c2b, c3):
        for k, ref in ((0, c0), (1, c1), (3, c3)):
            ref[:high] = a_ref[k] + b_ref[k]
            ref[high:] = f_ref[k] + e_ref[k]
        c2a[...] = a_ref[2, :half] + b_ref[2, :half]
        if half < high:
            c2b[: high - half] = a_ref[2, half:] + b_ref[2, half:]
        c2b[high - half :] = f_ref[2] + e_ref[2]

    full = like((rows, d), BF16)
    outs = [full, full, like((half, d), BF16), like((rows - half, d), BF16), full]
    return call(kernel, outs, (*keep, *came), name="add_cores_split")


def head_forward(pieces, table):
    count = sum(piece.shape[0] for piece in pieces)
    vocab, d = table.shape
    tiles = 3
    block = vocab // tiles
    part = block // 2
    chunk = 256
    many = len(pieces)

    def kernel(*refs):
        piece_refs, (w_ref, ctx_ref, lse_ref, x_ref, m_ref, s_ref, acc_ref) = refs[:many], refs[many:]
        step = pl.program_id(0)

        @pl.when(step == 0)
        def _():
            at = 0
            for ref in piece_refs:
                x_ref[at : at + ref.shape[0]] = ref[...]
                at += ref.shape[0]
            m_ref[...] = jnp.full(m_ref.shape, -1e30, F32)
            s_ref[...] = jnp.zeros(s_ref.shape, F32)
            acc_ref[...] = jnp.zeros(acc_ref.shape, F32)

        units = [(c, r) for c in range(2) for r in range(count // chunk)]

        def logits_of(unit):
            c, r = unit
            return nt(x_ref[r * chunk : (r + 1) * chunk], w_ref[c * part : (c + 1) * part])

        logits = logits_of(units[0])
        for n, (c, r) in enumerate(units):
            following = logits_of(units[n + 1]) if n + 1 < len(units) else None
            span = slice(r * chunk, (r + 1) * chunk)
            old = m_ref[span]
            new = jnp.maximum(old, jnp.max(logits, axis=-1, keepdims=True))
            keep = jnp.exp(old - new)
            weight = jnp.exp(logits - new)
            s_ref[span] = s_ref[span] * keep + jnp.sum(weight, axis=-1, keepdims=True)
            acc_ref[span] = acc_ref[span] * keep + nn(weight.astype(BF16), w_ref[c * part : (c + 1) * part])
            m_ref[span] = new
            logits = following

        @pl.when(step == tiles - 1)
        def _():
            total = s_ref[...]
            ctx_ref[...] = acc_ref[...] * (1.0 / total)
            lse = m_ref[...] + jnp.log(total)
            lse_ref[...] = jnp.broadcast_to(lse, (count, 128)).T[0:8]

    fixed = lambda i: (0, 0)
    return call(
        kernel,
        [like((count, d), F32), like((8, count), F32)],
        (*pieces, table),
        specs=[pl.BlockSpec(piece.shape, fixed) for piece in pieces] + [pl.BlockSpec((block, d), lambda i: (i, 0))],
        out_specs=[pl.BlockSpec((count, d), fixed), pl.BlockSpec((8, count), fixed)],
        scratch=[pltpu.VMEM((count, d), BF16), pltpu.VMEM((count, 1), F32), pltpu.VMEM((count, 1), F32), pltpu.VMEM((count, d), F32)],
        grid=(tiles,),
        flops=8 * count * vocab * d,
        moved=14 * MIB,
        name="head_forward",
    )


def head_combine(seq, ctxs, picked, ids_by, lses, vocab):
    shards = ids_by.shape[0]
    d = picked.shape[1]

    def kernel(x0_ref, x1_ref, x2_ref, x3_ref, p_ref, i_ref, a_ref, b_ref, c_ref, e_ref, out_ref, lse_ref):
        shard = lax.axis_index("shard")
        parts = (a_ref, b_ref, c_ref, e_ref)
        for k in range(shards):
            rows = [parts[m][:, ((k - m) % shards) * seq : ((k - m) % shards + 1) * seq] for m in range(shards)]
            top = rows[0]
            for row in rows[1:]:
                top = jnp.maximum(top, row)
            total = top + jnp.log(sum(jnp.exp(row - top) for row in rows))
            whole = upright(total, seq)
            span = slice(k * seq, (k + 1) * seq)
            lse_ref[span] = whole
            weight = upright(jnp.exp(rows[0] - total), seq)
            local = i_ref[k, 1:2] - shard * vocab
            inside = upright(jnp.where((local >= 0) & (local < vocab), 1.0, 0.0), seq)
            hit = jnp.where(inside > 0.5, p_ref[span].astype(F32), 0.0)
            ctx = (x0_ref, x1_ref, x2_ref, x3_ref)[k][...]
            target = pl.multiple_of(((shard + k) % shards) * seq, seq)
            out_ref[pl.ds(target, seq), :] = (ctx * weight - hit).astype(BF16)

    return call(
        kernel,
        [like((shards * seq, d), BF16), like((shards * seq, 1), F32)],
        (*ctxs, picked, ids_by, *lses),
        moved=7 * MIB,
        name="head_combine",
    )


def head_table(pieces, table, lse, ids_by, first_tile, tiles, block):
    count = sum(piece.shape[0] for piece in pieces)
    shards, _, seq = ids_by.shape
    vocab, d = table.shape
    width = min(vocab - first_tile * block, tiles * block)
    chunk = 256
    many = len(pieces)

    def kernel(*refs):
        piece_refs, (w_ref, lse_ref, i_ref, o_ref, x_ref, xt_ref, t_ref, p_ref) = refs[:many], refs[many:]
        step = pl.program_id(0)

        @pl.when(step == 0)
        def _():
            at = 0
            for ref in piece_refs:
                x_ref[at : at + ref.shape[0]] = ref[...]
                at += ref.shape[0]
            xt_ref[...] = x_ref[...].T
            start = lax.axis_index("shard") * vocab + first_tile * block
            for k in range(shards):
                t_ref[k * seq : (k + 1) * seq] = upright(i_ref[k, 1:2] - start, seq).astype(jnp.int32)

        w = w_ref[...]
        for r in range(count // chunk):
            span = slice(r * chunk, (r + 1) * chunk)
            logits = nt(x_ref[span], w)
            hit = iota(logits.shape, 1) == t_ref[span] - step * block
            p_ref[span] = (jnp.exp(logits - lse_ref[span]) - jnp.where(hit, 1.0, 0.0)).astype(BF16)
        o_ref[...] = nn(xt_ref[...], p_ref[...]).astype(BF16)

    fixed = lambda i: (0, 0)
    return call(
        kernel,
        [like((d, width), BF16)],
        (*pieces, table, lse, ids_by),
        specs=[pl.BlockSpec(piece.shape, fixed) for piece in pieces]
        + [
            pl.BlockSpec((block, d), lambda i: (i + first_tile, 0)),
            pl.BlockSpec((count, 1), fixed),
            pl.BlockSpec(ids_by.shape, lambda i: (0, 0, 0)),
        ],
        out_specs=[pl.BlockSpec((d, block), lambda i: (0, i))],
        scratch=[pltpu.VMEM((count, d), BF16), pltpu.VMEM((d, count), BF16), pltpu.VMEM((count, 1), jnp.int32), pltpu.VMEM((count, block), BF16)],
        grid=(tiles,),
        flops=6 * count * width * d,
        moved=8 * MIB,
        name="head_table",
    )[0]


def list_tokens(ids, vocab):
    count = ids.shape[1]
    unit = 1 << (vocab - 1).bit_length()

    def kernel(ids_ref, list_ref):
        start = lax.axis_index("shard") * vocab

        def step(i, many):
            local = ids_ref[0, i] - start
            list_ref[0, many] = i * unit + local
            return many + ((local >= 0) & (local < vocab)).astype(jnp.int32)

        list_ref[0, count] = lax.fori_loop(0, count, step, jnp.int32(0), unroll=8)

    smem = pl.BlockSpec(memory_space=pltpu.SMEM)
    return call(kernel, [like((1, count + 128), jnp.int32)], (ids,), specs=[smem], out_specs=[smem], name="list_tokens")[0]


def table_grad(dense, pieces, lists, vocab):
    width = dense.shape[0]
    sources, _, seq = pieces[0].shape
    shards = 4
    listed = shards * seq
    line = lists.shape[1]
    unit = 1 << (vocab - 1).bit_length()
    ways, each = 4, 4
    rows = (lists & (unit - 1)).reshape(-1)
    tokens = ((lists >> (unit.bit_length() - 1)) + listed * jnp.arange(sources, dtype=jnp.int32)[:, None]).reshape(-1)
    counts = lists[:, listed]

    def kernel(d_ref, own_ref, later_ref, before_ref, far_a_ref, far_b_ref, r_ref, t_ref, n_ref, o_ref, flat_ref, *acc):
        half = sources // 2
        for j in range(sources):
            far = far_a_ref[j] if j < half else far_b_ref[j - half]
            for k, block in enumerate((own_ref[j], later_ref[j], before_ref[j], far)):
                at = j * listed + k * seq
                flat_ref[at : at + seq] = block.astype(F32).T
        for ref in acc:
            ref[...] = jnp.zeros(ref.shape, F32)

        def source(j, carry):
            many = n_ref[j]
            rounds = many // (ways * each)

            def step(i, carry):
                at = j * line + i * ways * each
                place = [r_ref[at + n] for n in range(ways * each)]
                value = [flat_ref[pl.ds(t_ref[at + n], 1), :] for n in range(ways * each)]
                for n in range(each):
                    old = [ref[pl.ds(place[n * ways + way], 1), :] for way, ref in enumerate(acc)]
                    for way, ref in enumerate(acc):
                        ref[pl.ds(place[n * ways + way], 1), :] = old[way] + value[n * ways + way]
                return carry

            def rest(at, carry):
                acc[0][pl.ds(r_ref[j * line + at], 1), :] += flat_ref[pl.ds(t_ref[j * line + at], 1), :]
                return carry

            lax.fori_loop(0, rounds, step, jnp.int32(0))
            lax.fori_loop(rounds * ways * each, many, rest, jnp.int32(0))
            return carry

        lax.fori_loop(0, sources, source, jnp.int32(0))
        o_ref[...] = d_ref[...].astype(F32) + sum(ref[...] for ref in acc).T

    smem = pl.BlockSpec(memory_space=pltpu.SMEM)
    return call(
        kernel,
        [like((width, vocab), F32)],
        (dense, *pieces, rows, tokens, counts),
        specs=[None] * 6 + [smem] * 3,
        scratch=[pltpu.VMEM((sources * listed, width), F32)] + [pltpu.VMEM((vocab, width), F32)] * ways,
        limit=60,
        name="table_grad",
    )[0]


def unpack_grads(z, own, other):
    rows = z.rows + z.extra
    pos_rows = z.pos + 2 * z.extra

    def kernel(own_ref, other_ref, qkv_ref, out_ref, fin_ref, fout_ref, gain_ref, bias_ref, pos_ref, eg_ref, es_ref, all_ref):
        core = side_of(1)
        shard = lax.axis_index("shard")
        all_ref[core] = own_ref[...]
        all_ref[1 - core] = other_ref[...]

        def own_lanes(value):
            total = jnp.zeros((value.shape[0], z.part), F32)
            for h in range(z.shards):
                total = total + jnp.where(shard == h, value[:, h * z.part : (h + 1) * z.part], 0.0)
            return total

        out_ref[...] = all_ref[0, : z.part].astype(F32)
        fin_ref[...] = all_ref[0, z.part : z.rows].astype(F32).reshape(z.groups, z.gi, z.d)
        for c in range(3):
            part = all_ref[1, c * z.gi : (c + 1) * z.gi].astype(F32)
            for g in range(z.groups):
                qkv_ref[c, g] = part[:, g * z.gw : (g + 1) * z.gw]
        part = all_ref[1, z.part : z.rows].astype(F32)
        for g in range(z.groups):
            fout_ref[g] = part[:, g * z.gw : (g + 1) * z.gw]
        small = own_lanes(all_ref[1, z.at_small : z.at_small + 16].astype(F32))
        gain_ref[...] = small[0:2]
        bias_ref[...] = small[2:11]
        eg_ref[...] = small[11:12]
        es_ref[...] = small[12:13]
        pos_ref[: z.pos] = all_ref[1, z.at_small + 16 : z.part].astype(F32)
        for side in range(2):
            pos_ref[z.pos + side * z.extra : z.pos + (side + 1) * z.extra] = all_ref[side, z.rows :].astype(F32)

    return call(
        kernel,
        [
            like((3, z.groups, z.gi, z.gw), F32),
            like((z.part, z.d), F32),
            like((z.groups, z.gi, z.d), F32),
            like((z.groups, z.part, z.gw), F32),
            like((2, z.part), F32),
            like((9, z.part), F32),
            like((pos_rows, z.d), F32),
            like((1, z.part), F32),
            like((1, z.part), F32),
        ],
        (own, other),
        scratch=[pltpu.VMEM((2, rows, z.d), BF16)],
        name="unpack",
    )


def body(token_ids, targets, segment_ids, word_table, pos_table, embed_gain, embed_shift, qkv_weight, out_weight, ffn_in, ffn_out, layer_gains, layer_biases):
    micro, _, seq = token_ids.shape
    vocab, d = word_table.shape
    pos_rows = pos_table.shape[0]
    shards = lax.axis_size("shard")
    dp = lax.axis_size("dp")
    both = ("section", "dp")
    section = lax.axis_index("section")
    first = section == 0
    z = Sizes(qkv_weight.shape, out_weight.shape, shards, pos_rows)
    offset = lax.axis_index("shard") * vocab

    mine = lax.dynamic_index_in_dim(jnp.stack([token_ids[:, 0], targets[:, 0], segment_ids[:, 0]], axis=1), section, 0, keepdims=False)
    ids_by = jnp.stack([mine, turned(mine, "shard", -1), turned(mine, "shard", 2), turned(mine, "shard", 1)])
    seg_row = mine[2:3]

    def rows_of(ids):
        return word_table.at[jnp.clip(ids.reshape(-1) - offset, 0, vocab - 1)].get(mode="promise_in_bounds")

    small = jnp.concatenate([layer_gains[0], layer_biases[0], embed_gain[None], embed_shift[None]], axis=0)
    local, pair, packed = pack_weights(z, qkv_weight[0], out_weight[0], ffn_in[0], ffn_out[0], small)
    cross_pair = crossed(pair, "section", 1)
    near = gather_first(packed, "shard")
    picked = rows_of(ids_by[:, 0])
    near, pos_table = after((near, pos_table), near)
    word_parts = embed_parts(picked, ids_by, pos_table, vocab)
    near = after(near, word_parts)
    near_rows = jnp.concatenate(near, axis=0)
    near_y = crossed(near_rows, "dp", 2)
    cross_near = crossed(near_rows, "section", 1)
    target_rows = rows_of(after(ids_by[:, 1], near_rows))
    c0, c1, c2a, c2b, c3 = word_parts
    half, quarter = seq // 2, z.part // 2
    right = turned(jnp.concatenate([c2a, near[0][:quarter]], axis=0), "shard", 1)
    left = turned(jnp.concatenate([c2b, near[1][quarter:]], axis=0), "shard", -1)
    right, left = after((right, left), target_rows)
    c1 = jnp.concatenate([c1[:half] + right[:half], c1[half:]], axis=0)
    c3 = jnp.concatenate([c3[:half], c3[half:] + left[:half]], axis=0)
    words = scatter_second(c0, c1, c3, "shard")
    far = jnp.concatenate([right[half:], left[half:]], axis=0)
    cross_far = crossed(far, "section", 1)
    both_y = crossed(jnp.concatenate([far, cross_near], axis=0), "dp", 2)
    far_y, cross_near_y = both_y[: z.part], both_y[z.part :]
    cross_far_y = crossed(cross_far, "dp", 2)
    mine = (near_rows, far)
    mine = (*mine, *(crossed(b, "dp", 1) for b in mine), near_y, far_y, crossed(near_y, "dp", 1), crossed(far_y, "dp", 1))
    others = (cross_near, cross_far)
    others = (*others, *(crossed(b, "dp", 1) for b in others))
    others = (*others, cross_near_y, cross_far_y, crossed(cross_near_y, "dp", 1), crossed(cross_far_y, "dp", 1))
    pairs = (cross_pair, crossed(cross_pair, "dp", 1))
    weights_one, weights_two = (Pieces(z, local, mine, pairs, others, layer) for layer in range(2))
    one = layer_forward(z, weights_one, seg_row, True, words=words)
    two = layer_forward(z, weights_two, seg_row, False, layer_in=one["out"])
    two["x"] = one["out"]

    own_out = jnp.where(first, one["out"], two["out"])
    came_out = crossed(jnp.where(first, two["out"], one["out"]), "section", 1)

    before, later = gather_first(two["out"], "shard")
    ctx_own, lse_own = head_forward([two["out"]], word_table)
    before = after(before, ctx_own)
    far_a = turned(before[: seq // 2], "shard", 1)
    ctx_before, lse_before = head_forward([before], word_table)
    later = after(later, ctx_before)
    far_b = turned(later[seq // 2 :], "shard", -1)
    ctx_later, lse_later = head_forward([later], word_table)
    far_a, far_b = after((far_a, far_b), ctx_later)
    ctx_far, lse_far = head_forward([far_a, far_b], word_table)
    lse = jnp.concatenate([lse_own[0:1], lse_later[0:1], lse_far[0:1], lse_before[0:1]], axis=1)
    listed = jnp.stack([ids_by[0, 0], ids_by[1, 0], ids_by[3, 0], ids_by[2, 0]]).reshape(1, -1)
    lists = list_tokens(after(listed, lse), vocab)
    lses = (lse, turned(lse, "shard", -1), turned(lse, "shard", 2), turned(lse, "shard", 1))
    lses = after(lses, (lists, came_out))
    parts, whole_lse = head_combine(seq, (ctx_own, ctx_later, ctx_far, ctx_before), target_rows, ids_by, lses, vocab)
    out_grad = lax.psum_scatter(parts, "shard", scatter_dimension=0, tiled=True)
    dense = head_table([two["out"], later, far_a, far_b, before], word_table, whole_lse, ids_by, 0, 6, 1280)

    out_grad = after(out_grad, dense)
    dense = lax.psum_scatter(dense, both, scatter_dimension=0, tiled=True)

    d_middle, small_grads, keep_f, send_f = ffn_backward(z, weights_two, two, out_grad)
    in_two, in_low, keep_a, send_a = attention_backward(z, weights_two, two, d_middle, small_grads, False)
    came_f, came_a = crossed(send_f, "dp", 1), crossed(send_a, "dp", 1)
    d_middle, small_grads, keep_one_f, send_one_f = ffn_backward(z, weights_one, one, in_low)
    keep_f, came_f, keep_a, came_a = after((keep_f, came_f, keep_a, came_a), d_middle)
    split_two = add_cores_split(z, (keep_a, keep_f), (came_a, came_f))
    d_middle = after(d_middle, split_two)
    terms_two = scatter_first(*split_two, "shard")
    came_one_f = crossed(send_one_f, "dp", 1)
    in_one, in_one_low, keep_one_a, send_one_a, d_embed = attention_backward(z, weights_one, one, d_middle, small_grads, True, seg_row, pos_rows)
    keep_one_f, came_one_f = after((keep_one_f, came_one_f), d_embed)
    send_one_a, d_embed = after((send_one_a, d_embed), terms_two)
    came_one_a = crossed(send_one_a, "dp", 1)
    columns = d_embed[None]
    steps = [("dp", 1 << n) for n in range(dp.bit_length() - 1)]
    for n, (axis, bit) in enumerate(steps):
        middle = columns.shape[1] // 2
        columns = jnp.concatenate([columns[:, :middle], crossed(columns[:, middle:], axis, bit)], axis=0)
        if n == 0:
            came_one_a = after(came_one_a, columns)
    split_one = add_cores_split(z, (keep_one_a, keep_one_f), (came_one_a, came_one_f))
    columns = after(columns, split_one)
    columns = jnp.concatenate([columns[:, 0], crossed(columns[:, 1], "section", 1)], axis=0)
    second_two = scatter_second(*terms_two, "shard")
    terms_one = scatter_first(*split_one, "shard")
    own_in = jnp.where(first, in_one, in_two)
    came_in = crossed(jnp.where(first, in_two, in_one).astype(BF16), "section", 1)
    lists = after(lists, columns)
    bit = 1
    while bit < dp:
        lists = jnp.concatenate([lists, crossed(lists, "dp", bit)], axis=0)
        bit *= 2
    lists = jnp.concatenate([lists, crossed(lists, "section", 1)], axis=0)
    sum_two = sum(after(second_two, (columns, split_one)))
    second_one = scatter_second(*after(terms_one, sum_two), "shard")
    sum_one = sum(after(second_one, (sum_two, lists, came_in)))
    columns = after(columns, sum_one)
    ring_columns = gather_first(columns, "shard")
    high = z.part + z.extra
    extra = sum_one[z.part : high]
    layer_one = jnp.concatenate([sum_one[: z.part], sum_one[high:]], axis=0)
    row = jnp.arange(z.rows)[:, None]
    embed_rows = (row >= z.at_small + 11) & (row < z.part) & (side_of(1) == 1)
    layer_two = jnp.where(embed_rows, layer_one, sum_two)
    total = jnp.concatenate([jnp.where(first, layer_one, layer_two), extra], axis=0)
    total = total + crossed(jnp.concatenate([jnp.where(first, layer_two, layer_one), extra], axis=0), "section", 1)
    total, ring_columns = after((total, ring_columns), ())
    far_columns = gather_second(*ring_columns, "shard")
    word_grad = table_grad(dense, (columns, ring_columns[1], ring_columns[0], *far_columns), lists, vocab)
    bit = 2
    while bit < dp:
        total = total + after(crossed(total, "dp", bit), word_grad)
        bit *= 2
    unpacked = unpack_grads(z, total, crossed(total, "dp", 1))

    word_grad = word_grad.T

    def by_micro(own, came):
        return jnp.stack([jnp.where(first, own, came), jnp.where(first, came, own)]).reshape(1, micro, 1, seq, d)

    layer_outputs = by_micro(own_out, came_out)
    input_grads = by_micro(own_in, came_in.astype(F32))
    qkv_g, out_g, fin_g, fout_g, gain_g, bias_g, pos_g, eg_g, es_g = unpacked
    return (
        layer_outputs,
        input_grads,
        word_grad,
        pos_g,
        eg_g.reshape(-1),
        es_g.reshape(-1),
        qkv_g[None],
        out_g[None],
        fin_g[None],
        fout_g[None],
        gain_g[None],
        bias_g[None],
    )


def solution(mesh):
    rows = P(None, ("dp", "shard"), None)
    weights = (
        P("section", None, None, "shard", None),
        P("section", "shard", None),
        P("section", None, "shard", None),
        P("section", None, "shard", None),
        P("section", None, "shard"),
        P("section", None, "shard"),
    )
    states = P("section", None, ("dp", "shard"), None, None)
    return jax.shard_map(
        body,
        mesh=mesh,
        in_specs=(rows, rows, rows, P("shard", None), P("shard", None), P("shard"), P("shard"), *weights),
        out_specs=(states, states, P("shard", ("section", "dp")), P("shard", None), P("shard"), P("shard"), *weights),
        check_vma=False,
    )
```

```python
import math

import jax
import jax.numpy as jnp
from jax import lax
from jax.experimental import pallas as pl
from jax.experimental.pallas import tpu as pltpu
from jax.sharding import PartitionSpec as P

HEADS = 12
EPSILON = 1e-06
MASKED = -1000000000.0
F32 = jnp.float32
BF16 = jnp.bfloat16
MIB = 1 << 20


def nn(a, b):
    return jnp.dot(a, b, preferred_element_type=F32)


def nt(a, b):
    return lax.dot_general(a, b, (((1,), (1,)), ((), ())), preferred_element_type=F32)


def tn(a, b):
    return lax.dot_general(a, b, (((0,), (0,)), ((), ())), preferred_element_type=F32)


def iota(shape, axis):
    return lax.broadcasted_iota(jnp.int32, shape, axis)


def group_of(index, width, count):
    total = jnp.zeros(index.shape, jnp.int32)
    for step in range(1, count):
        total = total + (index >= step * width).astype(jnp.int32)
    return total


def normed(value):
    centered = value - jnp.mean(value, axis=-1, keepdims=True)
    scale = lax.rsqrt(jnp.mean(centered * centered, axis=-1, keepdims=True) + EPSILON)
    return centered * scale, scale


def norm_back(grad, unit, scale, gain):
    inner = grad * gain
    first = jnp.mean(inner, axis=-1, keepdims=True)
    second = jnp.mean(inner * unit, axis=-1, keepdims=True)
    return scale * (inner - first - unit * second)


def col_sum(value):
    return jnp.sum(value, axis=0, keepdims=True)


def upright(row, count):
    return jnp.broadcast_to(row.astype(F32), (128, count)).T[:, 0:1]


def call(kernel, outs, ins, specs=None, scratch=(), limit=56, flops=0, moved=0, grid=None, out_specs=None, name=None):
    vmem = pl.BlockSpec(memory_space=pltpu.VMEM)
    extra = {} if grid is None else {"grid": grid}
    return pl.pallas_call(
        kernel,
        out_shape=outs,
        in_specs=[vmem if s is None else s for s in (specs or [None] * len(ins))],
        out_specs=out_specs if out_specs is not None else [vmem] * len(outs),
        scratch_shapes=list(scratch),
        compiler_params=pltpu.CompilerParams(vmem_limit_bytes=limit * MIB),
        cost_estimate=pl.CostEstimate(flops=flops, bytes_accessed=0, transcendentals=0),
        name=name,
        **extra,
    )(*ins)


def like(shape, dtype):
    return jax.ShapeDtypeStruct(shape, dtype)


def turned(block, axis, by):
    size = lax.axis_size(axis)
    return lax.ppermute(block, axis, [(i, (i + by) % size) for i in range(size)])


def crossed(block, axis, bit):
    return lax.ppermute(block, axis, [(i, i ^ bit) for i in range(lax.axis_size(axis))])


def after(value, first):
    return lax.optimization_barrier((value, first))[0]


def scatter_first(c0, c1, c2a, c2b, c3, axis, wait=()):
    half = c2a.shape[0]
    right, left = after((turned(c2a, axis, 1), turned(c2b, axis, -1)), wait)
    return c0, jnp.concatenate([c1[:half] + right, c1[half:]], axis=0), jnp.concatenate([c3[:half], c3[half:] + left], axis=0)


def scatter_second(c0, c1, c3, axis):
    return c0, turned(c1, axis, 1), turned(c3, axis, -1)


def side_of(bit):
    return (lax.axis_index("dp") // bit) % 2


def direct_scatter(parts, axis):
    return parts[0], turned(parts[1], axis, 1), turned(parts[3], axis, -1), turned(parts[2], axis, 2)


def gather_first(block, axis):
    return turned(block, axis, 1), turned(block, axis, -1)


def gather_second(before, later, axis):
    half = before.shape[0] // 2
    return turned(before[:half], axis, 1), turned(later[half:], axis, -1)


def ring_gather(block, axis):
    first = gather_first(block, axis)
    return (*first, *gather_second(*first, axis))


class Sizes:
    def __init__(self, qkv, out, shards, pos_rows):
        _, _, groups, part, width = qkv
        self.shards, self.groups, self.gw, self.gi = shards, groups, width, part
        self.d = out[2]
        self.part = out[1]
        self.at_small = 3 * part
        self.rows = 2 * self.part
        self.pos = self.part - self.at_small - 16
        self.quarter = (pos_rows - self.pos) // 4
        self.extra = -(-self.quarter // 16) * 16


def pack_weights(z, qkv, out, fin, fout, small):
    def kernel(qkv_ref, out_ref, fin_ref, fout_ref, small_ref, o_ref, pair_ref, own_ref):
        shard = lax.axis_index("shard")

        def spread(pieces):
            return jnp.concatenate([piece.astype(F32) for piece in pieces], axis=1).astype(BF16)

        o_ref[0, 0] = out_ref[...]
        o_ref[0, 1] = fin_ref[...].reshape(z.part, z.d)
        for c in range(3):
            o_ref[1, 0, c * z.gi : (c + 1) * z.gi] = spread([qkv_ref[c, g] for g in range(z.groups)])
        tall = jnp.concatenate([small_ref[...].astype(F32), jnp.zeros((16 - small_ref.shape[0], z.part), F32)], axis=0)
        wide = jnp.concatenate([tall] * z.shards, axis=1)
        lane = group_of(iota(wide.shape, 1), z.part, z.shards)
        o_ref[1, 0, z.at_small : z.at_small + 16] = jnp.where(lane == shard, wide, 0.0).astype(BF16)
        o_ref[1, 0, z.at_small + 16 : z.part] = jnp.zeros((z.part - z.at_small - 16, z.d), BF16)
        o_ref[1, 1] = spread([fout_ref[g] for g in range(z.groups)])
        pair_ref[...] = o_ref[side_of(1)]
        own_ref[...] = o_ref[side_of(1), side_of(2)]

    outs = [like((2, 2, z.part, z.d), BF16), like((2, z.part, z.d), BF16), like((z.part, z.d), BF16)]
    return call(kernel, outs, (qkv, out, fin, fout, small), name="pack")


class Pieces:
    def __init__(self, z, local, mine, pairs, others, layer):
        self.z, self.layer = z, layer
        self.arrays = (local, *mine, *pairs, *others)
        self.specs = [pl.BlockSpec(memory_space=pl.ANY)] * len(self.arrays)
        self.scratch = [pltpu.VMEM((2, z.shards, z.rows, z.d), BF16), pltpu.SemaphoreType.DMA((2, 2, 4))]

    def start(self, refs, w_ref, sems, parts):
        z = self.z
        core, y = side_of(1), side_of(2)
        shard = lax.axis_index("shard")
        own_layer = lax.axis_index("section") == self.layer
        local, mine, pairs, others = refs[0], refs[1:9], refs[9:11], refs[11:19]
        waits = {}
        for part in parts:
            copies = []
            for side in range(2):
                place = core if side == 0 else 1 - core
                for n, by in enumerate((0, 3, 1, 2)):
                    target = w_ref.at[place, (shard + by) % z.shards, pl.ds(part * z.part, z.part)]
                    sem = sems.at[part, side, n]
                    rows = pl.ds((n - 1) * z.part, z.part)
                    choices = []
                    for across in range(2):
                        here = (y == part) if across == 0 else (y != part)
                        at = 2 * across + side
                        if n == 0:
                            own, other = local.at[place, part], pairs[side].at[part]
                        elif n < 3:
                            own, other = mine[2 * at].at[rows], others[2 * at].at[rows]
                        else:
                            own, other = mine[2 * at + 1], others[2 * at + 1]
                        choices.append((jnp.logical_and(here, own_layer), own))
                        choices.append((jnp.logical_and(here, jnp.logical_not(own_layer)), other))
                    for here, source in choices:
                        copy = pltpu.make_async_copy(source, target, sem)
                        pl.when(here)(copy.start)
                    copies.append(pltpu.make_async_copy(choices[1][1], target, sem))
            waits[part] = copies
        return waits


def wait_all(copies):
    for copy in copies:
        copy.wait()


class Loads:
    def __init__(self, arrays):
        self.names = list(arrays)
        self.arrays = list(arrays.values())
        self.specs = [pl.BlockSpec(memory_space=pl.ANY)] * len(self.arrays)
        self.scratch = [pltpu.VMEM(a.shape, a.dtype) for a in self.arrays] + [pltpu.SemaphoreType.DMA((len(self.arrays),))]

    def start(self, refs, scratch):
        self.buffers = dict(zip(self.names, scratch))
        self.copies = {
            name: pltpu.make_async_copy(ref, buffer, scratch[-1].at[n])
            for n, (name, ref, buffer) in enumerate(zip(self.names, refs, scratch))
        }
        for copy in self.copies.values():
            copy.start()

    def __getitem__(self, name):
        copy = self.copies.pop(name, None)
        if copy is not None:
            copy.wait()
        return self.buffers[name]


class Stores:
    def __init__(self, shapes, split=()):
        self.names = list(shapes)
        self.shapes = list(shapes.values())
        self.split = split
        self.specs = [pl.BlockSpec(memory_space=pl.ANY)] * len(self.shapes)
        count = sum(a.shape[0] if name in split else 1 for name, a in shapes.items())
        self.scratch = [pltpu.VMEM(a.shape, a.dtype) for a in self.shapes] + [pltpu.SemaphoreType.DMA((count,))]

    def bind(self, refs, scratch):
        self.refs = dict(zip(self.names, refs))
        self.buffers = dict(zip(self.names, scratch))
        self.sems = scratch[-1]
        self.copies = []

    def put(self, name, value, index=None):
        source = self.buffers[name] if index is None else self.buffers[name].at[index]
        source[...] = value.astype(source.dtype)
        self.send(name, index)

    def send(self, name, index=None):
        source, target = self.buffers[name], self.refs[name]
        if index is not None:
            source, target = source.at[index], target.at[index]
        copy = pltpu.make_async_copy(source, target, self.sems.at[len(self.copies)])
        copy.start()
        self.copies.append(copy)

    def finish(self):
        wait_all(self.copies)


class Weights:
    def __init__(self, z, w_ref):
        self.z, self.w = z, w_ref

    def out(self):
        z = self.z
        return self.w[0, :, 0 : z.part, :].reshape(z.d, z.d)

    def small(self):
        z = self.z
        return sum(self.w[1, h, z.at_small : z.at_small + 16, :].astype(F32) for h in range(z.shards))

    def proj(self, c, p):
        z = self.z
        lanes = slice(2 * p * z.gw, 2 * (p + 1) * z.gw)
        dense = self.w[1, :, c * z.gi : (c + 1) * z.gi, lanes].reshape(z.gw, 2 * z.gw)
        high = iota(dense.shape, 1) >= z.gw
        blank = jnp.zeros_like(dense)
        return jnp.concatenate([jnp.where(high, blank, dense), jnp.where(high, dense, blank)], axis=0)

    def project(self, value, c):
        z = self.z
        wide = 2 * z.gw
        return jnp.concatenate([nn(value[:, p * wide : (p + 1) * wide], self.proj(c, p)) for p in range(z.groups // 2)], axis=1)

    def fin(self, g):
        z = self.z
        row = z.part + g * z.gi
        dense = self.w[0, :, row : row + z.gi, :].reshape(z.gw, z.d)
        blank = jnp.zeros_like(dense)
        return jnp.concatenate([dense, blank] if g % 2 == 0 else [blank, dense], axis=0)

    def fout(self, g):
        z = self.z
        at = (g // 2) * 2 * z.gw
        pair = self.w[1, :, z.part : z.rows, at : at + 2 * z.gw].reshape(z.d, 2 * z.gw)
        keep = (iota(pair.shape, 1) >= z.gw) == (g % 2 == 1)
        return jnp.where(keep, pair, jnp.zeros_like(pair))


def embed_parts(picked, ids_by, pos_table, vocab):
    count, _, seq = ids_by.shape
    width = picked.shape[1]
    half = seq // 2
    rows = pos_table.shape[0]

    def kernel(p_ref, i_ref, t_ref, c0, c1, c2a, c2b, c3):
        shard = lax.axis_index("shard")
        for k in range(count):
            span = slice(k * seq, (k + 1) * seq)
            token, seg_row = i_ref[k, 0:1], i_ref[k, 2:3]
            seg_col = upright(seg_row, seq)
            same = seg_col == seg_row.astype(F32)
            earlier = iota((seq, seq), 1) < iota((seq, seq), 0)
            place = jnp.sum(jnp.where(same & earlier, 1.0, 0.0), axis=1, keepdims=True).astype(jnp.int32) - shard * rows
            spot = (iota((seq, rows), 1) == place).astype(BF16)
            local = token - shard * vocab
            inside = upright(jnp.where((local >= 0) & (local < vocab), 1.0, 0.0), seq)
            word = jnp.where(inside > 0.5, p_ref[span].astype(F32), 0.0)
            total = (word + nn(spot, t_ref[...])).astype(BF16)
            if k == 2:
                c2a[...] = total[:half]
                c2b[...] = total[half:]
            else:
                (c0, c1, None, c3)[k][...] = total

    full, part = like((seq, width), BF16), like((half, width), BF16)
    return call(kernel, [full, full, part, part, full], (picked, ids_by, pos_table), name="embed_parts")


def layer_forward(z, pieces, seg_row, first, words=None, layer_in=None):
    seq = seg_row.shape[1]
    d = z.d
    flat = like((seq, d), BF16)
    shapes = {"q": flat, "k": flat, "v": flat, "p": like((HEADS, seq, seq), BF16), "att": flat, "n1": flat, "mid": flat}
    shapes.update({"act": like((z.groups, seq, d), BF16), "slope": like((z.groups, seq, d), BF16)})
    shapes.update({"n2": flat, "stats": like((seq, 128), F32), "small": like((16, d), F32), "out": flat})
    if first:
        shapes.update({"x": flat, "n0": flat})
    stores = Stores(shapes, split=("p", "act", "slope"))
    head = d // HEADS
    inputs = list(words) if first else [layer_in]

    def kernel(*refs):
        piece_refs, refs = refs[: len(pieces.arrays)], refs[len(pieces.arrays) :]
        row_ref, refs = refs[0], refs[1:]
        in_refs, refs = refs[: len(inputs)], refs[len(inputs) :]
        out_refs, refs = refs[: len(shapes)], refs[len(shapes) :]
        w_ref, sems, *buffers = refs
        waits = pieces.start(piece_refs, w_ref, sems, (0, 1))
        stores.bind(out_refs, buffers)
        put, send = stores.put, stores.send
        w = Weights(z, w_ref)
        if first:
            unit, r0 = normed(sum(ref[...].astype(F32) for ref in in_refs))
            put("n0", unit)
        wait_all(waits[0])
        small = w.small()
        put("small", small)
        if first:
            x = unit * small[11:12] + small[12:13]
            x_low = x.astype(BF16)
            put("x", x_low)
        else:
            r0 = jnp.zeros((seq, 1), F32)
            x_low = in_refs[0][...]
            x = x_low.astype(F32)
        q = (w.project(x_low, 0).astype(BF16).astype(F32) * (1.0 / math.sqrt(head))).astype(BF16)
        k = w.project(x_low, 1).astype(BF16)
        v = (w.project(x_low, 2) + small[2:3]).astype(BF16)
        put("q", q)
        put("k", k)
        put("v", v)
        same = upright(row_ref[...], seq) == row_ref[...].astype(F32)
        second = iota((seq, 128), 1) >= head
        q_ref, k_ref, v_ref, att_ref = (stores.buffers[name] for name in ("q", "k", "v", "att"))

        def heads(t, carry):
            lanes = pl.ds(pl.multiple_of(t * 128, 128), 128)
            q_t, k_t, v_t = q_ref[:, lanes], k_ref[:, lanes], v_ref[:, lanes]
            raw = [nt(jnp.where(second == (j == 1), q_t, jnp.zeros_like(q_t)), k_t) for j in range(2)]
            results = []
            for j in range(2):
                scores = jnp.where(same, raw[j], MASKED)
                scores = jnp.exp(scores - jnp.max(scores, axis=-1, keepdims=True))
                probs = (scores * (1.0 / jnp.sum(scores, axis=-1, keepdims=True))).astype(BF16)
                stores.buffers["p"][2 * t + j] = probs
                results.append(nn(probs, v_t))
            att_ref[:, lanes] = jnp.where(second, results[1], results[0]).astype(BF16)
            return carry

        lax.fori_loop(0, d // 128, heads, jnp.int32(0))
        attended = att_ref[...]
        send("p")
        send("att")
        unit, r1 = normed(x + (nn(attended, w.out()) + small[3:4]))
        put("n1", unit)
        middle = unit * small[0:1] + small[4:5]
        middle_low = middle.astype(BF16)
        put("mid", middle_low)
        wait_all(waits[1])
        back = [None] * (z.groups // 2)

        def pre_of(g):
            pair = slice((g // 2) * 2 * z.gw, (g // 2 + 1) * 2 * z.gw)
            return nn(middle_low[:, pair], w.fin(g))

        raw = pre_of(0)
        for g in range(z.groups):
            following = pre_of(g + 1) if g + 1 < z.groups else None
            pre = raw + small[5 + g : 6 + g]
            half = 0.5 + 0.5 * lax.erf(pre * math.sqrt(0.5))
            slope = half + pre * (jnp.exp(-0.5 * pre * pre) * (1.0 / math.sqrt(2.0 * math.pi)))
            active = (pre * half).astype(BF16)
            put("act", active, g)
            put("slope", slope, g)
            added = nn(active, w.fout(g))
            back[g // 2] = added if back[g // 2] is None else back[g // 2] + added
            raw = following
        unit, r2 = normed(middle + (jnp.concatenate(back, axis=1) + small[9:10]))
        put("n2", unit)
        put("out", unit * small[1:2] + small[10:11])
        lane = iota((seq, 128), 1)
        put("stats", jnp.where(lane == 0, r0, jnp.where(lane == 1, r1, r2)))
        stores.finish()

    outs = call(
        kernel,
        stores.shapes,
        (*pieces.arrays, seg_row, *inputs),
        specs=pieces.specs + [None] * (1 + len(inputs)),
        out_specs=stores.specs,
        scratch=pieces.scratch + stores.scratch,
        flops=12 * 10**9,
        name="layer_first" if first else "layer_second",
    )
    return dict(zip(stores.names, outs))


def send_halves(z, g_ref, keep_ref, send_ref, sems):
    core = lax.axis_index("dp") % 2
    shard = lax.axis_index("shard")
    copies = []
    for k in range(z.shards):
        to = (shard + k) % z.shards
        copies.append(pltpu.make_async_copy(g_ref.at[1 - core, to], send_ref.at[k], sems.at[2 * k]))
        copies.append(pltpu.make_async_copy(g_ref.at[core, to], keep_ref.at[k], sems.at[2 * k + 1]))
    for copy in copies:
        copy.start()
    return copies


def ffn_backward(z, pieces, state, out_grad):
    seq, d = out_grad[0].shape
    loads = Loads({**{f"dy{n}": term for n, term in enumerate(out_grad)}, **{key: state[key] for key in ("n2", "stats", "small", "mid", "act", "slope")}})
    outs = [like((seq, d), F32), like((16, d), F32)] + [like((z.shards, z.part, d), BF16)] * 2

    def kernel(*refs):
        piece_refs, refs = refs[: len(pieces.arrays)], refs[len(pieces.arrays) :]
        load_refs, refs = refs[: len(loads.names)], refs[len(loads.names) :]
        dm_ref, small_ref, keep_ref, send_ref, w_ref, sems, g_ref, out_sems, *buffers = refs
        loads.start(load_refs, buffers)
        waits = pieces.start(piece_refs, w_ref, sems, (1,))
        w = Weights(z, w_ref)
        dy = sum(loads[f"dy{n}"][...].astype(F32) for n in range(len(out_grad)))
        n2 = loads["n2"][...].astype(F32)
        scale = loads["stats"][:, 2:3]
        small = loads["small"][...]
        gain_two, shift_two = col_sum(dy * n2), col_sum(dy)
        d_final = norm_back(dy, n2, scale, small[1:2])
        d_ffn = d_final.astype(BF16)
        ffn_shift = col_sum(d_ffn.astype(F32))
        middle_t = loads["mid"][...].T
        act, slope = loads["act"], loads["slope"]
        wait_all(waits[1])
        pre_shift = []
        pair_back = [None] * (z.groups // 2)
        wide = 2 * z.gw

        def act_grad(g):
            p = g // 2
            return nt(d_ffn[:, p * wide : (p + 1) * wide], w.fout(g))

        raw = act_grad(0)
        for p in range(z.groups // 2):
            lanes = slice(p * wide, (p + 1) * wide)
            out_pair = d_ffn[:, lanes]
            back_pair = []
            for g in (2 * p, 2 * p + 1):
                following = act_grad(g + 1) if g + 1 < z.groups else None
                d_pre = (raw * slope[g].astype(F32)).astype(BF16)
                pre_shift.append(col_sum(d_pre.astype(F32)))
                back_pair.append(tn(act[g], out_pair))
                grad_in = nn(middle_t[g * z.gw : (g + 1) * z.gw], d_pre)
                g_ref[0, :, g * z.gi : (g + 1) * z.gi, :] = grad_in.astype(BF16).reshape(z.shards, z.gi, d)
                added = nt(d_pre, w.fin(g))
                pair_back[p] = added if pair_back[p] is None else pair_back[p] + added
                raw = following
            odd = iota(back_pair[0].shape, 1) >= z.gw
            both = jnp.where(odd, back_pair[1], back_pair[0]).astype(BF16)
            g_ref[1, :, :, lanes] = both.reshape(z.shards, z.part, wide)
        copies = send_halves(z, g_ref, keep_ref, send_ref, out_sems)
        dm_ref[...] = d_final + jnp.concatenate(pair_back, axis=1)
        blank = jnp.zeros((1, d), F32)
        small_ref[...] = jnp.concatenate(
            [blank, gain_two, blank, blank, blank, *pre_shift, ffn_shift, shift_two, jnp.zeros((5, d), F32)], axis=0
        )
        wait_all(copies)

    anywhere = pl.BlockSpec(memory_space=pl.ANY)
    return call(
        kernel,
        outs,
        (*pieces.arrays, *loads.arrays),
        specs=pieces.specs + loads.specs,
        out_specs=[pl.BlockSpec(memory_space=pltpu.VMEM)] * 2 + [anywhere] * 2,
        scratch=pieces.scratch + [pltpu.VMEM((2, z.shards, z.part, d), BF16), pltpu.SemaphoreType.DMA((2 * z.shards,))] + loads.scratch,
        flops=9 * 10**9,
        name="ffn_back",
    )


def attention_backward(z, pieces, state, d_middle, small_in, first, seg_row=None, pos_rows=0):
    seq, d = d_middle.shape
    head = d // HEADS
    keys = ["n1", "stats", "small", "att", "q", "k", "v", "p", "x"] + (["n0"] if first else [])
    loads = Loads({"dm": d_middle, **{key: state[key] for key in keys}, "grads": small_in, **({"seg": seg_row} if first else {})})
    rows = z.part + (2 * z.extra if first else 0)
    outs = [like((seq, d), F32), like((seq, d), BF16)] + [like((z.shards, rows, d), BF16)] * 2
    blocks = 2 * lax.axis_size("dp")
    if first:
        outs.append(like((blocks, d // blocks, seq), BF16))

    def kernel(*refs):
        piece_refs, refs = refs[: len(pieces.arrays)], refs[len(pieces.arrays) :]
        load_refs, refs = refs[: len(loads.names)], refs[len(loads.names) :]
        dx_ref, low_ref, keep_ref, send_ref = refs[:4]
        de_ref = refs[4] if first else None
        w_ref, sems, g_ref, out_sems, *buffers = refs[len(outs) :]
        loads.start(load_refs, buffers)
        waits = pieces.start(piece_refs, w_ref, sems, (0,))
        w = Weights(z, w_ref)
        d_middle = loads["dm"][...]
        n1 = loads["n1"][...].astype(F32)
        stats = loads["stats"][...]
        r0, r1 = stats[:, 0:1], stats[:, 1:2]
        small = loads["small"][...]
        gain_one, shift_one = col_sum(d_middle * n1), col_sum(d_middle)
        d_mid = norm_back(d_middle, n1, r1, small[0:1])
        d_branch = d_mid.astype(BF16)
        branch_shift = col_sum(d_branch.astype(F32))
        g_ref[0, :, 0 : z.part, :] = tn(loads["att"][...], d_branch).astype(BF16).reshape(z.shards, z.part, d)
        wait_all(waits[0])
        d_att = nt(d_branch, w.out()).astype(BF16)
        second = iota((seq, 128), 1) >= head
        scale = 1.0 / math.sqrt(head)
        q_ref, k_ref, v_ref, p_ref = (loads[key] for key in ("q", "k", "v", "p"))
        units = [(t, j) for t in range(d // 128) for j in range(2)]

        def probs_grad(unit):
            t, j = unit
            lanes = slice(t * 128, (t + 1) * 128)
            a_j = jnp.where(second == (j == 1), d_att[:, lanes], jnp.zeros((seq, 128), BF16))
            return nt(a_j, v_ref[:, lanes])

        dq, dk, dv = [], [], []
        raw = probs_grad(units[0])
        for n, (t, j) in enumerate(units):
            following = probs_grad(units[n + 1]) if n + 1 < len(units) else None
            lanes = slice(t * 128, (t + 1) * 128)
            probs_low = p_ref[n]
            probs = probs_low.astype(F32)
            inner = jnp.sum(probs * raw, axis=-1, keepdims=True)
            d_scores = (probs * (raw - inner)).astype(BF16)
            result = (nn(d_scores, k_ref[:, lanes]), tn(d_scores, q_ref[:, lanes]), tn(probs_low, d_att[:, lanes]))
            if j == 0:
                kept = result
            else:
                dq.append((jnp.where(second, result[0], kept[0]) * scale).astype(BF16))
                dk.append(jnp.where(second, result[1], kept[1]).astype(BF16))
                dv.append(jnp.where(second, result[2], kept[2]).astype(BF16))
            raw = following
        value_shift = col_sum(jnp.concatenate(dv, axis=1).astype(F32))
        x_t = loads["x"][...].T
        d_in = [d_mid[:, : 2 * z.gw], d_mid[:, 2 * z.gw :]]
        high = iota((z.gw, 2 * z.gw), 1) >= z.gw
        for c, parts in enumerate((dq, dk, dv)):
            d_c = jnp.concatenate(parts, axis=1)
            for p in range(z.groups // 2):
                lanes = slice(2 * p * z.gw, 2 * (p + 1) * z.gw)
                full = nn(x_t[lanes], d_c[:, lanes])
                grad = jnp.where(high, full[z.gw :], full[: z.gw]).astype(BF16)
                g_ref[1, :, c * z.gi : (c + 1) * z.gi, lanes] = grad.reshape(z.shards, z.gi, 2 * z.gw)
                d_in[p] = d_in[p] + nt(d_c[:, lanes], w.proj(c, p))
        d_in = jnp.concatenate(d_in, axis=1)
        blank = jnp.zeros((1, d), F32)
        embed_grads = [blank, blank]
        if first:
            n0 = loads["n0"][...].astype(F32)
            embed_grads = [col_sum(d_in * n0), col_sum(d_in)]
            d_embed = norm_back(d_in, n0, r0, small[11:12])
            d_embed_t = d_embed.T
            bits = blocks.bit_length() - 1
            me = lax.axis_index("section") * (blocks // 2) + lax.axis_index("dp")
            for b in range(blocks):
                to = me ^ b
                place = sum(((to >> bit) & 1) << (bits - 1 - bit) for bit in range(bits))
                de_ref[place] = d_embed_t[b * (d // blocks) : (b + 1) * (d // blocks)].astype(BF16)
            seg = loads["seg"][...]
            same = upright(seg, seq) == seg.astype(F32)
            later = iota((seq, seq), 0) < iota((seq, seq), 1)
            place = jnp.sum(jnp.where(same & later, 1.0, 0.0), axis=0, keepdims=True).astype(jnp.int32)
            spot = (iota((pos_rows, seq), 0) == place).astype(BF16)
            pos_grad = nn(spot, d_embed.astype(BF16)).astype(BF16)
        small_grads = jnp.concatenate([gain_one, blank, value_shift, branch_shift, shift_one, jnp.zeros((6, d), F32), *embed_grads, jnp.zeros((3, d), F32)], axis=0)
        small_grads = (small_grads + loads["grads"][...]).astype(BF16)
        if first:
            blank = jnp.zeros((z.extra - z.quarter, d), BF16)
            others = [pos_grad[z.pos + n * z.quarter : z.pos + (n + 1) * z.quarter] for n in range(4)]
        for h in range(z.shards):
            g_ref[1, h, z.at_small : z.at_small + 16, :] = small_grads
            spare = pos_grad[: z.pos] if first and h == 0 else jnp.zeros((z.pos, d), BF16)
            g_ref[1, h, z.at_small + 16 : z.part, :] = spare
            if first:
                for side in range(2):
                    for y in range(2):
                        row = z.part + y * z.extra
                        part = jnp.concatenate([others[2 * side + y].astype(F32), blank.astype(F32)], axis=0).astype(BF16) if h == 0 else jnp.zeros((z.extra, d), BF16)
                        g_ref[side, h, row : row + z.extra, :] = part
        copies = send_halves(z, g_ref, keep_ref, send_ref, out_sems)
        dx_ref[...] = d_in
        low_ref[...] = d_in.astype(BF16)
        wait_all(copies)

    anywhere = pl.BlockSpec(memory_space=pl.ANY)
    vmem = pl.BlockSpec(memory_space=pltpu.VMEM)
    return call(
        kernel,
        outs,
        (*pieces.arrays, *loads.arrays),
        specs=pieces.specs + loads.specs,
        out_specs=[vmem, vmem, anywhere, anywhere] + [vmem] * (len(outs) - 4),
        scratch=pieces.scratch + [pltpu.VMEM((2, z.shards, rows, d), BF16), pltpu.SemaphoreType.DMA((2 * z.shards,))] + loads.scratch,
        flops=13 * 10**9,
        name="att_back",
    )


def add_cores_split(z, keep, came):
    shards, part, d = keep[0].shape

    def kernel(a_ref, f_ref, b_ref, e_ref, c0, c1, c2a, c2b, c3):
        for k, ref in ((0, c0), (1, c1), (3, c3)):
            ref[:part] = a_ref[k] + b_ref[k]
            ref[part:] = f_ref[k] + e_ref[k]
        c2a[...] = a_ref[2] + b_ref[2]
        c2b[...] = f_ref[2] + e_ref[2]

    full, half = like((2 * part, d), BF16), like((part, d), BF16)
    return call(kernel, [full, full, half, half, full], (*keep, *came), name="add_cores_split")


def halves_by_y(z, terms):
    def kernel(a_ref, b_ref, c_ref, keep_ref, send_ref):
        y = side_of(2)
        for ref, part in ((keep_ref, y), (send_ref, 1 - y)):
            span = pl.ds(pl.multiple_of(part * z.part, z.part), z.part)
            ref[...] = (a_ref[span].astype(F32) + b_ref[span].astype(F32) + c_ref[span].astype(F32)).astype(BF16)

    return call(kernel, [like((z.part, z.d), BF16)] * 2, terms, name="halves_by_y")


def add_core(z, keep_a, came_a, keep_f, came_f):
    rows = z.part + z.extra

    def kernel(a_ref, b_ref, c_ref, e_ref, keep_ref, send_ref):
        y = side_of(2)

        def place(ref, part):
            if part == 0:
                ref[:, : z.part] = a_ref[:, : z.part] + b_ref[:, : z.part]
            else:
                ref[:, : z.part] = c_ref[...] + e_ref[...]
            span = slice(z.part + part * z.extra, z.part + (part + 1) * z.extra)
            ref[:, z.part :] = a_ref[:, span] + b_ref[:, span]

        @pl.when(y == 0)
        def _():
            place(keep_ref, 0)
            place(send_ref, 1)

        @pl.when(y == 1)
        def _():
            place(keep_ref, 1)
            place(send_ref, 0)

    return call(kernel, [like((z.shards, rows, z.d), BF16)] * 2, (keep_a, came_a, keep_f, came_f), name="add_core")


def add_split(kept, came):
    _, rows, d = kept.shape
    half = rows // 32 * 16

    def kernel(a_ref, b_ref, c0, c1, c2a, c2b, c3):
        for k, ref in ((0, c0), (1, c1), (3, c3)):
            ref[...] = a_ref[k] + b_ref[k]
        c2a[...] = a_ref[2, :half] + b_ref[2, :half]
        c2b[...] = a_ref[2, half:] + b_ref[2, half:]

    full = like((rows, d), BF16)
    outs = [full, full, like((half, d), BF16), like((rows - half, d), BF16), full]
    return call(kernel, outs, (kept, came), name="add_split")


def head_forward(pieces, table):
    count = sum(piece.shape[0] for piece in pieces)
    vocab, d = table.shape
    tiles = 3
    block = vocab // tiles
    part = block // 2
    chunk = 256
    many = len(pieces)

    def kernel(*refs):
        piece_refs, (w_ref, ctx_ref, lse_ref, x_ref, m_ref, s_ref, acc_ref) = refs[:many], refs[many:]
        step = pl.program_id(0)

        @pl.when(step == 0)
        def _():
            at = 0
            for ref in piece_refs:
                x_ref[at : at + ref.shape[0]] = ref[...]
                at += ref.shape[0]
            m_ref[...] = jnp.full(m_ref.shape, -1e30, F32)
            s_ref[...] = jnp.zeros(s_ref.shape, F32)
            acc_ref[...] = jnp.zeros(acc_ref.shape, F32)

        units = [(c, r) for c in range(2) for r in range(count // chunk)]

        def logits_of(unit):
            c, r = unit
            return nt(x_ref[r * chunk : (r + 1) * chunk], w_ref[c * part : (c + 1) * part])

        logits = logits_of(units[0])
        for n, (c, r) in enumerate(units):
            following = logits_of(units[n + 1]) if n + 1 < len(units) else None
            span = slice(r * chunk, (r + 1) * chunk)
            old = m_ref[span]
            new = jnp.maximum(old, jnp.max(logits, axis=-1, keepdims=True))
            keep = jnp.exp(old - new)
            weight = jnp.exp(logits - new)
            s_ref[span] = s_ref[span] * keep + jnp.sum(weight, axis=-1, keepdims=True)
            acc_ref[span] = acc_ref[span] * keep + nn(weight.astype(BF16), w_ref[c * part : (c + 1) * part])
            m_ref[span] = new
            logits = following

        @pl.when(step == tiles - 1)
        def _():
            total = s_ref[...]
            ctx_ref[...] = acc_ref[...] * (1.0 / total)
            lse = m_ref[...] + jnp.log(total)
            lse_ref[...] = jnp.broadcast_to(lse, (count, 128)).T[0:8]

    fixed = lambda i: (0, 0)
    return call(
        kernel,
        [like((count, d), F32), like((8, count), F32)],
        (*pieces, table),
        specs=[pl.BlockSpec(piece.shape, fixed) for piece in pieces] + [pl.BlockSpec((block, d), lambda i: (i, 0))],
        out_specs=[pl.BlockSpec((count, d), fixed), pl.BlockSpec((8, count), fixed)],
        scratch=[pltpu.VMEM((count, d), BF16), pltpu.VMEM((count, 1), F32), pltpu.VMEM((count, 1), F32), pltpu.VMEM((count, d), F32)],
        grid=(tiles,),
        flops=11 * 10**9,
        name="head_forward",
    )


def head_combine(seq, ctxs, picked, ids_by, lses, vocab):
    shards = ids_by.shape[0]
    d = picked.shape[1]

    def kernel(x0_ref, x1_ref, x2_ref, x3_ref, p_ref, i_ref, a_ref, b_ref, c_ref, e_ref, *outs):
        lse_ref = outs[shards]
        shard = lax.axis_index("shard")
        parts = (a_ref, b_ref, c_ref, e_ref)
        for k in range(shards):
            rows = [parts[m][:, ((k - m) % shards) * seq : ((k - m) % shards + 1) * seq] for m in range(shards)]
            top = rows[0]
            for row in rows[1:]:
                top = jnp.maximum(top, row)
            total = top + jnp.log(sum(jnp.exp(row - top) for row in rows))
            whole = upright(total, seq)
            span = slice(k * seq, (k + 1) * seq)
            lse_ref[span] = whole
            weight = upright(jnp.exp(rows[0] - total), seq)
            local = i_ref[k, 1:2] - shard * vocab
            inside = upright(jnp.where((local >= 0) & (local < vocab), 1.0, 0.0), seq)
            hit = jnp.where(inside > 0.5, p_ref[span].astype(F32), 0.0)
            ctx = (x0_ref, x1_ref, x2_ref, x3_ref)[k][...]
            outs[k][...] = (ctx * weight - hit).astype(BF16)

    return call(
        kernel,
        [like((seq, d), BF16)] * shards + [like((shards * seq, 1), F32)],
        (*ctxs, picked, ids_by, *lses),
        name="head_combine",
    )


def head_table(pieces, table, lse, ids_by, core=None):
    count = sum(piece.shape[0] for piece in pieces)
    shards, _, seq = ids_by[0].shape
    vocab, d = table.shape
    block = 1280
    tiles = pl.cdiv(vocab, block)
    shared = core is not None
    if shared:
        tiles = (tiles + 1) // 2
    else:
        core = jnp.zeros((1,), jnp.int32)
    chunk = 256
    many, groups = len(pieces), len(ids_by)
    wide = d // 8

    def kernel(core_ref, *refs):
        piece_refs, refs = refs[:many], refs[many:]
        w_ref, refs = refs[0], refs[1:]
        lse_refs, i_refs, refs = refs[:groups], refs[groups : 2 * groups], refs[2 * groups :]
        out_refs, (x_ref, xt_ref, t_ref, l_ref, p_ref) = refs[:-5], refs[-5:]
        step = pl.program_id(0)
        first_tile = core_ref[0] * tiles

        @pl.when(step == 0)
        def _():
            at = 0
            for ref in piece_refs:
                x_ref[at : at + ref.shape[0]] = ref[...]
                at += ref.shape[0]
            xt_ref[...] = x_ref[...].T
            start = lax.axis_index("shard") * vocab + first_tile * block
            for n in range(groups):
                for k in range(shards):
                    at = (n * shards + k) * seq
                    t_ref[at : at + seq] = upright(i_refs[n][k, 1:2] - start, seq).astype(jnp.int32)
                at = n * shards * seq
                l_ref[at : at + shards * seq] = lse_refs[n][...]

        w = w_ref[...]
        for r in range(count // chunk):
            span = slice(r * chunk, (r + 1) * chunk)
            logits = nt(x_ref[span], w)
            hit = iota(logits.shape, 1) == t_ref[span] - step * block
            p_ref[span] = (jnp.exp(logits - l_ref[span]) - jnp.where(hit, 1.0, 0.0)).astype(BF16)
        result = nn(xt_ref[...], p_ref[...]).astype(BF16)
        if not shared:
            out_refs[0][...] = result
            return
        zero = jnp.zeros((wide, block), jnp.int32)
        first = zero + lax.axis_index("section") == 0
        front = zero + side_of(2) == 0
        blocks = [result[n * wide : (n + 1) * wide] for n in range(8)]
        for n in range(2):
            low, high = blocks[2 * n], blocks[4 + 2 * n]
            out_refs[0][n], out_refs[1][n] = jnp.where(first, low, high), jnp.where(first, high, low)
            low, high = blocks[4 * n + 1], blocks[4 * n + 3]
            out_refs[2][n], out_refs[3][n] = jnp.where(front, low, high), jnp.where(front, high, low)

    if shared:
        outs = [like((2, wide, tiles * block), BF16)] * 4
        out_specs = [pl.BlockSpec((2, wide, block), lambda i, c: (0, 0, i))] * 4
    else:
        outs, out_specs = [like((d, vocab), BF16)], [pl.BlockSpec((d, block), lambda i, c: (0, i))]
    fixed = lambda i, c: (0, 0)
    return pl.pallas_call(
        kernel,
        out_shape=outs,
        grid_spec=pltpu.PrefetchScalarGridSpec(
            num_scalar_prefetch=1,
            grid=(tiles,),
            in_specs=[pl.BlockSpec(piece.shape, fixed) for piece in pieces]
            + [pl.BlockSpec((block, d), lambda i, c: (i + c[0] * tiles, 0))]
            + [pl.BlockSpec((shards * seq, 1), fixed)] * groups
            + [pl.BlockSpec(ids_by[0].shape, lambda i, c: (0, 0, 0))] * groups,
            out_specs=out_specs,
            scratch_shapes=[
                pltpu.VMEM((count, d), BF16),
                pltpu.VMEM((d, count), BF16),
                pltpu.VMEM((count, 1), jnp.int32),
                pltpu.VMEM((count, 1), F32),
                pltpu.VMEM((count, block), BF16),
            ],
        ),
        compiler_params=pltpu.CompilerParams(vmem_limit_bytes=58 * MIB),
        cost_estimate=pl.CostEstimate(flops=32 * 10**9, bytes_accessed=0, transcendentals=0),
        name="head_table",
    )(core, *pieces, table, *lse, *ids_by)


def add_halves(even, odd):
    shape = even[0].shape[1:]

    def kernel(a_ref, b_ref, c_ref, e_ref, *outs):
        for n, (one, two, side) in enumerate(((a_ref, b_ref, side_of(2)), (c_ref, e_ref, lax.axis_index("section")))):
            outs[2 * n][...] = one[side] + two[side]
            outs[2 * n + 1][...] = one[1 - side] + two[1 - side]

    return call(kernel, [like(shape, BF16)] * 4, (*even, *odd), name="add_halves")


def add_last(even, odd):
    def kernel(a_ref, b_ref, c_ref, e_ref, own_ref, send_ref):
        first = (jnp.zeros(a_ref.shape, jnp.int32) + side_of(1)) == 0
        low, high = a_ref[...] + b_ref[...], c_ref[...] + e_ref[...]
        own_ref[...] = jnp.where(first, low, high)
        send_ref[...] = jnp.where(first, high, low)

    return call(kernel, [like(even[0].shape, BF16)] * 2, (*even, *odd), name="add_last")


def list_tokens(ids, vocab):
    count = ids.shape[1]
    unit = 1 << (vocab - 1).bit_length()

    def kernel(ids_ref, list_ref):
        start = lax.axis_index("shard") * vocab

        def step(i, many):
            local = ids_ref[0, i] - start
            list_ref[0, many] = i * unit + local
            return many + ((local >= 0) & (local < vocab)).astype(jnp.int32)

        list_ref[0, count] = lax.fori_loop(0, count, step, jnp.int32(0), unroll=8)

    smem = pl.BlockSpec(memory_space=pltpu.SMEM)
    return call(kernel, [like((1, count + 128), jnp.int32)], (ids,), specs=[smem], out_specs=[smem], name="list_tokens")[0]


def table_grad(dense, pieces, lists, vocab):
    width = pieces[0].shape[1]
    arrays = dense
    sources, _, seq = pieces[0].shape
    shards = 4
    listed = shards * seq
    line = lists.shape[1]
    unit = 1 << (vocab - 1).bit_length()
    ways, each = 4, 4
    rows = (lists & (unit - 1)).reshape(-1)
    tokens = ((lists >> (unit.bit_length() - 1)) + listed * jnp.arange(sources, dtype=jnp.int32)[:, None]).reshape(-1)
    counts = lists[:, listed]

    def kernel(*refs):
        d_refs, refs = refs[: len(arrays)], refs[len(arrays) :]
        own_ref, later_ref, before_ref, far_a_ref, far_b_ref, r_ref, t_ref, n_ref, o_ref, flat_ref, *acc = refs
        half = sources // 2
        for j in range(sources):
            far = far_a_ref[j] if j < half else far_b_ref[j - half]
            for k, block in enumerate((own_ref[j], later_ref[j], before_ref[j], far)):
                at = j * listed + k * seq
                flat_ref[at : at + seq] = block.astype(F32).T
        for ref in acc:
            ref[...] = jnp.zeros(ref.shape, F32)

        def source(j, carry):
            many = n_ref[j]
            rounds = many // (ways * each)

            def step(i, carry):
                at = j * line + i * ways * each
                place = [r_ref[at + n] for n in range(ways * each)]
                value = [flat_ref[pl.ds(t_ref[at + n], 1), :] for n in range(ways * each)]
                for n in range(each):
                    old = [ref[pl.ds(place[n * ways + way], 1), :] for way, ref in enumerate(acc)]
                    for way, ref in enumerate(acc):
                        ref[pl.ds(place[n * ways + way], 1), :] = old[way] + value[n * ways + way]
                return carry

            def rest(at, carry):
                acc[0][pl.ds(r_ref[j * line + at], 1), :] += flat_ref[pl.ds(t_ref[j * line + at], 1), :]
                return carry

            lax.fori_loop(0, rounds, step, jnp.int32(0))
            lax.fori_loop(rounds * ways * each, many, rest, jnp.int32(0))
            return carry

        lax.fori_loop(0, sources, source, jnp.int32(0))
        if len(d_refs) == 1:
            o_ref[...] = d_refs[0][...].astype(F32) + sum(ref[...] for ref in acc).T
            return
        half = d_refs[0].shape[1]
        first = (jnp.zeros((width, half), jnp.int32) + side_of(1)) == 0
        own, other = d_refs[0][...], d_refs[1][...]
        o_ref[:, :half] = jnp.where(first, own, other).astype(F32) + sum(ref[:half] for ref in acc).T
        last = jnp.where(first, other, own)[:, : vocab - half]
        o_ref[:, half:] = last.astype(F32) + sum(ref[half:] for ref in acc).T

    smem = pl.BlockSpec(memory_space=pltpu.SMEM)
    return call(
        kernel,
        [like((width, vocab), F32)],
        (*arrays, *pieces, rows, tokens, counts),
        specs=[None] * (len(arrays) + 5) + [smem] * 3,
        scratch=[pltpu.VMEM((sources * listed, width), F32)] + [pltpu.VMEM((vocab, width), F32)] * ways,
        limit=60,
        name="table_grad",
    )[0]


def unpack_grads(z, blocks):
    rows = z.part + z.extra
    pos_rows = z.pos + 4 * z.quarter

    def kernel(own_ref, y_ref, core_ref, both_ref, qkv_ref, out_ref, fin_ref, fout_ref, gain_ref, bias_ref, pos_ref, eg_ref, es_ref, all_ref):
        core, y = side_of(1), side_of(2)
        shard = lax.axis_index("shard")
        all_ref[core, y] = own_ref[...]
        all_ref[core, 1 - y] = y_ref[...]
        all_ref[1 - core, y] = core_ref[...]
        all_ref[1 - core, 1 - y] = both_ref[...]

        def own_lanes(value):
            total = jnp.zeros((value.shape[0], z.part), F32)
            for h in range(z.shards):
                total = total + jnp.where(shard == h, value[:, h * z.part : (h + 1) * z.part], 0.0)
            return total

        out_ref[...] = all_ref[0, 0, : z.part].astype(F32)
        fin_ref[...] = all_ref[0, 1, : z.part].astype(F32).reshape(z.groups, z.gi, z.d)
        for c in range(3):
            part = all_ref[1, 0, c * z.gi : (c + 1) * z.gi].astype(F32)
            for g in range(z.groups):
                qkv_ref[c, g] = part[:, g * z.gw : (g + 1) * z.gw]
        part = all_ref[1, 1, : z.part].astype(F32)
        for g in range(z.groups):
            fout_ref[g] = part[:, g * z.gw : (g + 1) * z.gw]
        small = own_lanes(all_ref[1, 0, z.at_small : z.at_small + 16].astype(F32))
        gain_ref[...] = small[0:2]
        bias_ref[...] = small[2:11]
        eg_ref[...] = small[11:12]
        es_ref[...] = small[12:13]
        pos_ref[: z.pos] = all_ref[1, 0, z.at_small + 16 : z.part].astype(F32)
        for n in range(4):
            row = z.pos + n * z.quarter
            pos_ref[row : row + z.quarter] = all_ref[n // 2, n % 2, z.part :].astype(F32)[: z.quarter]

    return call(
        kernel,
        [
            like((3, z.groups, z.gi, z.gw), F32),
            like((z.part, z.d), F32),
            like((z.groups, z.gi, z.d), F32),
            like((z.groups, z.part, z.gw), F32),
            like((2, z.part), F32),
            like((9, z.part), F32),
            like((pos_rows, z.d), F32),
            like((1, z.part), F32),
            like((1, z.part), F32),
        ],
        blocks,
        scratch=[pltpu.VMEM((2, 2, rows, z.d), BF16)],
        name="unpack",
    )


def body(token_ids, targets, segment_ids, word_table, pos_table, embed_gain, embed_shift, qkv_weight, out_weight, ffn_in, ffn_out, layer_gains, layer_biases):
    micro, _, seq = token_ids.shape
    vocab, d = word_table.shape
    pos_rows = pos_table.shape[0]
    shards = lax.axis_size("shard")
    dp = lax.axis_size("dp")
    both = ("section", "dp")
    section = lax.axis_index("section")
    first = section == 0
    z = Sizes(qkv_weight.shape, out_weight.shape, shards, pos_rows)
    offset = lax.axis_index("shard") * vocab

    mine = lax.dynamic_index_in_dim(jnp.stack([token_ids[:, 0], targets[:, 0], segment_ids[:, 0]], axis=1), section, 0, keepdims=False)
    ids_by = jnp.stack([mine, turned(mine, "shard", -1), turned(mine, "shard", 2), turned(mine, "shard", 1)])
    seg_row = mine[2:3]

    def rows_of(ids):
        return word_table.at[jnp.clip(ids.reshape(-1) - offset, 0, vocab - 1)].get(mode="promise_in_bounds")

    small = jnp.concatenate([layer_gains[0], layer_biases[0], embed_gain[None], embed_shift[None]], axis=0)
    local, pair, packed = pack_weights(z, qkv_weight[0], out_weight[0], ffn_in[0], ffn_out[0], small)
    cross_pair = crossed(pair, "section", 1)
    near = gather_first(packed, "shard")
    picked = rows_of(ids_by[:, 0])
    near, pos_table = after((near, pos_table), near)
    word_parts = embed_parts(picked, ids_by, pos_table, vocab)
    near = after(near, word_parts)
    near_rows = jnp.concatenate(near, axis=0)
    near_y = crossed(near_rows, "dp", 2)
    cross_near = crossed(near_rows, "section", 1)
    target_rows = rows_of(after(ids_by[:, 1], near_rows))
    c0, c1, c2a, c2b, c3 = word_parts
    half, quarter = seq // 2, z.part // 2
    right = turned(jnp.concatenate([c2a, near[0][:quarter]], axis=0), "shard", 1)
    left = turned(jnp.concatenate([c2b, near[1][quarter:]], axis=0), "shard", -1)
    right, left = after((right, left), target_rows)
    c1 = jnp.concatenate([c1[:half] + right[:half], c1[half:]], axis=0)
    c3 = jnp.concatenate([c3[:half], c3[half:] + left[:half]], axis=0)
    words = scatter_second(c0, c1, c3, "shard")
    near_y = after(near_y, words)
    far = jnp.concatenate([right[half:], left[half:]], axis=0)
    cross_far = crossed(far, "section", 1)
    both_y = crossed(jnp.concatenate([far, cross_near], axis=0), "dp", 2)
    far_y, cross_near_y = both_y[: z.part], both_y[z.part :]
    cross_far_y = crossed(cross_far, "dp", 2)
    mine = (near_rows, far)
    mine = (*mine, *(crossed(b, "dp", 1) for b in mine), near_y, far_y, crossed(near_y, "dp", 1), crossed(far_y, "dp", 1))
    others = (cross_near, cross_far)
    others = (*others, *(crossed(b, "dp", 1) for b in others))
    others = (*others, cross_near_y, cross_far_y, crossed(cross_near_y, "dp", 1), crossed(cross_far_y, "dp", 1))
    pairs = (cross_pair, crossed(cross_pair, "dp", 1))
    weights_one, weights_two = (Pieces(z, local, mine, pairs, others, layer) for layer in range(2))
    one = layer_forward(z, weights_one, seg_row, True, words=words)
    two = layer_forward(z, weights_two, seg_row, False, layer_in=one["out"])
    two["x"] = one["out"]

    own_out = jnp.where(first, one["out"], two["out"])
    came_out = crossed(jnp.where(first, two["out"], one["out"]), "section", 1)

    before, later = gather_first(two["out"], "shard")
    ctx_own, lse_own = head_forward([two["out"]], word_table)
    before = after(before, ctx_own)
    far_a = turned(before[: seq // 2], "shard", 1)
    ctx_before, lse_before = head_forward([before], word_table)
    later = after(later, ctx_before)
    far_b = turned(later[seq // 2 :], "shard", -1)
    ctx_later, lse_later = head_forward([later], word_table)
    far_a, far_b = after((far_a, far_b), ctx_later)
    ctx_far, lse_far = head_forward([far_a, far_b], word_table)
    lse = jnp.concatenate([lse_own[0:1], lse_later[0:1], lse_far[0:1], lse_before[0:1]], axis=1)
    listed = jnp.stack([ids_by[0, 0], ids_by[1, 0], ids_by[3, 0], ids_by[2, 0]]).reshape(1, -1)
    lses = (lse, turned(lse, "shard", -1), turned(lse, "shard", 2), turned(lse, "shard", 1))
    lses = after(lses, came_out)
    *parts, whole_lse = head_combine(seq, (ctx_own, ctx_later, ctx_far, ctx_before), target_rows, ids_by, lses, vocab)
    head_rows = [two["out"], later, far_a, far_b, before]
    dy_terms = direct_scatter(parts, "shard")
    if dp == 4:
        rows_other, ids_other, lse_other = [crossed(row, "dp", 1) for row in head_rows], crossed(ids_by, "dp", 1), crossed(whole_lse, "dp", 1)
        core = side_of(1).astype(jnp.int32).reshape(1)
        stay_x, leave_x, stay_y, leave_y = head_table([*head_rows, *rows_other], word_table, [whole_lse, lse_other], [ids_by, ids_other], core)
        came_x, came_y = crossed(leave_x, "section", 1), crossed(leave_y, "dp", 2)
        dy_terms = after(dy_terms, stay_x)
    else:
        dense = head_table(head_rows, word_table, [whole_lse], [ids_by])[0]
        dense = [lax.psum_scatter(dense, both, scatter_dimension=0, tiled=True)]
    d_middle, small_grads, keep_f, send_f = ffn_backward(z, weights_two, two, dy_terms)

    in_two, in_low, keep_a, send_a = attention_backward(z, weights_two, two, d_middle, small_grads, False)
    came_f, came_a = crossed(send_f, "dp", 1), crossed(send_a, "dp", 1)
    d_middle, small_grads, keep_one_f, send_one_f = ffn_backward(z, weights_one, one, [in_low])
    keep_f, came_f, keep_a, came_a = after((keep_f, came_f, keep_a, came_a), d_middle)
    split_two = add_cores_split(z, (keep_a, keep_f), (came_a, came_f))
    d_middle = after(d_middle, split_two)
    terms_two = scatter_first(*split_two, "shard")
    if dp == 4:
        d_middle, came_x, came_y = after((d_middle, came_x, came_y), ())
    came_one_f = crossed(send_one_f, "dp", 1)
    in_one, in_one_low, keep_one_a, send_one_a, d_embed = attention_backward(z, weights_one, one, d_middle, small_grads, True, seg_row, pos_rows)
    keep_one_f, came_one_f = after((keep_one_f, came_one_f), d_embed)
    send_one_a, d_embed = after((send_one_a, d_embed), terms_two)
    came_one_a = crossed(send_one_a, "dp", 1)
    columns = d_embed[None]
    steps = [("dp", 1 << n) for n in range(dp.bit_length() - 1)]
    for n, (axis, bit) in enumerate(steps):
        middle = columns.shape[1] // 2
        columns = jnp.concatenate([columns[:, :middle], crossed(columns[:, middle:], axis, bit)], axis=0)
        if n == 0:
            came_one_a = after(came_one_a, columns)
    second_two = scatter_second(*terms_two, "shard")
    stay_one, leave_one = add_core(z, keep_one_a, came_one_a, keep_one_f, came_one_f)
    came_one = crossed(after(leave_one, columns), "dp", 2)
    columns = after(columns, (stay_one, second_two))
    columns = jnp.concatenate([columns[:, 0], crossed(columns[:, 1], "section", 1)], axis=0)
    ring_columns = gather_first(columns, "shard")
    own_in = jnp.where(first, in_one, in_two)
    came_in = crossed(jnp.where(first, in_two, in_one).astype(BF16), "section", 1)
    stay_two, leave_two = halves_by_y(z, after(second_two, (columns, stay_one)))
    came_two = crossed(leave_two, "dp", 2)
    if dp == 4:
        stay_x, leave_x, stay_y, leave_y = add_halves(*after(((stay_x, came_x), (stay_y, came_y)), stay_two))
        last_x, last_y = crossed(leave_x, "dp", 2), crossed(leave_y, "section", 1)
    lists = list_tokens(after(listed, columns), vocab)
    bit = 1
    while bit < dp:
        lists = jnp.concatenate([lists, crossed(lists, "dp", bit)], axis=0)
        bit *= 2
    lists = jnp.concatenate([lists, crossed(lists, "section", 1)], axis=0)
    ring_columns = after(ring_columns, stay_two)
    far_columns = gather_second(*ring_columns, "shard")
    terms_one = scatter_first(*add_split(stay_one, after(came_one, (ring_columns, came_in))), "shard")
    second_one = scatter_second(*terms_one, "shard")
    if dp == 4:
        own_dense, send_dense = add_last(*after(((stay_x, last_x), (stay_y, last_y)), second_one))
        dense = [own_dense, crossed(send_dense, "dp", 1)]
    word_grad = table_grad(dense, (columns, ring_columns[1], ring_columns[0], *far_columns), lists, vocab)
    sum_two = stay_two + came_two
    sum_one = sum(after(second_one, sum_two))
    layer_one, extra = sum_one[: z.part], sum_one[z.part :]
    row = jnp.arange(z.part)[:, None]
    embed_rows = (row >= z.at_small + 11) & (side_of(1) == 1) & (side_of(2) == 0)
    layer_two = jnp.where(embed_rows, layer_one, sum_two)
    total = jnp.concatenate([jnp.where(first, layer_one, layer_two), extra], axis=0)
    came = crossed(jnp.concatenate([jnp.where(first, layer_two, layer_one), extra], axis=0), "section", 1)
    total = total + after(came, word_grad)
    bit = 4
    while bit < dp:
        total = total + crossed(total, "dp", bit)
        bit *= 2
    total_y = crossed(total, "dp", 2)
    unpacked = unpack_grads(z, (total, total_y, crossed(total, "dp", 1), crossed(total_y, "dp", 1)))

    word_grad = word_grad.T

    def by_micro(own, came):
        return jnp.stack([jnp.where(first, own, came), jnp.where(first, came, own)]).reshape(1, micro, 1, seq, d)

    layer_outputs = by_micro(own_out, came_out)
    input_grads = by_micro(own_in, came_in.astype(F32))
    qkv_g, out_g, fin_g, fout_g, gain_g, bias_g, pos_g, eg_g, es_g = unpacked
    return (
        layer_outputs,
        input_grads,
        word_grad,
        pos_g,
        eg_g.reshape(-1),
        es_g.reshape(-1),
        qkv_g[None],
        out_g[None],
        fin_g[None],
        fout_g[None],
        gain_g[None],
        bias_g[None],
    )


def solution(mesh):
    rows = P(None, ("dp", "shard"), None)
    weights = (
        P("section", None, None, "shard", None),
        P("section", "shard", None),
        P("section", None, "shard", None),
        P("section", None, "shard", None),
        P("section", None, "shard"),
        P("section", None, "shard"),
    )
    states = P("section", None, ("dp", "shard"), None, None)
    return jax.shard_map(
        body,
        mesh=mesh,
        in_specs=(rows, rows, rows, P("shard", None), P("shard", None), P("shard"), P("shard"), *weights),
        out_specs=(states, states, P("shard", ("section", "dp")), P("shard", None), P("shard"), P("shard"), *weights),
        check_vma=False,
    )
```

```python
import math

import jax
import jax.numpy as jnp
from jax import lax
from jax.experimental import pallas as pl
from jax.experimental.pallas import tpu as pltpu
from jax.sharding import PartitionSpec as P

HEADS = 12
EPSILON = 1e-06
MASKED = -1000000000.0
F32 = jnp.float32
BF16 = jnp.bfloat16
MIB = 1 << 20


def nn(a, b):
    return jnp.dot(a, b, preferred_element_type=F32)


def nt(a, b):
    return lax.dot_general(a, b, (((1,), (1,)), ((), ())), preferred_element_type=F32)


def tn(a, b):
    return lax.dot_general(a, b, (((0,), (0,)), ((), ())), preferred_element_type=F32)


def iota(shape, axis):
    return lax.broadcasted_iota(jnp.int32, shape, axis)


def group_of(index, width, count):
    total = jnp.zeros(index.shape, jnp.int32)
    for step in range(1, count):
        total = total + (index >= step * width).astype(jnp.int32)
    return total


def normed(value):
    centered = value - jnp.mean(value, axis=-1, keepdims=True)
    scale = lax.rsqrt(jnp.mean(centered * centered, axis=-1, keepdims=True) + EPSILON)
    return centered * scale, scale


def norm_back(grad, unit, scale, gain):
    inner = grad * gain
    first = jnp.mean(inner, axis=-1, keepdims=True)
    second = jnp.mean(inner * unit, axis=-1, keepdims=True)
    return scale * (inner - first - unit * second)


def col_sum(value):
    return jnp.sum(value, axis=0, keepdims=True)


def upright(row, count):
    return jnp.broadcast_to(row.astype(F32), (128, count)).T[:, 0:1]


def call(kernel, outs, ins, specs=None, scratch=(), limit=56, flops=0, moved=0, grid=None, out_specs=None, name=None):
    vmem = pl.BlockSpec(memory_space=pltpu.VMEM)
    extra = {} if grid is None else {"grid": grid}
    return pl.pallas_call(
        kernel,
        out_shape=outs,
        in_specs=[vmem if s is None else s for s in (specs or [None] * len(ins))],
        out_specs=out_specs if out_specs is not None else [vmem] * len(outs),
        scratch_shapes=list(scratch),
        compiler_params=pltpu.CompilerParams(vmem_limit_bytes=limit * MIB),
        cost_estimate=pl.CostEstimate(flops=flops, bytes_accessed=0, transcendentals=0),
        name=name,
        **extra,
    )(*ins)


def like(shape, dtype):
    return jax.ShapeDtypeStruct(shape, dtype)


def turned(block, axis, by):
    size = lax.axis_size(axis)
    return lax.ppermute(block, axis, [(i, (i + by) % size) for i in range(size)])


def crossed(block, axis, bit):
    return lax.ppermute(block, axis, [(i, i ^ bit) for i in range(lax.axis_size(axis))])


def after(value, first):
    return lax.optimization_barrier((value, first))[0]


def scatter_first(c0, c1, c2a, c2b, c3, axis, wait=()):
    half = c2a.shape[0]
    right, left = after((turned(c2a, axis, 1), turned(c2b, axis, -1)), wait)
    return c0, jnp.concatenate([c1[:half] + right, c1[half:]], axis=0), jnp.concatenate([c3[:half], c3[half:] + left], axis=0)


def scatter_second(c0, c1, c3, axis):
    return c0, turned(c1, axis, 1), turned(c3, axis, -1)


def side_of(bit):
    return (lax.axis_index("dp") // bit) % 2


def direct_scatter(parts, axis):
    return parts[0], turned(parts[1], axis, 1), turned(parts[3], axis, -1), turned(parts[2], axis, 2)


def gather_first(block, axis):
    return turned(block, axis, 1), turned(block, axis, -1)


def gather_second(before, later, axis):
    half = before.shape[0] // 2
    return turned(before[:half], axis, 1), turned(later[half:], axis, -1)


def ring_gather(block, axis):
    first = gather_first(block, axis)
    return (*first, *gather_second(*first, axis))


class Sizes:
    def __init__(self, qkv, out, shards, pos_rows):
        _, _, groups, part, width = qkv
        self.shards, self.groups, self.gw, self.gi = shards, groups, width, part
        self.d = out[2]
        self.part = out[1]
        self.at_small = 3 * part
        self.rows = 2 * self.part
        self.pos = self.part - self.at_small - 16
        self.quarter = (pos_rows - self.pos) // 4
        self.extra = -(-self.quarter // 16) * 16


def pack_weights(z, qkv, out, fin, fout, gains, biases, egain, eshift):
    def kernel(qkv_ref, out_ref, fin_ref, fout_ref, gain_ref, bias_ref, eg_ref, es_ref, o_ref, pair_ref, own_ref):
        shard = lax.axis_index("shard")

        def spread(pieces):
            return jnp.concatenate([piece.astype(F32) for piece in pieces], axis=1).astype(BF16)

        o_ref[0, 0] = out_ref[...]
        o_ref[0, 1] = fin_ref[...].reshape(z.part, z.d)
        for c in range(3):
            o_ref[1, 0, c * z.gi : (c + 1) * z.gi] = spread([qkv_ref[c, g] for g in range(z.groups)])
        embed = [ref[...].astype(F32).reshape(1, z.part) for ref in (eg_ref, es_ref)]
        tall = jnp.concatenate([gain_ref[...].astype(F32), bias_ref[...].astype(F32), *embed, jnp.zeros((3, z.part), F32)], axis=0)
        wide = jnp.concatenate([tall] * z.shards, axis=1)
        lane = group_of(iota(wide.shape, 1), z.part, z.shards)
        o_ref[1, 0, z.at_small : z.at_small + 16] = jnp.where(lane == shard, wide, 0.0).astype(BF16)
        o_ref[1, 0, z.at_small + 16 : z.part] = jnp.zeros((z.part - z.at_small - 16, z.d), BF16)
        o_ref[1, 1] = spread([fout_ref[g] for g in range(z.groups)])
        pair_ref[...] = o_ref[side_of(1)]
        own_ref[...] = o_ref[side_of(1), side_of(2)]

    outs = [like((2, 2, z.part, z.d), BF16), like((2, z.part, z.d), BF16), like((z.part, z.d), BF16)]
    return call(kernel, outs, (qkv, out, fin, fout, gains, biases, egain, eshift), name="pack")


class Pieces:
    def __init__(self, z, local, mine, pairs, others, layer):
        self.z, self.layer = z, layer
        self.arrays = (local, *mine, *pairs, *others)
        self.specs = [pl.BlockSpec(memory_space=pl.ANY)] * len(self.arrays)
        self.scratch = [pltpu.VMEM((2, z.shards, z.rows, z.d), BF16), pltpu.SemaphoreType.DMA((2, 2, 4))]

    def start(self, refs, w_ref, sems, parts):
        z = self.z
        core, y = side_of(1), side_of(2)
        shard = lax.axis_index("shard")
        own_layer = lax.axis_index("section") == self.layer
        local, mine, pairs, others = refs[0], refs[1:9], refs[9:11], refs[11:19]
        waits = {}
        for part in parts:
            copies = []
            for side in range(2):
                place = core if side == 0 else 1 - core
                for n, by in enumerate((0, 3, 1, 2)):
                    target = w_ref.at[place, (shard + by) % z.shards, pl.ds(part * z.part, z.part)]
                    sem = sems.at[part, side, n]
                    rows = pl.ds((n - 1) * z.part, z.part)
                    choices = []
                    for across in range(2):
                        here = (y == part) if across == 0 else (y != part)
                        at = 2 * across + side
                        if n == 0:
                            own, other = local.at[place, part], pairs[side].at[part]
                        elif n < 3:
                            own, other = mine[2 * at].at[rows], others[2 * at].at[rows]
                        else:
                            own, other = mine[2 * at + 1], others[2 * at + 1]
                        choices.append((jnp.logical_and(here, own_layer), own))
                        choices.append((jnp.logical_and(here, jnp.logical_not(own_layer)), other))
                    for here, source in choices:
                        copy = pltpu.make_async_copy(source, target, sem)
                        pl.when(here)(copy.start)
                    copies.append(pltpu.make_async_copy(choices[1][1], target, sem))
            waits[part] = copies
        return waits


def wait_all(copies):
    for copy in copies:
        copy.wait()


class Loads:
    def __init__(self, arrays):
        self.names = list(arrays)
        self.arrays = list(arrays.values())
        self.specs = [pl.BlockSpec(memory_space=pl.ANY)] * len(self.arrays)
        self.scratch = [pltpu.VMEM(a.shape, a.dtype) for a in self.arrays] + [pltpu.SemaphoreType.DMA((len(self.arrays),))]

    def start(self, refs, scratch):
        self.buffers = dict(zip(self.names, scratch))
        self.copies = {
            name: pltpu.make_async_copy(ref, buffer, scratch[-1].at[n])
            for n, (name, ref, buffer) in enumerate(zip(self.names, refs, scratch))
        }
        for copy in self.copies.values():
            copy.start()

    def __getitem__(self, name):
        copy = self.copies.pop(name, None)
        if copy is not None:
            copy.wait()
        return self.buffers[name]


class Stores:
    def __init__(self, shapes, split=()):
        self.names = list(shapes)
        self.shapes = list(shapes.values())
        self.split = split
        self.specs = [pl.BlockSpec(memory_space=pl.ANY)] * len(self.shapes)
        count = sum(a.shape[0] if name in split else 1 for name, a in shapes.items())
        self.scratch = [pltpu.VMEM(a.shape, a.dtype) for a in self.shapes] + [pltpu.SemaphoreType.DMA((count,))]

    def bind(self, refs, scratch):
        self.refs = dict(zip(self.names, refs))
        self.buffers = dict(zip(self.names, scratch))
        self.sems = scratch[-1]
        self.copies = []

    def put(self, name, value, index=None):
        source = self.buffers[name] if index is None else self.buffers[name].at[index]
        source[...] = value.astype(source.dtype)
        self.send(name, index)

    def send(self, name, index=None):
        source, target = self.buffers[name], self.refs[name]
        if index is not None:
            source, target = source.at[index], target.at[index]
        copy = pltpu.make_async_copy(source, target, self.sems.at[len(self.copies)])
        copy.start()
        self.copies.append(copy)

    def finish(self):
        wait_all(self.copies)


class Weights:
    def __init__(self, z, w_ref):
        self.z, self.w = z, w_ref

    def out(self):
        z = self.z
        return self.w[0, :, 0 : z.part, :].reshape(z.d, z.d)

    def small(self):
        z = self.z
        return sum(self.w[1, h, z.at_small : z.at_small + 16, :].astype(F32) for h in range(z.shards))

    def proj(self, c, p):
        z = self.z
        lanes = slice(2 * p * z.gw, 2 * (p + 1) * z.gw)
        dense = self.w[1, :, c * z.gi : (c + 1) * z.gi, lanes].reshape(z.gw, 2 * z.gw)
        high = iota(dense.shape, 1) >= z.gw
        blank = jnp.zeros_like(dense)
        return jnp.concatenate([jnp.where(high, blank, dense), jnp.where(high, dense, blank)], axis=0)

    def project(self, value, c):
        z = self.z
        wide = 2 * z.gw
        return jnp.concatenate([nn(value[:, p * wide : (p + 1) * wide], self.proj(c, p)) for p in range(z.groups // 2)], axis=1)

    def fin(self, g):
        z = self.z
        row = z.part + g * z.gi
        dense = self.w[0, :, row : row + z.gi, :].reshape(z.gw, z.d)
        blank = jnp.zeros_like(dense)
        return jnp.concatenate([dense, blank] if g % 2 == 0 else [blank, dense], axis=0)

    def fout(self, g):
        z = self.z
        at = (g // 2) * 2 * z.gw
        pair = self.w[1, :, z.part : z.rows, at : at + 2 * z.gw].reshape(z.d, 2 * z.gw)
        keep = (iota(pair.shape, 1) >= z.gw) == (g % 2 == 1)
        return jnp.where(keep, pair, jnp.zeros_like(pair))


def embed_parts(picked, ids_by, pos_table, vocab):
    count, _, seq = ids_by.shape
    width = picked.shape[1]
    half = seq // 2
    rows = pos_table.shape[0]

    def kernel(p_ref, i_ref, t_ref, c0, c1, c2a, c2b, c3):
        shard = lax.axis_index("shard")
        for k in range(count):
            span = slice(k * seq, (k + 1) * seq)
            token, seg_row = i_ref[k, 0:1], i_ref[k, 2:3]
            seg_col = upright(seg_row, seq)
            same = seg_col == seg_row.astype(F32)
            earlier = iota((seq, seq), 1) < iota((seq, seq), 0)
            place = jnp.sum(jnp.where(same & earlier, 1.0, 0.0), axis=1, keepdims=True).astype(jnp.int32) - shard * rows
            spot = (iota((seq, rows), 1) == place).astype(BF16)
            local = token - shard * vocab
            inside = upright(jnp.where((local >= 0) & (local < vocab), 1.0, 0.0), seq)
            word = jnp.where(inside > 0.5, p_ref[span].astype(F32), 0.0)
            total = (word + nn(spot, t_ref[...])).astype(BF16)
            if k == 2:
                c2a[...] = total[:half]
                c2b[...] = total[half:]
            else:
                (c0, c1, None, c3)[k][...] = total

    full, part = like((seq, width), BF16), like((half, width), BF16)
    return call(kernel, [full, full, part, part, full], (picked, ids_by, pos_table), limit=24, name="embed_parts")


def layer_forward(z, pieces, seg_row, first, words=None, layer_in=None):
    seq = seg_row.shape[1]
    d = z.d
    flat = like((seq, d), BF16)
    shapes = {"q": flat, "k": flat, "v": flat, "p": like((HEADS, seq, seq), BF16), "att": flat, "n1": flat, "mid": flat}
    shapes.update({"act": like((z.groups, seq, d), BF16), "slope": like((z.groups, seq, d), BF16)})
    shapes.update({"n2": flat, "stats": like((seq, 128), F32), "small": like((16, d), F32), "out": flat})
    if first:
        shapes.update({"x": flat, "n0": flat})
    stores = Stores(shapes, split=("p", "act", "slope"))
    head = d // HEADS
    inputs = list(words) if first else [layer_in]

    def kernel(*refs):
        piece_refs, refs = refs[: len(pieces.arrays)], refs[len(pieces.arrays) :]
        row_ref, refs = refs[0], refs[1:]
        in_refs, refs = refs[: len(inputs)], refs[len(inputs) :]
        out_refs, refs = refs[: len(shapes)], refs[len(shapes) :]
        w_ref, sems, *buffers = refs
        waits = pieces.start(piece_refs, w_ref, sems, (0, 1))
        stores.bind(out_refs, buffers)
        put = stores.put
        w = Weights(z, w_ref)
        if first:
            unit, r0 = normed(sum(ref[...].astype(F32) for ref in in_refs))
            put("n0", unit)
        wait_all(waits[0])
        small = w.small()
        put("small", small)
        if first:
            x = unit * small[11:12] + small[12:13]
            x_low = x.astype(BF16)
            put("x", x_low)
        else:
            r0 = jnp.zeros((seq, 1), F32)
            x_low = in_refs[0][...]
            x = x_low.astype(F32)
        q = (w.project(x_low, 0).astype(BF16).astype(F32) * (1.0 / math.sqrt(head))).astype(BF16)
        k = w.project(x_low, 1).astype(BF16)
        v = (w.project(x_low, 2) + small[2:3]).astype(BF16)
        put("q", q)
        put("k", k)
        put("v", v)
        same = upright(row_ref[...], seq) == row_ref[...].astype(F32)
        second = iota((seq, 128), 1) >= head
        units = [(t, j) for t in range(d // 128) for j in range(2)]

        def scores_of(unit):
            t, j = unit
            lanes = slice(t * 128, (t + 1) * 128)
            picked = jnp.where(second == (j == 1), q[:, lanes], jnp.zeros((seq, 128), BF16))
            return nt(picked, k[:, lanes])

        tiles = []
        raw = scores_of(units[0])
        for n, (t, j) in enumerate(units):
            following = scores_of(units[n + 1]) if n + 1 < len(units) else None
            scores = jnp.where(same, raw, MASKED)
            scores = jnp.exp(scores - jnp.max(scores, axis=-1, keepdims=True))
            probs = (scores * (1.0 / jnp.sum(scores, axis=-1, keepdims=True))).astype(BF16)
            put("p", probs, n)
            result = nn(probs, v[:, t * 128 : (t + 1) * 128])
            if j == 0:
                kept = result
            else:
                tiles.append(jnp.where(second, result, kept).astype(BF16))
            raw = following
        attended = jnp.concatenate(tiles, axis=1)
        put("att", attended)
        unit, r1 = normed(x + (nn(attended, w.out()) + small[3:4]))
        put("n1", unit)
        middle = unit * small[0:1] + small[4:5]
        middle_low = middle.astype(BF16)
        put("mid", middle_low)
        wait_all(waits[1])
        back = [None] * (z.groups // 2)

        def pre_of(g):
            pair = slice((g // 2) * 2 * z.gw, (g // 2 + 1) * 2 * z.gw)
            return nn(middle_low[:, pair], w.fin(g))

        raw = pre_of(0)
        for g in range(z.groups):
            following = pre_of(g + 1) if g + 1 < z.groups else None
            pre = raw + small[5 + g : 6 + g]
            half = 0.5 + 0.5 * lax.erf(pre * math.sqrt(0.5))
            slope = half + pre * (jnp.exp(-0.5 * pre * pre) * (1.0 / math.sqrt(2.0 * math.pi)))
            active = (pre * half).astype(BF16)
            put("act", active, g)
            put("slope", slope, g)
            added = nn(active, w.fout(g))
            back[g // 2] = added if back[g // 2] is None else back[g // 2] + added
            raw = following
        unit, r2 = normed(middle + (jnp.concatenate(back, axis=1) + small[9:10]))
        put("n2", unit)
        put("out", unit * small[1:2] + small[10:11])
        lane = iota((seq, 128), 1)
        put("stats", jnp.where(lane == 0, r0, jnp.where(lane == 1, r1, r2)))
        stores.finish()

    outs = call(
        kernel,
        stores.shapes,
        (*pieces.arrays, seg_row, *inputs),
        specs=pieces.specs + [None] * (1 + len(inputs)),
        out_specs=stores.specs,
        scratch=pieces.scratch + stores.scratch,
        flops=12 * 10**9,
        name="layer_first" if first else "layer_second",
    )
    return dict(zip(stores.names, outs))


def send_halves(z, g_ref, keep_ref, send_ref, sems):
    core = lax.axis_index("dp") % 2
    shard = lax.axis_index("shard")
    copies = []
    for k in range(z.shards):
        to = (shard + k) % z.shards
        copies.append(pltpu.make_async_copy(g_ref.at[1 - core, to], send_ref.at[k], sems.at[2 * k]))
        copies.append(pltpu.make_async_copy(g_ref.at[core, to], keep_ref.at[k], sems.at[2 * k + 1]))
    for copy in copies:
        copy.start()
    return copies


def ffn_backward(z, pieces, state, out_grad):
    seq, d = out_grad[0].shape
    loads = Loads({**{f"dy{n}": term for n, term in enumerate(out_grad)}, **{key: state[key] for key in ("n2", "stats", "small", "mid", "act", "slope")}})
    outs = [like((seq, d), F32), like((16, d), F32)] + [like((z.shards, z.part, d), BF16)] * 2

    def kernel(*refs):
        piece_refs, refs = refs[: len(pieces.arrays)], refs[len(pieces.arrays) :]
        load_refs, refs = refs[: len(loads.names)], refs[len(loads.names) :]
        dm_ref, small_ref, keep_ref, send_ref, w_ref, sems, g_ref, out_sems, *buffers = refs
        loads.start(load_refs, buffers)
        waits = pieces.start(piece_refs, w_ref, sems, (1,))
        w = Weights(z, w_ref)
        dy = sum(loads[f"dy{n}"][...].astype(F32) for n in range(len(out_grad)))
        n2 = loads["n2"][...].astype(F32)
        scale = loads["stats"][:, 2:3]
        small = loads["small"][...]
        gain_two, shift_two = col_sum(dy * n2), col_sum(dy)
        d_final = norm_back(dy, n2, scale, small[1:2])
        d_ffn = d_final.astype(BF16)
        ffn_shift = col_sum(d_ffn.astype(F32))
        middle_t = loads["mid"][...].T
        act, slope = loads["act"], loads["slope"]
        wait_all(waits[1])
        pre_shift = []
        pair_back = [None] * (z.groups // 2)
        wide = 2 * z.gw

        def act_grad(g):
            p = g // 2
            return nt(d_ffn[:, p * wide : (p + 1) * wide], w.fout(g))

        raw = act_grad(0)
        for p in range(z.groups // 2):
            lanes = slice(p * wide, (p + 1) * wide)
            out_pair = d_ffn[:, lanes]
            back_pair = []
            for g in (2 * p, 2 * p + 1):
                following = act_grad(g + 1) if g + 1 < z.groups else None
                d_pre = (raw * slope[g].astype(F32)).astype(BF16)
                pre_shift.append(col_sum(d_pre.astype(F32)))
                back_pair.append(tn(act[g], out_pair))
                grad_in = nn(middle_t[g * z.gw : (g + 1) * z.gw], d_pre)
                g_ref[0, :, g * z.gi : (g + 1) * z.gi, :] = grad_in.astype(BF16).reshape(z.shards, z.gi, d)
                added = nt(d_pre, w.fin(g))
                pair_back[p] = added if pair_back[p] is None else pair_back[p] + added
                raw = following
            odd = iota(back_pair[0].shape, 1) >= z.gw
            both = jnp.where(odd, back_pair[1], back_pair[0]).astype(BF16)
            g_ref[1, :, :, lanes] = both.reshape(z.shards, z.part, wide)
        copies = send_halves(z, g_ref, keep_ref, send_ref, out_sems)
        dm_ref[...] = d_final + jnp.concatenate(pair_back, axis=1)
        blank = jnp.zeros((1, d), F32)
        small_ref[...] = jnp.concatenate(
            [blank, gain_two, blank, blank, blank, *pre_shift, ffn_shift, shift_two, jnp.zeros((5, d), F32)], axis=0
        )
        wait_all(copies)

    anywhere = pl.BlockSpec(memory_space=pl.ANY)
    return call(
        kernel,
        outs,
        (*pieces.arrays, *loads.arrays),
        specs=pieces.specs + loads.specs,
        out_specs=[pl.BlockSpec(memory_space=pltpu.VMEM)] * 2 + [anywhere] * 2,
        scratch=pieces.scratch + [pltpu.VMEM((2, z.shards, z.part, d), BF16), pltpu.SemaphoreType.DMA((2 * z.shards,))] + loads.scratch,
        flops=9 * 10**9,
        name="ffn_back",
    )


def attention_backward(z, pieces, state, d_middle, small_in, first, seg_row=None, pos_rows=0):
    seq, d = d_middle.shape
    head = d // HEADS
    keys = ["n1", "stats", "small", "att", "q", "k", "v", "p", "x"] + (["n0"] if first else [])
    loads = Loads({"dm": d_middle, **{key: state[key] for key in keys}, "grads": small_in, **({"seg": seg_row} if first else {})})
    rows = z.part + (2 * z.extra if first else 0)
    outs = [like((seq, d), F32), like((seq, d), BF16)] + [like((z.shards, rows, d), BF16)] * 2
    blocks = 2 * lax.axis_size("dp")
    if first:
        outs.append(like((blocks, d // blocks, seq), BF16))

    def kernel(*refs):
        piece_refs, refs = refs[: len(pieces.arrays)], refs[len(pieces.arrays) :]
        load_refs, refs = refs[: len(loads.names)], refs[len(loads.names) :]
        dx_ref, low_ref, keep_ref, send_ref = refs[:4]
        de_ref = refs[4] if first else None
        w_ref, sems, g_ref, out_sems, *buffers = refs[len(outs) :]
        loads.start(load_refs, buffers)
        waits = pieces.start(piece_refs, w_ref, sems, (0,))
        w = Weights(z, w_ref)
        d_middle = loads["dm"][...]
        n1 = loads["n1"][...].astype(F32)
        stats = loads["stats"][...]
        r0, r1 = stats[:, 0:1], stats[:, 1:2]
        small = loads["small"][...]
        gain_one, shift_one = col_sum(d_middle * n1), col_sum(d_middle)
        d_mid = norm_back(d_middle, n1, r1, small[0:1])
        d_branch = d_mid.astype(BF16)
        branch_shift = col_sum(d_branch.astype(F32))
        g_ref[0, :, 0 : z.part, :] = tn(loads["att"][...], d_branch).astype(BF16).reshape(z.shards, z.part, d)
        wait_all(waits[0])
        d_att = nt(d_branch, w.out()).astype(BF16)
        second = iota((seq, 128), 1) >= head
        scale = 1.0 / math.sqrt(head)
        q_ref, k_ref, v_ref, p_ref = (loads[key] for key in ("q", "k", "v", "p"))
        units = [(t, j) for t in range(d // 128) for j in range(2)]

        def probs_grad(unit):
            t, j = unit
            lanes = slice(t * 128, (t + 1) * 128)
            a_j = jnp.where(second == (j == 1), d_att[:, lanes], jnp.zeros((seq, 128), BF16))
            return nt(a_j, v_ref[:, lanes])

        dq, dk, dv = [], [], []
        raw = probs_grad(units[0])
        for n, (t, j) in enumerate(units):
            following = probs_grad(units[n + 1]) if n + 1 < len(units) else None
            lanes = slice(t * 128, (t + 1) * 128)
            probs_low = p_ref[n]
            probs = probs_low.astype(F32)
            inner = jnp.sum(probs * raw, axis=-1, keepdims=True)
            d_scores = (probs * (raw - inner)).astype(BF16)
            result = (nn(d_scores, k_ref[:, lanes]), tn(d_scores, q_ref[:, lanes]), tn(probs_low, d_att[:, lanes]))
            if j == 0:
                kept = result
            else:
                dq.append((jnp.where(second, result[0], kept[0]) * scale).astype(BF16))
                dk.append(jnp.where(second, result[1], kept[1]).astype(BF16))
                dv.append(jnp.where(second, result[2], kept[2]).astype(BF16))
            raw = following
        value_shift = col_sum(jnp.concatenate(dv, axis=1).astype(F32))
        x_t = loads["x"][...].T
        d_in = [d_mid[:, : 2 * z.gw], d_mid[:, 2 * z.gw :]]
        high = iota((z.gw, 2 * z.gw), 1) >= z.gw
        for c, parts in enumerate((dq, dk, dv)):
            d_c = jnp.concatenate(parts, axis=1)
            for p in range(z.groups // 2):
                lanes = slice(2 * p * z.gw, 2 * (p + 1) * z.gw)
                full = nn(x_t[lanes], d_c[:, lanes])
                grad = jnp.where(high, full[z.gw :], full[: z.gw]).astype(BF16)
                g_ref[1, :, c * z.gi : (c + 1) * z.gi, lanes] = grad.reshape(z.shards, z.gi, 2 * z.gw)
                d_in[p] = d_in[p] + nt(d_c[:, lanes], w.proj(c, p))
        d_in = jnp.concatenate(d_in, axis=1)
        blank = jnp.zeros((1, d), F32)
        embed_grads = [blank, blank]
        if first:
            n0 = loads["n0"][...].astype(F32)
            embed_grads = [col_sum(d_in * n0), col_sum(d_in)]
            d_embed = norm_back(d_in, n0, r0, small[11:12])
            d_embed_t = d_embed.T
            bits = blocks.bit_length() - 1
            me = lax.axis_index("section") * (blocks // 2) + lax.axis_index("dp")
            for b in range(blocks):
                to = me ^ b
                place = sum(((to >> bit) & 1) << (bits - 1 - bit) for bit in range(bits))
                de_ref[place] = d_embed_t[b * (d // blocks) : (b + 1) * (d // blocks)].astype(BF16)
            seg = loads["seg"][...]
            same = upright(seg, seq) == seg.astype(F32)
            later = iota((seq, seq), 0) < iota((seq, seq), 1)
            place = jnp.sum(jnp.where(same & later, 1.0, 0.0), axis=0, keepdims=True).astype(jnp.int32)
            spot = (iota((pos_rows, seq), 0) == place).astype(BF16)
            pos_grad = nn(spot, d_embed.astype(BF16)).astype(BF16)
        small_grads = jnp.concatenate([gain_one, blank, value_shift, branch_shift, shift_one, jnp.zeros((6, d), F32), *embed_grads, jnp.zeros((3, d), F32)], axis=0)
        small_grads = (small_grads + loads["grads"][...]).astype(BF16)
        if first:
            blank = jnp.zeros((z.extra - z.quarter, d), BF16)
            others = [pos_grad[z.pos + n * z.quarter : z.pos + (n + 1) * z.quarter] for n in range(4)]
        for h in range(z.shards):
            g_ref[1, h, z.at_small : z.at_small + 16, :] = small_grads
            spare = pos_grad[: z.pos] if first and h == 0 else jnp.zeros((z.pos, d), BF16)
            g_ref[1, h, z.at_small + 16 : z.part, :] = spare
            if first:
                for side in range(2):
                    for y in range(2):
                        row = z.part + y * z.extra
                        part = jnp.concatenate([others[2 * side + y].astype(F32), blank.astype(F32)], axis=0).astype(BF16) if h == 0 else jnp.zeros((z.extra, d), BF16)
                        g_ref[side, h, row : row + z.extra, :] = part
        copies = send_halves(z, g_ref, keep_ref, send_ref, out_sems)
        dx_ref[...] = d_in
        low_ref[...] = d_in.astype(BF16)
        wait_all(copies)

    anywhere = pl.BlockSpec(memory_space=pl.ANY)
    vmem = pl.BlockSpec(memory_space=pltpu.VMEM)
    return call(
        kernel,
        outs,
        (*pieces.arrays, *loads.arrays),
        specs=pieces.specs + loads.specs,
        out_specs=[vmem, vmem, anywhere, anywhere] + [vmem] * (len(outs) - 4),
        scratch=pieces.scratch + [pltpu.VMEM((2, z.shards, rows, d), BF16), pltpu.SemaphoreType.DMA((2 * z.shards,))] + loads.scratch,
        flops=13 * 10**9,
        name="att_back",
    )


def add_cores_split(z, keep, came):
    shards, part, d = keep[0].shape

    def kernel(a_ref, f_ref, b_ref, e_ref, c0, c1, c2a, c2b, c3):
        for k, ref in ((0, c0), (1, c1), (3, c3)):
            ref[:part] = a_ref[k] + b_ref[k]
            ref[part:] = f_ref[k] + e_ref[k]
        c2a[...] = a_ref[2] + b_ref[2]
        c2b[...] = f_ref[2] + e_ref[2]

    full, half = like((2 * part, d), BF16), like((part, d), BF16)
    return call(kernel, [full, full, half, half, full], (*keep, *came), limit=24, name="add_cores_split")


def halves_by_y(z, terms):
    def kernel(a_ref, b_ref, c_ref, keep_ref, send_ref):
        y = side_of(2)
        for ref, part in ((keep_ref, y), (send_ref, 1 - y)):
            span = pl.ds(pl.multiple_of(part * z.part, z.part), z.part)
            ref[...] = (a_ref[span].astype(F32) + b_ref[span].astype(F32) + c_ref[span].astype(F32)).astype(BF16)

    return call(kernel, [like((z.part, z.d), BF16)] * 2, terms, limit=8, name="halves_by_y")


def add_core(z, keep_a, came_a, keep_f, came_f):
    rows = z.part + z.extra

    def kernel(a_ref, b_ref, c_ref, e_ref, keep_ref, send_ref):
        y = side_of(2)

        def place(ref, part):
            if part == 0:
                ref[:, : z.part] = a_ref[:, : z.part] + b_ref[:, : z.part]
            else:
                ref[:, : z.part] = c_ref[...] + e_ref[...]
            span = slice(z.part + part * z.extra, z.part + (part + 1) * z.extra)
            ref[:, z.part :] = a_ref[:, span] + b_ref[:, span]

        @pl.when(y == 0)
        def _():
            place(keep_ref, 0)
            place(send_ref, 1)

        @pl.when(y == 1)
        def _():
            place(keep_ref, 1)
            place(send_ref, 0)

    return call(kernel, [like((z.shards, rows, z.d), BF16)] * 2, (keep_a, came_a, keep_f, came_f), limit=24, name="add_core")


def add_split(kept, came):
    _, rows, d = kept.shape
    half = rows // 32 * 16

    def kernel(a_ref, b_ref, c0, c1, c2a, c2b, c3):
        for k, ref in ((0, c0), (1, c1), (3, c3)):
            ref[...] = a_ref[k] + b_ref[k]
        c2a[...] = a_ref[2, :half] + b_ref[2, :half]
        c2b[...] = a_ref[2, half:] + b_ref[2, half:]

    full = like((rows, d), BF16)
    outs = [full, full, like((half, d), BF16), like((rows - half, d), BF16), full]
    return call(kernel, outs, (kept, came), limit=16, name="add_split")


def head_forward(pieces, table):
    count = sum(piece.shape[0] for piece in pieces)
    vocab, d = table.shape
    tiles = 3
    block = vocab // tiles
    part = block // 2
    chunk = 256
    many = len(pieces)

    def kernel(*refs):
        piece_refs, (w_ref, ctx_ref, lse_ref, x_ref, m_ref, s_ref, acc_ref) = refs[:many], refs[many:]
        step = pl.program_id(0)

        @pl.when(step == 0)
        def _():
            at = 0
            for ref in piece_refs:
                x_ref[at : at + ref.shape[0]] = ref[...]
                at += ref.shape[0]
            m_ref[...] = jnp.full(m_ref.shape, -1e30, F32)
            s_ref[...] = jnp.zeros(s_ref.shape, F32)
            acc_ref[...] = jnp.zeros(acc_ref.shape, F32)

        units = [(c, r) for c in range(2) for r in range(count // chunk)]

        def logits_of(unit):
            c, r = unit
            return nt(x_ref[r * chunk : (r + 1) * chunk], w_ref[c * part : (c + 1) * part])

        logits = logits_of(units[0])
        for n, (c, r) in enumerate(units):
            following = logits_of(units[n + 1]) if n + 1 < len(units) else None
            span = slice(r * chunk, (r + 1) * chunk)
            old = m_ref[span]
            new = jnp.maximum(old, jnp.max(logits, axis=-1, keepdims=True))
            keep = jnp.exp(old - new)
            weight = jnp.exp(logits - new)
            s_ref[span] = s_ref[span] * keep + jnp.sum(weight, axis=-1, keepdims=True)
            acc_ref[span] = acc_ref[span] * keep + nn(weight.astype(BF16), w_ref[c * part : (c + 1) * part])
            m_ref[span] = new
            logits = following

        @pl.when(step == tiles - 1)
        def _():
            total = s_ref[...]
            ctx_ref[...] = acc_ref[...] * (1.0 / total)
            lse = m_ref[...] + jnp.log(total)
            lse_ref[...] = jnp.broadcast_to(lse, (count, 128)).T[0:8]

    fixed = lambda i: (0, 0)
    return call(
        kernel,
        [like((count, d), F32), like((8, count), F32)],
        (*pieces, table),
        specs=[pl.BlockSpec(piece.shape, fixed) for piece in pieces] + [pl.BlockSpec((block, d), lambda i: (i, 0))],
        out_specs=[pl.BlockSpec((count, d), fixed), pl.BlockSpec((8, count), fixed)],
        scratch=[pltpu.VMEM((count, d), BF16), pltpu.VMEM((count, 1), F32), pltpu.VMEM((count, 1), F32), pltpu.VMEM((count, d), F32)],
        grid=(tiles,),
        flops=11 * 10**9,
        limit=36,
        name="head_forward",
    )


def head_combine(seq, ctxs, picked, ids_by, lses, vocab):
    shards = ids_by.shape[0]
    d = picked.shape[1]

    def kernel(x0_ref, x1_ref, x2_ref, x3_ref, p_ref, i_ref, a_ref, b_ref, c_ref, e_ref, *outs):
        lse_ref = outs[shards]
        shard = lax.axis_index("shard")
        parts = (a_ref, b_ref, c_ref, e_ref)
        for k in range(shards):
            rows = [parts[m][:, ((k - m) % shards) * seq : ((k - m) % shards + 1) * seq] for m in range(shards)]
            top = rows[0]
            for row in rows[1:]:
                top = jnp.maximum(top, row)
            total = top + jnp.log(sum(jnp.exp(row - top) for row in rows))
            whole = upright(total, seq)
            span = slice(k * seq, (k + 1) * seq)
            lse_ref[span] = whole
            weight = upright(jnp.exp(rows[0] - total), seq)
            local = i_ref[k, 1:2] - shard * vocab
            inside = upright(jnp.where((local >= 0) & (local < vocab), 1.0, 0.0), seq)
            hit = jnp.where(inside > 0.5, p_ref[span].astype(F32), 0.0)
            ctx = (x0_ref, x1_ref, x2_ref, x3_ref)[k][...]
            outs[k][...] = (ctx * weight - hit).astype(BF16)

    return call(
        kernel,
        [like((seq, d), BF16)] * shards + [like((shards * seq, 1), F32)],
        (*ctxs, picked, ids_by, *lses),
        limit=20, name="head_combine",
    )


def head_table(pieces, table, lse, ids_by, core=None):
    count = sum(piece.shape[0] for piece in pieces)
    shards, _, seq = ids_by[0].shape
    vocab, d = table.shape
    block = 1280
    tiles = pl.cdiv(vocab, block)
    shared = core is not None
    if shared:
        tiles = (tiles + 1) // 2
    else:
        core = jnp.zeros((1,), jnp.int32)
    chunk = 256
    many, groups = len(pieces), len(ids_by)
    wide = d // 8

    def kernel(core_ref, *refs):
        piece_refs, refs = refs[:many], refs[many:]
        w_ref, refs = refs[0], refs[1:]
        lse_refs, i_refs, refs = refs[:groups], refs[groups : 2 * groups], refs[2 * groups :]
        out_refs, (x_ref, xt_ref, t_ref, l_ref, p_ref) = refs[:-5], refs[-5:]
        step = pl.program_id(0)
        first_tile = core_ref[0] * tiles

        @pl.when(step == 0)
        def _():
            at = 0
            for ref in piece_refs:
                x_ref[at : at + ref.shape[0]] = ref[...]
                at += ref.shape[0]
            xt_ref[...] = x_ref[...].T
            start = lax.axis_index("shard") * vocab + first_tile * block
            for n in range(groups):
                for k in range(shards):
                    at = (n * shards + k) * seq
                    t_ref[at : at + seq] = upright(i_refs[n][k, 1:2] - start, seq).astype(jnp.int32)
                at = n * shards * seq
                l_ref[at : at + shards * seq] = lse_refs[n][...]

        w = w_ref[...]
        for r in range(count // chunk):
            span = slice(r * chunk, (r + 1) * chunk)
            logits = nt(x_ref[span], w)
            hit = iota(logits.shape, 1) == t_ref[span] - step * block
            p_ref[span] = (jnp.exp(logits - l_ref[span]) - jnp.where(hit, 1.0, 0.0)).astype(BF16)
        result = nn(xt_ref[...], p_ref[...]).astype(BF16)
        if not shared:
            out_refs[0][...] = result
            return
        zero = jnp.zeros((wide, block), jnp.int32)
        first = zero + lax.axis_index("section") == 0
        front = zero + side_of(2) == 0
        blocks = [result[n * wide : (n + 1) * wide] for n in range(8)]
        for n in range(2):
            low, high = blocks[2 * n], blocks[4 + 2 * n]
            out_refs[0][n], out_refs[1][n] = jnp.where(first, low, high), jnp.where(first, high, low)
            low, high = blocks[4 * n + 1], blocks[4 * n + 3]
            out_refs[2][n], out_refs[3][n] = jnp.where(front, low, high), jnp.where(front, high, low)

    if shared:
        outs = [like((2, wide, tiles * block), BF16)] * 4
        out_specs = [pl.BlockSpec((2, wide, block), lambda i, c: (0, 0, i))] * 4
    else:
        outs, out_specs = [like((d, vocab), BF16)], [pl.BlockSpec((d, block), lambda i, c: (0, i))]
    fixed = lambda i, c: (0, 0)
    return pl.pallas_call(
        kernel,
        out_shape=outs,
        grid_spec=pltpu.PrefetchScalarGridSpec(
            num_scalar_prefetch=1,
            grid=(tiles,),
            in_specs=[pl.BlockSpec(piece.shape, fixed) for piece in pieces]
            + [pl.BlockSpec((block, d), lambda i, c: (i + c[0] * tiles, 0))]
            + [pl.BlockSpec((shards * seq, 1), fixed)] * groups
            + [pl.BlockSpec(ids_by[0].shape, lambda i, c: (0, 0, 0))] * groups,
            out_specs=out_specs,
            scratch_shapes=[
                pltpu.VMEM((count, d), BF16),
                pltpu.VMEM((d, count), BF16),
                pltpu.VMEM((count, 1), jnp.int32),
                pltpu.VMEM((count, 1), F32),
                pltpu.VMEM((count, block), BF16),
            ],
        ),
        compiler_params=pltpu.CompilerParams(vmem_limit_bytes=58 * MIB),
        cost_estimate=pl.CostEstimate(flops=32 * 10**9, bytes_accessed=0, transcendentals=0),
        name="head_table",
    )(core, *pieces, table, *lse, *ids_by)


def add_halves(even, odd):
    shape = even[0].shape[1:]

    def kernel(a_ref, b_ref, c_ref, e_ref, *outs):
        for n, (one, two, side) in enumerate(((a_ref, b_ref, side_of(2)), (c_ref, e_ref, lax.axis_index("section")))):
            outs[2 * n][...] = one[side] + two[side]
            outs[2 * n + 1][...] = one[1 - side] + two[1 - side]

    return call(kernel, [like(shape, BF16)] * 4, (*even, *odd), limit=32, name="add_halves")


def add_last(even, odd):
    def kernel(a_ref, b_ref, c_ref, e_ref, own_ref, send_ref):
        first = (jnp.zeros(a_ref.shape, jnp.int32) + side_of(1)) == 0
        low, high = a_ref[...] + b_ref[...], c_ref[...] + e_ref[...]
        own_ref[...] = jnp.where(first, low, high)
        send_ref[...] = jnp.where(first, high, low)

    return call(kernel, [like(even[0].shape, BF16)] * 2, (*even, *odd), limit=16, name="add_last")


def list_tokens(ids, vocab):
    count = ids.shape[1]
    unit = 1 << (vocab - 1).bit_length()

    def kernel(ids_ref, list_ref):
        start = lax.axis_index("shard") * vocab

        def step(i, many):
            local = ids_ref[0, i] - start
            list_ref[0, many] = i * unit + local
            return many + ((local >= 0) & (local < vocab)).astype(jnp.int32)

        list_ref[0, count] = lax.fori_loop(0, count, step, jnp.int32(0), unroll=8)

    smem = pl.BlockSpec(memory_space=pltpu.SMEM)
    return call(kernel, [like((1, count + 128), jnp.int32)], (ids,), specs=[smem], out_specs=[smem], limit=4, name="list_tokens")[0]


def table_grad(dense, pieces, lists, vocab):
    width = pieces[0].shape[1]
    arrays = dense
    sources, _, seq = pieces[0].shape
    shards = 4
    listed = shards * seq
    line = lists.shape[1]
    unit = 1 << (vocab - 1).bit_length()
    ways, each = 4, 4
    rows = (lists & (unit - 1)).reshape(-1)
    tokens = ((lists >> (unit.bit_length() - 1)) + listed * jnp.arange(sources, dtype=jnp.int32)[:, None]).reshape(-1)
    counts = lists[:, listed]

    def kernel(*refs):
        d_refs, refs = refs[: len(arrays)], refs[len(arrays) :]
        own_ref, later_ref, before_ref, far_a_ref, far_b_ref, r_ref, t_ref, n_ref, o_ref, flat_ref, *acc = refs
        half = sources // 2
        for j in range(sources):
            far = far_a_ref[j] if j < half else far_b_ref[j - half]
            for k, block in enumerate((own_ref[j], later_ref[j], before_ref[j], far)):
                at = j * listed + k * seq
                flat_ref[at : at + seq] = block.astype(F32).T
        for ref in acc:
            ref[...] = jnp.zeros(ref.shape, F32)

        def source(j, carry):
            many = n_ref[j]
            rounds = many // (ways * each)

            def step(i, carry):
                at = j * line + i * ways * each
                place = [r_ref[at + n] for n in range(ways * each)]
                value = [flat_ref[pl.ds(t_ref[at + n], 1), :] for n in range(ways * each)]
                for n in range(each):
                    old = [ref[pl.ds(place[n * ways + way], 1), :] for way, ref in enumerate(acc)]
                    for way, ref in enumerate(acc):
                        ref[pl.ds(place[n * ways + way], 1), :] = old[way] + value[n * ways + way]
                return carry

            def rest(at, carry):
                acc[0][pl.ds(r_ref[j * line + at], 1), :] += flat_ref[pl.ds(t_ref[j * line + at], 1), :]
                return carry

            lax.fori_loop(0, rounds, step, jnp.int32(0))
            lax.fori_loop(rounds * ways * each, many, rest, jnp.int32(0))
            return carry

        lax.fori_loop(0, sources, source, jnp.int32(0))
        if len(d_refs) == 1:
            o_ref[...] = d_refs[0][...].astype(F32) + sum(ref[...] for ref in acc).T
            return
        half = d_refs[0].shape[1]
        first = (jnp.zeros((width, half), jnp.int32) + side_of(1)) == 0
        own, other = d_refs[0][...], d_refs[1][...]
        o_ref[:, :half] = jnp.where(first, own, other).astype(F32) + sum(ref[:half] for ref in acc).T
        last = jnp.where(first, other, own)[:, : vocab - half]
        o_ref[:, half:] = last.astype(F32) + sum(ref[half:] for ref in acc).T

    smem = pl.BlockSpec(memory_space=pltpu.SMEM)
    return call(
        kernel,
        [like((width, vocab), F32)],
        (*arrays, *pieces, rows, tokens, counts),
        specs=[None] * (len(arrays) + 5) + [smem] * 3,
        scratch=[pltpu.VMEM((sources * listed, width), F32)] + [pltpu.VMEM((vocab, width), F32)] * ways,
        limit=60,
        name="table_grad",
    )[0]


def unpack_grads(z, blocks):
    rows = z.part + z.extra
    pos_rows = z.pos + 4 * z.quarter

    def kernel(own_ref, y_ref, core_ref, both_ref, qkv_ref, out_ref, fin_ref, fout_ref, gain_ref, bias_ref, pos_ref, eg_ref, es_ref, all_ref):
        core, y = side_of(1), side_of(2)
        shard = lax.axis_index("shard")
        all_ref[core, y] = own_ref[...]
        all_ref[core, 1 - y] = y_ref[...]
        all_ref[1 - core, y] = core_ref[...]
        all_ref[1 - core, 1 - y] = both_ref[...]

        def own_lanes(value):
            total = jnp.zeros((value.shape[0], z.part), F32)
            for h in range(z.shards):
                total = total + jnp.where(shard == h, value[:, h * z.part : (h + 1) * z.part], 0.0)
            return total

        out_ref[...] = all_ref[0, 0, : z.part].astype(F32)
        fin_ref[...] = all_ref[0, 1, : z.part].astype(F32).reshape(z.groups, z.gi, z.d)
        for c in range(3):
            part = all_ref[1, 0, c * z.gi : (c + 1) * z.gi].astype(F32)
            for g in range(z.groups):
                qkv_ref[c, g] = part[:, g * z.gw : (g + 1) * z.gw]
        part = all_ref[1, 1, : z.part].astype(F32)
        for g in range(z.groups):
            fout_ref[g] = part[:, g * z.gw : (g + 1) * z.gw]
        small = own_lanes(all_ref[1, 0, z.at_small : z.at_small + 16].astype(F32))
        for n in range(9):
            bias_ref[n] = small[2 + n : 3 + n]
        gain_ref[...] = small[0:2]
        eg_ref[...] = small[11:12]
        es_ref[...] = small[12:13]
        pos_ref[: z.pos] = all_ref[1, 0, z.at_small + 16 : z.part].astype(F32)
        for n in range(4):
            row = z.pos + n * z.quarter
            pos_ref[row : row + z.quarter] = all_ref[n // 2, n % 2, z.part :].astype(F32)[: z.quarter]

    return call(
        kernel,
        [
            like((3, z.groups, z.gi, z.gw), F32),
            like((z.part, z.d), F32),
            like((z.groups, z.gi, z.d), F32),
            like((z.groups, z.part, z.gw), F32),
            like((2, z.part), F32),
            like((9, 1, z.part), F32),
            like((pos_rows, z.d), F32),
            like((1, z.part), F32),
            like((1, z.part), F32),
        ],
        blocks,
        scratch=[pltpu.VMEM((2, 2, rows, z.d), BF16)],
        limit=16, name="unpack",
    )


def body(token_ids, targets, segment_ids, word_table, pos_table, embed_gain, embed_shift, qkv_weight, out_weight, ffn_in, ffn_out, layer_gains, layer_biases):
    micro, _, seq = token_ids.shape
    vocab, d = word_table.shape
    pos_rows = pos_table.shape[0]
    shards = lax.axis_size("shard")
    dp = lax.axis_size("dp")
    both = ("section", "dp")
    section = lax.axis_index("section")
    first = section == 0
    z = Sizes(qkv_weight.shape, out_weight.shape, shards, pos_rows)
    offset = lax.axis_index("shard") * vocab

    local, pair, packed = pack_weights(
        z, qkv_weight[0], out_weight[0], ffn_in[0], ffn_out[0], layer_gains[0], layer_biases[0], embed_gain, embed_shift
    )

    mine = lax.dynamic_index_in_dim(jnp.stack([token_ids[:, 0], targets[:, 0], segment_ids[:, 0]], axis=1), section, 0, keepdims=False)
    mine = after(mine, packed)
    ids_by = jnp.stack([mine, turned(mine, "shard", -1), turned(mine, "shard", 2), turned(mine, "shard", 1)])
    seg_row = mine[2:3]

    def rows_of(ids):
        return word_table.at[jnp.clip(ids.reshape(-1) - offset, 0, vocab - 1)].get(mode="promise_in_bounds")

    cross_pair = crossed(pair, "section", 1)
    near = gather_first(packed, "shard")
    picked = rows_of(ids_by[:, 0])
    near, pos_table = after((near, pos_table), near)
    word_parts = embed_parts(picked, ids_by, pos_table, vocab)
    near = after(near, word_parts)
    near_rows = jnp.concatenate(near, axis=0)
    near_y = crossed(near_rows, "dp", 2)
    cross_near = crossed(near_rows, "section", 1)
    target_rows = rows_of(after(ids_by[:, 1], near_rows))
    c0, c1, c2a, c2b, c3 = word_parts
    half, quarter = seq // 2, z.part // 2
    right = turned(jnp.concatenate([c2a, near[0][:quarter]], axis=0), "shard", 1)
    left = turned(jnp.concatenate([c2b, near[1][quarter:]], axis=0), "shard", -1)
    right, left = after((right, left), target_rows)
    c1 = jnp.concatenate([c1[:half] + right[:half], c1[half:]], axis=0)
    c3 = jnp.concatenate([c3[:half], c3[half:] + left[:half]], axis=0)
    words = scatter_second(c0, c1, c3, "shard")
    near_y = after(near_y, words)
    far = jnp.concatenate([right[half:], left[half:]], axis=0)
    cross_far = crossed(far, "section", 1)
    both_y = crossed(jnp.concatenate([far, cross_near], axis=0), "dp", 2)
    far_y, cross_near_y = both_y[: z.part], both_y[z.part :]
    cross_far_y = crossed(cross_far, "dp", 2)
    mine = (near_rows, far)
    mine = (*mine, *(crossed(b, "dp", 1) for b in mine), near_y, far_y, crossed(near_y, "dp", 1), crossed(far_y, "dp", 1))
    others = (cross_near, cross_far)
    others = (*others, *(crossed(b, "dp", 1) for b in others))
    others = (*others, cross_near_y, cross_far_y, crossed(cross_near_y, "dp", 1), crossed(cross_far_y, "dp", 1))
    pairs = (cross_pair, crossed(cross_pair, "dp", 1))
    weights_one, weights_two = (Pieces(z, local, mine, pairs, others, layer) for layer in range(2))
    one = layer_forward(z, weights_one, seg_row, True, words=words)
    two = layer_forward(z, weights_two, seg_row, False, layer_in=one["out"])
    two["x"] = one["out"]

    own_out = jnp.where(first, one["out"], two["out"])
    came_out = crossed(jnp.where(first, two["out"], one["out"]), "section", 1)

    before, later = gather_first(two["out"], "shard")
    ctx_own, lse_own = head_forward([two["out"]], word_table)
    before = after(before, ctx_own)
    far_a = turned(before[: seq // 2], "shard", 1)
    ctx_before, lse_before = head_forward([before], word_table)
    later = after(later, ctx_before)
    far_b = turned(later[seq // 2 :], "shard", -1)
    ctx_later, lse_later = head_forward([later], word_table)
    far_a, far_b = after((far_a, far_b), ctx_later)
    ctx_far, lse_far = head_forward([far_a, far_b], word_table)
    lse = jnp.concatenate([lse_own[0:1], lse_later[0:1], lse_far[0:1], lse_before[0:1]], axis=1)
    listed = jnp.stack([ids_by[0, 0], ids_by[1, 0], ids_by[3, 0], ids_by[2, 0]]).reshape(1, -1)
    lses = (lse, turned(lse, "shard", -1), turned(lse, "shard", 2), turned(lse, "shard", 1))
    lses = after(lses, came_out)
    *parts, whole_lse = head_combine(seq, (ctx_own, ctx_later, ctx_far, ctx_before), target_rows, ids_by, lses, vocab)
    head_rows = [two["out"], later, far_a, far_b, before]
    dy_terms = direct_scatter(parts, "shard")
    if dp == 4:
        rows_other, ids_other, lse_other = [crossed(row, "dp", 1) for row in head_rows], crossed(ids_by, "dp", 1), crossed(whole_lse, "dp", 1)
        core = side_of(1).astype(jnp.int32).reshape(1)
        stay_x, leave_x, stay_y, leave_y = head_table([*head_rows, *rows_other], word_table, [whole_lse, lse_other], [ids_by, ids_other], core)
        came_x, came_y = crossed(leave_x, "section", 1), crossed(leave_y, "dp", 2)
        dy_terms = after(dy_terms, stay_x)
    else:
        dense = head_table(head_rows, word_table, [whole_lse], [ids_by])[0]
        dense = [lax.psum_scatter(dense, both, scatter_dimension=0, tiled=True)]
    d_middle, small_grads, keep_f, send_f = ffn_backward(z, weights_two, two, dy_terms)

    in_two, in_low, keep_a, send_a = attention_backward(z, weights_two, two, d_middle, small_grads, False)
    came_f, came_a = crossed(send_f, "dp", 1), crossed(send_a, "dp", 1)
    d_middle, small_grads, keep_one_f, send_one_f = ffn_backward(z, weights_one, one, [in_low])
    keep_f, came_f, keep_a, came_a = after((keep_f, came_f, keep_a, came_a), d_middle)
    split_two = add_cores_split(z, (keep_a, keep_f), (came_a, came_f))
    d_middle = after(d_middle, split_two)
    terms_two = scatter_first(*split_two, "shard")
    if dp == 4:
        d_middle, came_x, came_y = after((d_middle, came_x, came_y), ())
    came_one_f = crossed(send_one_f, "dp", 1)
    in_one, in_one_low, keep_one_a, send_one_a, d_embed = attention_backward(z, weights_one, one, d_middle, small_grads, True, seg_row, pos_rows)
    keep_one_f, came_one_f = after((keep_one_f, came_one_f), d_embed)
    send_one_a, d_embed = after((send_one_a, d_embed), terms_two)
    came_one_a = crossed(send_one_a, "dp", 1)
    columns = d_embed[None]
    steps = [("dp", 1 << n) for n in range(dp.bit_length() - 1)]
    for n, (axis, bit) in enumerate(steps):
        middle = columns.shape[1] // 2
        columns = jnp.concatenate([columns[:, :middle], crossed(columns[:, middle:], axis, bit)], axis=0)
        if n == 0:
            came_one_a = after(came_one_a, columns)
    second_two = scatter_second(*terms_two, "shard")
    stay_one, leave_one = add_core(z, keep_one_a, came_one_a, keep_one_f, came_one_f)
    came_one = crossed(after(leave_one, columns), "dp", 2)
    columns = after(columns, (stay_one, second_two))
    columns = jnp.concatenate([columns[:, 0], crossed(columns[:, 1], "section", 1)], axis=0)
    ring_columns = gather_first(columns, "shard")
    own_in = jnp.where(first, in_one, in_two)
    came_in = crossed(jnp.where(first, in_two, in_one).astype(BF16), "section", 1)
    stay_two, leave_two = halves_by_y(z, after(second_two, (columns, stay_one)))
    came_two = crossed(leave_two, "dp", 2)
    if dp == 4:
        stay_x, leave_x, stay_y, leave_y = add_halves(*after(((stay_x, came_x), (stay_y, came_y)), stay_two))
        last_x, last_y = crossed(leave_x, "dp", 2), crossed(leave_y, "section", 1)
    lists = list_tokens(after(listed, columns), vocab)
    bit = 1
    while bit < dp:
        lists = jnp.concatenate([lists, crossed(lists, "dp", bit)], axis=0)
        bit *= 2
    lists = jnp.concatenate([lists, crossed(lists, "section", 1)], axis=0)
    ring_columns = after(ring_columns, stay_two)
    far_columns = gather_second(*ring_columns, "shard")
    terms_one = scatter_first(*add_split(stay_one, after(came_one, (ring_columns, came_in))), "shard")
    second_one = scatter_second(*terms_one, "shard")
    if dp == 4:
        own_dense, send_dense = add_last(*after(((stay_x, last_x), (stay_y, last_y)), second_one))
        dense = [own_dense, crossed(send_dense, "dp", 1)]
    word_grad = table_grad(dense, (columns, ring_columns[1], ring_columns[0], *far_columns), lists, vocab)
    sum_two = stay_two + came_two
    sum_one = sum(after(second_one, sum_two))
    layer_one, extra = sum_one[: z.part], sum_one[z.part :]
    row = jnp.arange(z.part)[:, None]
    embed_rows = (row >= z.at_small + 11) & (side_of(1) == 1) & (side_of(2) == 0)
    layer_two = jnp.where(embed_rows, layer_one, sum_two)
    total = jnp.concatenate([jnp.where(first, layer_one, layer_two), extra], axis=0)
    came = crossed(jnp.concatenate([jnp.where(first, layer_two, layer_one), extra], axis=0), "section", 1)
    total = total + after(came, word_grad)
    bit = 4
    while bit < dp:
        total = total + crossed(total, "dp", bit)
        bit *= 2
    total_y = crossed(total, "dp", 2)
    def by_micro(own, came):
        return jnp.stack([jnp.where(first, own, came), jnp.where(first, came, own)]).reshape(1, micro, 1, seq, d)

    layer_outputs = by_micro(own_out, came_out)
    input_grads = by_micro(own_in, came_in.astype(F32))
    total_y = after(total_y, (layer_outputs, input_grads))
    unpacked = unpack_grads(z, (total, total_y, crossed(total, "dp", 1), crossed(total_y, "dp", 1)))

    word_grad = word_grad.T

    qkv_g, out_g, fin_g, fout_g, gain_g, bias_g, pos_g, eg_g, es_g = unpacked
    return (
        layer_outputs,
        input_grads,
        word_grad,
        pos_g,
        eg_g.reshape(-1),
        es_g.reshape(-1),
        qkv_g[None],
        out_g[None],
        fin_g[None],
        fout_g[None],
        gain_g[None],
        bias_g.transpose(1, 0, 2),
    )


def solution(mesh):
    rows = P(None, ("dp", "shard"), None)
    weights = (
        P("section", None, None, "shard", None),
        P("section", "shard", None),
        P("section", None, "shard", None),
        P("section", None, "shard", None),
        P("section", None, "shard"),
        P("section", None, "shard"),
    )
    states = P("section", None, ("dp", "shard"), None, None)
    return jax.shard_map(
        body,
        mesh=mesh,
        in_specs=(rows, rows, rows, P("shard", None), P("shard", None), P("shard"), P("shard"), *weights),
        out_specs=(states, states, P("shard", ("section", "dp")), P("shard", None), P("shard"), P("shard"), *weights),
        check_vma=False,
    )
```

```python
import math

import jax
import jax.numpy as jnp
from jax import lax
from jax.experimental import pallas as pl
from jax.experimental.pallas import tpu as pltpu
from jax.sharding import PartitionSpec as P

HEADS = 12
EPSILON = 1e-06
MASKED = -1000000000.0
F32 = jnp.float32
BF16 = jnp.bfloat16
MIB = 1 << 20


def nn(a, b):
    return jnp.dot(a, b, preferred_element_type=F32)


def nt(a, b):
    return lax.dot_general(a, b, (((1,), (1,)), ((), ())), preferred_element_type=F32)


def tn(a, b):
    return lax.dot_general(a, b, (((0,), (0,)), ((), ())), preferred_element_type=F32)


def iota(shape, axis):
    return lax.broadcasted_iota(jnp.int32, shape, axis)


def group_of(index, width, count):
    total = jnp.zeros(index.shape, jnp.int32)
    for step in range(1, count):
        total = total + (index >= step * width).astype(jnp.int32)
    return total


def normed(value):
    centered = value - jnp.mean(value, axis=-1, keepdims=True)
    scale = lax.rsqrt(jnp.mean(centered * centered, axis=-1, keepdims=True) + EPSILON)
    return centered * scale, scale


def norm_back(grad, unit, scale, gain):
    inner = grad * gain
    first = jnp.mean(inner, axis=-1, keepdims=True)
    second = jnp.mean(inner * unit, axis=-1, keepdims=True)
    return scale * (inner - first - unit * second)


def col_sum(value):
    return jnp.sum(value, axis=0, keepdims=True)


def upright(row, count):
    return jnp.broadcast_to(row.astype(F32), (128, count)).T[:, 0:1]


def call(kernel, outs, ins, specs=None, scratch=(), limit=56, flops=0, moved=0, grid=None, out_specs=None, name=None):
    vmem = pl.BlockSpec(memory_space=pltpu.VMEM)
    extra = {} if grid is None else {"grid": grid}
    return pl.pallas_call(
        kernel,
        out_shape=outs,
        in_specs=[vmem if s is None else s for s in (specs or [None] * len(ins))],
        out_specs=out_specs if out_specs is not None else [vmem] * len(outs),
        scratch_shapes=list(scratch),
        compiler_params=pltpu.CompilerParams(vmem_limit_bytes=limit * MIB),
        cost_estimate=pl.CostEstimate(flops=flops, bytes_accessed=0, transcendentals=0),
        name=name,
        **extra,
    )(*ins)


def like(shape, dtype):
    return jax.ShapeDtypeStruct(shape, dtype)


def turned(block, axis, by):
    size = lax.axis_size(axis)
    return lax.ppermute(block, axis, [(i, (i + by) % size) for i in range(size)])


def crossed(block, axis, bit):
    return lax.ppermute(block, axis, [(i, i ^ bit) for i in range(lax.axis_size(axis))])


def after(value, first):
    return lax.optimization_barrier((value, first))[0]


def scatter_first(c0, c1, c2a, c2b, c3, axis, wait=()):
    half = c2a.shape[0]
    right, left = after((turned(c2a, axis, 1), turned(c2b, axis, -1)), wait)
    return c0, jnp.concatenate([c1[:half] + right, c1[half:]], axis=0), jnp.concatenate([c3[:half], c3[half:] + left], axis=0)


def scatter_second(c0, c1, c3, axis):
    return c0, turned(c1, axis, 1), turned(c3, axis, -1)


def side_of(bit):
    return (lax.axis_index("dp") // bit) % 2


def direct_scatter(parts, axis):
    return parts[0], turned(parts[1], axis, 1), turned(parts[3], axis, -1), turned(parts[2], axis, 2)


def gather_first(block, axis):
    return turned(block, axis, 1), turned(block, axis, -1)


def gather_second(before, later, axis):
    half = before.shape[0] // 2
    return turned(before[:half], axis, 1), turned(later[half:], axis, -1)


def ring_gather(block, axis):
    first = gather_first(block, axis)
    return (*first, *gather_second(*first, axis))


class Sizes:
    def __init__(self, qkv, out, shards, pos_rows):
        _, _, groups, part, width = qkv
        self.shards, self.groups, self.gw, self.gi = shards, groups, width, part
        self.d = out[2]
        self.part = out[1]
        self.at_small = 3 * part
        self.rows = 2 * self.part
        self.pos = self.part - self.at_small - 16
        self.quarter = (pos_rows - self.pos) // 4
        self.extra = -(-self.quarter // 16) * 16


def pack_weights(z, qkv, out, fin, fout, gains, biases, egain, eshift):
    def kernel(qkv_ref, out_ref, fin_ref, fout_ref, gain_ref, bias_ref, eg_ref, es_ref, o_ref, pair_ref, own_ref):
        shard = lax.axis_index("shard")

        def spread(pieces):
            return jnp.concatenate([piece.astype(F32) for piece in pieces], axis=1).astype(BF16)

        o_ref[0, 0] = out_ref[...]
        o_ref[0, 1] = fin_ref[...].reshape(z.part, z.d)
        for c in range(3):
            o_ref[1, 0, c * z.gi : (c + 1) * z.gi] = spread([qkv_ref[c, g] for g in range(z.groups)])
        embed = [ref[...].astype(F32).reshape(1, z.part) for ref in (eg_ref, es_ref)]
        tall = jnp.concatenate([gain_ref[...].astype(F32), bias_ref[...].astype(F32), *embed, jnp.zeros((3, z.part), F32)], axis=0)
        wide = jnp.concatenate([tall] * z.shards, axis=1)
        lane = group_of(iota(wide.shape, 1), z.part, z.shards)
        o_ref[1, 0, z.at_small : z.at_small + 16] = jnp.where(lane == shard, wide, 0.0).astype(BF16)
        o_ref[1, 0, z.at_small + 16 : z.part] = jnp.zeros((z.part - z.at_small - 16, z.d), BF16)
        o_ref[1, 1] = spread([fout_ref[g] for g in range(z.groups)])
        pair_ref[...] = o_ref[side_of(1)]
        own_ref[...] = o_ref[side_of(1), side_of(2)]

    outs = [like((2, 2, z.part, z.d), BF16), like((2, z.part, z.d), BF16), like((z.part, z.d), BF16)]
    return call(kernel, outs, (qkv, out, fin, fout, gains, biases, egain, eshift), name="pack")


class Pieces:
    def __init__(self, z, local, mine, pairs, others, layer):
        self.z, self.layer = z, layer
        self.arrays = (local, *mine, *pairs, *others)
        self.specs = [pl.BlockSpec(memory_space=pl.ANY)] * len(self.arrays)
        self.scratch = [pltpu.VMEM((2, z.shards, z.rows, z.d), BF16), pltpu.SemaphoreType.DMA((2, 2, 4))]

    def start(self, refs, w_ref, sems, parts):
        z = self.z
        core, y = side_of(1), side_of(2)
        shard = lax.axis_index("shard")
        own_layer = lax.axis_index("section") == self.layer
        local, mine, pairs, others = refs[0], refs[1:9], refs[9:11], refs[11:19]
        waits = {}
        for part in parts:
            copies = []
            for side in range(2):
                place = core if side == 0 else 1 - core
                for n, by in enumerate((0, 3, 1, 2)):
                    target = w_ref.at[place, (shard + by) % z.shards, pl.ds(part * z.part, z.part)]
                    sem = sems.at[part, side, n]
                    rows = pl.ds((n - 1) * z.part, z.part)
                    choices = []
                    for across in range(2):
                        here = (y == part) if across == 0 else (y != part)
                        at = 2 * across + side
                        if n == 0:
                            own, other = local.at[place, part], pairs[side].at[part]
                        elif n < 3:
                            own, other = mine[2 * at].at[rows], others[2 * at].at[rows]
                        else:
                            own, other = mine[2 * at + 1], others[2 * at + 1]
                        choices.append((jnp.logical_and(here, own_layer), own))
                        choices.append((jnp.logical_and(here, jnp.logical_not(own_layer)), other))
                    for here, source in choices:
                        copy = pltpu.make_async_copy(source, target, sem)
                        pl.when(here)(copy.start)
                    copies.append(pltpu.make_async_copy(choices[1][1], target, sem))
            waits[part] = copies
        return waits


def wait_all(copies):
    for copy in copies:
        copy.wait()


class Loads:
    def __init__(self, arrays):
        self.names = list(arrays)
        self.arrays = list(arrays.values())
        self.specs = [pl.BlockSpec(memory_space=pl.ANY)] * len(self.arrays)
        self.scratch = [pltpu.VMEM(a.shape, a.dtype) for a in self.arrays] + [pltpu.SemaphoreType.DMA((len(self.arrays),))]

    def start(self, refs, scratch):
        self.buffers = dict(zip(self.names, scratch))
        self.copies = {
            name: pltpu.make_async_copy(ref, buffer, scratch[-1].at[n])
            for n, (name, ref, buffer) in enumerate(zip(self.names, refs, scratch))
        }
        for copy in self.copies.values():
            copy.start()

    def __getitem__(self, name):
        copy = self.copies.pop(name, None)
        if copy is not None:
            copy.wait()
        return self.buffers[name]


class Stores:
    def __init__(self, shapes, split=()):
        self.names = list(shapes)
        self.shapes = list(shapes.values())
        self.split = split
        self.specs = [pl.BlockSpec(memory_space=pl.ANY)] * len(self.shapes)
        count = sum(a.shape[0] if name in split else 1 for name, a in shapes.items())
        self.scratch = [pltpu.VMEM(a.shape, a.dtype) for a in self.shapes] + [pltpu.SemaphoreType.DMA((count,))]

    def bind(self, refs, scratch):
        self.refs = dict(zip(self.names, refs))
        self.buffers = dict(zip(self.names, scratch))
        self.sems = scratch[-1]
        self.copies = []

    def put(self, name, value, index=None):
        source = self.buffers[name] if index is None else self.buffers[name].at[index]
        source[...] = value.astype(source.dtype)
        self.send(name, index)

    def send(self, name, index=None):
        source, target = self.buffers[name], self.refs[name]
        if index is not None:
            source, target = source.at[index], target.at[index]
        copy = pltpu.make_async_copy(source, target, self.sems.at[len(self.copies)])
        copy.start()
        self.copies.append(copy)

    def finish(self):
        wait_all(self.copies)


class Weights:
    def __init__(self, z, w_ref):
        self.z, self.w = z, w_ref

    def out(self):
        z = self.z
        return self.w[0, :, 0 : z.part, :].reshape(z.d, z.d)

    def small(self):
        z = self.z
        return sum(self.w[1, h, z.at_small : z.at_small + 16, :].astype(F32) for h in range(z.shards))

    def proj(self, c, p):
        z = self.z
        lanes = slice(2 * p * z.gw, 2 * (p + 1) * z.gw)
        dense = self.w[1, :, c * z.gi : (c + 1) * z.gi, lanes].reshape(z.gw, 2 * z.gw)
        high = iota(dense.shape, 1) >= z.gw
        blank = jnp.zeros_like(dense)
        return jnp.concatenate([jnp.where(high, blank, dense), jnp.where(high, dense, blank)], axis=0)

    def project(self, value, c):
        z = self.z
        wide = 2 * z.gw
        return jnp.concatenate([nn(value[:, p * wide : (p + 1) * wide], self.proj(c, p)) for p in range(z.groups // 2)], axis=1)

    def fin(self, g):
        z = self.z
        row = z.part + g * z.gi
        dense = self.w[0, :, row : row + z.gi, :].reshape(z.gw, z.d)
        blank = jnp.zeros_like(dense)
        return jnp.concatenate([dense, blank] if g % 2 == 0 else [blank, dense], axis=0)

    def fout(self, g):
        z = self.z
        at = (g // 2) * 2 * z.gw
        pair = self.w[1, :, z.part : z.rows, at : at + 2 * z.gw].reshape(z.d, 2 * z.gw)
        keep = (iota(pair.shape, 1) >= z.gw) == (g % 2 == 1)
        return jnp.where(keep, pair, jnp.zeros_like(pair))


def embed_parts(picked, ids_by, pos_table, vocab):
    count, _, seq = ids_by.shape
    width = picked.shape[1]
    half = seq // 2
    rows = pos_table.shape[0]

    def kernel(p_ref, i_ref, t_ref, c0, c1, c2a, c2b, c3):
        shard = lax.axis_index("shard")
        for k in range(count):
            span = slice(k * seq, (k + 1) * seq)
            token, seg_row = i_ref[k, 0:1], i_ref[k, 2:3]
            seg_col = upright(seg_row, seq)
            same = seg_col == seg_row.astype(F32)
            earlier = iota((seq, seq), 1) < iota((seq, seq), 0)
            place = jnp.sum(jnp.where(same & earlier, 1.0, 0.0), axis=1, keepdims=True).astype(jnp.int32) - shard * rows
            spot = (iota((seq, rows), 1) == place).astype(BF16)
            local = token - shard * vocab
            inside = upright(jnp.where((local >= 0) & (local < vocab), 1.0, 0.0), seq)
            word = jnp.where(inside > 0.5, p_ref[span].astype(F32), 0.0)
            total = (word + nn(spot, t_ref[...])).astype(BF16)
            if k == 2:
                c2a[...] = total[:half]
                c2b[...] = total[half:]
            else:
                (c0, c1, None, c3)[k][...] = total

    full, part = like((seq, width), BF16), like((half, width), BF16)
    return call(kernel, [full, full, part, part, full], (picked, ids_by, pos_table), limit=24, name="embed_parts")


def layer_forward(z, pieces, seg_row, first, words=None, layer_in=None):
    seq = seg_row.shape[1]
    d = z.d
    flat = like((seq, d), BF16)
    shapes = {"q": flat, "k": flat, "v": flat, "p": like((HEADS, seq, seq), BF16), "att": flat, "n1": flat, "mid": flat}
    shapes.update({"act": like((z.groups, seq, d), BF16), "slope": like((z.groups, seq, d), BF16)})
    shapes.update({"n2": flat, "stats": like((seq, 128), F32), "small": like((16, d), F32), "out": flat})
    if first:
        shapes.update({"x": flat, "n0": flat})
    stores = Stores(shapes, split=("p", "act", "slope"))
    head = d // HEADS
    inputs = list(words) if first else [layer_in]

    def kernel(*refs):
        piece_refs, refs = refs[: len(pieces.arrays)], refs[len(pieces.arrays) :]
        row_ref, refs = refs[0], refs[1:]
        in_refs, refs = refs[: len(inputs)], refs[len(inputs) :]
        out_refs, refs = refs[: len(shapes)], refs[len(shapes) :]
        w_ref, sems, *buffers = refs
        waits = pieces.start(piece_refs, w_ref, sems, (0, 1))
        stores.bind(out_refs, buffers)
        put = stores.put
        w = Weights(z, w_ref)
        if first:
            unit, r0 = normed(sum(ref[...].astype(F32) for ref in in_refs))
            put("n0", unit)
        wait_all(waits[0])
        small = w.small()
        put("small", small)
        if first:
            x = unit * small[11:12] + small[12:13]
            x_low = x.astype(BF16)
            put("x", x_low)
        else:
            r0 = jnp.zeros((seq, 1), F32)
            x_low = in_refs[0][...]
            x = x_low.astype(F32)
        q = (w.project(x_low, 0).astype(BF16).astype(F32) * (1.0 / math.sqrt(head))).astype(BF16)
        k = w.project(x_low, 1).astype(BF16)
        v = (w.project(x_low, 2) + small[2:3]).astype(BF16)
        put("q", q)
        put("k", k)
        put("v", v)
        same = upright(row_ref[...], seq) == row_ref[...].astype(F32)
        second = iota((seq, 128), 1) >= head
        units = [(t, j) for t in range(d // 128) for j in range(2)]

        def scores_of(unit):
            t, j = unit
            lanes = slice(t * 128, (t + 1) * 128)
            picked = jnp.where(second == (j == 1), q[:, lanes], jnp.zeros((seq, 128), BF16))
            return nt(picked, k[:, lanes])

        tiles = []
        raw = scores_of(units[0])
        for n, (t, j) in enumerate(units):
            following = scores_of(units[n + 1]) if n + 1 < len(units) else None
            scores = jnp.where(same, raw, MASKED)
            scores = jnp.exp(scores - jnp.max(scores, axis=-1, keepdims=True))
            probs = (scores * (1.0 / jnp.sum(scores, axis=-1, keepdims=True))).astype(BF16)
            put("p", probs, n)
            result = nn(probs, v[:, t * 128 : (t + 1) * 128])
            if j == 0:
                kept = result
            else:
                tiles.append(jnp.where(second, result, kept).astype(BF16))
            raw = following
        attended = jnp.concatenate(tiles, axis=1)
        put("att", attended)
        unit, r1 = normed(x + (nn(attended, w.out()) + small[3:4]))
        put("n1", unit)
        middle = unit * small[0:1] + small[4:5]
        middle_low = middle.astype(BF16)
        put("mid", middle_low)
        wait_all(waits[1])
        back = [None] * (z.groups // 2)

        def pre_of(g):
            pair = slice((g // 2) * 2 * z.gw, (g // 2 + 1) * 2 * z.gw)
            return nn(middle_low[:, pair], w.fin(g))

        raw = pre_of(0)
        for g in range(z.groups):
            following = pre_of(g + 1) if g + 1 < z.groups else None
            pre = raw + small[5 + g : 6 + g]
            half = 0.5 + 0.5 * lax.erf(pre * math.sqrt(0.5))
            slope = half + pre * (jnp.exp(-0.5 * pre * pre) * (1.0 / math.sqrt(2.0 * math.pi)))
            active = (pre * half).astype(BF16)
            put("act", active, g)
            put("slope", slope, g)
            added = nn(active, w.fout(g))
            back[g // 2] = added if back[g // 2] is None else back[g // 2] + added
            raw = following
        unit, r2 = normed(middle + (jnp.concatenate(back, axis=1) + small[9:10]))
        put("n2", unit)
        put("out", unit * small[1:2] + small[10:11])
        lane = iota((seq, 128), 1)
        put("stats", jnp.where(lane == 0, r0, jnp.where(lane == 1, r1, r2)))
        stores.finish()

    outs = call(
        kernel,
        stores.shapes,
        (*pieces.arrays, seg_row, *inputs),
        specs=pieces.specs + [None] * (1 + len(inputs)),
        out_specs=stores.specs,
        scratch=pieces.scratch + stores.scratch,
        flops=12 * 10**9,
        name="layer_first" if first else "layer_second",
    )
    return dict(zip(stores.names, outs))


def send_halves(z, g_ref, keep_ref, send_ref, sems):
    core = lax.axis_index("dp") % 2
    shard = lax.axis_index("shard")
    copies = []
    for k in range(z.shards):
        to = (shard + k) % z.shards
        copies.append(pltpu.make_async_copy(g_ref.at[1 - core, to], send_ref.at[k], sems.at[2 * k]))
        copies.append(pltpu.make_async_copy(g_ref.at[core, to], keep_ref.at[k], sems.at[2 * k + 1]))
    for copy in copies:
        copy.start()
    return copies


def ffn_backward(z, pieces, state, out_grad):
    seq, d = out_grad[0].shape
    loads = Loads({**{f"dy{n}": term for n, term in enumerate(out_grad)}, **{key: state[key] for key in ("n2", "stats", "small", "mid", "act", "slope")}})
    outs = [like((seq, d), F32), like((16, d), F32)] + [like((z.shards, z.part, d), BF16)] * 2

    def kernel(*refs):
        piece_refs, refs = refs[: len(pieces.arrays)], refs[len(pieces.arrays) :]
        load_refs, refs = refs[: len(loads.names)], refs[len(loads.names) :]
        dm_ref, small_ref, keep_ref, send_ref, w_ref, sems, g_ref, out_sems, *buffers = refs
        loads.start(load_refs, buffers)
        waits = pieces.start(piece_refs, w_ref, sems, (1,))
        w = Weights(z, w_ref)
        dy = sum(loads[f"dy{n}"][...].astype(F32) for n in range(len(out_grad)))
        n2 = loads["n2"][...].astype(F32)
        scale = loads["stats"][:, 2:3]
        small = loads["small"][...]
        gain_two, shift_two = col_sum(dy * n2), col_sum(dy)
        d_final = norm_back(dy, n2, scale, small[1:2])
        d_ffn = d_final.astype(BF16)
        ffn_shift = col_sum(d_ffn.astype(F32))
        middle_t = loads["mid"][...].T
        act, slope = loads["act"], loads["slope"]
        wait_all(waits[1])
        pre_shift = []
        pair_back = [None] * (z.groups // 2)
        wide = 2 * z.gw

        def act_grad(g):
            p = g // 2
            return nt(d_ffn[:, p * wide : (p + 1) * wide], w.fout(g))

        raw = act_grad(0)
        for p in range(z.groups // 2):
            lanes = slice(p * wide, (p + 1) * wide)
            out_pair = d_ffn[:, lanes]
            back_pair = []
            for g in (2 * p, 2 * p + 1):
                following = act_grad(g + 1) if g + 1 < z.groups else None
                d_pre = (raw * slope[g].astype(F32)).astype(BF16)
                pre_shift.append(col_sum(d_pre.astype(F32)))
                back_pair.append(tn(act[g], out_pair))
                grad_in = nn(middle_t[g * z.gw : (g + 1) * z.gw], d_pre)
                g_ref[0, :, g * z.gi : (g + 1) * z.gi, :] = grad_in.astype(BF16).reshape(z.shards, z.gi, d)
                added = nt(d_pre, w.fin(g))
                pair_back[p] = added if pair_back[p] is None else pair_back[p] + added
                raw = following
            odd = iota(back_pair[0].shape, 1) >= z.gw
            both = jnp.where(odd, back_pair[1], back_pair[0]).astype(BF16)
            g_ref[1, :, :, lanes] = both.reshape(z.shards, z.part, wide)
        copies = send_halves(z, g_ref, keep_ref, send_ref, out_sems)
        dm_ref[...] = d_final + jnp.concatenate(pair_back, axis=1)
        blank = jnp.zeros((1, d), F32)
        small_ref[...] = jnp.concatenate(
            [blank, gain_two, blank, blank, blank, *pre_shift, ffn_shift, shift_two, jnp.zeros((5, d), F32)], axis=0
        )
        wait_all(copies)

    anywhere = pl.BlockSpec(memory_space=pl.ANY)
    return call(
        kernel,
        outs,
        (*pieces.arrays, *loads.arrays),
        specs=pieces.specs + loads.specs,
        out_specs=[pl.BlockSpec(memory_space=pltpu.VMEM)] * 2 + [anywhere] * 2,
        scratch=pieces.scratch + [pltpu.VMEM((2, z.shards, z.part, d), BF16), pltpu.SemaphoreType.DMA((2 * z.shards,))] + loads.scratch,
        flops=9 * 10**9,
        name="ffn_back",
    )


def attention_backward(z, pieces, state, d_middle, small_in, first, seg_row=None, pos_rows=0):
    seq, d = d_middle.shape
    head = d // HEADS
    keys = ["n1", "stats", "small", "att", "q", "k", "v", "p", "x"] + (["n0"] if first else [])
    loads = Loads({"dm": d_middle, **{key: state[key] for key in keys}, "grads": small_in, **({"seg": seg_row} if first else {})})
    rows = z.part + (2 * z.extra if first else 0)
    outs = [like((seq, d), F32), like((seq, d), BF16)] + [like((z.shards, rows, d), BF16)] * 2
    blocks = 2 * lax.axis_size("dp")
    if first:
        outs.append(like((blocks, d // blocks, seq), BF16))

    def kernel(*refs):
        piece_refs, refs = refs[: len(pieces.arrays)], refs[len(pieces.arrays) :]
        load_refs, refs = refs[: len(loads.names)], refs[len(loads.names) :]
        dx_ref, low_ref, keep_ref, send_ref = refs[:4]
        de_ref = refs[4] if first else None
        w_ref, sems, g_ref, out_sems, *buffers = refs[len(outs) :]
        loads.start(load_refs, buffers)
        waits = pieces.start(piece_refs, w_ref, sems, (0,))
        w = Weights(z, w_ref)
        d_middle = loads["dm"][...]
        n1 = loads["n1"][...].astype(F32)
        stats = loads["stats"][...]
        r0, r1 = stats[:, 0:1], stats[:, 1:2]
        small = loads["small"][...]
        gain_one, shift_one = col_sum(d_middle * n1), col_sum(d_middle)
        d_mid = norm_back(d_middle, n1, r1, small[0:1])
        d_branch = d_mid.astype(BF16)
        branch_shift = col_sum(d_branch.astype(F32))
        g_ref[0, :, 0 : z.part, :] = tn(loads["att"][...], d_branch).astype(BF16).reshape(z.shards, z.part, d)
        wait_all(waits[0])
        d_att = nt(d_branch, w.out()).astype(BF16)
        second = iota((seq, 128), 1) >= head
        scale = 1.0 / math.sqrt(head)
        q_ref, k_ref, v_ref, p_ref = (loads[key] for key in ("q", "k", "v", "p"))
        units = [(t, j) for t in range(d // 128) for j in range(2)]

        def probs_grad(unit):
            t, j = unit
            lanes = slice(t * 128, (t + 1) * 128)
            a_j = jnp.where(second == (j == 1), d_att[:, lanes], jnp.zeros((seq, 128), BF16))
            return nt(a_j, v_ref[:, lanes])

        dq, dk, dv = [], [], []
        raw = probs_grad(units[0])
        for n, (t, j) in enumerate(units):
            following = probs_grad(units[n + 1]) if n + 1 < len(units) else None
            lanes = slice(t * 128, (t + 1) * 128)
            probs_low = p_ref[n]
            probs = probs_low.astype(F32)
            inner = jnp.sum(probs * raw, axis=-1, keepdims=True)
            d_scores = (probs * (raw - inner)).astype(BF16)
            result = (nn(d_scores, k_ref[:, lanes]), tn(d_scores, q_ref[:, lanes]), tn(probs_low, d_att[:, lanes]))
            if j == 0:
                kept = result
            else:
                dq.append((jnp.where(second, result[0], kept[0]) * scale).astype(BF16))
                dk.append(jnp.where(second, result[1], kept[1]).astype(BF16))
                dv.append(jnp.where(second, result[2], kept[2]).astype(BF16))
            raw = following
        value_shift = col_sum(jnp.concatenate(dv, axis=1).astype(F32))
        x_t = loads["x"][...].T
        d_in = [d_mid[:, : 2 * z.gw], d_mid[:, 2 * z.gw :]]
        high = iota((z.gw, 2 * z.gw), 1) >= z.gw
        for c, parts in enumerate((dq, dk, dv)):
            d_c = jnp.concatenate(parts, axis=1)
            for p in range(z.groups // 2):
                lanes = slice(2 * p * z.gw, 2 * (p + 1) * z.gw)
                full = nn(x_t[lanes], d_c[:, lanes])
                grad = jnp.where(high, full[z.gw :], full[: z.gw]).astype(BF16)
                g_ref[1, :, c * z.gi : (c + 1) * z.gi, lanes] = grad.reshape(z.shards, z.gi, 2 * z.gw)
                d_in[p] = d_in[p] + nt(d_c[:, lanes], w.proj(c, p))
        d_in = jnp.concatenate(d_in, axis=1)
        blank = jnp.zeros((1, d), F32)
        embed_grads = [blank, blank]
        if first:
            n0 = loads["n0"][...].astype(F32)
            embed_grads = [col_sum(d_in * n0), col_sum(d_in)]
            d_embed = norm_back(d_in, n0, r0, small[11:12])
            d_embed_t = d_embed.T
            bits = blocks.bit_length() - 1
            me = lax.axis_index("section") * (blocks // 2) + lax.axis_index("dp")
            for b in range(blocks):
                to = me ^ b
                place = sum(((to >> bit) & 1) << (bits - 1 - bit) for bit in range(bits))
                de_ref[place] = d_embed_t[b * (d // blocks) : (b + 1) * (d // blocks)].astype(BF16)
            seg = loads["seg"][...]
            same = upright(seg, seq) == seg.astype(F32)
            later = iota((seq, seq), 0) < iota((seq, seq), 1)
            place = jnp.sum(jnp.where(same & later, 1.0, 0.0), axis=0, keepdims=True).astype(jnp.int32)
            spot = (iota((pos_rows, seq), 0) == place).astype(BF16)
            pos_grad = nn(spot, d_embed.astype(BF16)).astype(BF16)
        small_grads = jnp.concatenate([gain_one, blank, value_shift, branch_shift, shift_one, jnp.zeros((6, d), F32), *embed_grads, jnp.zeros((3, d), F32)], axis=0)
        small_grads = (small_grads + loads["grads"][...]).astype(BF16)
        if first:
            blank = jnp.zeros((z.extra - z.quarter, d), BF16)
            others = [pos_grad[z.pos + n * z.quarter : z.pos + (n + 1) * z.quarter] for n in range(4)]
        for h in range(z.shards):
            g_ref[1, h, z.at_small : z.at_small + 16, :] = small_grads
            spare = pos_grad[: z.pos] if first and h == 0 else jnp.zeros((z.pos, d), BF16)
            g_ref[1, h, z.at_small + 16 : z.part, :] = spare
            if first:
                for side in range(2):
                    for y in range(2):
                        row = z.part + y * z.extra
                        part = jnp.concatenate([others[2 * side + y].astype(F32), blank.astype(F32)], axis=0).astype(BF16) if h == 0 else jnp.zeros((z.extra, d), BF16)
                        g_ref[side, h, row : row + z.extra, :] = part
        copies = send_halves(z, g_ref, keep_ref, send_ref, out_sems)
        dx_ref[...] = d_in
        low_ref[...] = d_in.astype(BF16)
        wait_all(copies)

    anywhere = pl.BlockSpec(memory_space=pl.ANY)
    vmem = pl.BlockSpec(memory_space=pltpu.VMEM)
    return call(
        kernel,
        outs,
        (*pieces.arrays, *loads.arrays),
        specs=pieces.specs + loads.specs,
        out_specs=[vmem, vmem, anywhere, anywhere] + [vmem] * (len(outs) - 4),
        scratch=pieces.scratch + [pltpu.VMEM((2, z.shards, rows, d), BF16), pltpu.SemaphoreType.DMA((2 * z.shards,))] + loads.scratch,
        flops=13 * 10**9,
        name="att_back",
    )


def add_cores_split(z, keep, came):
    shards, part, d = keep[0].shape

    def kernel(a_ref, f_ref, b_ref, e_ref, c0, c1, c2a, c2b, c3):
        for k, ref in ((0, c0), (1, c1), (3, c3)):
            ref[:part] = a_ref[k] + b_ref[k]
            ref[part:] = f_ref[k] + e_ref[k]
        c2a[...] = a_ref[2] + b_ref[2]
        c2b[...] = f_ref[2] + e_ref[2]

    full, half = like((2 * part, d), BF16), like((part, d), BF16)
    return call(kernel, [full, full, half, half, full], (*keep, *came), limit=24, name="add_cores_split")


def halves_by_y(z, terms):
    def kernel(a_ref, b_ref, c_ref, keep_ref, send_ref):
        y = side_of(2)
        for ref, part in ((keep_ref, y), (send_ref, 1 - y)):
            span = pl.ds(pl.multiple_of(part * z.part, z.part), z.part)
            ref[...] = (a_ref[span].astype(F32) + b_ref[span].astype(F32) + c_ref[span].astype(F32)).astype(BF16)

    return call(kernel, [like((z.part, z.d), BF16)] * 2, terms, limit=8, name="halves_by_y")


def add_core(z, keep_a, came_a, keep_f, came_f):
    rows = z.part + z.extra

    def kernel(a_ref, b_ref, c_ref, e_ref, keep_ref, send_ref):
        y = side_of(2)

        def place(ref, part):
            if part == 0:
                ref[:, : z.part] = a_ref[:, : z.part] + b_ref[:, : z.part]
            else:
                ref[:, : z.part] = c_ref[...] + e_ref[...]
            span = slice(z.part + part * z.extra, z.part + (part + 1) * z.extra)
            ref[:, z.part :] = a_ref[:, span] + b_ref[:, span]

        @pl.when(y == 0)
        def _():
            place(keep_ref, 0)
            place(send_ref, 1)

        @pl.when(y == 1)
        def _():
            place(keep_ref, 1)
            place(send_ref, 0)

    return call(kernel, [like((z.shards, rows, z.d), BF16)] * 2, (keep_a, came_a, keep_f, came_f), limit=24, name="add_core")


def add_split(kept, came):
    _, rows, d = kept.shape
    half = rows // 32 * 16

    def kernel(a_ref, b_ref, c0, c1, c2a, c2b, c3):
        for k, ref in ((0, c0), (1, c1), (3, c3)):
            ref[...] = a_ref[k] + b_ref[k]
        c2a[...] = a_ref[2, :half] + b_ref[2, :half]
        c2b[...] = a_ref[2, half:] + b_ref[2, half:]

    full = like((rows, d), BF16)
    outs = [full, full, like((half, d), BF16), like((rows - half, d), BF16), full]
    return call(kernel, outs, (kept, came), limit=16, name="add_split")


def head_forward(pieces, table):
    count = sum(piece.shape[0] for piece in pieces)
    vocab, d = table.shape
    tiles = 3
    block = vocab // tiles
    part = block // 2
    chunk = 256
    many = len(pieces)

    def kernel(*refs):
        piece_refs, (w_ref, ctx_ref, lse_ref, x_ref, m_ref, s_ref, acc_ref) = refs[:many], refs[many:]
        step = pl.program_id(0)

        @pl.when(step == 0)
        def _():
            at = 0
            for ref in piece_refs:
                x_ref[at : at + ref.shape[0]] = ref[...]
                at += ref.shape[0]
            m_ref[...] = jnp.full(m_ref.shape, -1e30, F32)
            s_ref[...] = jnp.zeros(s_ref.shape, F32)
            acc_ref[...] = jnp.zeros(acc_ref.shape, F32)

        units = [(c, r) for c in range(2) for r in range(count // chunk)]

        def logits_of(unit):
            c, r = unit
            return nt(x_ref[r * chunk : (r + 1) * chunk], w_ref[c * part : (c + 1) * part])

        logits = logits_of(units[0])
        for n, (c, r) in enumerate(units):
            following = logits_of(units[n + 1]) if n + 1 < len(units) else None
            span = slice(r * chunk, (r + 1) * chunk)
            old = m_ref[span]
            new = jnp.maximum(old, jnp.max(logits, axis=-1, keepdims=True))
            keep = jnp.exp(old - new)
            weight = jnp.exp(logits - new)
            s_ref[span] = s_ref[span] * keep + jnp.sum(weight, axis=-1, keepdims=True)
            acc_ref[span] = acc_ref[span] * keep + nn(weight.astype(BF16), w_ref[c * part : (c + 1) * part])
            m_ref[span] = new
            logits = following

        @pl.when(step == tiles - 1)
        def _():
            total = s_ref[...]
            ctx_ref[...] = acc_ref[...] * (1.0 / total)
            lse = m_ref[...] + jnp.log(total)
            lse_ref[...] = jnp.broadcast_to(lse, (count, 128)).T[0:8]

    fixed = lambda i: (0, 0)
    return call(
        kernel,
        [like((count, d), F32), like((8, count), F32)],
        (*pieces, table),
        specs=[pl.BlockSpec(piece.shape, fixed) for piece in pieces] + [pl.BlockSpec((block, d), lambda i: (i, 0))],
        out_specs=[pl.BlockSpec((count, d), fixed), pl.BlockSpec((8, count), fixed)],
        scratch=[pltpu.VMEM((count, d), BF16), pltpu.VMEM((count, 1), F32), pltpu.VMEM((count, 1), F32), pltpu.VMEM((count, d), F32)],
        grid=(tiles,),
        flops=11 * 10**9,
        limit=36,
        name="head_forward",
    )


def head_combine(seq, ctxs, picked, ids_by, lses, vocab):
    shards = ids_by.shape[0]
    d = picked.shape[1]

    def kernel(x0_ref, x1_ref, x2_ref, x3_ref, p_ref, i_ref, a_ref, b_ref, c_ref, e_ref, *outs):
        lse_ref = outs[shards]
        shard = lax.axis_index("shard")
        parts = (a_ref, b_ref, c_ref, e_ref)
        for k in range(shards):
            rows = [parts[m][:, ((k - m) % shards) * seq : ((k - m) % shards + 1) * seq] for m in range(shards)]
            top = rows[0]
            for row in rows[1:]:
                top = jnp.maximum(top, row)
            total = top + jnp.log(sum(jnp.exp(row - top) for row in rows))
            whole = upright(total, seq)
            span = slice(k * seq, (k + 1) * seq)
            lse_ref[span] = whole
            weight = upright(jnp.exp(rows[0] - total), seq)
            local = i_ref[k, 1:2] - shard * vocab
            inside = upright(jnp.where((local >= 0) & (local < vocab), 1.0, 0.0), seq)
            hit = jnp.where(inside > 0.5, p_ref[span].astype(F32), 0.0)
            ctx = (x0_ref, x1_ref, x2_ref, x3_ref)[k][...]
            outs[k][...] = (ctx * weight - hit).astype(BF16)

    return call(
        kernel,
        [like((seq, d), BF16)] * shards + [like((shards * seq, 1), F32)],
        (*ctxs, picked, ids_by, *lses),
        limit=20, name="head_combine",
    )


def head_table(pieces, table, lse, ids_by, core=None):
    count = sum(piece.shape[0] for piece in pieces)
    shards, _, seq = ids_by[0].shape
    vocab, d = table.shape
    block = 1280
    tiles = pl.cdiv(vocab, block)
    shared = core is not None
    if shared:
        tiles = (tiles + 1) // 2
    else:
        core = jnp.zeros((1,), jnp.int32)
    chunk = 256
    many, groups = len(pieces), len(ids_by)
    wide = d // 8

    def kernel(core_ref, *refs):
        piece_refs, refs = refs[:many], refs[many:]
        w_ref, refs = refs[0], refs[1:]
        lse_refs, i_refs, refs = refs[:groups], refs[groups : 2 * groups], refs[2 * groups :]
        out_refs, (x_ref, xt_ref, t_ref, l_ref, p_ref) = refs[:-5], refs[-5:]
        step = pl.program_id(0)
        first_tile = core_ref[0] * tiles

        @pl.when(step == 0)
        def _():
            at = 0
            for ref in piece_refs:
                x_ref[at : at + ref.shape[0]] = ref[...]
                at += ref.shape[0]
            xt_ref[...] = x_ref[...].T
            start = lax.axis_index("shard") * vocab + first_tile * block
            for n in range(groups):
                for k in range(shards):
                    at = (n * shards + k) * seq
                    t_ref[at : at + seq] = upright(i_refs[n][k, 1:2] - start, seq).astype(jnp.int32)
                at = n * shards * seq
                l_ref[at : at + shards * seq] = lse_refs[n][...]

        w = w_ref[...]
        for r in range(count // chunk):
            span = slice(r * chunk, (r + 1) * chunk)
            logits = nt(x_ref[span], w)
            hit = iota(logits.shape, 1) == t_ref[span] - step * block
            p_ref[span] = (jnp.exp(logits - l_ref[span]) - jnp.where(hit, 1.0, 0.0)).astype(BF16)
        result = nn(xt_ref[...], p_ref[...]).astype(BF16)
        if not shared:
            out_refs[0][...] = result
            return
        zero = jnp.zeros((wide, block), jnp.int32)
        first = zero + lax.axis_index("section") == 0
        front = zero + side_of(2) == 0
        blocks = [result[n * wide : (n + 1) * wide] for n in range(8)]
        for n in range(2):
            low, high = blocks[2 * n], blocks[4 + 2 * n]
            out_refs[0][n], out_refs[1][n] = jnp.where(first, low, high), jnp.where(first, high, low)
            low, high = blocks[4 * n + 1], blocks[4 * n + 3]
            out_refs[2][n], out_refs[3][n] = jnp.where(front, low, high), jnp.where(front, high, low)

    if shared:
        outs = [like((2, wide, tiles * block), BF16)] * 4
        out_specs = [pl.BlockSpec((2, wide, block), lambda i, c: (0, 0, i))] * 4
    else:
        outs, out_specs = [like((d, vocab), BF16)], [pl.BlockSpec((d, block), lambda i, c: (0, i))]
    fixed = lambda i, c: (0, 0)
    return pl.pallas_call(
        kernel,
        out_shape=outs,
        grid_spec=pltpu.PrefetchScalarGridSpec(
            num_scalar_prefetch=1,
            grid=(tiles,),
            in_specs=[pl.BlockSpec(piece.shape, fixed) for piece in pieces]
            + [pl.BlockSpec((block, d), lambda i, c: (i + c[0] * tiles, 0))]
            + [pl.BlockSpec((shards * seq, 1), fixed)] * groups
            + [pl.BlockSpec(ids_by[0].shape, lambda i, c: (0, 0, 0))] * groups,
            out_specs=out_specs,
            scratch_shapes=[
                pltpu.VMEM((count, d), BF16),
                pltpu.VMEM((d, count), BF16),
                pltpu.VMEM((count, 1), jnp.int32),
                pltpu.VMEM((count, 1), F32),
                pltpu.VMEM((count, block), BF16),
            ],
        ),
        compiler_params=pltpu.CompilerParams(vmem_limit_bytes=58 * MIB),
        cost_estimate=pl.CostEstimate(flops=32 * 10**9, bytes_accessed=0, transcendentals=0),
        name="head_table",
    )(core, *pieces, table, *lse, *ids_by)


def add_halves(even, odd):
    shape = even[0].shape[1:]

    def kernel(a_ref, b_ref, c_ref, e_ref, *outs):
        for n, (one, two, side) in enumerate(((a_ref, b_ref, side_of(2)), (c_ref, e_ref, lax.axis_index("section")))):
            outs[2 * n][...] = one[side] + two[side]
            outs[2 * n + 1][...] = one[1 - side] + two[1 - side]

    return call(kernel, [like(shape, BF16)] * 4, (*even, *odd), limit=32, name="add_halves")


def add_last(even, odd):
    def kernel(a_ref, b_ref, c_ref, e_ref, own_ref, send_ref):
        first = (jnp.zeros(a_ref.shape, jnp.int32) + side_of(1)) == 0
        low, high = a_ref[...] + b_ref[...], c_ref[...] + e_ref[...]
        own_ref[...] = jnp.where(first, low, high)
        send_ref[...] = jnp.where(first, high, low)

    return call(kernel, [like(even[0].shape, BF16)] * 2, (*even, *odd), limit=16, name="add_last")


def list_tokens(ids, vocab):
    count = ids.shape[1]
    unit = 1 << (vocab - 1).bit_length()

    def kernel(ids_ref, list_ref):
        start = lax.axis_index("shard") * vocab

        def step(i, many):
            local = ids_ref[0, i] - start
            list_ref[0, many] = i * unit + local
            return many + ((local >= 0) & (local < vocab)).astype(jnp.int32)

        list_ref[0, count] = lax.fori_loop(0, count, step, jnp.int32(0), unroll=8)

    smem = pl.BlockSpec(memory_space=pltpu.SMEM)
    return call(kernel, [like((1, count + 128), jnp.int32)], (ids,), specs=[smem], out_specs=[smem], limit=4, name="list_tokens")[0]


def table_grad(dense, pieces, lists, vocab):
    width = pieces[0].shape[1]
    arrays = dense
    sources, _, seq = pieces[0].shape
    shards = 4
    listed = shards * seq
    line = lists.shape[1]
    unit = 1 << (vocab - 1).bit_length()
    ways, each = 4, 4
    rows = (lists & (unit - 1)).reshape(-1)
    tokens = ((lists >> (unit.bit_length() - 1)) + listed * jnp.arange(sources, dtype=jnp.int32)[:, None]).reshape(-1)
    counts = lists[:, listed]

    def kernel(*refs):
        d_refs, refs = refs[: len(arrays)], refs[len(arrays) :]
        own_ref, later_ref, before_ref, far_a_ref, far_b_ref, r_ref, t_ref, n_ref, o_ref, flat_ref, *acc = refs
        half = sources // 2
        for j in range(sources):
            far = far_a_ref[j] if j < half else far_b_ref[j - half]
            for k, block in enumerate((own_ref[j], later_ref[j], before_ref[j], far)):
                at = j * listed + k * seq
                flat_ref[at : at + seq] = block.astype(F32).T
        for ref in acc:
            ref[...] = jnp.zeros(ref.shape, F32)

        def source(j, carry):
            many = n_ref[j]
            rounds = many // (ways * each)

            def step(i, carry):
                at = j * line + i * ways * each
                place = [r_ref[at + n] for n in range(ways * each)]
                value = [flat_ref[pl.ds(t_ref[at + n], 1), :] for n in range(ways * each)]
                for n in range(each):
                    old = [ref[pl.ds(place[n * ways + way], 1), :] for way, ref in enumerate(acc)]
                    for way, ref in enumerate(acc):
                        ref[pl.ds(place[n * ways + way], 1), :] = old[way] + value[n * ways + way]
                return carry

            def rest(at, carry):
                acc[0][pl.ds(r_ref[j * line + at], 1), :] += flat_ref[pl.ds(t_ref[j * line + at], 1), :]
                return carry

            lax.fori_loop(0, rounds, step, jnp.int32(0))
            lax.fori_loop(rounds * ways * each, many, rest, jnp.int32(0))
            return carry

        lax.fori_loop(0, sources, source, jnp.int32(0))
        if len(d_refs) == 1:
            o_ref[...] = d_refs[0][...].astype(F32) + sum(ref[...] for ref in acc).T
            return
        half = d_refs[0].shape[1]
        first = (jnp.zeros((width, half), jnp.int32) + side_of(1)) == 0
        own, other = d_refs[0][...], d_refs[1][...]
        o_ref[:, :half] = jnp.where(first, own, other).astype(F32) + sum(ref[:half] for ref in acc).T
        last = jnp.where(first, other, own)[:, : vocab - half]
        o_ref[:, half:] = last.astype(F32) + sum(ref[half:] for ref in acc).T

    smem = pl.BlockSpec(memory_space=pltpu.SMEM)
    return call(
        kernel,
        [like((width, vocab), F32)],
        (*arrays, *pieces, rows, tokens, counts),
        specs=[None] * (len(arrays) + 5) + [smem] * 3,
        scratch=[pltpu.VMEM((sources * listed, width), F32)] + [pltpu.VMEM((vocab, width), F32)] * ways,
        limit=60,
        name="table_grad",
    )[0]


def unpack_grads(z, blocks):
    rows = z.part + z.extra
    pos_rows = z.pos + 4 * z.quarter

    def kernel(own_ref, y_ref, core_ref, both_ref, qkv_ref, out_ref, fin_ref, fout_ref, gain_ref, bias_ref, pos_ref, eg_ref, es_ref, all_ref):
        core, y = side_of(1), side_of(2)
        shard = lax.axis_index("shard")
        all_ref[core, y] = own_ref[...]
        all_ref[core, 1 - y] = y_ref[...]
        all_ref[1 - core, y] = core_ref[...]
        all_ref[1 - core, 1 - y] = both_ref[...]

        def own_lanes(value):
            total = jnp.zeros((value.shape[0], z.part), F32)
            for h in range(z.shards):
                total = total + jnp.where(shard == h, value[:, h * z.part : (h + 1) * z.part], 0.0)
            return total

        out_ref[...] = all_ref[0, 0, : z.part].astype(F32)
        fin_ref[...] = all_ref[0, 1, : z.part].astype(F32).reshape(z.groups, z.gi, z.d)
        for c in range(3):
            part = all_ref[1, 0, c * z.gi : (c + 1) * z.gi].astype(F32)
            for g in range(z.groups):
                qkv_ref[c, g] = part[:, g * z.gw : (g + 1) * z.gw]
        part = all_ref[1, 1, : z.part].astype(F32)
        for g in range(z.groups):
            fout_ref[g] = part[:, g * z.gw : (g + 1) * z.gw]
        small = own_lanes(all_ref[1, 0, z.at_small : z.at_small + 16].astype(F32))
        for n in range(9):
            bias_ref[n] = small[2 + n : 3 + n]
        gain_ref[...] = small[0:2]
        eg_ref[...] = small[11:12]
        es_ref[...] = small[12:13]
        pos_ref[: z.pos] = all_ref[1, 0, z.at_small + 16 : z.part].astype(F32)
        for n in range(4):
            row = z.pos + n * z.quarter
            pos_ref[row : row + z.quarter] = all_ref[n // 2, n % 2, z.part :].astype(F32)[: z.quarter]

    return call(
        kernel,
        [
            like((3, z.groups, z.gi, z.gw), F32),
            like((z.part, z.d), F32),
            like((z.groups, z.gi, z.d), F32),
            like((z.groups, z.part, z.gw), F32),
            like((2, z.part), F32),
            like((9, 1, z.part), F32),
            like((pos_rows, z.d), F32),
            like((1, z.part), F32),
            like((1, z.part), F32),
        ],
        blocks,
        scratch=[pltpu.VMEM((2, 2, rows, z.d), BF16)],
        limit=16, name="unpack",
    )


def body(token_ids, targets, segment_ids, word_table, pos_table, embed_gain, embed_shift, qkv_weight, out_weight, ffn_in, ffn_out, layer_gains, layer_biases):
    micro, _, seq = token_ids.shape
    vocab, d = word_table.shape
    pos_rows = pos_table.shape[0]
    shards = lax.axis_size("shard")
    dp = lax.axis_size("dp")
    both = ("section", "dp")
    section = lax.axis_index("section")
    first = section == 0
    z = Sizes(qkv_weight.shape, out_weight.shape, shards, pos_rows)
    offset = lax.axis_index("shard") * vocab

    local, pair, packed = pack_weights(
        z, qkv_weight[0], out_weight[0], ffn_in[0], ffn_out[0], layer_gains[0], layer_biases[0], embed_gain, embed_shift
    )

    mine = lax.dynamic_index_in_dim(jnp.stack([token_ids[:, 0], targets[:, 0], segment_ids[:, 0]], axis=1), section, 0, keepdims=False)
    mine = after(mine, packed)
    ids_by = jnp.stack([mine, turned(mine, "shard", -1), turned(mine, "shard", 2), turned(mine, "shard", 1)])
    seg_row = mine[2:3]

    def rows_of(ids):
        return word_table.at[jnp.clip(ids.reshape(-1) - offset, 0, vocab - 1)].get(mode="promise_in_bounds")

    cross_pair = crossed(pair, "section", 1)
    near = gather_first(packed, "shard")
    picked = rows_of(ids_by[:, 0])
    near, pos_table = after((near, pos_table), near)
    word_parts = embed_parts(picked, ids_by, pos_table, vocab)
    near = after(near, word_parts)
    c0, c1, c2a, c2b, c3 = word_parts
    half, quarter = seq // 2, z.part // 2
    right = jnp.concatenate([c2a, near[0][:quarter]], axis=0)
    left = jnp.concatenate([c2b, near[1][quarter:]], axis=0)
    near_rows = jnp.concatenate(after(near, (right, left)), axis=0)
    right, left = turned(right, "shard", 1), turned(left, "shard", -1)
    near_y = crossed(near_rows, "dp", 2)
    cross_near = crossed(near_rows, "section", 1)
    target_rows = rows_of(after(ids_by[:, 1], near_rows))
    right, left = after((right, left), target_rows)
    c1 = jnp.concatenate([c1[:half] + right[:half], c1[half:]], axis=0)
    c3 = jnp.concatenate([c3[:half], c3[half:] + left[:half]], axis=0)
    words = scatter_second(c0, c1, c3, "shard")
    near_y = after(near_y, words)
    far = jnp.concatenate([right[half:], left[half:]], axis=0)
    cross_far = crossed(far, "section", 1)
    both_y = crossed(jnp.concatenate([far, cross_near], axis=0), "dp", 2)
    far_y, cross_near_y = both_y[: z.part], both_y[z.part :]
    cross_far_y = crossed(cross_far, "dp", 2)
    mine = (near_rows, far)
    mine = (*mine, *(crossed(b, "dp", 1) for b in mine), near_y, far_y, crossed(near_y, "dp", 1), crossed(far_y, "dp", 1))
    others = (cross_near, cross_far)
    others = (*others, *(crossed(b, "dp", 1) for b in others))
    others = (*others, cross_near_y, cross_far_y, crossed(cross_near_y, "dp", 1), crossed(cross_far_y, "dp", 1))
    pairs = (cross_pair, crossed(cross_pair, "dp", 1))
    weights_one, weights_two = (Pieces(z, local, mine, pairs, others, layer) for layer in range(2))
    one = layer_forward(z, weights_one, seg_row, True, words=words)
    two = layer_forward(z, weights_two, seg_row, False, layer_in=one["out"])
    two["x"] = one["out"]

    own_out = jnp.where(first, one["out"], two["out"])
    came_out = crossed(jnp.where(first, two["out"], one["out"]), "section", 1)

    before, later = gather_first(two["out"], "shard")
    ctx_own, lse_own = head_forward([two["out"]], word_table)
    before = after(before, ctx_own)
    far_a = turned(before[: seq // 2], "shard", 1)
    ctx_before, lse_before = head_forward([before], word_table)
    later = after(later, ctx_before)
    far_b = turned(later[seq // 2 :], "shard", -1)
    ctx_later, lse_later = head_forward([later], word_table)
    far_a, far_b = after((far_a, far_b), ctx_later)
    ctx_far, lse_far = head_forward([far_a, far_b], word_table)
    lse = jnp.concatenate([lse_own[0:1], lse_later[0:1], lse_far[0:1], lse_before[0:1]], axis=1)
    listed = jnp.stack([ids_by[0, 0], ids_by[1, 0], ids_by[3, 0], ids_by[2, 0]]).reshape(1, -1)
    lses = (lse, turned(lse, "shard", -1), turned(lse, "shard", 2), turned(lse, "shard", 1))
    lses = after(lses, came_out)
    *parts, whole_lse = head_combine(seq, (ctx_own, ctx_later, ctx_far, ctx_before), target_rows, ids_by, lses, vocab)
    head_rows = [two["out"], later, far_a, far_b, before]
    dy_terms = direct_scatter(parts, "shard")
    if dp == 4:
        rows_other, ids_other, lse_other = [crossed(row, "dp", 1) for row in head_rows], crossed(ids_by, "dp", 1), crossed(whole_lse, "dp", 1)
        core = side_of(1).astype(jnp.int32).reshape(1)
        stay_x, leave_x, stay_y, leave_y = head_table([*head_rows, *rows_other], word_table, [whole_lse, lse_other], [ids_by, ids_other], core)
        came_x, came_y = crossed(leave_x, "section", 1), crossed(leave_y, "dp", 2)
        dy_terms = after(dy_terms, stay_x)
    else:
        dense = head_table(head_rows, word_table, [whole_lse], [ids_by])[0]
        dense = [lax.psum_scatter(dense, both, scatter_dimension=0, tiled=True)]
    d_middle, small_grads, keep_f, send_f = ffn_backward(z, weights_two, two, dy_terms)

    in_two, in_low, keep_a, send_a = attention_backward(z, weights_two, two, d_middle, small_grads, False)
    came_f, came_a = crossed(send_f, "dp", 1), crossed(send_a, "dp", 1)
    d_middle, small_grads, keep_one_f, send_one_f = ffn_backward(z, weights_one, one, [in_low])
    keep_f, came_f, keep_a, came_a = after((keep_f, came_f, keep_a, came_a), d_middle)
    split_two = add_cores_split(z, (keep_a, keep_f), (came_a, came_f))
    d_middle = after(d_middle, split_two)
    terms_two = scatter_first(*split_two, "shard")
    if dp == 4:
        d_middle, came_x, came_y = after((d_middle, came_x, came_y), ())
    came_one_f = crossed(send_one_f, "dp", 1)
    in_one, in_one_low, keep_one_a, send_one_a, d_embed = attention_backward(z, weights_one, one, d_middle, small_grads, True, seg_row, pos_rows)
    keep_one_f, came_one_f = after((keep_one_f, came_one_f), d_embed)
    send_one_a, d_embed = after((send_one_a, d_embed), terms_two)
    came_one_a = crossed(send_one_a, "dp", 1)
    columns = d_embed[None]
    steps = [("dp", 1 << n) for n in range(dp.bit_length() - 1)]
    for n, (axis, bit) in enumerate(steps):
        middle = columns.shape[1] // 2
        columns = jnp.concatenate([columns[:, :middle], crossed(columns[:, middle:], axis, bit)], axis=0)
        if n == 0:
            came_one_a = after(came_one_a, columns)
    second_two = scatter_second(*terms_two, "shard")
    stay_one, leave_one = add_core(z, keep_one_a, came_one_a, keep_one_f, came_one_f)
    came_one = crossed(after(leave_one, columns), "dp", 2)
    columns = after(columns, (stay_one, second_two))
    columns = jnp.concatenate([columns[:, 0], crossed(columns[:, 1], "section", 1)], axis=0)
    ring_columns = gather_first(columns, "shard")
    own_in = jnp.where(first, in_one, in_two)
    came_in = crossed(jnp.where(first, in_two, in_one).astype(BF16), "section", 1)
    stay_two, leave_two = halves_by_y(z, after(second_two, (columns, stay_one)))
    came_two = crossed(leave_two, "dp", 2)
    if dp == 4:
        stay_x, leave_x, stay_y, leave_y = add_halves(*after(((stay_x, came_x), (stay_y, came_y)), stay_two))
        last_x, last_y = crossed(leave_x, "dp", 2), crossed(leave_y, "section", 1)
    lists = list_tokens(after(listed, columns), vocab)
    bit = 1
    while bit < dp:
        lists = jnp.concatenate([lists, crossed(lists, "dp", bit)], axis=0)
        bit *= 2
    lists = jnp.concatenate([lists, crossed(lists, "section", 1)], axis=0)
    ring_columns = after(ring_columns, stay_two)
    far_columns = gather_second(*ring_columns, "shard")
    terms_one = scatter_first(*add_split(stay_one, after(came_one, (ring_columns, came_in))), "shard")
    second_one = scatter_second(*terms_one, "shard")
    if dp == 4:
        own_dense, send_dense = add_last(*after(((stay_x, last_x), (stay_y, last_y)), second_one[1]))
        dense = [own_dense, crossed(send_dense, "dp", 1)]
    word_grad = table_grad(dense, (columns, ring_columns[1], ring_columns[0], *far_columns), lists, vocab)
    sum_two = stay_two + came_two
    sum_one = sum(after(second_one, sum_two))
    layer_one, extra = sum_one[: z.part], sum_one[z.part :]
    row = jnp.arange(z.part)[:, None]
    embed_rows = (row >= z.at_small + 11) & (side_of(1) == 1) & (side_of(2) == 0)
    layer_two = jnp.where(embed_rows, layer_one, sum_two)
    total = jnp.concatenate([jnp.where(first, layer_one, layer_two), extra], axis=0)
    came = crossed(jnp.concatenate([jnp.where(first, layer_two, layer_one), extra], axis=0), "section", 1)
    total = total + after(came, word_grad)
    bit = 4
    while bit < dp:
        total = total + crossed(total, "dp", bit)
        bit *= 2
    total_y = crossed(total, "dp", 2)
    def by_micro(own, came):
        return jnp.stack([jnp.where(first, own, came), jnp.where(first, came, own)]).reshape(1, micro, 1, seq, d)

    layer_outputs = by_micro(own_out, came_out)
    input_grads = by_micro(own_in, came_in.astype(F32))
    total_y = after(total_y, (layer_outputs, input_grads))
    unpacked = unpack_grads(z, (total, total_y, crossed(total, "dp", 1), crossed(total_y, "dp", 1)))

    word_grad = word_grad.T

    qkv_g, out_g, fin_g, fout_g, gain_g, bias_g, pos_g, eg_g, es_g = unpacked
    return (
        layer_outputs,
        input_grads,
        word_grad,
        pos_g,
        eg_g.reshape(-1),
        es_g.reshape(-1),
        qkv_g[None],
        out_g[None],
        fin_g[None],
        fout_g[None],
        gain_g[None],
        bias_g.transpose(1, 0, 2),
    )


def solution(mesh):
    rows = P(None, ("dp", "shard"), None)
    weights = (
        P("section", None, None, "shard", None),
        P("section", "shard", None),
        P("section", None, "shard", None),
        P("section", None, "shard", None),
        P("section", None, "shard"),
        P("section", None, "shard"),
    )
    states = P("section", None, ("dp", "shard"), None, None)
    return jax.shard_map(
        body,
        mesh=mesh,
        in_specs=(rows, rows, rows, P("shard", None), P("shard", None), P("shard"), P("shard"), *weights),
        out_specs=(states, states, P("shard", ("section", "dp")), P("shard", None), P("shard"), P("shard"), *weights),
        check_vma=False,
    )
```

```python
import math

import jax
import jax.numpy as jnp
from jax import lax
from jax.experimental import pallas as pl
from jax.experimental.pallas import tpu as pltpu
from jax.sharding import PartitionSpec as P

HEADS = 12
EPSILON = 1e-06
MASKED = -1000000000.0
F32 = jnp.float32
BF16 = jnp.bfloat16
MIB = 1 << 20


def nn(a, b):
    return jnp.dot(a, b, preferred_element_type=F32)


def nt(a, b):
    return lax.dot_general(a, b, (((1,), (1,)), ((), ())), preferred_element_type=F32)


def tn(a, b):
    return lax.dot_general(a, b, (((0,), (0,)), ((), ())), preferred_element_type=F32)


def iota(shape, axis):
    return lax.broadcasted_iota(jnp.int32, shape, axis)


def group_of(index, width, count):
    total = jnp.zeros(index.shape, jnp.int32)
    for step in range(1, count):
        total = total + (index >= step * width).astype(jnp.int32)
    return total


def normed(value):
    centered = value - jnp.mean(value, axis=-1, keepdims=True)
    scale = lax.rsqrt(jnp.mean(centered * centered, axis=-1, keepdims=True) + EPSILON)
    return centered * scale, scale


def norm_back(grad, unit, scale, gain):
    inner = grad * gain
    first = jnp.mean(inner, axis=-1, keepdims=True)
    second = jnp.mean(inner * unit, axis=-1, keepdims=True)
    return scale * (inner - first - unit * second)


def col_sum(value):
    return jnp.sum(value, axis=0, keepdims=True)


def upright(row, count):
    return jnp.broadcast_to(row.astype(F32), (128, count)).T[:, 0:1]


def call(kernel, outs, ins, specs=None, scratch=(), limit=56, flops=0, moved=0, grid=None, out_specs=None, name=None):
    vmem = pl.BlockSpec(memory_space=pltpu.VMEM)
    extra = {} if grid is None else {"grid": grid}
    return pl.pallas_call(
        kernel,
        out_shape=outs,
        in_specs=[vmem if s is None else s for s in (specs or [None] * len(ins))],
        out_specs=out_specs if out_specs is not None else [vmem] * len(outs),
        scratch_shapes=list(scratch),
        compiler_params=pltpu.CompilerParams(vmem_limit_bytes=limit * MIB),
        cost_estimate=pl.CostEstimate(flops=flops, bytes_accessed=0, transcendentals=0),
        name=name,
        **extra,
    )(*ins)


def like(shape, dtype):
    return jax.ShapeDtypeStruct(shape, dtype)


def turned(block, axis, by):
    size = lax.axis_size(axis)
    return lax.ppermute(block, axis, [(i, (i + by) % size) for i in range(size)])


def crossed(block, axis, bit):
    return lax.ppermute(block, axis, [(i, i ^ bit) for i in range(lax.axis_size(axis))])


def after(value, first):
    return lax.optimization_barrier((value, first))[0]


def scatter_first(c0, c1, c2a, c2b, c3, axis, wait=()):
    half = c2a.shape[0]
    right, left = after((turned(c2a, axis, 1), turned(c2b, axis, -1)), wait)
    return c0, jnp.concatenate([c1[:half] + right, c1[half:]], axis=0), jnp.concatenate([c3[:half], c3[half:] + left], axis=0)


def scatter_second(c0, c1, c3, axis):
    return c0, turned(c1, axis, 1), turned(c3, axis, -1)


def side_of(bit):
    return (lax.axis_index("dp") // bit) % 2


def direct_scatter(parts, axis):
    return parts[0], turned(parts[1], axis, 1), turned(parts[3], axis, -1), turned(parts[2], axis, 2)


def gather_first(block, axis):
    return turned(block, axis, 1), turned(block, axis, -1)


def gather_second(before, later, axis):
    half = before.shape[0] // 2
    return turned(before[:half], axis, 1), turned(later[half:], axis, -1)


def ring_gather(block, axis):
    first = gather_first(block, axis)
    return (*first, *gather_second(*first, axis))


class Sizes:
    def __init__(self, qkv, out, shards, pos_rows):
        _, _, groups, part, width = qkv
        self.shards, self.groups, self.gw, self.gi = shards, groups, width, part
        self.d = out[2]
        self.part = out[1]
        self.at_small = 3 * part
        self.rows = 2 * self.part
        self.pos = self.part - self.at_small - 16
        self.quarter = (pos_rows - self.pos) // 4
        self.extra = -(-self.quarter // 16) * 16


def pack_weights(z, qkv, out, fin, fout, gains, biases, egain, eshift):
    def kernel(qkv_ref, out_ref, fin_ref, fout_ref, gain_ref, bias_ref, eg_ref, es_ref, o_ref, pair_ref, own_ref):
        shard = lax.axis_index("shard")

        def spread(pieces):
            return jnp.concatenate([piece.astype(F32) for piece in pieces], axis=1).astype(BF16)

        o_ref[0, 0] = out_ref[...]
        o_ref[0, 1] = fin_ref[...].reshape(z.part, z.d)
        for c in range(3):
            o_ref[1, 0, c * z.gi : (c + 1) * z.gi] = spread([qkv_ref[c, g] for g in range(z.groups)])
        embed = [ref[...].astype(F32).reshape(1, z.part) for ref in (eg_ref, es_ref)]
        tall = jnp.concatenate([gain_ref[...].astype(F32), bias_ref[...].astype(F32), *embed, jnp.zeros((3, z.part), F32)], axis=0)
        wide = jnp.concatenate([tall] * z.shards, axis=1)
        lane = group_of(iota(wide.shape, 1), z.part, z.shards)
        o_ref[1, 0, z.at_small : z.at_small + 16] = jnp.where(lane == shard, wide, 0.0).astype(BF16)
        o_ref[1, 0, z.at_small + 16 : z.part] = jnp.zeros((z.part - z.at_small - 16, z.d), BF16)
        o_ref[1, 1] = spread([fout_ref[g] for g in range(z.groups)])
        pair_ref[...] = o_ref[side_of(1)]
        own_ref[...] = o_ref[side_of(1), side_of(2)]

    outs = [like((2, 2, z.part, z.d), BF16), like((2, z.part, z.d), BF16), like((z.part, z.d), BF16)]
    return call(kernel, outs, (qkv, out, fin, fout, gains, biases, egain, eshift), name="pack")


class Pieces:
    def __init__(self, z, local, mine, pairs, others, layer):
        self.z, self.layer = z, layer
        self.arrays = (local, *mine, *pairs, *others)
        self.specs = [pl.BlockSpec(memory_space=pl.ANY)] * len(self.arrays)
        self.scratch = [pltpu.VMEM((2, z.shards, z.rows, z.d), BF16), pltpu.SemaphoreType.DMA((2, 2, 4))]

    def start(self, refs, w_ref, sems, parts):
        z = self.z
        core, y = side_of(1), side_of(2)
        shard = lax.axis_index("shard")
        own_layer = lax.axis_index("section") == self.layer
        local, mine, pairs, others = refs[0], refs[1:9], refs[9:11], refs[11:19]
        waits = {}
        for part in parts:
            copies = []
            for side in range(2):
                place = core if side == 0 else 1 - core
                for n, by in enumerate((0, 3, 1, 2)):
                    target = w_ref.at[place, (shard + by) % z.shards, pl.ds(part * z.part, z.part)]
                    sem = sems.at[part, side, n]
                    rows = pl.ds((n - 1) * z.part, z.part)
                    choices = []
                    for across in range(2):
                        here = (y == part) if across == 0 else (y != part)
                        at = 2 * across + side
                        if n == 0:
                            own, other = local.at[place, part], pairs[side].at[part]
                        elif n < 3:
                            own, other = mine[2 * at].at[rows], others[2 * at].at[rows]
                        else:
                            own, other = mine[2 * at + 1], others[2 * at + 1]
                        choices.append((jnp.logical_and(here, own_layer), own))
                        choices.append((jnp.logical_and(here, jnp.logical_not(own_layer)), other))
                    for here, source in choices:
                        copy = pltpu.make_async_copy(source, target, sem)
                        pl.when(here)(copy.start)
                    copies.append(pltpu.make_async_copy(choices[1][1], target, sem))
            waits[part] = copies
        return waits


def wait_all(copies):
    for copy in copies:
        copy.wait()


class Loads:
    def __init__(self, arrays):
        self.names = list(arrays)
        self.arrays = list(arrays.values())
        self.specs = [pl.BlockSpec(memory_space=pl.ANY)] * len(self.arrays)
        self.scratch = [pltpu.VMEM(a.shape, a.dtype) for a in self.arrays] + [pltpu.SemaphoreType.DMA((len(self.arrays),))]

    def start(self, refs, scratch):
        self.buffers = dict(zip(self.names, scratch))
        self.copies = {
            name: pltpu.make_async_copy(ref, buffer, scratch[-1].at[n])
            for n, (name, ref, buffer) in enumerate(zip(self.names, refs, scratch))
        }
        for copy in self.copies.values():
            copy.start()

    def __getitem__(self, name):
        copy = self.copies.pop(name, None)
        if copy is not None:
            copy.wait()
        return self.buffers[name]


class Stores:
    def __init__(self, shapes, split=()):
        self.names = list(shapes)
        self.shapes = list(shapes.values())
        self.split = split
        self.specs = [pl.BlockSpec(memory_space=pl.ANY)] * len(self.shapes)
        count = sum(a.shape[0] if name in split else 1 for name, a in shapes.items())
        self.scratch = [pltpu.VMEM(a.shape, a.dtype) for a in self.shapes] + [pltpu.SemaphoreType.DMA((count,))]

    def bind(self, refs, scratch):
        self.refs = dict(zip(self.names, refs))
        self.buffers = dict(zip(self.names, scratch))
        self.sems = scratch[-1]
        self.copies = []

    def put(self, name, value, index=None):
        source = self.buffers[name] if index is None else self.buffers[name].at[index]
        source[...] = value.astype(source.dtype)
        self.send(name, index)

    def send(self, name, index=None):
        source, target = self.buffers[name], self.refs[name]
        if index is not None:
            source, target = source.at[index], target.at[index]
        copy = pltpu.make_async_copy(source, target, self.sems.at[len(self.copies)])
        copy.start()
        self.copies.append(copy)

    def finish(self):
        wait_all(self.copies)


class Weights:
    def __init__(self, z, w_ref):
        self.z, self.w = z, w_ref

    def out(self):
        z = self.z
        return self.w[0, :, 0 : z.part, :].reshape(z.d, z.d)

    def small(self):
        z = self.z
        return sum(self.w[1, h, z.at_small : z.at_small + 16, :].astype(F32) for h in range(z.shards))

    def proj(self, c, p):
        z = self.z
        lanes = slice(2 * p * z.gw, 2 * (p + 1) * z.gw)
        dense = self.w[1, :, c * z.gi : (c + 1) * z.gi, lanes].reshape(z.gw, 2 * z.gw)
        high = iota(dense.shape, 1) >= z.gw
        blank = jnp.zeros_like(dense)
        return jnp.concatenate([jnp.where(high, blank, dense), jnp.where(high, dense, blank)], axis=0)

    def project(self, value, c):
        z = self.z
        wide = 2 * z.gw
        return jnp.concatenate([nn(value[:, p * wide : (p + 1) * wide], self.proj(c, p)) for p in range(z.groups // 2)], axis=1)

    def fin(self, g):
        z = self.z
        row = z.part + g * z.gi
        dense = self.w[0, :, row : row + z.gi, :].reshape(z.gw, z.d)
        blank = jnp.zeros_like(dense)
        return jnp.concatenate([dense, blank] if g % 2 == 0 else [blank, dense], axis=0)

    def fout(self, g):
        z = self.z
        at = (g // 2) * 2 * z.gw
        pair = self.w[1, :, z.part : z.rows, at : at + 2 * z.gw].reshape(z.d, 2 * z.gw)
        keep = (iota(pair.shape, 1) >= z.gw) == (g % 2 == 1)
        return jnp.where(keep, pair, jnp.zeros_like(pair))


def embed_parts(picked, ids_by, pos_table, vocab):
    count, _, seq = ids_by.shape
    width = picked.shape[1]
    half = seq // 2
    rows = pos_table.shape[0]

    def kernel(p_ref, i_ref, t_ref, c0, c1, c2a, c2b, c3):
        shard = lax.axis_index("shard")
        for k in range(count):
            span = slice(k * seq, (k + 1) * seq)
            token, seg_row = i_ref[k, 0:1], i_ref[k, 2:3]
            seg_col = upright(seg_row, seq)
            same = seg_col == seg_row.astype(F32)
            earlier = iota((seq, seq), 1) < iota((seq, seq), 0)
            place = jnp.sum(jnp.where(same & earlier, 1.0, 0.0), axis=1, keepdims=True).astype(jnp.int32) - shard * rows
            spot = (iota((seq, rows), 1) == place).astype(BF16)
            local = token - shard * vocab
            inside = upright(jnp.where((local >= 0) & (local < vocab), 1.0, 0.0), seq)
            word = jnp.where(inside > 0.5, p_ref[span].astype(F32), 0.0)
            total = (word + nn(spot, t_ref[...])).astype(BF16)
            if k == 2:
                c2a[...] = total[:half]
                c2b[...] = total[half:]
            else:
                (c0, c1, None, c3)[k][...] = total

    full, part = like((seq, width), BF16), like((half, width), BF16)
    return call(kernel, [full, full, part, part, full], (picked, ids_by, pos_table), limit=24, name="embed_parts")


def layer_forward(z, pieces, seg_row, first, words=None, layer_in=None):
    seq = seg_row.shape[1]
    d = z.d
    flat = like((seq, d), BF16)
    shapes = {"q": flat, "k": flat, "v": flat, "p": like((HEADS, seq, seq), BF16), "att": flat, "n1": flat, "mid": flat}
    shapes.update({"act": like((z.groups, seq, d), BF16), "slope": like((z.groups, seq, d), BF16)})
    shapes.update({"n2": flat, "stats": like((seq, 128), F32), "small": like((16, d), F32), "out": flat})
    if first:
        shapes.update({"x": flat, "n0": flat})
    stores = Stores(shapes, split=("p", "act", "slope"))
    head = d // HEADS
    inputs = list(words) if first else [layer_in]

    def kernel(*refs):
        piece_refs, refs = refs[: len(pieces.arrays)], refs[len(pieces.arrays) :]
        row_ref, refs = refs[0], refs[1:]
        in_refs, refs = refs[: len(inputs)], refs[len(inputs) :]
        out_refs, refs = refs[: len(shapes)], refs[len(shapes) :]
        w_ref, sems, *buffers = refs
        waits = pieces.start(piece_refs, w_ref, sems, (0, 1))
        stores.bind(out_refs, buffers)
        put = stores.put
        w = Weights(z, w_ref)
        if first:
            unit, r0 = normed(sum(ref[...].astype(F32) for ref in in_refs))
            put("n0", unit)
        wait_all(waits[0])
        small = w.small()
        put("small", small)
        if first:
            x = unit * small[11:12] + small[12:13]
            x_low = x.astype(BF16)
            put("x", x_low)
        else:
            r0 = jnp.zeros((seq, 1), F32)
            x_low = in_refs[0][...]
            x = x_low.astype(F32)
        q = (w.project(x_low, 0).astype(BF16).astype(F32) * (1.0 / math.sqrt(head))).astype(BF16)
        k = w.project(x_low, 1).astype(BF16)
        v = (w.project(x_low, 2) + small[2:3]).astype(BF16)
        put("q", q)
        put("k", k)
        put("v", v)
        same = upright(row_ref[...], seq) == row_ref[...].astype(F32)
        second = iota((seq, 128), 1) >= head
        units = [(t, j) for t in range(d // 128) for j in range(2)]

        def scores_of(unit):
            t, j = unit
            lanes = slice(t * 128, (t + 1) * 128)
            picked = jnp.where(second == (j == 1), q[:, lanes], jnp.zeros((seq, 128), BF16))
            return nt(picked, k[:, lanes])

        tiles = []
        raw = scores_of(units[0])
        for n, (t, j) in enumerate(units):
            following = scores_of(units[n + 1]) if n + 1 < len(units) else None
            scores = jnp.where(same, raw, MASKED)
            scores = jnp.exp(scores - jnp.max(scores, axis=-1, keepdims=True))
            probs = (scores * (1.0 / jnp.sum(scores, axis=-1, keepdims=True))).astype(BF16)
            put("p", probs, n)
            result = nn(probs, v[:, t * 128 : (t + 1) * 128])
            if j == 0:
                kept = result
            else:
                tiles.append(jnp.where(second, result, kept).astype(BF16))
            raw = following
        attended = jnp.concatenate(tiles, axis=1)
        put("att", attended)
        unit, r1 = normed(x + (nn(attended, w.out()) + small[3:4]))
        put("n1", unit)
        middle = unit * small[0:1] + small[4:5]
        middle_low = middle.astype(BF16)
        put("mid", middle_low)
        wait_all(waits[1])
        back = [None] * (z.groups // 2)

        def pre_of(g):
            pair = slice((g // 2) * 2 * z.gw, (g // 2 + 1) * 2 * z.gw)
            return nn(middle_low[:, pair], w.fin(g))

        raw = pre_of(0)
        for g in range(z.groups):
            following = pre_of(g + 1) if g + 1 < z.groups else None
            pre = raw + small[5 + g : 6 + g]
            half = 0.5 + 0.5 * lax.erf(pre * math.sqrt(0.5))
            slope = half + pre * (jnp.exp(-0.5 * pre * pre) * (1.0 / math.sqrt(2.0 * math.pi)))
            active = (pre * half).astype(BF16)
            put("act", active, g)
            put("slope", slope, g)
            added = nn(active, w.fout(g))
            back[g // 2] = added if back[g // 2] is None else back[g // 2] + added
            raw = following
        unit, r2 = normed(middle + (jnp.concatenate(back, axis=1) + small[9:10]))
        put("n2", unit)
        put("out", unit * small[1:2] + small[10:11])
        lane = iota((seq, 128), 1)
        put("stats", jnp.where(lane == 0, r0, jnp.where(lane == 1, r1, r2)))
        stores.finish()

    outs = call(
        kernel,
        stores.shapes,
        (*pieces.arrays, seg_row, *inputs),
        specs=pieces.specs + [None] * (1 + len(inputs)),
        out_specs=stores.specs,
        scratch=pieces.scratch + stores.scratch,
        flops=12 * 10**9,
        name="layer_first" if first else "layer_second",
    )
    return dict(zip(stores.names, outs))


def send_halves(z, g_ref, keep_ref, send_ref, sems):
    core = lax.axis_index("dp") % 2
    shard = lax.axis_index("shard")
    copies = []
    for k in range(z.shards):
        to = (shard + k) % z.shards
        copies.append(pltpu.make_async_copy(g_ref.at[1 - core, to], send_ref.at[k], sems.at[2 * k]))
        copies.append(pltpu.make_async_copy(g_ref.at[core, to], keep_ref.at[k], sems.at[2 * k + 1]))
    for copy in copies:
        copy.start()
    return copies


def ffn_backward(z, pieces, state, out_grad):
    seq, d = out_grad[0].shape
    loads = Loads({**{f"dy{n}": term for n, term in enumerate(out_grad)}, **{key: state[key] for key in ("n2", "stats", "small", "mid", "act", "slope")}})
    outs = [like((seq, d), F32), like((16, d), F32)] + [like((z.shards, z.part, d), BF16)] * 2

    def kernel(*refs):
        piece_refs, refs = refs[: len(pieces.arrays)], refs[len(pieces.arrays) :]
        load_refs, refs = refs[: len(loads.names)], refs[len(loads.names) :]
        dm_ref, small_ref, keep_ref, send_ref, w_ref, sems, g_ref, out_sems, *buffers = refs
        loads.start(load_refs, buffers)
        waits = pieces.start(piece_refs, w_ref, sems, (1,))
        w = Weights(z, w_ref)
        dy = sum(loads[f"dy{n}"][...].astype(F32) for n in range(len(out_grad)))
        n2 = loads["n2"][...].astype(F32)
        scale = loads["stats"][:, 2:3]
        small = loads["small"][...]
        gain_two, shift_two = col_sum(dy * n2), col_sum(dy)
        d_final = norm_back(dy, n2, scale, small[1:2])
        d_ffn = d_final.astype(BF16)
        ffn_shift = col_sum(d_ffn.astype(F32))
        middle_t = loads["mid"][...].T
        act, slope = loads["act"], loads["slope"]
        wait_all(waits[1])
        pre_shift = []
        pair_back = [None] * (z.groups // 2)
        wide = 2 * z.gw

        def act_grad(g):
            p = g // 2
            return nt(d_ffn[:, p * wide : (p + 1) * wide], w.fout(g))

        raw = act_grad(0)
        for p in range(z.groups // 2):
            lanes = slice(p * wide, (p + 1) * wide)
            out_pair = d_ffn[:, lanes]
            back_pair = []
            for g in (2 * p, 2 * p + 1):
                following = act_grad(g + 1) if g + 1 < z.groups else None
                d_pre = (raw * slope[g].astype(F32)).astype(BF16)
                pre_shift.append(col_sum(d_pre.astype(F32)))
                back_pair.append(tn(act[g], out_pair))
                grad_in = nn(middle_t[g * z.gw : (g + 1) * z.gw], d_pre)
                g_ref[0, :, g * z.gi : (g + 1) * z.gi, :] = grad_in.astype(BF16).reshape(z.shards, z.gi, d)
                added = nt(d_pre, w.fin(g))
                pair_back[p] = added if pair_back[p] is None else pair_back[p] + added
                raw = following
            odd = iota(back_pair[0].shape, 1) >= z.gw
            both = jnp.where(odd, back_pair[1], back_pair[0]).astype(BF16)
            g_ref[1, :, :, lanes] = both.reshape(z.shards, z.part, wide)
        copies = send_halves(z, g_ref, keep_ref, send_ref, out_sems)
        dm_ref[...] = d_final + jnp.concatenate(pair_back, axis=1)
        blank = jnp.zeros((1, d), F32)
        small_ref[...] = jnp.concatenate(
            [blank, gain_two, blank, blank, blank, *pre_shift, ffn_shift, shift_two, jnp.zeros((5, d), F32)], axis=0
        )
        wait_all(copies)

    anywhere = pl.BlockSpec(memory_space=pl.ANY)
    return call(
        kernel,
        outs,
        (*pieces.arrays, *loads.arrays),
        specs=pieces.specs + loads.specs,
        out_specs=[pl.BlockSpec(memory_space=pltpu.VMEM)] * 2 + [anywhere] * 2,
        scratch=pieces.scratch + [pltpu.VMEM((2, z.shards, z.part, d), BF16), pltpu.SemaphoreType.DMA((2 * z.shards,))] + loads.scratch,
        flops=9 * 10**9,
        name="ffn_back",
    )


def attention_backward(z, pieces, state, d_middle, small_in, first, seg_row=None, pos_rows=0):
    seq, d = d_middle.shape
    head = d // HEADS
    keys = ["n1", "stats", "small", "att", "q", "k", "v", "p", "x"] + (["n0"] if first else [])
    loads = Loads({"dm": d_middle, **{key: state[key] for key in keys}, "grads": small_in, **({"seg": seg_row} if first else {})})
    rows = z.part + (2 * z.extra if first else 0)
    outs = [like((seq, d), F32)] + [like((z.shards, rows, d), BF16)] * 2
    blocks = 2 * lax.axis_size("dp")
    if first:
        outs.append(like((blocks, d // blocks, seq), BF16))
    else:
        outs.append(like((seq, d), BF16))

    def kernel(*refs):
        piece_refs, refs = refs[: len(pieces.arrays)], refs[len(pieces.arrays) :]
        load_refs, refs = refs[: len(loads.names)], refs[len(loads.names) :]
        dx_ref, keep_ref, send_ref, last_ref = refs[:4]
        de_ref = last_ref if first else None
        w_ref, sems, g_ref, out_sems, *buffers = refs[len(outs) :]
        loads.start(load_refs, buffers)
        waits = pieces.start(piece_refs, w_ref, sems, (0,))
        w = Weights(z, w_ref)
        d_middle = loads["dm"][...]
        n1 = loads["n1"][...].astype(F32)
        stats = loads["stats"][...]
        r0, r1 = stats[:, 0:1], stats[:, 1:2]
        small = loads["small"][...]
        gain_one, shift_one = col_sum(d_middle * n1), col_sum(d_middle)
        d_mid = norm_back(d_middle, n1, r1, small[0:1])
        d_branch = d_mid.astype(BF16)
        branch_shift = col_sum(d_branch.astype(F32))
        g_ref[0, :, 0 : z.part, :] = tn(loads["att"][...], d_branch).astype(BF16).reshape(z.shards, z.part, d)
        wait_all(waits[0])
        d_att = nt(d_branch, w.out()).astype(BF16)
        second = iota((seq, 128), 1) >= head
        scale = 1.0 / math.sqrt(head)
        q_ref, k_ref, v_ref, p_ref = (loads[key] for key in ("q", "k", "v", "p"))
        units = [(t, j) for t in range(d // 128) for j in range(2)]

        def probs_grad(unit):
            t, j = unit
            lanes = slice(t * 128, (t + 1) * 128)
            a_j = jnp.where(second == (j == 1), d_att[:, lanes], jnp.zeros((seq, 128), BF16))
            return nt(a_j, v_ref[:, lanes])

        dq, dk, dv = [], [], []
        raw = probs_grad(units[0])
        for n, (t, j) in enumerate(units):
            following = probs_grad(units[n + 1]) if n + 1 < len(units) else None
            lanes = slice(t * 128, (t + 1) * 128)
            probs_low = p_ref[n]
            probs = probs_low.astype(F32)
            inner = jnp.sum(probs * raw, axis=-1, keepdims=True)
            d_scores = (probs * (raw - inner)).astype(BF16)
            result = (nn(d_scores, k_ref[:, lanes]), tn(d_scores, q_ref[:, lanes]), tn(probs_low, d_att[:, lanes]))
            if j == 0:
                kept = result
            else:
                dq.append((jnp.where(second, result[0], kept[0]) * scale).astype(BF16))
                dk.append(jnp.where(second, result[1], kept[1]).astype(BF16))
                dv.append(jnp.where(second, result[2], kept[2]).astype(BF16))
            raw = following
        value_shift = col_sum(jnp.concatenate(dv, axis=1).astype(F32))
        x_t = loads["x"][...].T
        d_in = [d_mid[:, : 2 * z.gw], d_mid[:, 2 * z.gw :]]
        high = iota((z.gw, 2 * z.gw), 1) >= z.gw
        for c, parts in enumerate((dq, dk, dv)):
            d_c = jnp.concatenate(parts, axis=1)
            for p in range(z.groups // 2):
                lanes = slice(2 * p * z.gw, 2 * (p + 1) * z.gw)
                full = nn(x_t[lanes], d_c[:, lanes])
                grad = jnp.where(high, full[z.gw :], full[: z.gw]).astype(BF16)
                g_ref[1, :, c * z.gi : (c + 1) * z.gi, lanes] = grad.reshape(z.shards, z.gi, 2 * z.gw)
                d_in[p] = d_in[p] + nt(d_c[:, lanes], w.proj(c, p))
        d_in = jnp.concatenate(d_in, axis=1)
        blank = jnp.zeros((1, d), F32)
        embed_grads = [blank, blank]
        if first:
            n0 = loads["n0"][...].astype(F32)
            embed_grads = [col_sum(d_in * n0), col_sum(d_in)]
            d_embed = norm_back(d_in, n0, r0, small[11:12])
            d_embed_t = d_embed.T
            bits = blocks.bit_length() - 1
            me = lax.axis_index("section") * (blocks // 2) + lax.axis_index("dp")
            for b in range(blocks):
                to = me ^ b
                place = sum(((to >> bit) & 1) << (bits - 1 - bit) for bit in range(bits))
                de_ref[place] = d_embed_t[b * (d // blocks) : (b + 1) * (d // blocks)].astype(BF16)
            seg = loads["seg"][...]
            same = upright(seg, seq) == seg.astype(F32)
            later = iota((seq, seq), 0) < iota((seq, seq), 1)
            place = jnp.sum(jnp.where(same & later, 1.0, 0.0), axis=0, keepdims=True).astype(jnp.int32)
            spot = (iota((pos_rows, seq), 0) == place).astype(BF16)
            pos_grad = nn(spot, d_embed.astype(BF16)).astype(BF16)
        small_grads = jnp.concatenate([gain_one, blank, value_shift, branch_shift, shift_one, jnp.zeros((6, d), F32), *embed_grads, jnp.zeros((3, d), F32)], axis=0)
        small_grads = (small_grads + loads["grads"][...]).astype(BF16)
        if first:
            blank = jnp.zeros((z.extra - z.quarter, d), BF16)
            others = [pos_grad[z.pos + n * z.quarter : z.pos + (n + 1) * z.quarter] for n in range(4)]
        for h in range(z.shards):
            g_ref[1, h, z.at_small : z.at_small + 16, :] = small_grads
            spare = pos_grad[: z.pos] if first and h == 0 else jnp.zeros((z.pos, d), BF16)
            g_ref[1, h, z.at_small + 16 : z.part, :] = spare
            if first:
                for side in range(2):
                    for y in range(2):
                        row = z.part + y * z.extra
                        part = jnp.concatenate([others[2 * side + y].astype(F32), blank.astype(F32)], axis=0).astype(BF16) if h == 0 else jnp.zeros((z.extra, d), BF16)
                        g_ref[side, h, row : row + z.extra, :] = part
        copies = send_halves(z, g_ref, keep_ref, send_ref, out_sems)
        dx_ref[...] = d_in
        if not first:
            last_ref[...] = d_in.astype(BF16)
        wait_all(copies)

    anywhere = pl.BlockSpec(memory_space=pl.ANY)
    vmem = pl.BlockSpec(memory_space=pltpu.VMEM)
    return call(
        kernel,
        outs,
        (*pieces.arrays, *loads.arrays),
        specs=pieces.specs + loads.specs,
        out_specs=[vmem, anywhere, anywhere, vmem],
        scratch=pieces.scratch + [pltpu.VMEM((2, z.shards, rows, d), BF16), pltpu.SemaphoreType.DMA((2 * z.shards,))] + loads.scratch,
        flops=13 * 10**9,
        name="att_back",
    )


def add_cores_split(z, keep, came):
    shards, part, d = keep[0].shape

    def kernel(a_ref, f_ref, b_ref, e_ref, c0, c1, c2a, c2b, c3):
        for k, ref in ((0, c0), (1, c1), (3, c3)):
            ref[:part] = a_ref[k] + b_ref[k]
            ref[part:] = f_ref[k] + e_ref[k]
        c2a[...] = a_ref[2] + b_ref[2]
        c2b[...] = f_ref[2] + e_ref[2]

    full, half = like((2 * part, d), BF16), like((part, d), BF16)
    return call(kernel, [full, full, half, half, full], (*keep, *came), limit=24, name="add_cores_split")


def halves_by_y(z, terms):
    def kernel(a_ref, b_ref, c_ref, keep_ref, send_ref):
        y = side_of(2)
        for ref, part in ((keep_ref, y), (send_ref, 1 - y)):
            span = pl.ds(pl.multiple_of(part * z.part, z.part), z.part)
            ref[...] = (a_ref[span].astype(F32) + b_ref[span].astype(F32) + c_ref[span].astype(F32)).astype(BF16)

    return call(kernel, [like((z.part, z.d), BF16)] * 2, terms, limit=8, name="halves_by_y")


def add_core(z, keep_a, came_a, keep_f, came_f):
    rows = z.part + z.extra

    def kernel(a_ref, b_ref, c_ref, e_ref, keep_ref, send_ref):
        y = side_of(2)

        def place(ref, part):
            if part == 0:
                ref[:, : z.part] = a_ref[:, : z.part] + b_ref[:, : z.part]
            else:
                ref[:, : z.part] = c_ref[...] + e_ref[...]
            span = slice(z.part + part * z.extra, z.part + (part + 1) * z.extra)
            ref[:, z.part :] = a_ref[:, span] + b_ref[:, span]

        @pl.when(y == 0)
        def _():
            place(keep_ref, 0)
            place(send_ref, 1)

        @pl.when(y == 1)
        def _():
            place(keep_ref, 1)
            place(send_ref, 0)

    return call(kernel, [like((z.shards, rows, z.d), BF16)] * 2, (keep_a, came_a, keep_f, came_f), limit=24, name="add_core")


def add_split(kept, came):
    _, rows, d = kept.shape
    half = rows // 32 * 16

    def kernel(a_ref, b_ref, c0, c1, c2a, c2b, c3):
        for k, ref in ((0, c0), (1, c1), (3, c3)):
            ref[...] = a_ref[k] + b_ref[k]
        c2a[...] = a_ref[2, :half] + b_ref[2, :half]
        c2b[...] = a_ref[2, half:] + b_ref[2, half:]

    full = like((rows, d), BF16)
    outs = [full, full, like((half, d), BF16), like((rows - half, d), BF16), full]
    return call(kernel, outs, (kept, came), limit=16, name="add_split")


def head_forward(pieces, table):
    count = sum(piece.shape[0] for piece in pieces)
    vocab, d = table.shape
    tiles = 3
    block = vocab // tiles
    part = block // 2
    chunk = 256
    many = len(pieces)

    def kernel(*refs):
        piece_refs, (w_ref, ctx_ref, lse_ref, x_ref, m_ref, s_ref, acc_ref) = refs[:many], refs[many:]
        step = pl.program_id(0)

        @pl.when(step == 0)
        def _():
            at = 0
            for ref in piece_refs:
                x_ref[at : at + ref.shape[0]] = ref[...]
                at += ref.shape[0]
            m_ref[...] = jnp.full(m_ref.shape, -1e30, F32)
            s_ref[...] = jnp.zeros(s_ref.shape, F32)
            acc_ref[...] = jnp.zeros(acc_ref.shape, F32)

        units = [(c, r) for c in range(2) for r in range(count // chunk)]

        def logits_of(unit):
            c, r = unit
            return nt(x_ref[r * chunk : (r + 1) * chunk], w_ref[c * part : (c + 1) * part])

        logits = logits_of(units[0])
        for n, (c, r) in enumerate(units):
            following = logits_of(units[n + 1]) if n + 1 < len(units) else None
            span = slice(r * chunk, (r + 1) * chunk)
            old = m_ref[span]
            new = jnp.maximum(old, jnp.max(logits, axis=-1, keepdims=True))
            keep = jnp.exp(old - new)
            weight = jnp.exp(logits - new)
            s_ref[span] = s_ref[span] * keep + jnp.sum(weight, axis=-1, keepdims=True)
            acc_ref[span] = acc_ref[span] * keep + nn(weight.astype(BF16), w_ref[c * part : (c + 1) * part])
            m_ref[span] = new
            logits = following

        @pl.when(step == tiles - 1)
        def _():
            total = s_ref[...]
            ctx_ref[...] = acc_ref[...] * (1.0 / total)
            lse = m_ref[...] + jnp.log(total)
            lse_ref[...] = jnp.broadcast_to(lse, (count, 128)).T[0:8]

    fixed = lambda i: (0, 0)
    return call(
        kernel,
        [like((count, d), F32), like((8, count), F32)],
        (*pieces, table),
        specs=[pl.BlockSpec(piece.shape, fixed) for piece in pieces] + [pl.BlockSpec((block, d), lambda i: (i, 0))],
        out_specs=[pl.BlockSpec((count, d), fixed), pl.BlockSpec((8, count), fixed)],
        scratch=[pltpu.VMEM((count, d), BF16), pltpu.VMEM((count, 1), F32), pltpu.VMEM((count, 1), F32), pltpu.VMEM((count, d), F32)],
        grid=(tiles,),
        flops=11 * 10**9,
        limit=36,
        name="head_forward",
    )


def head_combine(seq, ctxs, picked, ids_by, lses, vocab):
    shards = ids_by.shape[0]
    d = picked.shape[1]

    def kernel(x0_ref, x1_ref, x2_ref, x3_ref, p_ref, i_ref, a_ref, b_ref, c_ref, e_ref, *outs):
        lse_ref = outs[shards]
        shard = lax.axis_index("shard")
        parts = (a_ref, b_ref, c_ref, e_ref)
        for k in range(shards):
            rows = [parts[m][:, ((k - m) % shards) * seq : ((k - m) % shards + 1) * seq] for m in range(shards)]
            top = rows[0]
            for row in rows[1:]:
                top = jnp.maximum(top, row)
            total = top + jnp.log(sum(jnp.exp(row - top) for row in rows))
            whole = upright(total, seq)
            span = slice(k * seq, (k + 1) * seq)
            lse_ref[span] = whole
            weight = upright(jnp.exp(rows[0] - total), seq)
            local = i_ref[k, 1:2] - shard * vocab
            inside = upright(jnp.where((local >= 0) & (local < vocab), 1.0, 0.0), seq)
            hit = jnp.where(inside > 0.5, p_ref[span].astype(F32), 0.0)
            ctx = (x0_ref, x1_ref, x2_ref, x3_ref)[k][...]
            outs[k][...] = (ctx * weight - hit).astype(BF16)

    return call(
        kernel,
        [like((seq, d), BF16)] * shards + [like((shards * seq, 1), F32)],
        (*ctxs, picked, ids_by, *lses),
        limit=20, name="head_combine",
    )


def head_table(pieces, table, lse, ids_by, core=None):
    count = sum(piece.shape[0] for piece in pieces)
    shards, _, seq = ids_by[0].shape
    vocab, d = table.shape
    block = 1280
    tiles = pl.cdiv(vocab, block)
    shared = core is not None
    if shared:
        tiles = (tiles + 1) // 2
    else:
        core = jnp.zeros((1,), jnp.int32)
    chunk = 256
    many, groups = len(pieces), len(ids_by)
    wide = d // 8

    def kernel(core_ref, *refs):
        piece_refs, refs = refs[:many], refs[many:]
        w_ref, refs = refs[0], refs[1:]
        lse_refs, i_refs, refs = refs[:groups], refs[groups : 2 * groups], refs[2 * groups :]
        out_refs, (x_ref, xt_ref, t_ref, l_ref, p_ref) = refs[:-5], refs[-5:]
        step = pl.program_id(0)
        first_tile = core_ref[0] * tiles

        @pl.when(step == 0)
        def _():
            at = 0
            for ref in piece_refs:
                x_ref[at : at + ref.shape[0]] = ref[...]
                at += ref.shape[0]
            xt_ref[...] = x_ref[...].T
            start = lax.axis_index("shard") * vocab + first_tile * block
            for n in range(groups):
                for k in range(shards):
                    at = (n * shards + k) * seq
                    t_ref[at : at + seq] = upright(i_refs[n][k, 1:2] - start, seq).astype(jnp.int32)
                at = n * shards * seq
                l_ref[at : at + shards * seq] = lse_refs[n][...]

        w = w_ref[...]
        for r in range(count // chunk):
            span = slice(r * chunk, (r + 1) * chunk)
            logits = nt(x_ref[span], w)
            hit = iota(logits.shape, 1) == t_ref[span] - step * block
            p_ref[span] = (jnp.exp(logits - l_ref[span]) - jnp.where(hit, 1.0, 0.0)).astype(BF16)
        result = nn(xt_ref[...], p_ref[...]).astype(BF16)
        if not shared:
            out_refs[0][...] = result
            return
        zero = jnp.zeros((wide, block), jnp.int32)
        first = zero + lax.axis_index("section") == 0
        front = zero + side_of(2) == 0
        blocks = [result[n * wide : (n + 1) * wide] for n in range(8)]
        for n in range(2):
            low, high = blocks[2 * n], blocks[4 + 2 * n]
            out_refs[0][n], out_refs[1][n] = jnp.where(first, low, high), jnp.where(first, high, low)
            low, high = blocks[4 * n + 1], blocks[4 * n + 3]
            out_refs[2][n], out_refs[3][n] = jnp.where(front, low, high), jnp.where(front, high, low)

    if shared:
        outs = [like((2, wide, tiles * block), BF16)] * 4
        out_specs = [pl.BlockSpec((2, wide, block), lambda i, c: (0, 0, i))] * 4
    else:
        outs, out_specs = [like((d, vocab), BF16)], [pl.BlockSpec((d, block), lambda i, c: (0, i))]
    fixed = lambda i, c: (0, 0)
    return pl.pallas_call(
        kernel,
        out_shape=outs,
        grid_spec=pltpu.PrefetchScalarGridSpec(
            num_scalar_prefetch=1,
            grid=(tiles,),
            in_specs=[pl.BlockSpec(piece.shape, fixed) for piece in pieces]
            + [pl.BlockSpec((block, d), lambda i, c: (i + c[0] * tiles, 0))]
            + [pl.BlockSpec((shards * seq, 1), fixed)] * groups
            + [pl.BlockSpec(ids_by[0].shape, lambda i, c: (0, 0, 0))] * groups,
            out_specs=out_specs,
            scratch_shapes=[
                pltpu.VMEM((count, d), BF16),
                pltpu.VMEM((d, count), BF16),
                pltpu.VMEM((count, 1), jnp.int32),
                pltpu.VMEM((count, 1), F32),
                pltpu.VMEM((count, block), BF16),
            ],
        ),
        compiler_params=pltpu.CompilerParams(vmem_limit_bytes=58 * MIB),
        cost_estimate=pl.CostEstimate(flops=32 * 10**9, bytes_accessed=0, transcendentals=0),
        name="head_table",
    )(core, *pieces, table, *lse, *ids_by)


def add_halves(even, odd):
    shape = even[0].shape[1:]

    def kernel(a_ref, b_ref, c_ref, e_ref, *outs):
        for n, (one, two, side) in enumerate(((a_ref, b_ref, side_of(2)), (c_ref, e_ref, lax.axis_index("section")))):
            outs[2 * n][...] = one[side] + two[side]
            outs[2 * n + 1][...] = one[1 - side] + two[1 - side]

    return call(kernel, [like(shape, BF16)] * 4, (*even, *odd), limit=32, name="add_halves")


def add_last(even, odd):
    def kernel(a_ref, b_ref, c_ref, e_ref, own_ref, send_ref):
        first = (jnp.zeros(a_ref.shape, jnp.int32) + side_of(1)) == 0
        low, high = a_ref[...] + b_ref[...], c_ref[...] + e_ref[...]
        own_ref[...] = jnp.where(first, low, high)
        send_ref[...] = jnp.where(first, high, low)

    return call(kernel, [like(even[0].shape, BF16)] * 2, (*even, *odd), limit=16, name="add_last")


def list_tokens(ids, vocab):
    count = ids.shape[1]
    unit = 1 << (vocab - 1).bit_length()

    def kernel(ids_ref, list_ref):
        start = lax.axis_index("shard") * vocab

        def step(i, many):
            local = ids_ref[0, i] - start
            list_ref[0, many] = i * unit + local
            return many + ((local >= 0) & (local < vocab)).astype(jnp.int32)

        list_ref[0, count] = lax.fori_loop(0, count, step, jnp.int32(0), unroll=8)

    smem = pl.BlockSpec(memory_space=pltpu.SMEM)
    return call(kernel, [like((1, count + 128), jnp.int32)], (ids,), specs=[smem], out_specs=[smem], limit=4, name="list_tokens")[0]


def table_grad(dense, pieces, lists, vocab):
    width = pieces[0].shape[1]
    arrays = dense
    sources, _, seq = pieces[0].shape
    shards = 4
    listed = shards * seq
    line = lists.shape[1]
    unit = 1 << (vocab - 1).bit_length()
    ways, each = 4, 4
    rows = (lists & (unit - 1)).reshape(-1)
    tokens = ((lists >> (unit.bit_length() - 1)) + listed * jnp.arange(sources, dtype=jnp.int32)[:, None]).reshape(-1)
    counts = lists[:, listed]

    def kernel(*refs):
        d_refs, refs = refs[: len(arrays)], refs[len(arrays) :]
        own_ref, later_ref, before_ref, far_a_ref, far_b_ref, r_ref, t_ref, n_ref, o_ref, flat_ref, *acc = refs
        half = sources // 2
        for j in range(sources):
            far = far_a_ref[j] if j < half else far_b_ref[j - half]
            for k, block in enumerate((own_ref[j], later_ref[j], before_ref[j], far)):
                at = j * listed + k * seq
                flat_ref[at : at + seq] = block.astype(F32).T
        for ref in acc:
            ref[...] = jnp.zeros(ref.shape, F32)

        def source(j, carry):
            many = n_ref[j]
            rounds = many // (ways * each)

            def step(i, carry):
                at = j * line + i * ways * each
                place = [r_ref[at + n] for n in range(ways * each)]
                value = [flat_ref[pl.ds(t_ref[at + n], 1), :] for n in range(ways * each)]
                for n in range(each):
                    old = [ref[pl.ds(place[n * ways + way], 1), :] for way, ref in enumerate(acc)]
                    for way, ref in enumerate(acc):
                        ref[pl.ds(place[n * ways + way], 1), :] = old[way] + value[n * ways + way]
                return carry

            def rest(at, carry):
                acc[0][pl.ds(r_ref[j * line + at], 1), :] += flat_ref[pl.ds(t_ref[j * line + at], 1), :]
                return carry

            lax.fori_loop(0, rounds, step, jnp.int32(0))
            lax.fori_loop(rounds * ways * each, many, rest, jnp.int32(0))
            return carry

        lax.fori_loop(0, sources, source, jnp.int32(0))
        if len(d_refs) == 1:
            o_ref[...] = d_refs[0][...].astype(F32) + sum(ref[...] for ref in acc).T
            return
        half = d_refs[0].shape[1]
        first = (jnp.zeros((width, half), jnp.int32) + side_of(1)) == 0
        own, other = d_refs[0][...], d_refs[1][...]
        o_ref[:, :half] = jnp.where(first, own, other).astype(F32) + sum(ref[:half] for ref in acc).T
        last = jnp.where(first, other, own)[:, : vocab - half]
        o_ref[:, half:] = last.astype(F32) + sum(ref[half:] for ref in acc).T

    smem = pl.BlockSpec(memory_space=pltpu.SMEM)
    return call(
        kernel,
        [like((width, vocab), F32)],
        (*arrays, *pieces, rows, tokens, counts),
        specs=[None] * (len(arrays) + 5) + [smem] * 3,
        scratch=[pltpu.VMEM((sources * listed, width), F32)] + [pltpu.VMEM((vocab, width), F32)] * ways,
        limit=60,
        name="table_grad",
    )[0]


def unpack_grads(z, blocks):
    rows = z.part + z.extra
    pos_rows = z.pos + 4 * z.quarter

    def kernel(own_ref, y_ref, core_ref, both_ref, qkv_ref, out_ref, fin_ref, fout_ref, gain_ref, bias_ref, pos_ref, eg_ref, es_ref, all_ref):
        core, y = side_of(1), side_of(2)
        shard = lax.axis_index("shard")
        all_ref[core, y] = own_ref[...]
        all_ref[core, 1 - y] = y_ref[...]
        all_ref[1 - core, y] = core_ref[...]
        all_ref[1 - core, 1 - y] = both_ref[...]

        def own_lanes(value):
            total = jnp.zeros((value.shape[0], z.part), F32)
            for h in range(z.shards):
                total = total + jnp.where(shard == h, value[:, h * z.part : (h + 1) * z.part], 0.0)
            return total

        out_ref[...] = all_ref[0, 0, : z.part].astype(F32)
        fin_ref[...] = all_ref[0, 1, : z.part].astype(F32).reshape(z.groups, z.gi, z.d)
        for c in range(3):
            part = all_ref[1, 0, c * z.gi : (c + 1) * z.gi].astype(F32)
            for g in range(z.groups):
                qkv_ref[c, g] = part[:, g * z.gw : (g + 1) * z.gw]
        part = all_ref[1, 1, : z.part].astype(F32)
        for g in range(z.groups):
            fout_ref[g] = part[:, g * z.gw : (g + 1) * z.gw]
        small = own_lanes(all_ref[1, 0, z.at_small : z.at_small + 16].astype(F32))
        for n in range(9):
            bias_ref[n] = small[2 + n : 3 + n]
        gain_ref[...] = small[0:2]
        eg_ref[...] = small[11:12]
        es_ref[...] = small[12:13]
        pos_ref[: z.pos] = all_ref[1, 0, z.at_small + 16 : z.part].astype(F32)
        for n in range(4):
            row = z.pos + n * z.quarter
            pos_ref[row : row + z.quarter] = all_ref[n // 2, n % 2, z.part :].astype(F32)[: z.quarter]

    return call(
        kernel,
        [
            like((3, z.groups, z.gi, z.gw), F32),
            like((z.part, z.d), F32),
            like((z.groups, z.gi, z.d), F32),
            like((z.groups, z.part, z.gw), F32),
            like((2, z.part), F32),
            like((9, 1, z.part), F32),
            like((pos_rows, z.d), F32),
            like((1, z.part), F32),
            like((1, z.part), F32),
        ],
        blocks,
        scratch=[pltpu.VMEM((2, 2, rows, z.d), BF16)],
        limit=16, name="unpack",
    )


def body(token_ids, targets, segment_ids, word_table, pos_table, embed_gain, embed_shift, qkv_weight, out_weight, ffn_in, ffn_out, layer_gains, layer_biases):
    micro, _, seq = token_ids.shape
    vocab, d = word_table.shape
    pos_rows = pos_table.shape[0]
    shards = lax.axis_size("shard")
    dp = lax.axis_size("dp")
    both = ("section", "dp")
    section = lax.axis_index("section")
    first = section == 0
    z = Sizes(qkv_weight.shape, out_weight.shape, shards, pos_rows)
    offset = lax.axis_index("shard") * vocab

    local, pair, packed = pack_weights(
        z, qkv_weight[0], out_weight[0], ffn_in[0], ffn_out[0], layer_gains[0], layer_biases[0], embed_gain, embed_shift
    )

    mine = lax.dynamic_index_in_dim(jnp.stack([token_ids[:, 0], targets[:, 0], segment_ids[:, 0]], axis=1), section, 0, keepdims=False)
    mine = after(mine, packed)
    ids_by = jnp.stack([mine, turned(mine, "shard", -1), turned(mine, "shard", 2), turned(mine, "shard", 1)])
    seg_row = mine[2:3]

    def rows_of(ids):
        return word_table.at[jnp.clip(ids.reshape(-1) - offset, 0, vocab - 1)].get(mode="promise_in_bounds")

    cross_pair = crossed(pair, "section", 1)
    near = gather_first(packed, "shard")
    picked = rows_of(ids_by[:, 0])
    near, pos_table = after((near, pos_table), near)
    word_parts = embed_parts(picked, ids_by, pos_table, vocab)
    near = after(near, word_parts)
    c0, c1, c2a, c2b, c3 = word_parts
    half, quarter = seq // 2, z.part // 2
    right = jnp.concatenate([c2a, near[0][:quarter]], axis=0)
    left = jnp.concatenate([c2b, near[1][quarter:]], axis=0)
    near_rows = jnp.concatenate(after(near, (right, left)), axis=0)
    right, left = turned(right, "shard", 1), turned(left, "shard", -1)
    near_y = crossed(near_rows, "dp", 2)
    cross_near = crossed(near_rows, "section", 1)
    target_rows = rows_of(after(ids_by[:, 1], near_rows))
    right, left = after((right, left), target_rows)
    c1 = jnp.concatenate([c1[:half] + right[:half], c1[half:]], axis=0)
    c3 = jnp.concatenate([c3[:half], c3[half:] + left[:half]], axis=0)
    words = scatter_second(c0, c1, c3, "shard")
    near_y = after(near_y, words)
    far = jnp.concatenate([right[half:], left[half:]], axis=0)
    cross_far = crossed(far, "section", 1)
    both_y = crossed(jnp.concatenate([far, cross_near], axis=0), "dp", 2)
    far_y, cross_near_y = both_y[: z.part], both_y[z.part :]
    cross_far_y = crossed(cross_far, "dp", 2)
    mine = (near_rows, far)
    mine = (*mine, *(crossed(b, "dp", 1) for b in mine), near_y, far_y, crossed(near_y, "dp", 1), crossed(far_y, "dp", 1))
    others = (cross_near, cross_far)
    others = (*others, *(crossed(b, "dp", 1) for b in others))
    others = (*others, cross_near_y, cross_far_y, crossed(cross_near_y, "dp", 1), crossed(cross_far_y, "dp", 1))
    pairs = (cross_pair, crossed(cross_pair, "dp", 1))
    weights_one, weights_two = (Pieces(z, local, mine, pairs, others, layer) for layer in range(2))
    one = layer_forward(z, weights_one, seg_row, True, words=words)
    two = layer_forward(z, weights_two, seg_row, False, layer_in=one["out"])
    two["x"] = one["out"]

    own_out = jnp.where(first, one["out"], two["out"])
    came_out = crossed(jnp.where(first, two["out"], one["out"]), "section", 1)

    before, later = gather_first(two["out"], "shard")
    ctx_own, lse_own = head_forward([two["out"]], word_table)
    before = after(before, ctx_own)
    far_a = turned(before[: seq // 2], "shard", 1)
    ctx_before, lse_before = head_forward([before], word_table)
    later = after(later, ctx_before)
    far_b = turned(later[seq // 2 :], "shard", -1)
    ctx_later, lse_later = head_forward([later], word_table)
    far_a, far_b = after((far_a, far_b), ctx_later)
    ctx_far, lse_far = head_forward([far_a, far_b], word_table)
    lse = jnp.concatenate([lse_own[0:1], lse_later[0:1], lse_far[0:1], lse_before[0:1]], axis=1)
    listed = jnp.stack([ids_by[0, 0], ids_by[1, 0], ids_by[3, 0], ids_by[2, 0]]).reshape(1, -1)
    lses = (lse, turned(lse, "shard", -1), turned(lse, "shard", 2), turned(lse, "shard", 1))
    lses = after(lses, came_out)
    *parts, whole_lse = head_combine(seq, (ctx_own, ctx_later, ctx_far, ctx_before), target_rows, ids_by, lses, vocab)
    head_rows = [two["out"], later, far_a, far_b, before]
    dy_terms = direct_scatter(parts, "shard")
    if dp == 4:
        rows_other, ids_other, lse_other = [crossed(row, "dp", 1) for row in head_rows], crossed(ids_by, "dp", 1), crossed(whole_lse, "dp", 1)
        core = side_of(1).astype(jnp.int32).reshape(1)
        stay_x, leave_x, stay_y, leave_y = head_table([*head_rows, *rows_other], word_table, [whole_lse, lse_other], [ids_by, ids_other], core)
        came_x, came_y = crossed(leave_x, "section", 1), crossed(leave_y, "dp", 2)
        dy_terms = after(dy_terms, stay_x)
    else:
        dense = head_table(head_rows, word_table, [whole_lse], [ids_by])[0]
        dense = [lax.psum_scatter(dense, both, scatter_dimension=0, tiled=True)]
    d_middle, small_grads, keep_f, send_f = ffn_backward(z, weights_two, two, dy_terms)

    in_two, keep_a, send_a, in_low = attention_backward(z, weights_two, two, d_middle, small_grads, False)
    came_f, came_a = crossed(send_f, "dp", 1), crossed(send_a, "dp", 1)
    d_middle, small_grads, keep_one_f, send_one_f = ffn_backward(z, weights_one, one, [in_low])
    keep_f, came_f, keep_a, came_a = after((keep_f, came_f, keep_a, came_a), d_middle)
    split_two = add_cores_split(z, (keep_a, keep_f), (came_a, came_f))
    d_middle = after(d_middle, split_two)
    terms_two = scatter_first(*split_two, "shard")
    if dp == 4:
        d_middle, came_x, came_y = after((d_middle, came_x, came_y), ())
    came_one_f = crossed(send_one_f, "dp", 1)
    in_one, keep_one_a, send_one_a, d_embed = attention_backward(z, weights_one, one, d_middle, small_grads, True, seg_row, pos_rows)
    keep_one_f, came_one_f = after((keep_one_f, came_one_f), d_embed)
    send_one_a, d_embed = after((send_one_a, d_embed), terms_two)
    came_one_a = crossed(send_one_a, "dp", 1)
    columns = d_embed[None]
    steps = [("dp", 1 << n) for n in range(dp.bit_length() - 1)]
    for n, (axis, bit) in enumerate(steps):
        middle = columns.shape[1] // 2
        columns = jnp.concatenate([columns[:, :middle], crossed(columns[:, middle:], axis, bit)], axis=0)
        if n == 0:
            came_one_a = after(came_one_a, columns)
    second_two = scatter_second(*terms_two, "shard")
    stay_one, leave_one = add_core(z, keep_one_a, came_one_a, keep_one_f, came_one_f)
    came_one = crossed(after(leave_one, columns), "dp", 2)
    columns = after(columns, (stay_one, second_two))
    columns = jnp.concatenate([columns[:, 0], crossed(columns[:, 1], "section", 1)], axis=0)
    ring_columns = gather_first(columns, "shard")
    own_in = jnp.where(first, in_one, in_two)
    came_in = crossed(jnp.where(first, in_two, in_one).astype(BF16), "section", 1)
    stay_two, leave_two = halves_by_y(z, after(second_two, (columns, stay_one)))
    came_two = crossed(leave_two, "dp", 2)
    if dp == 4:
        stay_x, leave_x, stay_y, leave_y = add_halves(*after(((stay_x, came_x), (stay_y, came_y)), stay_two))
        last_x, last_y = crossed(leave_x, "dp", 2), crossed(leave_y, "section", 1)
    lists = list_tokens(after(listed, columns), vocab)
    bit = 1
    while bit < dp:
        lists = jnp.concatenate([lists, crossed(lists, "dp", bit)], axis=0)
        bit *= 2
    lists = jnp.concatenate([lists, crossed(lists, "section", 1)], axis=0)
    ring_columns = after(ring_columns, stay_two)
    far_columns = gather_second(*ring_columns, "shard")
    terms_one = scatter_first(*add_split(stay_one, after(came_one, (ring_columns, came_in))), "shard")
    second_one = scatter_second(*terms_one, "shard")
    if dp == 4:
        own_dense, send_dense = add_last(*after(((stay_x, last_x), (stay_y, last_y)), second_one[1]))
        dense = [own_dense, crossed(send_dense, "dp", 1)]
    word_grad = table_grad(dense, (columns, ring_columns[1], ring_columns[0], *far_columns), lists, vocab)
    sum_two = stay_two + came_two
    sum_one = sum(after(second_one, sum_two))
    layer_one, extra = sum_one[: z.part], sum_one[z.part :]
    row = jnp.arange(z.part)[:, None]
    embed_rows = (row >= z.at_small + 11) & (side_of(1) == 1) & (side_of(2) == 0)
    layer_two = jnp.where(embed_rows, layer_one, sum_two)
    total = jnp.concatenate([jnp.where(first, layer_one, layer_two), extra], axis=0)
    came = crossed(jnp.concatenate([jnp.where(first, layer_two, layer_one), extra], axis=0), "section", 1)
    total = total + after(came, word_grad)
    bit = 4
    while bit < dp:
        total = total + crossed(total, "dp", bit)
        bit *= 2
    total_y = crossed(total, "dp", 2)
    def by_micro(own, came):
        return jnp.stack([jnp.where(first, own, came), jnp.where(first, came, own)]).reshape(1, micro, 1, seq, d)

    layer_outputs = by_micro(own_out, came_out)
    input_grads = by_micro(own_in, came_in.astype(F32))
    total_y = after(total_y, (layer_outputs, input_grads))
    unpacked = unpack_grads(z, (total, total_y, crossed(total, "dp", 1), crossed(total_y, "dp", 1)))

    word_grad = word_grad.T

    qkv_g, out_g, fin_g, fout_g, gain_g, bias_g, pos_g, eg_g, es_g = unpacked
    return (
        layer_outputs,
        input_grads,
        word_grad,
        pos_g,
        eg_g.reshape(-1),
        es_g.reshape(-1),
        qkv_g[None],
        out_g[None],
        fin_g[None],
        fout_g[None],
        gain_g[None],
        bias_g.transpose(1, 0, 2),
    )


def solution(mesh):
    rows = P(None, ("dp", "shard"), None)
    weights = (
        P("section", None, None, "shard", None),
        P("section", "shard", None),
        P("section", None, "shard", None),
        P("section", None, "shard", None),
        P("section", None, "shard"),
        P("section", None, "shard"),
    )
    states = P("section", None, ("dp", "shard"), None, None)
    return jax.shard_map(
        body,
        mesh=mesh,
        in_specs=(rows, rows, rows, P("shard", None), P("shard", None), P("shard"), P("shard"), *weights),
        out_specs=(states, states, P("shard", ("section", "dp")), P("shard", None), P("shard"), P("shard"), *weights),
        check_vma=False,
    )
```
